32 devices in a mesh: dp: 8 (over z, x), tensor: 4 (over y, core).
Axes of the slice: x: 2, y: 2, z: 4, core: 2. Of those that a mesh axis runs over, the one named last changes fastest.
Arguments:
- hidden_in: bfloat16 [16384, 1536], P('dp'), may hold values from -6 to 6
- out_grad: bfloat16 [16384, 1536], P('dp'), may hold values from -6 to 6
- seq_lengths: int32 [8, 4], P('dp'), may hold values from 0 to 2048, as said below
- owner_map: int32 [36], replicated, may hold values from 0 to 39, as said below
- muon_master: float32 [40, 1536, 256], P('dp', None, 'tensor')
- muon_moment: float32 [40, 1536, 256], P('dp', None, 'tensor'), may hold values from -224 to 224
- state_proj: float32 [1536, 256], replicated, may hold values from -0.15625 to 0.15625
- state_moment: float32 [1536, 256], replicated, may hold values from -32 to 32
- step_proj: float32 [1536, 48], P(None, 'tensor'), may hold values from -0.15625 to 0.15625
- step_moment: float32 [1536, 48], P(None, 'tensor'), may hold values from -32 to 32
- norm_gain: float32 [1536], replicated, may hold values from 0.5 to 1.5
- gain_moment: float32 [1536], replicated, may hold values from -32 to 32
- head_params: float32 [3, 48], P(None, 'tensor')
- head_moment: float32 [3, 48], P(None, 'tensor'), may hold values from -32 to 32
- conv_params: float32 [6, 3072], P(None, 'tensor')
- conv_moment: float32 [6, 3072], P(None, 'tensor'), may hold values from -32 to 32
- state_conv: float32 [5, 256], replicated, may hold values from -0.5 to 0.5
- state_conv_moment: float32 [5, 256], replicated, may hold values from -32 to 32
Outputs:
- block_out: bfloat16 [16384, 1536], P('dp')
- input_grad: bfloat16 [16384, 1536], P('dp')
- muon_moment_new: float32 [40, 1536, 256], P('dp', None, 'tensor')
- muon_master_new: float32 [40, 1536, 256], P('dp', None, 'tensor')
- state_moment_new: float32 [1536, 256], replicated
- state_proj_new: float32 [1536, 256], replicated
- step_moment_new: float32 [1536, 48], P(None, 'tensor')
- step_proj_new: float32 [1536, 48], P(None, 'tensor')
- gain_moment_new: float32 [1536], replicated
- norm_gain_new: float32 [1536], replicated
- head_moment_new: float32 [3, 48], P(None, 'tensor')
- head_params_new: float32 [3, 48], P(None, 'tensor')
- conv_moment_new: float32 [6, 3072], P(None, 'tensor')
- conv_params_new: float32 [6, 3072], P(None, 'tensor')
- state_conv_moment_new: float32 [5, 256], replicated
- state_conv_new: float32 [5, 256], replicated
The draws below stay inside these ranges and needn't reach their ends.
Inputs may be any that keep to these rules, and one draw needn't show every extreme that they name: `seq_lengths`: each row sums to at most 2048; zero lengths stand for unused sequence slots; in every draw some index of dp holds one sequence of exactly 2048 tokens. `owner_map`: distinct slots; slots 0 and 39 are always named.
All inputs are finite; a program needn't handle non-finite values.
Results may differ from the reference program's by a relative error of at most 0.012.
Values may be sent and summed in bfloat16 or wider, within the bound.
A program may use at most 256 MiB of HBM per device.

```python
import math
import jax
import jax.numpy as jnp
from jax import lax

D = 1536
HEADS = 48
HEADDIM = 64
D_STATE = 128
SCAN_BLOCK = 256
NS_STEPS = 5
TOK_DEV = 2048
SEQ_DEV = 4
D_INNER = 3072
TOKENS = 16384
HEADS_TP = 12
MATS_TP = 36
SLOTS_ALL = 40
N_DP = 8
N_TENSOR = 4


def draw_seq_lengths(key, part):
    key = jax.random.fold_in(key, 11)
    key_full, key_total, key_cut = jax.random.split(key, 3)
    full_device = jax.random.randint(key_full, (), 0, N_DP)
    totals = jax.random.randint(key_total, (N_DP, 1), TOK_DEV // 2, TOK_DEV + 1)
    cut_points = jax.random.randint(key_cut, (N_DP, SEQ_DEV - 1), 0, totals + 1)
    cut_points = jnp.sort(cut_points, axis=1)
    bounds = jnp.concatenate([jnp.zeros((N_DP, 1), jnp.int32), cut_points, totals], axis=1)
    lengths = bounds[:, 1:] - bounds[:, :-1]
    full_row = jnp.zeros((SEQ_DEV,), jnp.int32).at[0].set(TOK_DEV)
    chosen = (jnp.arange(N_DP) == full_device)[:, None]
    return jnp.where(chosen, full_row[None, :], lengths).astype(jnp.int32)


def draw_owner_map(key, part):
    key = jax.random.fold_in(key, 12)
    key_pick, key_order = jax.random.split(key)
    middle = jax.random.permutation(key_pick, SLOTS_ALL - 2)[:MATS_TP - 2] + 1
    values = jnp.concatenate([jnp.array([0, SLOTS_ALL - 1], jnp.int32), middle.astype(jnp.int32)])
    return values[jax.random.permutation(key_order, MATS_TP)].astype(jnp.int32)


def draw_muon_master(key, part):
    key = jax.random.fold_in(key, 13)
    full_shape = (SLOTS_ALL, D, N_TENSOR * HEADDIM)
    normal_part = jax.random.normal(key, full_shape, jnp.float32)
    rising = jnp.linspace(0.75, 1.3, full_shape[2])
    return normal_part * rising[None, None, :] * D ** (-0.5)


def draw_head_params(key, part):
    key = jax.random.fold_in(key, 14)
    key_bias, key_decay, key_skip = jax.random.split(key, 3)
    bias_row = jax.random.uniform(key_bias, (HEADS,), jnp.float32, -6.0, -3.5)
    decay_row = jax.random.uniform(key_decay, (HEADS,), jnp.float32, -3.0, 2.5)
    skip_row = jax.random.uniform(key_skip, (HEADS,), jnp.float32, 0.5, 1.5)
    return jnp.stack([bias_row, decay_row, skip_row])


def draw_conv_params(key, part):
    key = jax.random.fold_in(key, 15)
    key_taps, key_gain = jax.random.split(key)
    tap_rows = jax.random.uniform(key_taps, (5, D_INNER), jnp.float32, -0.5, 0.5)
    gain_row = jax.random.uniform(key_gain, (1, D_INNER), jnp.float32, 0.5, 1.5)
    return jnp.concatenate([tap_rows, gain_row], axis=0)


def levels(own_key, dims, cuts, low, high):
    def one(position, parts):
        heights = jax.random.uniform(jax.random.fold_in(jax.random.fold_in(own_key, 6), position), (parts,), jnp.float32, low / len(cuts), high / len(cuts))
        return jnp.repeat(jnp.exp(heights), dims[position] // parts).reshape((-1,) + (1,) * (len(dims) - position - 1))

    factor_of = one(*cuts[0])
    for cut in cuts[1:]:
        factor_of = factor_of * one(*cut)
    return factor_of


def noise(rng, dims, scale, reach, cuts=(), kind=jnp.bfloat16):
    entries = jax.random.normal(rng, dims, jnp.float32) * scale
    if len(cuts) > 0:
        entries = levels(rng, dims, cuts, -0.22, 0.18) * entries
    return jnp.clip(entries, min=-reach, max=reach).astype(kind)


def setup_inputs(seed: int = 0) -> dict:
    key_list = jax.random.split(jax.random.key(seed), 19)
    return {
        "hidden_in": noise(key_list[0], (TOKENS, D), 1.0, 6.0, ((0, 8),)),
        "out_grad": noise(key_list[1], (TOKENS, D), 1.0, 6.0, ((0, 8),)),
        "seq_lengths": draw_seq_lengths(jax.random.fold_in(key_list[18], 71), 0),
        "owner_map": draw_owner_map(jax.random.fold_in(key_list[18], 71), 0),
        "muon_master": draw_muon_master(jax.random.fold_in(key_list[18], 71), 0),
        "muon_moment": noise(key_list[5], (SLOTS_ALL, D, N_TENSOR * HEADDIM), (0.3 * TOKENS ** 0.5), 224.0, ((0, 8), (2, 4)), jnp.float32),
        "state_proj": noise(key_list[6], (D, 2 * D_STATE), D ** -0.5, 0.15625, (), jnp.float32),
        "state_moment": noise(key_list[7], (D, 2 * D_STATE), (0.04 * TOKENS ** 0.5), 32.0, (), jnp.float32),
        "step_proj": noise(key_list[8], (D, HEADS), D ** -0.5, 0.15625, ((1, 4),), jnp.float32),
        "step_moment": noise(key_list[9], (D, HEADS), (0.04 * TOKENS ** 0.5), 32.0, ((1, 4),), jnp.float32),
        "norm_gain": jnp.clip(1.0 + 0.1 * jax.random.normal(key_list[10], (D,), jnp.float32), 0.5, 1.5),
        "gain_moment": noise(key_list[11], (D,), (0.04 * TOKENS ** 0.5), 32.0, (), jnp.float32),
        "head_params": draw_head_params(jax.random.fold_in(key_list[18], 71), 0),
        "head_moment": noise(key_list[13], (3, HEADS), (0.04 * TOKENS ** 0.5), 32.0, ((1, 4),), jnp.float32),
        "conv_params": draw_conv_params(jax.random.fold_in(key_list[18], 71), 0),
        "conv_moment": noise(key_list[15], (6, D_INNER), (0.04 * TOKENS ** 0.5), 32.0, ((1, 4),), jnp.float32),
        "state_conv": jnp.clip(jax.random.uniform(key_list[16], (5, 2 * D_STATE), jnp.float32, -0.5, 0.5), -0.5, 0.5),
        "state_conv_moment": noise(key_list[17], (5, 2 * D_STATE), (0.04 * TOKENS ** 0.5), 32.0, (), jnp.float32),
    }


exact_mode = lax.Precision.HIGHEST
norm_eps = 1e-05
schulz_coefs = (3.4445, -4.775, 2.0315)
muon_decay = 0.95
muon_rate = 0.02
small_decay = 0.9
small_rate = 2.0

@jax.custom_vjp
def low(v):
    return lax.optimization_barrier(v.astype(jnp.bfloat16)).astype(jnp.float32)

@jax.custom_vjp
def low_back(v):
    return v

def low_keep(v):
    return (low(v), None)

def low_pass(kept, grad):
    return (grad,)

def back_keep(v):
    return (v, None)

def back_low(kept, grad):
    return (low(grad),)
low.defvjp(low_keep, low_pass)
low_back.defvjp(back_keep, back_low)

def conv_silu(values, tap_weights, tap_bias, segment):
    length = values.shape[0]
    padded = jnp.pad(values, ((3, 0), (0, 0)))
    seg_padded = jnp.pad(segment, (3, 0), constant_values=-1)
    summed = jnp.zeros_like(values) + tap_bias[None, :]
    for offset in range(4):
        shifted = padded[offset:offset + length]
        same_seq = (seg_padded[offset:offset + length] == segment).astype(values.dtype)
        summed = summed + tap_weights[offset][None, :] * shifted * same_seq[:, None]
    return jax.nn.silu(summed)

def ssd_scan(inputs_x, step_sizes, decay_rate, b_state, c_state, segment):
    length, head_count, head_width = inputs_x.shape
    blocks = length // SCAN_BLOCK
    log_rates = (step_sizes * decay_rate[None, :]).T.reshape(head_count, blocks, SCAN_BLOCK).transpose(1, 0, 2)
    weighted = (inputs_x * step_sizes[:, :, None]).reshape(blocks, SCAN_BLOCK, head_count, head_width)
    b_blocks = b_state.reshape(blocks, SCAN_BLOCK, b_state.shape[1])
    c_blocks = c_state.reshape(blocks, SCAN_BLOCK, c_state.shape[1])
    seg_blocks = segment.reshape(blocks, SCAN_BLOCK)
    places = jnp.arange(SCAN_BLOCK, dtype=jnp.int32)
    causal = places[:, None] >= places[None, :]

    def advance(carried_in, block_in):
        state_now, last_seg = carried_in
        rate_block, input_block, b_block, c_block, seg_block = block_in
        cumulative = jnp.cumsum(rate_block, axis=1)
        same_seq = (seg_block[:, None] == seg_block[None, :]) & causal
        log_gaps = jnp.where(same_seq[None], cumulative[:, :, None] - cumulative[:, None, :], 0.0)
        decays = jnp.where(same_seq[None], jnp.exp(log_gaps), 0.0)
        scores = jnp.einsum('tn,sn->ts', c_block, b_block, precision=exact_mode)
        within = jnp.einsum('hts,shp->thp', decays * scores[None], input_block, precision=exact_mode)
        carried = (seg_block == last_seg).astype(rate_block.dtype)
        entry_decay = jnp.exp(cumulative).T * carried[:, None]
        across = jnp.einsum('tn,hpn->thp', c_block, state_now, precision=exact_mode) * entry_decay[:, :, None]
        tail_same = (seg_block == seg_block[-1]).astype(rate_block.dtype)
        tail_decay = jnp.exp(cumulative[:, -1:] - cumulative).T * tail_same[:, None]
        fresh_state = jnp.einsum('shp,sn->hpn', input_block * tail_decay[:, :, None], b_block, precision=exact_mode)
        state_next = fresh_state + state_now * (jnp.exp(cumulative[:, -1]) * carried[-1])[:, None, None]
        return ((state_next, seg_block[-1]), within + across)
    initial = (jnp.zeros((head_count, head_width, b_state.shape[1]), dtype=inputs_x.dtype), jnp.array(-1, dtype=jnp.int32))
    last_carry, outputs = lax.scan(jax.checkpoint(advance), initial, (log_rates, weighted, b_blocks, c_blocks, seg_blocks))
    return outputs.reshape(length, head_count, head_width)

def mixer_local(gate_part, input_part, state_part, step_part, head_params, conv_rows, state_conv, segment):
    x_conv = low(conv_silu(input_part, conv_rows[0:4], conv_rows[4], segment))
    bc_conv = low(conv_silu(state_part, state_conv[0:4], state_conv[4], segment))
    length = input_part.shape[0]
    head_count = step_part.shape[1]
    head_width = input_part.shape[1] // head_count
    state_size = state_part.shape[1] // 2
    step_sizes = jax.nn.softplus(step_part + head_params[0][None, :])
    decay_rate = -jnp.exp(head_params[1])
    inputs_x = x_conv.reshape(length, head_count, head_width)
    mixed = ssd_scan(inputs_x, step_sizes, decay_rate, bc_conv[:, :state_size], bc_conv[:, state_size:], segment)
    mixed = mixed + head_params[2][None, :, None] * inputs_x
    return mixed.reshape(length, head_count * head_width) * jax.nn.silu(gate_part)

def newton_schulz(matrices):
    first_coef, second_coef, third_coef = schulz_coefs
    frob_norm = jnp.sqrt(lax.optimization_barrier(jnp.sum(matrices * matrices, axis=(-2, -1), keepdims=True)))
    current = matrices / (frob_norm + 1e-07)
    for _ in range(NS_STEPS):
        gram_matrix = jnp.einsum('...ij,...kj->...ik', current, current, precision=exact_mode)
        polynomial = second_coef * gram_matrix + third_coef * jnp.einsum('...ij,...jk->...ik', gram_matrix, gram_matrix, precision=exact_mode)
        current = first_coef * current + jnp.einsum('...ij,...jk->...ik', polynomial, current, precision=exact_mode)
    return current

def weight_blocks(picked):
    grouped = picked.reshape(3, HEADS_TP, D, N_TENSOR, HEADDIM)
    return [grouped[kind_index].transpose(1, 2, 0, 3).reshape(D, D_INNER) for kind_index in range(3)]

def forward(hidden_rows, muon_master, state_proj, step_proj, norm_gain, head_params, conv_params, state_conv, owner_map, segment, valid):
    gate_weight, input_weight, output_weight = weight_blocks(low(muon_master[owner_map]))
    inv_rms = lax.rsqrt(lax.optimization_barrier(jnp.mean(hidden_rows * hidden_rows, axis=1, keepdims=True)) + norm_eps)
    normed = low(hidden_rows * inv_rms * norm_gain[None, :])
    gate_part = low_back(jnp.dot(normed, gate_weight, precision=exact_mode))
    input_part = low_back(jnp.dot(normed, input_weight, precision=exact_mode))
    state_part = low_back(jnp.dot(normed, low(state_proj), precision=exact_mode))
    step_part = low_back(jnp.dot(normed, low(step_proj), precision=exact_mode))
    gated = mixer_local(gate_part, input_part, state_part, step_part, head_params, conv_params[0:5], state_conv, segment)
    gate_inv = lax.rsqrt(lax.optimization_barrier(jnp.mean(gated * gated, axis=1, keepdims=True)) + norm_eps)
    scaled = low(gated * gate_inv * conv_params[5][None, :])
    branch = low_back(jnp.dot(scaled, output_weight.T, precision=exact_mode))
    return (hidden_rows + branch) * valid[:, None]

def segment_of(lengths):
    positions = jnp.arange(TOK_DEV, dtype=jnp.int32)
    seq_ends = jnp.cumsum(lengths, dtype=jnp.int32)
    segment = lax.optimization_barrier(jnp.sum((positions[:, None] >= seq_ends[None, :]).astype(jnp.int32), axis=1, dtype=jnp.int32))
    valid = (positions < seq_ends[-1]).astype(jnp.float32)
    return (segment, valid)

def small_update(weight, moment, gradient):
    moment_new = small_decay * moment + (1.0 - small_decay) * gradient
    return (moment_new, weight - small_rate / math.sqrt(TOKENS) * moment_new)

def reference(hidden_in, out_grad, seq_lengths, owner_map, muon_master, muon_moment, state_proj, state_moment, step_proj, step_moment, norm_gain, gain_moment, head_params, head_moment, conv_params, conv_moment, state_conv, state_conv_moment):
    params = (muon_master, state_proj, step_proj, norm_gain, head_params, conv_params, state_conv)

    def device_step(totals, item):
        hidden_rows, cotangent, lengths = item
        segment, valid = segment_of(lengths)

        def run_block(hidden_now, master_now, state_now, step_now, gain_now, head_now, conv_now, shared_now):
            return forward(hidden_now, master_now, state_now, step_now, gain_now, head_now, conv_now, shared_now, owner_map, segment, valid)
        result, pull = jax.vjp(run_block, hidden_rows.astype(jnp.float32), *params)
        grads = pull(cotangent.astype(jnp.float32))
        new_totals = tuple((total_now + grad_now for total_now, grad_now in zip(totals, grads[1:])))
        return (new_totals, (result.astype(jnp.bfloat16), grads[0].astype(jnp.bfloat16)))
    zeros = tuple((jnp.zeros_like(param_now) for param_now in params))
    totals, (outputs, in_grads) = lax.scan(device_step, zeros, (hidden_in.reshape(N_DP, TOK_DEV, D), out_grad.reshape(N_DP, TOK_DEV, D), seq_lengths))
    block_out = outputs.reshape(TOKENS, D)
    input_grad = in_grads.reshape(TOKENS, D)
    muon_moment_new = muon_decay * muon_moment + totals[0]
    stacked = muon_moment_new.reshape(SLOTS_ALL, D, N_TENSOR, HEADDIM).transpose(0, 2, 3, 1)
    ortho = newton_schulz(stacked).transpose(0, 3, 1, 2).reshape(SLOTS_ALL, D, N_TENSOR * HEADDIM)
    muon_master_new = muon_master - muon_rate * math.sqrt(max(D, HEADDIM)) * ortho
    state_moment_new, state_proj_new = small_update(state_proj, state_moment, totals[1])
    step_moment_new, step_proj_new = small_update(step_proj, step_moment, totals[2])
    gain_moment_new, norm_gain_new = small_update(norm_gain, gain_moment, totals[3])
    head_moment_new, head_params_new = small_update(head_params, head_moment, totals[4])
    conv_moment_new, conv_params_new = small_update(conv_params, conv_moment, totals[5])
    state_conv_moment_new, state_conv_new = small_update(state_conv, state_conv_moment, totals[6])
    return (block_out, input_grad, muon_moment_new, muon_master_new, state_moment_new, state_proj_new, step_moment_new, step_proj_new, gain_moment_new, norm_gain_new, head_moment_new, head_params_new, conv_moment_new, conv_params_new, state_conv_moment_new, state_conv_new)
```

```python
import functools
import math

import jax
import jax.numpy as jnp
from jax import lax
from jax.experimental import pallas as pl
from jax.experimental.pallas import tpu as pltpu
from jax.sharding import PartitionSpec as P

HEADDIM = 64
NS_STEPS = 5
ROWS = 256
SUB = 128
LANES = 128
NARROW = 384
CHUNK = 384

exact_mode = lax.Precision.HIGHEST
norm_eps = 1e-05
schulz_coefs = (3.4445, -4.775, 2.0315)
muon_decay = 0.95
muon_rate = 0.02
small_decay = 0.9
small_rate = 2.0
log2_e = 1.4426950408889634
f32 = jnp.float32
bf16 = jnp.bfloat16
far_below = -1e30


def dot_nn(left, right, precision=None):
    return lax.dot_general(
        left, right, (((1,), (0,)), ((), ())), precision=precision, preferred_element_type=f32
    )


def dot_nt(left, right, precision=None):
    return lax.dot_general(
        left, right, (((1,), (1,)), ((), ())), precision=precision, preferred_element_type=f32
    )


def dot_tn(left, right, precision=None):
    return lax.dot_general(
        left, right, (((0,), (0,)), ((), ())), precision=precision, preferred_element_type=f32
    )


def sigmoid(values):
    return 0.5 * jnp.tanh(0.5 * values) + 0.5


def iota(shape, dim):
    return lax.broadcasted_iota(jnp.int32, shape, dim)


def segment_at(place, ends_ref, count):
    total = (place >= ends_ref[0]).astype(jnp.int32)
    for k in range(1, count):
        total = total + (place >= ends_ref[k]).astype(jnp.int32)
    return total


def step_terms(step_part, head_ref):
    shifted = step_part + head_ref[0:1, :]
    small = jnp.exp(-jnp.abs(shifted))
    tail = jnp.where(
        small < 0.01, small * (1.0 - small * (0.5 - small * (1.0 / 3.0))), jnp.log(1.0 + small)
    )
    step = jnp.maximum(shifted, 0.0) + tail
    decay = -jnp.exp(head_ref[1:2, :])
    log_rate = step * (decay * log2_e)
    lower = (iota((SUB, SUB), 0) >= iota((SUB, SUB), 1)).astype(f32)
    cum = dot_nn(lower, log_rate, exact_mode)
    source = cum - jnp.log(step) * log2_e
    return shifted, step, decay, cum, source


def expand(values, pair):
    shape = (values.shape[0], LANES)
    low = jnp.broadcast_to(values[:, 2 * pair : 2 * pair + 1], shape)
    high = jnp.broadcast_to(values[:, 2 * pair + 1 : 2 * pair + 2], shape)
    return jnp.where(iota(shape, 1) < HEADDIM, low, high)


def split_pair(values):
    low = iota(values.shape, 1) < HEADDIM
    zero = jnp.zeros_like(values)
    return jnp.where(low, values, zero), jnp.where(low, zero, values)


def lanes_of(pair):
    return slice(pair * LANES, (pair + 1) * LANES)


def shift_mask(place, shift, ends_ref, count, rows_all):
    other = place + shift
    inside = (other >= 0) & (other < rows_all)
    same = segment_at(place, ends_ref, count) == segment_at(other, ends_ref, count)
    return jnp.where(inside & same, 1.0, 0.0).astype(f32)


def conv_tile(buf_ref, first, lanes, taps, masks):
    total = taps[4:5, :] + taps[3:4, :] * buf_ref[first + 8 : first + 8 + SUB, lanes]
    for back in (1, 2, 3):
        rows = buf_ref[first + 8 - back : first + 8 - back + SUB, lanes]
        total = total + taps[3 - back : 4 - back, :] * (rows * masks[back - 1])
    return total


def block_terms(base, ends_ref, count):
    row_at = base + iota((SUB, SUB), 0)
    col_at = base + iota((SUB, SUB), 1)
    seg_row = segment_at(row_at, ends_ref, count)
    seg_col = segment_at(col_at, ends_ref, count)
    seg_last = segment_at(base + SUB - 1, ends_ref, count)
    seg_before = jnp.where(base == 0, -1, segment_at(base - 1, ends_ref, count))
    carried = jnp.where(seg_row == seg_before, 1.0, 0.0).astype(f32)
    tail_same = jnp.where(seg_row == seg_last, 1.0, 0.0).astype(f32)
    through = jnp.where(seg_last == seg_before, 1.0, 0.0).astype(f32)
    same = seg_row == seg_col
    return row_at, col_at, same, carried, tail_same, through


def load_weights(stack_ref, place_ref, held_ref, sems, first, count):
    copies = []
    for m in range(count):
        copies.append(
            pltpu.make_async_copy(
                stack_ref.at[place_ref[first + m]],
                held_ref.at[pl.ds(m * HEADDIM, HEADDIM)],
                sems.at[m],
            )
        )
    for copy in copies:
        copy.start()
    return copies


def forward_kernel(
    heads, seq_count, rows_all,
    place_ref, ends_ref,
    hidden_ref, cot_ref, stack_ref, gain_ref, narrow_ref, head_ref, conv_ref, shared_ref,
    normed_ref, gate_ref, input_ref, mixed_ref, dscaled_ref, shared_in_ref, step_ref, state_ref,
    sums_ref, part_ref,
    weights, sems, in_buf, shared_buf, state, low_buf, tail_buf, across,
):
    block = pl.program_id(0)
    inner = heads * HEADDIM
    pairs = heads // 2

    @pl.when(block == 0)
    def _():
        copies = load_weights(stack_ref, place_ref, weights, sems, 0, 3 * heads)
        in_buf[0:8, :] = jnp.zeros((8, inner), f32)
        shared_buf[0:8, :] = jnp.zeros((8, 2 * LANES), f32)
        state[...] = jnp.zeros_like(state)
        for copy in copies:
            copy.wait()

    first_row = block * ROWS
    hidden = hidden_ref[...].astype(f32)
    inv_rms = lax.rsqrt(jnp.mean(hidden * hidden, axis=1, keepdims=True) + norm_eps)
    normed = (hidden * inv_rms * gain_ref[0:1, :]).astype(bf16)
    normed_ref[...] = normed
    in_buf[8:, :] = dot_nt(normed, weights[inner : 2 * inner, :])
    narrow = dot_nn(normed, narrow_ref[...])
    shared_buf[8:, :] = narrow[:, 0 : 2 * LANES]
    step_ref[...] = narrow[:, 2 * LANES : 3 * LANES]
    gate_ref[...] = dot_nt(normed, weights[0:inner, :])
    row_at = first_row + iota((ROWS, cot_ref.shape[1]), 0)
    cot = jnp.where(row_at < ends_ref[seq_count - 1], cot_ref[...].astype(f32), 0.0).astype(bf16)
    dscaled_ref[...] = dot_nt(cot, weights[2 * inner : 3 * inner, :])
    input_ref[...] = in_buf[8:, :]
    shared_in_ref[...] = shared_buf[8:, :]

    for sub in range(ROWS // SUB):
        first = sub * SUB
        base = first_row + first
        row_at, col_at, same, carried, tail_same, through = block_terms(base, ends_ref, seq_count)
        causal = jnp.where(same & (row_at >= col_at), 0.0, far_below).astype(f32)
        masks = [shift_mask(row_at, -back, ends_ref, seq_count, rows_all) for back in (1, 2, 3)]
        bc = []
        for part in range(2):
            lanes = lanes_of(part)
            u = conv_tile(shared_buf, first, lanes, shared_ref[:, lanes], masks)
            bc.append((u * sigmoid(u)).astype(bf16))
        b_low, c_low = bc
        _, _, _, cum, source = step_terms(step_ref[first : first + SUB, :], head_ref)
        source_row = source.T
        scores = dot_nt(c_low, b_low)
        cum_last = cum[SUB - 1 : SUB, :]
        entry = jnp.exp2(cum) * carried
        leave = jnp.exp2(cum_last - source) * tail_same
        pass_on = jnp.exp2(cum_last) * through
        state_ref[sub] = state[...]
        across[...] = dot_nn(c_low, state[...].astype(bf16))
        square = jnp.zeros((SUB, LANES), f32)
        inner_dot = jnp.zeros((SUB, LANES), f32)
        for pair in range(pairs):
            lanes = lanes_of(pair)
            u = conv_tile(in_buf, first, lanes, conv_ref[:, lanes], masks)
            x_low = (u * sigmoid(u)).astype(bf16)
            x = x_low.astype(f32)
            mats = []
            for h in (2 * pair, 2 * pair + 1):
                gap = cum[:, h : h + 1] - source_row[h : h + 1, :]
                mats.append((jnp.exp2(gap + causal) * scores).astype(bf16))
            x_a, x_b = split_pair(x_low)
            mixed = dot_nn(jnp.concatenate(mats, axis=1), jnp.concatenate([x_a, x_b], axis=0))
            mixed = mixed + across[:, lanes] * expand(entry, pair)
            mixed = mixed + expand(head_ref[2:3, :], pair) * x
            mixed_ref[first : first + SUB, lanes] = mixed
            gate = gate_ref[first : first + SUB, lanes]
            gated = mixed * (gate * sigmoid(gate))
            gated_gain = gated * conv_ref[5:6, lanes]
            low_buf[first : first + SUB, lanes] = gated_gain.astype(bf16)
            square = square + gated * gated
            inner_dot = inner_dot + dscaled_ref[first : first + SUB, lanes] * gated_gain
            tail_buf[:, lanes] = (x * expand(leave, pair)).astype(bf16)
        fresh = dot_tn(b_low, tail_buf[...])
        for pair in range(pairs):
            lanes = lanes_of(pair)
            state[:, lanes] = state[:, lanes] * expand(pass_on, pair) + fresh[:, lanes]
        sums_ref[0:1, first : first + SUB] = jnp.sum(square.T, axis=0, keepdims=True)
        sums_ref[1:2, first : first + SUB] = jnp.sum(inner_dot.T, axis=0, keepdims=True)
    sums_ref[2:8, :] = jnp.zeros((6, ROWS), f32)
    in_buf[0:8, :] = in_buf[ROWS : ROWS + 8, :]
    shared_buf[0:8, :] = shared_buf[ROWS : ROWS + 8, :]
    part_ref[...] = dot_nn(low_buf[...], weights[2 * inner : 3 * inner, :]).astype(bf16)


def forward_call(place, ends, hidden, cot, stack, gain, narrow, head_rows, conv_rows, shared_rows, heads):
    rows_all, width = hidden.shape
    inner = heads * HEADDIM
    blocks = rows_all // ROWS

    def rows(columns):
        return pl.BlockSpec((ROWS, columns), lambda i, *_: (i, 0))

    def whole(array):
        return pl.BlockSpec(array.shape, lambda i, *_: (0,) * array.ndim)

    state_shape = (ROWS // SUB, LANES, inner)
    out_shape = [
        jax.ShapeDtypeStruct((rows_all, width), bf16),
        jax.ShapeDtypeStruct((rows_all, inner), f32),
        jax.ShapeDtypeStruct((rows_all, inner), f32),
        jax.ShapeDtypeStruct((rows_all, inner), f32),
        jax.ShapeDtypeStruct((rows_all, inner), f32),
        jax.ShapeDtypeStruct((rows_all, 2 * LANES), f32),
        jax.ShapeDtypeStruct((rows_all, LANES), f32),
        jax.ShapeDtypeStruct((rows_all // SUB, LANES, inner), f32),
        jax.ShapeDtypeStruct((8, rows_all), f32),
        jax.ShapeDtypeStruct((rows_all, width), bf16),
    ]
    out_specs = [
        rows(width), rows(inner), rows(inner), rows(inner), rows(inner), rows(2 * LANES), rows(LANES),
        pl.BlockSpec(state_shape, lambda i, *_: (i, 0, 0)),
        pl.BlockSpec((8, ROWS), lambda i, *_: (0, i)),
        rows(width),
    ]
    return pl.pallas_call(
        functools.partial(forward_kernel, heads, ends.shape[0], rows_all),
        grid_spec=pltpu.PrefetchScalarGridSpec(
            num_scalar_prefetch=2,
            grid=(blocks,),
            in_specs=[
                rows(width), rows(width), pl.BlockSpec(memory_space=pl.ANY), whole(gain), whole(narrow),
                whole(head_rows), whole(conv_rows), whole(shared_rows),
            ],
            out_specs=out_specs,
            scratch_shapes=[
                pltpu.VMEM((3 * inner, width), bf16),
                pltpu.SemaphoreType.DMA((3 * heads,)),
                pltpu.VMEM((ROWS + 8, inner), f32),
                pltpu.VMEM((ROWS + 8, 2 * LANES), f32),
                pltpu.VMEM((LANES, inner), f32),
                pltpu.VMEM((ROWS, inner), bf16),
                pltpu.VMEM((SUB, inner), bf16),
                pltpu.VMEM((SUB, inner), f32),
            ],
        ),
        out_shape=out_shape,
        compiler_params=pltpu.CompilerParams(
            dimension_semantics=("arbitrary",), vmem_limit_bytes=56 * 2**20
        ),
        cost_estimate=pl.CostEstimate(
            flops=2 * rows_all * width * (4 * inner + NARROW), bytes_accessed=60 * 2**20, transcendentals=0
        ),
        name="mixer_forward",
    )(place, ends, hidden, cot, stack, gain, narrow, head_rows, conv_rows, shared_rows)


def backward_kernel(
    heads, seq_count, rows_all, inner_all,
    place_ref, ends_ref,
    hidden_ref, gate_ref, input_ref, before_ref, mixed_ref, dscaled_ref, shared_in_ref,
    shared_before_ref, step_ref, state_ref, sums_ref,
    stack_ref, narrow_ref, gain_ref, head_ref, conv_ref, shared_ref,
    dboth_ref, scaled_ref, dnarrow_ref, dnormed_ref, conv_grad_ref, shared_grad_ref, head_grad_ref,
    skip_grad_ref, gain_grad_ref,
    weights, sems, in_buf, shared_buf, du_buf, dshared_buf, dstate, state_after, from_state, terms,
    source_terms, tail_buf, entry_buf,
):
    turn = pl.program_id(0)
    block = pl.num_programs(0) - 1 - turn
    inner = heads * HEADDIM
    pairs = heads // 2

    @pl.when(turn == 0)
    def _():
        copies = load_weights(stack_ref, place_ref, weights, sems, 0, 2 * heads)
        du_buf[ROWS:, :] = jnp.zeros((8, inner), f32)
        dshared_buf[ROWS:, :] = jnp.zeros((8, 2 * LANES), f32)
        dstate[...] = jnp.zeros_like(dstate)
        state_after[...] = jnp.zeros_like(state_after)
        conv_grad_ref[...] = jnp.zeros_like(conv_grad_ref)
        shared_grad_ref[...] = jnp.zeros_like(shared_grad_ref)
        head_grad_ref[...] = jnp.zeros_like(head_grad_ref)
        skip_grad_ref[...] = jnp.zeros_like(skip_grad_ref)
        gain_grad_ref[...] = jnp.zeros_like(gain_grad_ref)
        for copy in copies:
            copy.wait()

    first_row = block * ROWS
    in_buf[0:8, :] = jnp.where(block == 0, 0.0, before_ref[...])
    in_buf[8:, :] = input_ref[...]
    shared_buf[0:8, :] = jnp.where(block == 0, 0.0, shared_before_ref[...])
    shared_buf[8:, :] = shared_in_ref[...]
    reduce_heads = (iota((inner, LANES), 0) // HEADDIM == iota((inner, LANES), 1)).astype(f32)
    upper = (iota((SUB, SUB), 0) <= iota((SUB, SUB), 1)).astype(f32)

    for sub in reversed(range(ROWS // SUB)):
        first = sub * SUB
        here = slice(first, first + SUB)
        base = first_row + first
        row_at, col_at, same, carried, tail_same, through = block_terms(base, ends_ref, seq_count)
        causal = jnp.where(same & (row_at <= col_at), 0.0, far_below).astype(f32)
        masks = [shift_mask(row_at, -back, ends_ref, seq_count, rows_all) for back in (1, 2, 3)]
        bc, bc_slope = [], []
        for part in range(2):
            lanes = lanes_of(part)
            u = conv_tile(shared_buf, first, lanes, shared_ref[:, lanes], masks)
            sig = sigmoid(u)
            bc.append((u * sig).astype(bf16))
            bc_slope.append(sig * (1.0 + u * (1.0 - sig)))
        b_low, c_low = bc
        shifted, step, decay, cum, source = step_terms(step_ref[here, :], head_ref)
        cum_row = cum.T
        scores = dot_nt(b_low, c_low)
        cum_last = cum[SUB - 1 : SUB, :]
        entry = jnp.exp2(cum) * carried
        leave = jnp.exp2(cum_last - source) * tail_same
        pass_on = jnp.exp2(cum_last) * through
        square = sums_ref[0:1, here]
        inner_dot = sums_ref[1:2, here]
        inv_row = lax.rsqrt(square * (1.0 / inner_all) + norm_eps)
        fix_row = inv_row * inv_row * inv_row * inner_dot * (1.0 / inner_all)
        inv = jnp.broadcast_to(inv_row, (SUB, SUB)).T
        fix = jnp.broadcast_to(fix_row, (SUB, SUB)).T
        dstate_low = dstate[...].astype(bf16)
        from_state[...] = dot_nn(b_low, dstate_low)
        dscores = jnp.zeros((SUB, SUB), f32)
        for pair in range(pairs):
            lanes = lanes_of(pair)
            u = conv_tile(in_buf, first, lanes, conv_ref[:, lanes], masks)
            sig = sigmoid(u)
            x_low = (u * sig).astype(bf16)
            x = x_low.astype(f32)
            slope = sig * (1.0 + u * (1.0 - sig))
            gate = gate_ref[here, lanes]
            gate_sig = sigmoid(gate)
            gate_silu = gate * gate_sig
            mixed = mixed_ref[here, lanes]
            gated = mixed * gate_silu
            gain = conv_ref[5:6, lanes]
            dscaled = dscaled_ref[here, lanes]
            normal = gated * inv
            scaled_ref[here, lanes] = (normal * gain).astype(bf16)
            conv_grad_ref[5:6, lanes] += jnp.sum(dscaled * normal, axis=0, keepdims=True)
            dgated = inv * (dscaled * gain) - gated * fix
            dgate = dgated * mixed * (gate_sig * (1.0 + gate * (1.0 - gate_sig)))
            dboth_ref[here, lanes] = dgate.astype(bf16)
            dmixed = dgated * gate_silu
            dy_low = dmixed.astype(bf16)
            dy = dy_low.astype(f32)
            skip = expand(head_ref[2:3, :], pair)
            skip_grad_ref[0:1, lanes] += jnp.sum(dmixed * x, axis=0, keepdims=True)
            x_parts = split_pair(x_low)
            dy_parts = split_pair(dy_low)
            mats = []
            for k in range(2):
                h = 2 * pair + k
                gap = cum_row[h : h + 1, :] - source[:, h : h + 1]
                decays = jnp.exp2(gap + causal)
                mats.append((decays * scores).astype(bf16))
                dscores = dscores + dot_nt(x_parts[k], dy_low) * decays
            dx = dot_nn(jnp.concatenate(mats, axis=1), jnp.concatenate(dy_parts, axis=0))
            leave_here = expand(leave, pair)
            dx = dx + leave_here * from_state[:, lanes]
            source_term = x * dx
            source_terms[:, lanes] = source_term
            terms[:, lanes] = dy * (mixed - skip * x) - source_term
            tail_buf[:, lanes] = (x * leave_here).astype(bf16)
            entry_buf[:, lanes] = (dy * expand(entry, pair)).astype(bf16)
            du_buf[here, lanes] = (dx + skip * dmixed) * slope
        state_low = state_ref[sub].astype(bf16)
        dscores_low = dscores.astype(bf16)
        db = dot_nn(dscores_low, c_low) + dot_nt(tail_buf[...], dstate_low)
        dc = dot_tn(dscores_low, b_low) + dot_nt(entry_buf[...], state_low)
        dshared_buf[here, 0:LANES] = db * bc_slope[0]
        dshared_buf[here, LANES : 2 * LANES] = dc * bc_slope[1]
        at_end = jnp.sum(dstate[...] * state_after[...], axis=0, keepdims=True)
        state_after[...] = state_ref[sub]
        fresh = dot_tn(c_low, entry_buf[...])
        for pair in range(pairs):
            lanes = lanes_of(pair)
            dstate[:, lanes] = dstate[:, lanes] * expand(pass_on, pair) + fresh[:, lanes]
        last = iota((SUB, inner), 0) == SUB - 1
        dcum = dot_nn(terms[...] + jnp.where(last, at_end, 0.0), reduce_heads, exact_mode)
        from_source = dot_nn(source_terms[...], reduce_heads, exact_mode)
        dlog = dot_nn(upper, dcum, exact_mode)
        sig = sigmoid(shifted)
        ratio = jnp.where(shifted < -15.0, 1.0, sig / step)
        dlog_decay = dlog * decay
        dstep = from_source * ratio + dlog_decay * sig
        dnarrow_ref[here, 2 * LANES : 3 * LANES] = dstep.astype(bf16)
        head_grad_ref[0:1, :] += jnp.sum(dstep, axis=0, keepdims=True)
        head_grad_ref[1:2, :] += jnp.sum(dlog_decay * step, axis=0, keepdims=True)

    for sub in range(ROWS // SUB):
        first = sub * SUB
        here = slice(first, first + SUB)
        row_at = first_row + first + iota((SUB, LANES), 0)
        ahead = [shift_mask(row_at, k, ends_ref, seq_count, rows_all) for k in (1, 2, 3)]
        groups = [(pair, True) for pair in range(pairs)] + [(0, False), (1, False)]
        for group, wide in groups:
            lanes = lanes_of(group)
            grads, held = (du_buf, in_buf) if wide else (dshared_buf, shared_buf)
            taps = conv_ref[:, lanes] if wide else shared_ref[:, lanes]
            sums = conv_grad_ref if wide else shared_grad_ref
            du = grads[here, lanes]
            v = held[first + 8 : first + 8 + SUB, lanes]
            dv = taps[3:4, :] * du
            sums[3:4, lanes] += jnp.sum(du * v, axis=0, keepdims=True)
            sums[4:5, lanes] += jnp.sum(du, axis=0, keepdims=True)
            for k in (1, 2, 3):
                moved = grads[first + k : first + k + SUB, lanes] * ahead[k - 1]
                dv = dv + taps[3 - k : 4 - k, :] * moved
                sums[3 - k : 4 - k, lanes] += jnp.sum(moved * v, axis=0, keepdims=True)
            if wide:
                dboth_ref[here, inner + group * LANES : inner + (group + 1) * LANES] = dv.astype(bf16)
            else:
                dnarrow_ref[here, lanes] = dv.astype(bf16)
    du_buf[ROWS:, :] = du_buf[0:8, :]
    dshared_buf[ROWS:, :] = dshared_buf[0:8, :]

    dnormed = dot_nn(dboth_ref[...], weights[...]) + dot_nt(dnarrow_ref[...], narrow_ref[...])
    hidden = hidden_ref[...].astype(f32)
    inv_rms = lax.rsqrt(jnp.mean(hidden * hidden, axis=1, keepdims=True) + norm_eps)
    gain_grad_ref[0:1, :] += jnp.sum(dnormed * (hidden * inv_rms), axis=0, keepdims=True)
    dnormed_ref[...] = dnormed.astype(bf16)


def backward_call(
    place, ends, hidden, gate, input_part, mixed, dscaled, shared_in, step_part, states, sums, stack,
    narrow, gain, head_rows, conv_rows, shared_rows, heads, inner_all,
):
    rows_all, width = hidden.shape
    inner = heads * HEADDIM
    blocks = rows_all // ROWS

    def rows(columns):
        return pl.BlockSpec((ROWS, columns), lambda i, *_: (blocks - 1 - i, 0))

    def before(columns):
        step = ROWS // 8
        return pl.BlockSpec(
            (8, columns), lambda i, *_: (jnp.maximum((blocks - 1 - i) * step - 1, 0), 0)
        )

    def whole(shape):
        return pl.BlockSpec(shape, lambda i, *_: (0,) * len(shape))

    out_shape = [
        jax.ShapeDtypeStruct((rows_all, 2 * inner), bf16),
        jax.ShapeDtypeStruct((rows_all, inner), bf16),
        jax.ShapeDtypeStruct((rows_all, NARROW), bf16),
        jax.ShapeDtypeStruct((rows_all, width), bf16),
        jax.ShapeDtypeStruct((8, inner), f32),
        jax.ShapeDtypeStruct((8, 2 * LANES), f32),
        jax.ShapeDtypeStruct((8, LANES), f32),
        jax.ShapeDtypeStruct((8, inner), f32),
        jax.ShapeDtypeStruct((8, width), f32),
    ]
    out_specs = [rows(2 * inner), rows(inner), rows(NARROW), rows(width)] + [
        whole(shape.shape) for shape in out_shape[4:]
    ]
    return pl.pallas_call(
        functools.partial(backward_kernel, heads, ends.shape[0], rows_all, inner_all),
        grid_spec=pltpu.PrefetchScalarGridSpec(
            num_scalar_prefetch=2,
            grid=(blocks,),
            in_specs=[
                rows(width), rows(inner), rows(inner), before(inner), rows(inner), rows(inner),
                rows(2 * LANES), before(2 * LANES), rows(LANES),
                pl.BlockSpec((ROWS // SUB, LANES, inner), lambda i, *_: (blocks - 1 - i, 0, 0)),
                pl.BlockSpec((8, ROWS), lambda i, *_: (0, blocks - 1 - i)),
                pl.BlockSpec(memory_space=pl.ANY), whole(narrow.shape), whole(gain.shape),
                whole(head_rows.shape), whole(conv_rows.shape), whole(shared_rows.shape),
            ],
            out_specs=out_specs,
            scratch_shapes=[
                pltpu.VMEM((2 * inner, width), bf16),
                pltpu.SemaphoreType.DMA((2 * heads,)),
                pltpu.VMEM((ROWS + 8, inner), f32),
                pltpu.VMEM((ROWS + 8, 2 * LANES), f32),
                pltpu.VMEM((ROWS + 8, inner), f32),
                pltpu.VMEM((ROWS + 8, 2 * LANES), f32),
                pltpu.VMEM((LANES, inner), f32),
                pltpu.VMEM((LANES, inner), f32),
                pltpu.VMEM((SUB, inner), f32),
                pltpu.VMEM((SUB, inner), f32),
                pltpu.VMEM((SUB, inner), f32),
                pltpu.VMEM((SUB, inner), bf16),
                pltpu.VMEM((SUB, inner), bf16),
            ],
        ),
        out_shape=out_shape,
        compiler_params=pltpu.CompilerParams(
            dimension_semantics=("arbitrary",), vmem_limit_bytes=56 * 2**20
        ),
        cost_estimate=pl.CostEstimate(
            flops=4 * rows_all * width * (2 * inner + NARROW), bytes_accessed=60 * 2**20, transcendentals=0
        ),
        name="mixer_backward",
    )(
        place, ends, hidden, gate, input_part, input_part, mixed, dscaled, shared_in, shared_in, step_part,
        states, sums, stack, narrow, gain, head_rows, conv_rows, shared_rows,
    )


def grads_kernel(
    heads, slots, seq_count, role_ref, ends_ref, dboth_ref, scaled_ref, dnarrow_ref, normed_ref, cot_ref,
    out_ref, narrow_out_ref, held, sems,
):
    chunk = pl.program_id(0)
    inner = heads * HEADDIM
    width = normed_ref.shape[1]
    held[0 : 2 * inner, :] = dot_tn(dboth_ref[...], normed_ref[...]).astype(bf16)
    narrow_out_ref[...] = dot_tn(dnarrow_ref[...], normed_ref[...])
    row_at = iota(cot_ref.shape, 0)
    cot = jnp.where(row_at < ends_ref[seq_count - 1], cot_ref[...].astype(f32), 0.0).astype(bf16)
    held[2 * inner : 3 * inner, :] = dot_tn(scaled_ref[...], cot).astype(bf16)
    held[3 * inner :, :] = jnp.zeros((HEADDIM, width), bf16)
    copies = []
    for s in range(slots):
        at = pl.multiple_of(role_ref[s] * HEADDIM, HEADDIM)
        copies.append(
            pltpu.make_async_copy(
                held.at[pl.ds(at, HEADDIM), :],
                out_ref.at[s, :, pl.ds(pl.multiple_of(chunk * width, width), width)],
                sems.at[s],
            )
        )
    for copy in copies:
        copy.start()
    for copy in copies:
        copy.wait()


def grads_call(role, ends, dboth, scaled, dnarrow, normed, cot, heads, slots):
    rows_all, width = normed.shape
    inner = heads * HEADDIM

    def whole(array):
        return pl.BlockSpec(array.shape, lambda i, *_: (0, 0), pipeline_mode=pl.Buffered(1))

    part = pl.BlockSpec((rows_all, CHUNK), lambda i, *_: (0, i))
    return pl.pallas_call(
        functools.partial(grads_kernel, heads, slots, ends.shape[0]),
        grid_spec=pltpu.PrefetchScalarGridSpec(
            num_scalar_prefetch=2,
            grid=(width // CHUNK,),
            in_specs=[whole(dboth), whole(scaled), whole(dnarrow), part, part],
            out_specs=[
                pl.BlockSpec(memory_space=pl.ANY),
                pl.BlockSpec((NARROW, CHUNK), lambda i, *_: (0, i)),
            ],
            scratch_shapes=[
                pltpu.VMEM((3 * inner + HEADDIM, CHUNK), bf16),
                pltpu.SemaphoreType.DMA((slots,)),
            ],
        ),
        out_shape=[
            jax.ShapeDtypeStruct((slots, HEADDIM, width), bf16),
            jax.ShapeDtypeStruct((NARROW, width), f32),
        ],
        compiler_params=pltpu.CompilerParams(
            dimension_semantics=("arbitrary",), vmem_limit_bytes=56 * 2**20
        ),
        cost_estimate=pl.CostEstimate(
            flops=2 * rows_all * width * (3 * inner + NARROW), bytes_accessed=40 * 2**20, transcendentals=0
        ),
        name="weight_grads",
    )(role, ends, dboth, scaled, dnarrow, normed, cot)


def muon_kernel(rate, grad_ref, moment_ref, master_ref, moment_out, master_out):
    first_coef, second_coef, third_coef = schulz_coefs
    side = HEADDIM
    same = iota((side, side), 0) == iota((side, side), 1)
    eye = jnp.where(same, 1.0, 0.0).astype(f32)
    slots = grad_ref.shape[0]
    grams, totals, scales = [], [], []
    for s in range(slots):
        moment = muon_decay * moment_ref[s] + grad_ref[s].astype(f32)
        moment_out[s] = moment
        square = jnp.sum(jnp.sum(moment * moment, axis=1, keepdims=True), axis=0, keepdims=True)
        scale = 1.0 / (jnp.sqrt(square) + 1e-07)
        scaled = moment * scale
        grams.append(dot_nt(scaled, scaled, exact_mode))
        totals.append(eye)
        scales.append(scale)
    for _ in range(NS_STEPS):
        for s in range(slots):
            gram = grams[s]
            factor = (
                first_coef * eye + second_coef * gram + third_coef * dot_nn(gram, gram, exact_mode)
            )
            totals[s] = dot_nn(factor, totals[s], exact_mode)
            grams[s] = dot_nn(dot_nn(factor, gram, exact_mode), factor, exact_mode)
    for s in range(slots):
        ortho = dot_nn(totals[s], moment_out[s] * scales[s], exact_mode)
        master_out[s] = master_ref[s] - rate * ortho


def muon_call(grad, moment, master):
    slots, side, width = moment.shape
    spec = pl.BlockSpec(memory_space=pltpu.VMEM)
    return pl.pallas_call(
        functools.partial(muon_kernel, muon_rate * math.sqrt(max(width, side))),
        in_specs=[spec] * 3,
        out_specs=[spec] * 2,
        out_shape=[jax.ShapeDtypeStruct(moment.shape, f32)] * 2,
        compiler_params=pltpu.CompilerParams(vmem_limit_bytes=56 * 2**20),
        name="muon",
    )(grad, moment, master)


def small_update(weight, moment, gradient, tokens_all):
    moment_new = small_decay * moment + (1.0 - small_decay) * gradient
    return (moment_new, weight - small_rate / math.sqrt(tokens_all) * moment_new)


def pad_to(array, rows, columns):
    return jnp.pad(array, ((0, rows - array.shape[0]), (0, columns - array.shape[1])))


def swap(values, bit):
    return lax.ppermute(values, "tensor", [(t, t ^ bit) for t in range(4)])


def half_sum(part):
    half = part.shape[0] // 2
    core = lax.axis_index("tensor") % 2
    mine = lax.dynamic_slice_in_dim(part, core * half, half)
    other = lax.dynamic_slice_in_dim(part, (1 - core) * half, half)
    near = (mine.astype(f32) + swap(other, 1).astype(f32)).astype(bf16)
    return near.astype(f32) + swap(near, 2).astype(f32)


def join_halves(half):
    core = lax.axis_index("tensor") % 2
    other = swap(half, 1)
    first = jnp.where(core == 0, half, other)
    second = jnp.where(core == 0, other, half)
    return jnp.concatenate([first, second], axis=0)


def half_of(values, axis=0):
    half = values.shape[axis] // 2
    core = lax.axis_index("tensor") % 2
    return lax.dynamic_slice_in_dim(values, core * half, half, axis=axis)


def per_device(
    hidden_in,
    out_grad,
    seq_lengths,
    owner_map,
    muon_master,
    muon_moment,
    state_proj,
    state_moment,
    step_proj,
    step_moment,
    norm_gain,
    gain_moment,
    head_params,
    head_moment,
    conv_params,
    conv_moment,
    state_conv,
    state_conv_moment,
):
    tok_rows, width = hidden_in.shape
    heads = step_proj.shape[1]
    inner = conv_params.shape[1]
    dp_size = lax.axis_size("dp")
    inner_all = inner * lax.axis_size("tensor")
    slots = muon_master.shape[0] * dp_size
    ends = jnp.cumsum(seq_lengths[0], dtype=jnp.int32)
    master = muon_master.transpose(0, 2, 1)
    moment = muon_moment.transpose(0, 2, 1)
    stack = lax.all_gather(master.astype(bf16), "dp", axis=0, tiled=True)
    narrow = pad_to(jnp.concatenate([state_proj, step_proj], axis=1), width, NARROW).astype(bf16)
    gain = norm_gain[None, :]
    head_rows = pad_to(head_params, 8, LANES)
    conv_rows = pad_to(conv_params, 8, inner)
    shared_rows = pad_to(state_conv, 8, state_conv.shape[1])

    normed, gate, input_part, mixed, dscaled, shared_in, step_part, states, sums, part = forward_call(
        owner_map, ends, hidden_in, out_grad, stack, gain, narrow, head_rows, conv_rows, shared_rows, heads
    )
    sums = lax.psum(sums, "tensor")
    core = lax.axis_index("tensor") % 2
    half = tok_rows // 2
    valid = ((core * half + jnp.arange(half, dtype=jnp.int32)) < ends[-1]).astype(f32)[:, None]
    hidden_half = half_of(hidden_in).astype(f32)
    gate_inv = lax.rsqrt(half_of(sums[0]) / inner_all + norm_eps)[:, None]
    branch = half_sum(part) * gate_inv
    block_out = join_halves(((hidden_half + branch) * valid).astype(bf16))

    dboth, scaled, dnarrow, dnormed, conv_grad, shared_grad, head_grad, skip_grad, gain_grad = backward_call(
        owner_map, ends, hidden_in, gate, input_part, mixed, dscaled, shared_in, step_part, states, sums,
        stack, narrow, gain, head_rows, conv_rows, shared_rows, heads, inner_all,
    )
    dnormed_half = half_sum(dnormed)
    inv_rms = lax.rsqrt(jnp.mean(hidden_half * hidden_half, axis=1, keepdims=True) + norm_eps)
    gain_part = dnormed_half * gain
    row_grad = inv_rms * gain_part - hidden_half * (inv_rms * inv_rms * inv_rms) * (
        jnp.sum(gain_part * hidden_half, axis=1, keepdims=True) / width
    )
    input_grad = join_halves((row_grad + half_of(out_grad).astype(f32) * valid).astype(bf16))

    role = jnp.full((slots,), 3 * heads, jnp.int32).at[owner_map].set(jnp.arange(3 * heads, dtype=jnp.int32))
    slotted, narrow_grad = grads_call(role, ends, dboth, scaled, dnarrow, normed, out_grad, heads, slots)
    owned = lax.psum_scatter(slotted, "dp", scatter_dimension=0, tiled=True)
    moment_new, master_new = muon_call(owned, moment, master)

    skip_sum = jnp.sum(skip_grad[0].reshape(heads, HEADDIM), axis=1)
    head_all = jnp.concatenate([head_grad[0:2, :heads], skip_sum[None, :]], axis=0)
    states_width = state_proj.shape[1]
    gain_total, state_total, shared_total = lax.psum(
        (gain_grad[0], narrow_grad[:states_width].T, shared_grad[0:5]), ("dp", "tensor")
    )
    step_total, head_total, conv_total = lax.psum(
        (narrow_grad[states_width : states_width + heads].T, head_all, conv_grad[0:6]), "dp"
    )
    tokens_all = tok_rows * dp_size
    gain_moment_new, norm_gain_new = small_update(norm_gain, gain_moment, gain_total, tokens_all)
    state_moment_new, state_proj_new = small_update(state_proj, state_moment, state_total, tokens_all)
    step_moment_new, step_proj_new = small_update(step_proj, step_moment, step_total, tokens_all)
    head_moment_new, head_params_new = small_update(head_params, head_moment, head_total, tokens_all)
    conv_moment_new, conv_params_new = small_update(conv_params, conv_moment, conv_total, tokens_all)
    state_conv_moment_new, state_conv_new = small_update(
        state_conv, state_conv_moment, shared_total, tokens_all
    )
    return (
        block_out,
        input_grad,
        moment_new.transpose(0, 2, 1),
        master_new.transpose(0, 2, 1),
        state_moment_new,
        state_proj_new,
        step_moment_new,
        step_proj_new,
        gain_moment_new,
        norm_gain_new,
        head_moment_new,
        head_params_new,
        conv_moment_new,
        conv_params_new,
        state_conv_moment_new,
        state_conv_new,
    )


def solution(mesh):
    in_specs = (
        P("dp", None),
        P("dp", None),
        P("dp", None),
        P(),
        P("dp", None, "tensor"),
        P("dp", None, "tensor"),
        P(),
        P(),
        P(None, "tensor"),
        P(None, "tensor"),
        P(),
        P(),
        P(None, "tensor"),
        P(None, "tensor"),
        P(None, "tensor"),
        P(None, "tensor"),
        P(),
        P(),
    )
    out_specs = (
        P("dp", None),
        P("dp", None),
        P("dp", None, "tensor"),
        P("dp", None, "tensor"),
        P(),
        P(),
        P(None, "tensor"),
        P(None, "tensor"),
        P(),
        P(),
        P(None, "tensor"),
        P(None, "tensor"),
        P(None, "tensor"),
        P(None, "tensor"),
        P(),
        P(),
    )
    return jax.shard_map(
        per_device, mesh=mesh, in_specs=in_specs, out_specs=out_specs, check_vma=False
    )
```

```python
import functools
import math

import jax
import jax.numpy as jnp
from jax import lax
from jax.experimental import pallas as pl
from jax.experimental.pallas import tpu as pltpu
from jax.sharding import PartitionSpec as P

HEADDIM = 64
NS_STEPS = 5
ROWS = 256
SUB = 128
LANES = 128
NARROW = 384
CHUNK = 384

exact_mode = lax.Precision.HIGHEST
norm_eps = 1e-05
schulz_coefs = (3.4445, -4.775, 2.0315)
muon_decay = 0.95
muon_rate = 0.02
small_decay = 0.9
small_rate = 2.0
log2_e = 1.4426950408889634
f32 = jnp.float32
bf16 = jnp.bfloat16
far_below = -1e30


def dot_nn(left, right, precision=None):
    return lax.dot_general(
        left, right, (((1,), (0,)), ((), ())), precision=precision, preferred_element_type=f32
    )


def dot_nt(left, right, precision=None):
    return lax.dot_general(
        left, right, (((1,), (1,)), ((), ())), precision=precision, preferred_element_type=f32
    )


def dot_tn(left, right, precision=None):
    return lax.dot_general(
        left, right, (((0,), (0,)), ((), ())), precision=precision, preferred_element_type=f32
    )


def sigmoid(values):
    return 0.5 * jnp.tanh(0.5 * values) + 0.5


def iota(shape, dim):
    return lax.broadcasted_iota(jnp.int32, shape, dim)


def segment_at(place, ends_ref, count):
    total = (place >= ends_ref[0]).astype(jnp.int32)
    for k in range(1, count):
        total = total + (place >= ends_ref[k]).astype(jnp.int32)
    return total


def step_terms(step_part, head_ref):
    shifted = step_part + head_ref[0:1, :]
    small = jnp.exp(-jnp.abs(shifted))
    tail = jnp.where(
        small < 0.01, small * (1.0 - small * (0.5 - small * (1.0 / 3.0))), jnp.log(1.0 + small)
    )
    step = jnp.maximum(shifted, 0.0) + tail
    decay = -jnp.exp(head_ref[1:2, :])
    log_rate = step * (decay * log2_e)
    lower = (iota((SUB, SUB), 0) >= iota((SUB, SUB), 1)).astype(f32)
    cum = dot_nn(lower, log_rate, exact_mode)
    source = cum - jnp.log(step) * log2_e
    return shifted, step, decay, cum, source


def expand(values, pair):
    shape = (values.shape[0], LANES)
    low = jnp.broadcast_to(values[:, 2 * pair : 2 * pair + 1], shape)
    high = jnp.broadcast_to(values[:, 2 * pair + 1 : 2 * pair + 2], shape)
    return jnp.where(iota(shape, 1) < HEADDIM, low, high)


def split_pair(values):
    low = iota(values.shape, 1) < HEADDIM
    zero = jnp.zeros_like(values)
    return jnp.where(low, values, zero), jnp.where(low, zero, values)


def lanes_of(pair):
    return slice(pair * LANES, (pair + 1) * LANES)


def shift_mask(place, shift, ends_ref, count, rows_all):
    other = place + shift
    inside = (other >= 0) & (other < rows_all)
    same = segment_at(place, ends_ref, count) == segment_at(other, ends_ref, count)
    return jnp.where(inside & same, 1.0, 0.0).astype(f32)


def conv_tile(buf_ref, first, lanes, taps, masks):
    total = taps[4:5, :] + taps[3:4, :] * buf_ref[first + 8 : first + 8 + SUB, lanes]
    for back in (1, 2, 3):
        rows = buf_ref[first + 8 - back : first + 8 - back + SUB, lanes]
        total = total + taps[3 - back : 4 - back, :] * (rows * masks[back - 1])
    return total


def block_terms(base, ends_ref, count):
    row_at = base + iota((SUB, SUB), 0)
    col_at = base + iota((SUB, SUB), 1)
    seg_row = segment_at(row_at, ends_ref, count)
    seg_col = segment_at(col_at, ends_ref, count)
    seg_last = segment_at(base + SUB - 1, ends_ref, count)
    seg_before = jnp.where(base == 0, -1, segment_at(base - 1, ends_ref, count))
    carried = jnp.where(seg_row == seg_before, 1.0, 0.0).astype(f32)
    tail_same = jnp.where(seg_row == seg_last, 1.0, 0.0).astype(f32)
    through = jnp.where(seg_last == seg_before, 1.0, 0.0).astype(f32)
    same = seg_row == seg_col
    return row_at, col_at, same, carried, tail_same, through


def load_weights(stack_ref, place_ref, held_ref, sems, first, count):
    copies = []
    for m in range(count):
        copies.append(
            pltpu.make_async_copy(
                stack_ref.at[place_ref[first + m]],
                held_ref.at[pl.ds(m * HEADDIM, HEADDIM)],
                sems.at[m],
            )
        )
    for copy in copies:
        copy.start()
    return copies


def forward_kernel(
    heads, seq_count, rows_all,
    place_ref, ends_ref,
    hidden_ref, cot_ref, stack_ref, gain_ref, narrow_ref, head_ref, conv_ref, shared_ref,
    normed_ref, gate_ref, input_ref, mixed_ref, dscaled_ref, shared_in_ref, step_ref, state_ref,
    sums_ref, part_ref,
    weights, sems, in_buf, shared_buf, state, low_buf, tail_buf, across,
):
    block = pl.program_id(0)
    inner = heads * HEADDIM
    pairs = heads // 2

    @pl.when(block == 0)
    def _():
        copies = load_weights(stack_ref, place_ref, weights, sems, 0, 3 * heads)
        in_buf[0:8, :] = jnp.zeros((8, inner), f32)
        shared_buf[0:8, :] = jnp.zeros((8, 2 * LANES), f32)
        state[...] = jnp.zeros_like(state)
        for copy in copies:
            copy.wait()

    first_row = block * ROWS
    hidden = hidden_ref[...].astype(f32)
    inv_rms = lax.rsqrt(jnp.mean(hidden * hidden, axis=1, keepdims=True) + norm_eps)
    normed = (hidden * inv_rms * gain_ref[0:1, :]).astype(bf16)
    normed_ref[...] = normed
    in_buf[8:, :] = dot_nt(normed, weights[inner : 2 * inner, :])
    narrow = dot_nn(normed, narrow_ref[...])
    shared_buf[8:, :] = narrow[:, 0 : 2 * LANES]
    step_ref[...] = narrow[:, 2 * LANES : 3 * LANES]
    gate_ref[...] = dot_nt(normed, weights[0:inner, :])
    row_at = first_row + iota((ROWS, cot_ref.shape[1]), 0)
    cot = jnp.where(row_at < ends_ref[seq_count - 1], cot_ref[...].astype(f32), 0.0).astype(bf16)
    dscaled_ref[...] = dot_nt(cot, weights[2 * inner : 3 * inner, :])
    input_ref[...] = in_buf[8:, :]
    shared_in_ref[...] = shared_buf[8:, :]

    for sub in range(ROWS // SUB):
        first = sub * SUB
        base = first_row + first
        row_at, col_at, same, carried, tail_same, through = block_terms(base, ends_ref, seq_count)
        causal = jnp.where(same & (row_at >= col_at), 0.0, far_below).astype(f32)
        masks = [shift_mask(row_at, -back, ends_ref, seq_count, rows_all) for back in (1, 2, 3)]
        bc = []
        for part in range(2):
            lanes = lanes_of(part)
            u = conv_tile(shared_buf, first, lanes, shared_ref[:, lanes], masks)
            bc.append((u * sigmoid(u)).astype(bf16))
        b_low, c_low = bc
        _, _, _, cum, source = step_terms(step_ref[first : first + SUB, :], head_ref)
        source_row = source.T
        scores = dot_nt(c_low, b_low)
        cum_last = cum[SUB - 1 : SUB, :]
        entry = jnp.exp2(cum) * carried
        leave = jnp.exp2(cum_last - source) * tail_same
        pass_on = jnp.exp2(cum_last) * through
        state_ref[sub] = state[...]
        across[...] = dot_nn(c_low, state[...].astype(bf16))
        square = jnp.zeros((SUB, LANES), f32)
        inner_dot = jnp.zeros((SUB, LANES), f32)
        for pair in range(pairs):
            lanes = lanes_of(pair)
            u = conv_tile(in_buf, first, lanes, conv_ref[:, lanes], masks)
            x_low = (u * sigmoid(u)).astype(bf16)
            x = x_low.astype(f32)
            mats = []
            for h in (2 * pair, 2 * pair + 1):
                gap = cum[:, h : h + 1] - source_row[h : h + 1, :]
                mats.append((jnp.exp2(gap + causal) * scores).astype(bf16))
            x_a, x_b = split_pair(x_low)
            mixed = dot_nn(jnp.concatenate(mats, axis=1), jnp.concatenate([x_a, x_b], axis=0))
            mixed = mixed + across[:, lanes] * expand(entry, pair)
            mixed = mixed + expand(head_ref[2:3, :], pair) * x
            mixed_ref[first : first + SUB, lanes] = mixed
            gate = gate_ref[first : first + SUB, lanes]
            gated = mixed * (gate * sigmoid(gate))
            gated_gain = gated * conv_ref[5:6, lanes]
            low_buf[first : first + SUB, lanes] = gated_gain.astype(bf16)
            square = square + gated * gated
            inner_dot = inner_dot + dscaled_ref[first : first + SUB, lanes] * gated_gain
            tail_buf[:, lanes] = (x * expand(leave, pair)).astype(bf16)
        fresh = dot_tn(b_low, tail_buf[...])
        for pair in range(pairs):
            lanes = lanes_of(pair)
            state[:, lanes] = state[:, lanes] * expand(pass_on, pair) + fresh[:, lanes]
        sums_ref[0:1, first : first + SUB] = jnp.sum(square.T, axis=0, keepdims=True)
        sums_ref[1:2, first : first + SUB] = jnp.sum(inner_dot.T, axis=0, keepdims=True)
    sums_ref[2:8, :] = jnp.zeros((6, ROWS), f32)
    in_buf[0:8, :] = in_buf[ROWS : ROWS + 8, :]
    shared_buf[0:8, :] = shared_buf[ROWS : ROWS + 8, :]
    part_ref[...] = dot_nn(low_buf[...], weights[2 * inner : 3 * inner, :]).astype(bf16)


def forward_call(place, ends, hidden, cot, stack, gain, narrow, head_rows, conv_rows, shared_rows, heads):
    rows_all, width = hidden.shape
    inner = heads * HEADDIM
    blocks = rows_all // ROWS

    def rows(columns):
        return pl.BlockSpec((ROWS, columns), lambda i, *_: (i, 0))

    def whole(array):
        return pl.BlockSpec(array.shape, lambda i, *_: (0,) * array.ndim)

    state_shape = (ROWS // SUB, LANES, inner)
    out_shape = [
        jax.ShapeDtypeStruct((rows_all, width), bf16),
        jax.ShapeDtypeStruct((rows_all, inner), f32),
        jax.ShapeDtypeStruct((rows_all, inner), f32),
        jax.ShapeDtypeStruct((rows_all, inner), f32),
        jax.ShapeDtypeStruct((rows_all, inner), f32),
        jax.ShapeDtypeStruct((rows_all, 2 * LANES), f32),
        jax.ShapeDtypeStruct((rows_all, LANES), f32),
        jax.ShapeDtypeStruct((rows_all // SUB, LANES, inner), f32),
        jax.ShapeDtypeStruct((8, rows_all), f32),
        jax.ShapeDtypeStruct((rows_all, width), bf16),
    ]
    out_specs = [
        rows(width), rows(inner), rows(inner), rows(inner), rows(inner), rows(2 * LANES), rows(LANES),
        pl.BlockSpec(state_shape, lambda i, *_: (i, 0, 0)),
        pl.BlockSpec((8, ROWS), lambda i, *_: (0, i)),
        rows(width),
    ]
    return pl.pallas_call(
        functools.partial(forward_kernel, heads, ends.shape[0], rows_all),
        grid_spec=pltpu.PrefetchScalarGridSpec(
            num_scalar_prefetch=2,
            grid=(blocks,),
            in_specs=[
                rows(width), rows(width), pl.BlockSpec(memory_space=pl.ANY), whole(gain), whole(narrow),
                whole(head_rows), whole(conv_rows), whole(shared_rows),
            ],
            out_specs=out_specs,
            scratch_shapes=[
                pltpu.VMEM((3 * inner, width), bf16),
                pltpu.SemaphoreType.DMA((3 * heads,)),
                pltpu.VMEM((ROWS + 8, inner), f32),
                pltpu.VMEM((ROWS + 8, 2 * LANES), f32),
                pltpu.VMEM((LANES, inner), f32),
                pltpu.VMEM((ROWS, inner), bf16),
                pltpu.VMEM((SUB, inner), bf16),
                pltpu.VMEM((SUB, inner), f32),
            ],
        ),
        out_shape=out_shape,
        compiler_params=pltpu.CompilerParams(
            dimension_semantics=("arbitrary",), vmem_limit_bytes=56 * 2**20
        ),
        cost_estimate=pl.CostEstimate(
            flops=2 * rows_all * width * (4 * inner + NARROW), bytes_accessed=60 * 2**20, transcendentals=0
        ),
        name="mixer_forward",
    )(place, ends, hidden, cot, stack, gain, narrow, head_rows, conv_rows, shared_rows)


def backward_kernel(
    heads, seq_count, rows_all, inner_all,
    place_ref, ends_ref,
    hidden_ref, gate_ref, input_ref, before_ref, mixed_ref, dscaled_ref, shared_in_ref,
    shared_before_ref, step_ref, state_ref, sums_ref,
    stack_ref, narrow_ref, gain_ref, head_ref, conv_ref, shared_ref,
    dboth_ref, scaled_ref, dnarrow_ref, dnormed_ref, conv_grad_ref, shared_grad_ref, head_grad_ref,
    skip_grad_ref, gain_grad_ref, narrow_grad_ref,
    weights, sems, in_buf, shared_buf, du_buf, dshared_buf, dstate, state_after, from_state, terms,
    source_terms, tail_buf, entry_buf,
):
    turn = pl.program_id(0)
    block = pl.num_programs(0) - 1 - turn
    inner = heads * HEADDIM
    pairs = heads // 2

    @pl.when(turn == 0)
    def _():
        copies = load_weights(stack_ref, place_ref, weights, sems, 0, 2 * heads)
        du_buf[ROWS:, :] = jnp.zeros((8, inner), f32)
        dshared_buf[ROWS:, :] = jnp.zeros((8, 2 * LANES), f32)
        dstate[...] = jnp.zeros_like(dstate)
        state_after[...] = jnp.zeros_like(state_after)
        conv_grad_ref[...] = jnp.zeros_like(conv_grad_ref)
        shared_grad_ref[...] = jnp.zeros_like(shared_grad_ref)
        head_grad_ref[...] = jnp.zeros_like(head_grad_ref)
        skip_grad_ref[...] = jnp.zeros_like(skip_grad_ref)
        gain_grad_ref[...] = jnp.zeros_like(gain_grad_ref)
        narrow_grad_ref[...] = jnp.zeros_like(narrow_grad_ref)
        for copy in copies:
            copy.wait()

    first_row = block * ROWS
    in_buf[0:8, :] = jnp.where(block == 0, 0.0, before_ref[...])
    in_buf[8:, :] = input_ref[...]
    shared_buf[0:8, :] = jnp.where(block == 0, 0.0, shared_before_ref[...])
    shared_buf[8:, :] = shared_in_ref[...]
    reduce_heads = (iota((inner, LANES), 0) // HEADDIM == iota((inner, LANES), 1)).astype(f32)
    upper = (iota((SUB, SUB), 0) <= iota((SUB, SUB), 1)).astype(f32)

    for sub in reversed(range(ROWS // SUB)):
        first = sub * SUB
        here = slice(first, first + SUB)
        base = first_row + first
        row_at, col_at, same, carried, tail_same, through = block_terms(base, ends_ref, seq_count)
        causal = jnp.where(same & (row_at <= col_at), 0.0, far_below).astype(f32)
        masks = [shift_mask(row_at, -back, ends_ref, seq_count, rows_all) for back in (1, 2, 3)]
        bc, bc_slope = [], []
        for part in range(2):
            lanes = lanes_of(part)
            u = conv_tile(shared_buf, first, lanes, shared_ref[:, lanes], masks)
            sig = sigmoid(u)
            bc.append((u * sig).astype(bf16))
            bc_slope.append(sig * (1.0 + u * (1.0 - sig)))
        b_low, c_low = bc
        shifted, step, decay, cum, source = step_terms(step_ref[here, :], head_ref)
        cum_row = cum.T
        scores = dot_nt(b_low, c_low)
        cum_last = cum[SUB - 1 : SUB, :]
        entry = jnp.exp2(cum) * carried
        leave = jnp.exp2(cum_last - source) * tail_same
        pass_on = jnp.exp2(cum_last) * through
        square = sums_ref[0:1, here]
        inner_dot = sums_ref[1:2, here]
        inv_row = lax.rsqrt(square * (1.0 / inner_all) + norm_eps)
        fix_row = inv_row * inv_row * inv_row * inner_dot * (1.0 / inner_all)
        inv = jnp.broadcast_to(inv_row, (SUB, SUB)).T
        fix = jnp.broadcast_to(fix_row, (SUB, SUB)).T
        dstate_low = dstate[...].astype(bf16)
        from_state[...] = dot_nn(b_low, dstate_low)
        dscores = jnp.zeros((SUB, SUB), f32)
        for pair in range(pairs):
            lanes = lanes_of(pair)
            u = conv_tile(in_buf, first, lanes, conv_ref[:, lanes], masks)
            sig = sigmoid(u)
            x_low = (u * sig).astype(bf16)
            x = x_low.astype(f32)
            slope = sig * (1.0 + u * (1.0 - sig))
            gate = gate_ref[here, lanes]
            gate_sig = sigmoid(gate)
            gate_silu = gate * gate_sig
            mixed = mixed_ref[here, lanes]
            gated = mixed * gate_silu
            gain = conv_ref[5:6, lanes]
            dscaled = dscaled_ref[here, lanes]
            normal = gated * inv
            scaled_ref[here, lanes] = (normal * gain).astype(bf16)
            conv_grad_ref[5:6, lanes] += jnp.sum(dscaled * normal, axis=0, keepdims=True)
            dgated = inv * (dscaled * gain) - gated * fix
            dgate = dgated * mixed * (gate_sig * (1.0 + gate * (1.0 - gate_sig)))
            dboth_ref[here, lanes] = dgate.astype(bf16)
            dmixed = dgated * gate_silu
            dy_low = dmixed.astype(bf16)
            dy = dy_low.astype(f32)
            skip = expand(head_ref[2:3, :], pair)
            skip_grad_ref[0:1, lanes] += jnp.sum(dmixed * x, axis=0, keepdims=True)
            x_parts = split_pair(x_low)
            dy_parts = split_pair(dy_low)
            mats = []
            for k in range(2):
                h = 2 * pair + k
                gap = cum_row[h : h + 1, :] - source[:, h : h + 1]
                decays = jnp.exp2(gap + causal)
                mats.append((decays * scores).astype(bf16))
                dscores = dscores + dot_nt(x_parts[k], dy_low) * decays
            dx = dot_nn(jnp.concatenate(mats, axis=1), jnp.concatenate(dy_parts, axis=0))
            leave_here = expand(leave, pair)
            dx = dx + leave_here * from_state[:, lanes]
            source_term = x * dx
            source_terms[:, lanes] = source_term
            terms[:, lanes] = dy * (mixed - skip * x) - source_term
            tail_buf[:, lanes] = (x * leave_here).astype(bf16)
            entry_buf[:, lanes] = (dy * expand(entry, pair)).astype(bf16)
            du_buf[here, lanes] = (dx + skip * dmixed) * slope
        state_low = state_ref[sub].astype(bf16)
        dscores_low = dscores.astype(bf16)
        db = dot_nn(dscores_low, c_low) + dot_nt(tail_buf[...], dstate_low)
        dc = dot_tn(dscores_low, b_low) + dot_nt(entry_buf[...], state_low)
        dshared_buf[here, 0:LANES] = db * bc_slope[0]
        dshared_buf[here, LANES : 2 * LANES] = dc * bc_slope[1]
        at_end = jnp.sum(dstate[...] * state_after[...], axis=0, keepdims=True)
        state_after[...] = state_ref[sub]
        fresh = dot_tn(c_low, entry_buf[...])
        for pair in range(pairs):
            lanes = lanes_of(pair)
            dstate[:, lanes] = dstate[:, lanes] * expand(pass_on, pair) + fresh[:, lanes]
        last = iota((SUB, inner), 0) == SUB - 1
        dcum = dot_nn(terms[...] + jnp.where(last, at_end, 0.0), reduce_heads, exact_mode)
        from_source = dot_nn(source_terms[...], reduce_heads, exact_mode)
        dlog = dot_nn(upper, dcum, exact_mode)
        sig = sigmoid(shifted)
        ratio = jnp.where(shifted < -15.0, 1.0, sig / step)
        dlog_decay = dlog * decay
        dstep = from_source * ratio + dlog_decay * sig
        dnarrow_ref[here, 2 * LANES : 3 * LANES] = dstep.astype(bf16)
        head_grad_ref[0:1, :] += jnp.sum(dstep, axis=0, keepdims=True)
        head_grad_ref[1:2, :] += jnp.sum(dlog_decay * step, axis=0, keepdims=True)

    for sub in range(ROWS // SUB):
        first = sub * SUB
        here = slice(first, first + SUB)
        row_at = first_row + first + iota((SUB, LANES), 0)
        ahead = [shift_mask(row_at, k, ends_ref, seq_count, rows_all) for k in (1, 2, 3)]
        groups = [(pair, True) for pair in range(pairs)] + [(0, False), (1, False)]
        for group, wide in groups:
            lanes = lanes_of(group)
            grads, held = (du_buf, in_buf) if wide else (dshared_buf, shared_buf)
            taps = conv_ref[:, lanes] if wide else shared_ref[:, lanes]
            sums = conv_grad_ref if wide else shared_grad_ref
            du = grads[here, lanes]
            v = held[first + 8 : first + 8 + SUB, lanes]
            dv = taps[3:4, :] * du
            sums[3:4, lanes] += jnp.sum(du * v, axis=0, keepdims=True)
            sums[4:5, lanes] += jnp.sum(du, axis=0, keepdims=True)
            for k in (1, 2, 3):
                moved = grads[first + k : first + k + SUB, lanes] * ahead[k - 1]
                dv = dv + taps[3 - k : 4 - k, :] * moved
                sums[3 - k : 4 - k, lanes] += jnp.sum(moved * v, axis=0, keepdims=True)
            if wide:
                dboth_ref[here, inner + group * LANES : inner + (group + 1) * LANES] = dv.astype(bf16)
            else:
                dnarrow_ref[here, lanes] = dv.astype(bf16)
    du_buf[ROWS:, :] = du_buf[0:8, :]
    dshared_buf[ROWS:, :] = dshared_buf[0:8, :]

    dnormed = dot_nn(dboth_ref[...], weights[...]) + dot_nt(dnarrow_ref[...], narrow_ref[...])
    hidden = hidden_ref[...].astype(f32)
    inv_rms = lax.rsqrt(jnp.mean(hidden * hidden, axis=1, keepdims=True) + norm_eps)
    unit = hidden * inv_rms
    gain_grad_ref[0:1, :] += jnp.sum(dnormed * unit, axis=0, keepdims=True)
    narrow_grad_ref[...] += dot_tn(dnarrow_ref[...], (unit * gain_ref[0:1, :]).astype(bf16))
    dnormed_ref[...] = dnormed.astype(bf16)


def backward_call(
    place, ends, hidden, gate, input_part, mixed, dscaled, shared_in, step_part, states, sums, stack,
    narrow, gain, head_rows, conv_rows, shared_rows, heads, inner_all,
):
    rows_all, width = hidden.shape
    inner = heads * HEADDIM
    blocks = rows_all // ROWS

    def rows(columns):
        return pl.BlockSpec((ROWS, columns), lambda i, *_: (blocks - 1 - i, 0))

    def before(columns):
        step = ROWS // 8
        return pl.BlockSpec(
            (8, columns), lambda i, *_: (jnp.maximum((blocks - 1 - i) * step - 1, 0), 0)
        )

    def whole(shape):
        return pl.BlockSpec(shape, lambda i, *_: (0,) * len(shape))

    out_shape = [
        jax.ShapeDtypeStruct((rows_all, 2 * inner), bf16),
        jax.ShapeDtypeStruct((rows_all, inner), bf16),
        jax.ShapeDtypeStruct((rows_all, NARROW), bf16),
        jax.ShapeDtypeStruct((rows_all, width), bf16),
        jax.ShapeDtypeStruct((8, inner), f32),
        jax.ShapeDtypeStruct((8, 2 * LANES), f32),
        jax.ShapeDtypeStruct((8, LANES), f32),
        jax.ShapeDtypeStruct((8, inner), f32),
        jax.ShapeDtypeStruct((8, width), f32),
        jax.ShapeDtypeStruct((NARROW, width), f32),
    ]
    out_specs = [rows(2 * inner), rows(inner), rows(NARROW), rows(width)] + [
        whole(shape.shape) for shape in out_shape[4:]
    ]
    return pl.pallas_call(
        functools.partial(backward_kernel, heads, ends.shape[0], rows_all, inner_all),
        grid_spec=pltpu.PrefetchScalarGridSpec(
            num_scalar_prefetch=2,
            grid=(blocks,),
            in_specs=[
                rows(width), rows(inner), rows(inner), before(inner), rows(inner), rows(inner),
                rows(2 * LANES), before(2 * LANES), rows(LANES),
                pl.BlockSpec((ROWS // SUB, LANES, inner), lambda i, *_: (blocks - 1 - i, 0, 0)),
                pl.BlockSpec((8, ROWS), lambda i, *_: (0, blocks - 1 - i)),
                pl.BlockSpec(memory_space=pl.ANY), whole(narrow.shape), whole(gain.shape),
                whole(head_rows.shape), whole(conv_rows.shape), whole(shared_rows.shape),
            ],
            out_specs=out_specs,
            scratch_shapes=[
                pltpu.VMEM((2 * inner, width), bf16),
                pltpu.SemaphoreType.DMA((2 * heads,)),
                pltpu.VMEM((ROWS + 8, inner), f32),
                pltpu.VMEM((ROWS + 8, 2 * LANES), f32),
                pltpu.VMEM((ROWS + 8, inner), f32),
                pltpu.VMEM((ROWS + 8, 2 * LANES), f32),
                pltpu.VMEM((LANES, inner), f32),
                pltpu.VMEM((LANES, inner), f32),
                pltpu.VMEM((SUB, inner), f32),
                pltpu.VMEM((SUB, inner), f32),
                pltpu.VMEM((SUB, inner), f32),
                pltpu.VMEM((SUB, inner), bf16),
                pltpu.VMEM((SUB, inner), bf16),
            ],
        ),
        out_shape=out_shape,
        compiler_params=pltpu.CompilerParams(
            dimension_semantics=("arbitrary",), vmem_limit_bytes=56 * 2**20
        ),
        cost_estimate=pl.CostEstimate(
            flops=4 * rows_all * width * (2 * inner + NARROW), bytes_accessed=60 * 2**20, transcendentals=0
        ),
        name="mixer_backward",
    )(
        place, ends, hidden, gate, input_part, input_part, mixed, dscaled, shared_in, shared_in, step_part,
        states, sums, stack, narrow, gain, head_rows, conv_rows, shared_rows,
    )


def grads_kernel(
    heads, slots, seq_count, role_ref, ends_ref, dboth_ref, scaled_ref, normed_ref, cot_ref,
    out_ref, held, sems,
):
    chunk = pl.program_id(0)
    inner = heads * HEADDIM
    width = normed_ref.shape[1]
    held[0 : 2 * inner, :] = dot_tn(dboth_ref[...], normed_ref[...]).astype(bf16)
    row_at = iota(cot_ref.shape, 0)
    cot = jnp.where(row_at < ends_ref[seq_count - 1], cot_ref[...].astype(f32), 0.0).astype(bf16)
    held[2 * inner : 3 * inner, :] = dot_tn(scaled_ref[...], cot).astype(bf16)
    held[3 * inner :, :] = jnp.zeros((HEADDIM, width), bf16)
    copies = []
    for s in range(slots):
        at = pl.multiple_of(role_ref[s] * HEADDIM, HEADDIM)
        copies.append(
            pltpu.make_async_copy(
                held.at[pl.ds(at, HEADDIM), :],
                out_ref.at[s, :, pl.ds(pl.multiple_of(chunk * width, width), width)],
                sems.at[s],
            )
        )
    for copy in copies:
        copy.start()
    for copy in copies:
        copy.wait()


def grads_call(role, ends, dboth, scaled, normed, cot, heads, slots):
    rows_all, width = normed.shape
    inner = heads * HEADDIM

    def whole(array):
        return pl.BlockSpec(array.shape, lambda i, *_: (0, 0), pipeline_mode=pl.Buffered(1))

    part = pl.BlockSpec((rows_all, CHUNK), lambda i, *_: (0, i))
    return pl.pallas_call(
        functools.partial(grads_kernel, heads, slots, ends.shape[0]),
        grid_spec=pltpu.PrefetchScalarGridSpec(
            num_scalar_prefetch=2,
            grid=(width // CHUNK,),
            in_specs=[whole(dboth), whole(scaled), part, part],
            out_specs=pl.BlockSpec(memory_space=pl.ANY),
            scratch_shapes=[
                pltpu.VMEM((3 * inner + HEADDIM, CHUNK), bf16),
                pltpu.SemaphoreType.DMA((slots,)),
            ],
        ),
        out_shape=jax.ShapeDtypeStruct((slots, HEADDIM, width), bf16),
        compiler_params=pltpu.CompilerParams(
            dimension_semantics=("arbitrary",), vmem_limit_bytes=56 * 2**20
        ),
        cost_estimate=pl.CostEstimate(
            flops=2 * rows_all * width * 3 * inner, bytes_accessed=40 * 2**20, transcendentals=0
        ),
        name="weight_grads",
    )(role, ends, dboth, scaled, normed, cot)


def remote(src, dst, send_sem, recv_sem, target):
    return pltpu.make_async_remote_copy(
        src_ref=src,
        dst_ref=dst,
        send_sem=send_sem,
        recv_sem=recv_sem,
        device_id=target,
        device_id_type=pl.DeviceIdType.MESH,
    )


def greet(targets):
    barrier = pltpu.get_barrier_semaphore()
    for target, condition in targets:
        if condition is None:
            pl.semaphore_signal(barrier, inc=1, device_id=target, device_id_type=pl.DeviceIdType.MESH)
        else:

            @pl.when(condition)
            def _(target=target):
                pl.semaphore_signal(
                    barrier, inc=1, device_id=target, device_id_type=pl.DeviceIdType.MESH
                )

    peers = sum(1 if condition is None else condition.astype(jnp.int32) for _, condition in targets)
    pl.semaphore_wait(barrier, peers)


def gather_kernel(
    lines, own_ref, out_ref, local_sem, x_send, x_recv, up_send, up_recv, down_send, down_recv
):
    here = lax.axis_index("dp")
    tensor = lax.axis_index("tensor")
    line, side = here // 2, here % 2
    partner = here + 1 - 2 * side
    slots = own_ref.shape[0]
    most = slots - 1
    has_up, has_down = line < lines - 1, line > 0
    across, above, below = (partner, tensor), (here + 2, tensor), (here - 2, tensor)

    greet([(across, None), (above, has_up), (below, has_down)])
    local = pltpu.make_async_copy(own_ref, out_ref.at[pl.ds(here * slots, slots)], local_sem)
    local.start()

    def most_of(device):
        return out_ref.at[pl.ds(device * slots, most)]

    def last_of(device):
        return out_ref.at[pl.ds(device * slots + most, 1)]

    def x_most(device, index, own=False):
        src = own_ref.at[pl.ds(0, most)] if own else most_of(device)
        return remote(src, most_of(device), x_send.at[index], x_recv.at[index], across)

    def line_copies(sends, recvs, step, at, target, own=False):
        mine, theirs = 2 * at + side, 2 * at + 1 - side
        src_most = own_ref.at[pl.ds(0, most)] if own else most_of(mine)
        src_last = own_ref.at[pl.ds(most, 1)] if own else last_of(mine)
        return [
            remote(src_most, most_of(mine), sends.at[step, 0], recvs.at[step, 0], target),
            remote(src_last, last_of(mine), sends.at[step, 1], recvs.at[step, 1], target),
            remote(last_of(theirs), last_of(theirs), sends.at[step, 2], recvs.at[step, 2], target),
        ]

    x_last = remote(own_ref.at[pl.ds(most, 1)], last_of(here), x_send.at[0], x_recv.at[0], across)
    x_last.start()
    first_up = line_copies(up_send, up_recv, 0, line, above, True)
    first_down = line_copies(down_send, down_recv, 0, line, below, True)

    @pl.when(has_up)
    def _():
        first_up[1].start()
        first_up[0].start()

    @pl.when(has_down)
    def _():
        first_down[1].start()
        first_down[0].start()

    x_most(here, 1, True).start()
    x_last.wait_recv()

    @pl.when(has_up)
    def _():
        first_up[2].start()

    @pl.when(has_down)
    def _():
        first_down[2].start()

    for k in range(1, lines):

        @pl.when(line >= k)
        def _(k=k):
            for copy in line_copies(up_send, up_recv, k - 1, line - k, above):
                copy.wait_recv()
            if k < lines - 1:

                @pl.when(has_up)
                def _():
                    for copy in line_copies(up_send, up_recv, k, line - k, above):
                        copy.start()

            x_most(2 * (line - k) + side, 1 + k).start()

        @pl.when(line + k < lines)
        def _(k=k):
            for copy in line_copies(down_send, down_recv, k - 1, line + k, below):
                copy.wait_recv()
            if k < lines - 1:

                @pl.when(has_down)
                def _():
                    for copy in line_copies(down_send, down_recv, k, line + k, below):
                        copy.start()

            x_most(2 * (line + k) + side, lines + k).start()

    local.wait()
    x_last.wait_send()
    x_most(partner, 1).wait()
    for k in range(1, lines):

        @pl.when(line >= k)
        def _(k=k):
            x_most(2 * (line - k) + 1 - side, 1 + k).wait()

        @pl.when(line + k < lines)
        def _(k=k):
            x_most(2 * (line + k) + 1 - side, lines + k).wait()

    for k in range(lines - 1):

        @pl.when(has_up & (line >= k))
        def _(k=k):
            for copy in line_copies(up_send, up_recv, k, line - k, above):
                copy.wait_send()

        @pl.when(has_down & (line + k < lines))
        def _(k=k):
            for copy in line_copies(down_send, down_recv, k, line + k, below):
                copy.wait_send()


def gather_call(own, dp_size):
    slots, side, width = own.shape
    lines = dp_size // 2
    step_sems = pltpu.SemaphoreType.DMA((lines - 1, 3))
    x_sems = pltpu.SemaphoreType.DMA((2 * lines,))
    return pl.pallas_call(
        functools.partial(gather_kernel, lines),
        in_specs=[pl.BlockSpec(memory_space=pl.ANY)],
        out_specs=pl.BlockSpec(memory_space=pl.ANY),
        out_shape=jax.ShapeDtypeStruct((slots * dp_size, side, width), own.dtype),
        scratch_shapes=[
            pltpu.SemaphoreType.DMA, x_sems, x_sems, step_sems, step_sems, step_sems, step_sems,
        ],
        compiler_params=pltpu.CompilerParams(collective_id=0, has_side_effects=True),
        name="gather_weights",
    )(own)


def reduce_kernel(
    lines,
    grads, narrow_ref, extra_ref, owned_ref, totals_ref,
    x_in, up_in, down_in, last_out, last_in, quarter_in, quarter_out, fold_in, halves, half_in, group_in,
    group_out, group_back,
    x_send, x_recv, up_send, up_recv, down_send, down_recv, last_sems, small_sems, group_sems, back_sems,
):
    here = lax.axis_index("dp")
    tensor = lax.axis_index("tensor")
    line, side = here // 2, here % 2
    core, chip = tensor % 2, tensor // 2
    slots = owned_ref.shape[0]
    most = slots - 1
    width = narrow_ref.shape[1]
    half = width // 2
    group = halves.shape[1] // lines
    has_up, has_down = line < lines - 1, line > 0
    across = (here + 1 - 2 * side, tensor)
    above, below = (here + 2, tensor), (here - 2, tensor)
    other_core = (here, tensor + 1 - 2 * core)
    other_chip = (here, (tensor + 2) % 4)
    on_line = [(2 * ((line + k) % lines) + side, tensor) for k in range(1, lines)]

    greet([(target, None) for target in [across, other_core, other_chip] + on_line])

    def add(*parts):
        total = parts[0].astype(f32)
        for part in parts[1:]:
            total = total + part.astype(f32)
        return total

    def quarter_copy(k):
        rows = pl.ds(pl.multiple_of((2 * k + 1 - core) * HEADDIM, HEADDIM), HEADDIM)
        return remote(
            narrow_ref.at[rows], quarter_in.at[k], small_sems.at[0, k], small_sems.at[1, k], other_core
        )

    fold_copy = remote(quarter_out, fold_in, small_sems.at[0, 2], small_sems.at[1, 2], other_chip)
    half_copy = remote(
        halves.at[1 - side], half_in, small_sems.at[0, 3], small_sems.at[1, 3], across
    )

    def group_copy(k):
        to = (line + k) % lines
        rows = pl.ds(pl.multiple_of(to * group, group), group)
        return remote(
            halves.at[side, rows], group_in.at[k - 1], group_sems.at[0, k - 1], group_sems.at[1, k - 1],
            on_line[k - 1],
        )

    def back_copy(k):
        return remote(
            group_out, group_back.at[k - 1], back_sems.at[0, k - 1], back_sems.at[1, k - 1], on_line[k - 1]
        )

    total_half = remote(
        totals_ref.at[tensor, side], totals_ref.at[tensor, side], small_sems.at[0, 4], small_sems.at[1, 4],
        across,
    )
    total_chip = remote(
        totals_ref.at[tensor], totals_ref.at[tensor], small_sems.at[0, 5], small_sems.at[1, 5], other_chip
    )

    def total_core(k):
        at = core + 2 * k
        return remote(
            totals_ref.at[at], totals_ref.at[at], small_sems.at[0, 6 + k], small_sems.at[1, 6 + k], other_core
        )

    def small_0():
        for k in range(2):
            quarter_copy(k).start()

    def small_1():
        for k in range(2):
            quarter_copy(k).wait()
        far = pl.ds(pl.multiple_of((2 * (1 - chip) + core) * HEADDIM, HEADDIM), HEADDIM)
        quarter_out[...] = narrow_ref[far, :] + quarter_in[1 - chip]
        fold_copy.start()

    def small_2():
        fold_copy.wait()
        near = pl.ds(pl.multiple_of((2 * chip + core) * HEADDIM, HEADDIM), HEADDIM)
        mine = narrow_ref[near, :] + quarter_in[chip] + fold_in[...]
        rest = extra_ref[...]
        for k in range(2):
            columns = slice(k * half, (k + 1) * half)
            halves[k, 0:HEADDIM, :] = mine[:, columns]
            halves[k, HEADDIM:, :] = rest[:, columns]
        half_copy.start()

    def small_3():
        half_copy.wait()
        halves[side] = halves[side] + half_in[...]
        for k in range(1, lines):
            group_copy(k).start()

    def small_4():
        for k in range(1, lines):
            group_copy(k).wait()
        rows = pl.ds(pl.multiple_of(line * group, group), group)
        total = halves[side, rows, :]
        for k in range(1, lines):
            total = total + group_in[k - 1]
        group_out[...] = total
        for k in range(1, lines):
            back_copy(k).start()

    def small_5():
        for k in range(1, lines):
            back_copy(k).wait()
        rows = pl.ds(pl.multiple_of(line * group, group), group)
        totals_ref[tensor, side, rows, :] = group_out[...]
        for k in range(1, lines):
            source = (line + lines - k) % lines
            rows = pl.ds(pl.multiple_of(source * group, group), group)
            totals_ref[tensor, side, rows, :] = group_back[k - 1]
        total_half.start()

    def small_6():
        total_half.wait()
        total_chip.start()

    def small_7():
        total_chip.wait()
        for k in range(2):
            total_core(k).start()

    def small_8():
        for k in range(2):
            total_core(k).wait()

    small = [small_1, small_2, small_3, small_4, small_5, small_6, small_7]

    def x_copy(at, i):
        return remote(
            grads.at[(2 * at + 1 - side) * slots + i], x_in.at[at, i], x_send.at[at, i], x_recv.at[at, i], across
        )

    def x_start(at):
        def one(i, carry):
            x_copy(at, i).start()
            return carry

        lax.fori_loop(0, most, one, 0)

    def x_needed(step):
        if step < lines - 1:

            @pl.when(lines - 1 - step > line)
            def _():
                x_start(lines - 1 - step)

            @pl.when(step < line)
            def _():
                x_start(step)
        else:
            x_start(line)

    def line_copy(src, at, i, upward):
        if upward:
            return remote(src, up_in.at[at, i], up_send.at[at, i], up_recv.at[at, i], above)
        return remote(src, down_in.at[at, i], down_send.at[at, i], down_recv.at[at, i], below)

    def line_most(at, i, upward):
        arrived = up_in if upward else down_in
        x_copy(at, i).wait_recv()
        own = add(grads[(2 * at + side) * slots + i], x_in[at, i])

        @pl.when(has_down if upward else has_up)
        def _():
            line_copy(x_in.at[at, i], at, i, upward).wait_recv()
            x_in[at, i] = add(own, arrived[at, i]).astype(bf16)

        @pl.when(jnp.logical_not(has_down if upward else has_up))
        def _():
            x_in[at, i] = own.astype(bf16)

        line_copy(x_in.at[at, i], at, i, upward).start()

    def line_last(at, k, upward):
        arrived = up_in if upward else down_in
        own = grads.at[(2 * at + k) * slots + most]

        @pl.when(has_down if upward else has_up)
        def _():
            line_copy(own, at, most + k, upward).wait_recv()
            arrived[at, most + k] = add(own[...], arrived[at, most + k]).astype(bf16)
            line_copy(arrived.at[at, most + k], at, most + k, upward).start()

        @pl.when(jnp.logical_not(has_down if upward else has_up))
        def _():
            line_copy(own, at, most + k, upward).start()

    def each_way(step, work):
        @pl.when(lines - 1 - step > line)
        def _():
            work(lines - 1 - step, True)

        @pl.when(step < line)
        def _():
            work(step, False)

    small_0()
    x_needed(0)
    for step in range(lines - 1):
        for k in range(2):
            each_way(step, lambda at, upward, k=k: line_last(at, k, upward))
        x_needed(step + 1)
        if small:
            small.pop(0)()

        def one(i, carry, step=step):
            each_way(step, lambda at, upward: line_most(at, i, upward))
            return carry

        lax.fori_loop(0, most, one, 0)
        if small:
            small.pop(0)()

    def gathered_last(k):
        return grads[(2 * line + k) * slots + most].astype(f32)

    owned_ref[most] = gathered_last(side)
    to_send = gathered_last(1 - side)
    last_out[...] = to_send

    @pl.when(has_down)
    def _():
        for k in range(2):
            line_copy(last_in, line, most + k, True).wait_recv()
        owned_ref[most] = owned_ref[most] + up_in[line, most + side].astype(f32)
        last_out[...] = last_out[...] + up_in[line, most + 1 - side].astype(f32)

    @pl.when(has_up)
    def _():
        for k in range(2):
            line_copy(last_in, line, most + k, False).wait_recv()
        owned_ref[most] = owned_ref[most] + down_in[line, most + side].astype(f32)
        last_out[...] = last_out[...] + down_in[line, most + 1 - side].astype(f32)

    x_in[line, most] = last_out[...].astype(bf16)
    last_copy = remote(x_in.at[line, most], last_in, last_sems.at[0], last_sems.at[1], across)
    last_copy.start()
    while small:
        small.pop(0)()

    def finish(i, carry):
        x_copy(line, i).wait_recv()
        owned_ref[i] = add(grads[(2 * line + side) * slots + i], x_in[line, i])

        @pl.when(has_down)
        def _():
            line_copy(last_in, line, i, True).wait_recv()
            owned_ref[i] = owned_ref[i] + up_in[line, i].astype(f32)

        @pl.when(has_up)
        def _():
            line_copy(last_in, line, i, False).wait_recv()
            owned_ref[i] = owned_ref[i] + down_in[line, i].astype(f32)

        return carry

    lax.fori_loop(0, most, finish, 0)
    last_copy.wait()
    owned_ref[most] = owned_ref[most] + last_in[...].astype(f32)
    small_8()

    def x_sent(at):
        def one(i, carry):
            x_copy(at, i).wait_send()
            return carry

        lax.fori_loop(0, most, one, 0)

    def line_sent(at, upward):
        def one(i, carry):
            line_copy(last_in, at, i, upward).wait_send()
            return carry

        lax.fori_loop(0, slots + 1, one, 0)

    x_sent(line)
    for step in range(lines - 1):
        each_way(step, lambda at, upward: x_sent(at))
        each_way(step, line_sent)


def reduce_call(grads, narrow, extra, dp_size):
    slots_all, side, width = grads.shape
    slots = slots_all // dp_size
    lines = dp_size // 2
    small_rows = HEADDIM + extra.shape[0]
    group = small_rows // lines
    spec = pl.BlockSpec(memory_space=pltpu.VMEM)
    sems = pltpu.SemaphoreType.DMA
    return pl.pallas_call(
        functools.partial(reduce_kernel, lines),
        in_specs=[spec] * 3,
        out_specs=[spec] * 2,
        out_shape=[
            jax.ShapeDtypeStruct((slots, side, width), f32),
            jax.ShapeDtypeStruct((4, 2, small_rows, width // 2), f32),
        ],
        scratch_shapes=[
            pltpu.VMEM((lines, slots, side, width), bf16),
            pltpu.VMEM((lines, slots + 1, side, width), bf16),
            pltpu.VMEM((lines, slots + 1, side, width), bf16),
            pltpu.VMEM((side, width), f32),
            pltpu.VMEM((side, width), bf16),
            pltpu.VMEM((2, side, width), f32),
            pltpu.VMEM((side, width), f32),
            pltpu.VMEM((side, width), f32),
            pltpu.VMEM((2, small_rows, width // 2), f32),
            pltpu.VMEM((small_rows, width // 2), f32),
            pltpu.VMEM((lines - 1, group, width // 2), f32),
            pltpu.VMEM((group, width // 2), f32),
            pltpu.VMEM((lines - 1, group, width // 2), f32),
            sems((lines, slots)), sems((lines, slots)),
            sems((lines, slots + 1)), sems((lines, slots + 1)),
            sems((lines, slots + 1)), sems((lines, slots + 1)),
            sems((2,)), sems((2, 8)), sems((2, lines - 1)), sems((2, lines - 1)),
        ],
        compiler_params=pltpu.CompilerParams(
            collective_id=1, has_side_effects=True, vmem_limit_bytes=56 * 2**20
        ),
        cost_estimate=pl.CostEstimate(flops=10**11, bytes_accessed=40 * 2**20, transcendentals=0),
        name="reduce_grads",
    )(grads, narrow, extra)


def muon_kernel(rate, grad_ref, moment_ref, master_ref, moment_out, master_out):
    first_coef, second_coef, third_coef = schulz_coefs
    side = HEADDIM
    same = iota((side, side), 0) == iota((side, side), 1)
    eye = jnp.where(same, 1.0, 0.0).astype(f32)
    slots = grad_ref.shape[0]
    grams, totals, scales = [], [], []
    for s in range(slots):
        moment = muon_decay * moment_ref[s] + grad_ref[s].astype(f32)
        moment_out[s] = moment
        square = jnp.sum(jnp.sum(moment * moment, axis=1, keepdims=True), axis=0, keepdims=True)
        scale = 1.0 / (jnp.sqrt(square) + 1e-07)
        scaled = moment * scale
        grams.append(dot_nt(scaled, scaled, exact_mode))
        totals.append(eye)
        scales.append(scale)
    for _ in range(NS_STEPS):
        for s in range(slots):
            gram = grams[s]
            factor = (
                first_coef * eye + second_coef * gram + third_coef * dot_nn(gram, gram, exact_mode)
            )
            totals[s] = dot_nn(factor, totals[s], exact_mode)
            grams[s] = dot_nn(dot_nn(factor, gram, exact_mode), factor, exact_mode)
    for s in range(slots):
        ortho = dot_nn(totals[s], moment_out[s] * scales[s], exact_mode)
        master_out[s] = master_ref[s] - rate * ortho


def muon_call(grad, moment, master):
    slots, side, width = moment.shape
    spec = pl.BlockSpec(memory_space=pltpu.VMEM)
    return pl.pallas_call(
        functools.partial(muon_kernel, muon_rate * math.sqrt(max(width, side))),
        in_specs=[spec] * 3,
        out_specs=[spec] * 2,
        out_shape=[jax.ShapeDtypeStruct(moment.shape, f32)] * 2,
        compiler_params=pltpu.CompilerParams(vmem_limit_bytes=56 * 2**20),
        name="muon",
    )(grad, moment, master)


def small_update(weight, moment, gradient, tokens_all):
    moment_new = small_decay * moment + (1.0 - small_decay) * gradient
    return (moment_new, weight - small_rate / math.sqrt(tokens_all) * moment_new)


def pad_to(array, rows, columns):
    return jnp.pad(array, ((0, rows - array.shape[0]), (0, columns - array.shape[1])))


def swap(values, bit):
    return lax.ppermute(values, "tensor", [(t, t ^ bit) for t in range(4)])


def near_half(part):
    half = part.shape[0] // 2
    core = lax.axis_index("tensor") % 2
    mine = lax.dynamic_slice_in_dim(part, core * half, half)
    other = lax.dynamic_slice_in_dim(part, (1 - core) * half, half)
    return (mine.astype(f32) + swap(other, 1).astype(f32)).astype(bf16)


def join_halves(half):
    core = lax.axis_index("tensor") % 2
    other = swap(half, 1)
    first = jnp.where(core == 0, half, other)
    second = jnp.where(core == 0, other, half)
    return jnp.concatenate([first, second], axis=0)


def half_of(values, axis=0):
    half = values.shape[axis] // 2
    core = lax.axis_index("tensor") % 2
    return lax.dynamic_slice_in_dim(values, core * half, half, axis=axis)


def per_device(
    hidden_in,
    out_grad,
    seq_lengths,
    owner_map,
    muon_master,
    muon_moment,
    state_proj,
    state_moment,
    step_proj,
    step_moment,
    norm_gain,
    gain_moment,
    head_params,
    head_moment,
    conv_params,
    conv_moment,
    state_conv,
    state_conv_moment,
):
    tok_rows, width = hidden_in.shape
    heads = step_proj.shape[1]
    inner = conv_params.shape[1]
    dp_size = lax.axis_size("dp")
    inner_all = inner * lax.axis_size("tensor")
    slots = muon_master.shape[0] * dp_size
    ends = jnp.cumsum(seq_lengths[0], dtype=jnp.int32)
    master = muon_master.transpose(0, 2, 1)
    moment = muon_moment.transpose(0, 2, 1)
    stack = gather_call(master.astype(bf16), dp_size)
    narrow = pad_to(jnp.concatenate([state_proj, step_proj], axis=1), width, NARROW).astype(bf16)
    gain = norm_gain[None, :]
    head_rows = pad_to(head_params, 8, LANES)
    conv_rows = pad_to(conv_params, 8, inner)
    shared_rows = pad_to(state_conv, 8, state_conv.shape[1])

    normed, gate, input_part, mixed, dscaled, shared_in, step_part, states, sums, part = forward_call(
        owner_map, ends, hidden_in, out_grad, stack, gain, narrow, head_rows, conv_rows, shared_rows, heads
    )
    sums = jnp.pad(lax.psum(sums[0:2], "tensor"), ((0, 6), (0, 0)))
    near = near_half(part)
    near, sums = lax.optimization_barrier((near, sums))
    far = swap(near, 2)
    core = lax.axis_index("tensor") % 2
    half = tok_rows // 2
    valid = ((core * half + jnp.arange(half, dtype=jnp.int32)) < ends[-1]).astype(f32)[:, None]
    hidden_half = half_of(hidden_in).astype(f32)
    gate_inv = lax.rsqrt(half_of(sums[0]) / inner_all + norm_eps)[:, None]
    dboth, scaled, _, dnormed, conv_grad, shared_grad, head_grad, skip_grad, gain_grad, narrow_grad = (
        backward_call(
            owner_map, ends, hidden_in, gate, input_part, mixed, dscaled, shared_in, step_part, states, sums,
            stack, narrow, gain, head_rows, conv_rows, shared_rows, heads, inner_all,
        )
    )
    far, dnormed, dboth = lax.optimization_barrier((far, dnormed, dboth))
    branch = (near.astype(f32) + far.astype(f32)) * gate_inv
    block_out = join_halves(((hidden_half + branch) * valid).astype(bf16))
    role = jnp.full((slots,), 3 * heads, jnp.int32).at[owner_map].set(jnp.arange(3 * heads, dtype=jnp.int32))
    slotted = grads_call(role, ends, dboth, scaled, normed, out_grad, heads, slots)

    states_width = state_proj.shape[1]
    skip_sum = jnp.sum(skip_grad[0].reshape(heads, HEADDIM), axis=1)
    shared_size, head_size = 5 * states_width, 3 * heads
    tiny = jnp.concatenate(
        [shared_grad[0:5].reshape(-1), head_grad[0, :heads], head_grad[1, :heads], skip_sum]
    )
    conv_lines = conv_params.size // width
    misc = jnp.concatenate(
        [conv_grad[0:6].reshape(conv_lines, width), gain_grad[0:1], pad_to(tiny[None, :], 1, width)], axis=0
    )
    small_rows = -(-(HEADDIM + 32) // (8 * (dp_size // 2))) * (8 * (dp_size // 2))
    step_grad = narrow_grad[states_width : states_width + 16]
    extra = jnp.concatenate([step_grad, pad_to(misc, small_rows - HEADDIM - 16, width)], axis=0)

    near_grad = near_half(dnormed)
    near_grad, slotted, extra = lax.optimization_barrier((near_grad, slotted, extra))
    far_grad = swap(near_grad, 2)
    owned, totals = reduce_call(slotted, narrow_grad, extra, dp_size)
    owned, totals, far_grad = lax.optimization_barrier((owned, totals, far_grad))
    dnormed_half = near_grad.astype(f32) + far_grad.astype(f32)
    inv_rms = lax.rsqrt(jnp.mean(hidden_half * hidden_half, axis=1, keepdims=True) + norm_eps)
    gain_part = dnormed_half * gain
    row_grad = inv_rms * gain_part - hidden_half * (inv_rms * inv_rms * inv_rms) * (
        jnp.sum(gain_part * hidden_half, axis=1, keepdims=True) / width
    )
    input_grad = join_halves((row_grad + half_of(out_grad).astype(f32) * valid).astype(bf16))

    moment_new, master_new = muon_call(owned, moment, master)

    state_total = jnp.concatenate([totals[:, k, :HEADDIM] for k in range(2)], axis=2)
    state_total = state_total.reshape(states_width, width).T
    rest = lax.dynamic_index_in_dim(totals, lax.axis_index("tensor"), 0, keepdims=False)[:, HEADDIM:]
    rest = jnp.concatenate([rest[0], rest[1]], axis=1)
    step_total = rest[:heads].T
    conv_total = rest[16 : 16 + conv_lines].reshape(conv_params.shape)
    tiny_row = rest[17 + conv_lines]
    head_total = tiny_row[shared_size : shared_size + head_size].reshape(3, heads)
    both = jnp.sum(totals[:, :, HEADDIM + 16 + conv_lines : HEADDIM + 18 + conv_lines], axis=0)
    both = jnp.concatenate([both[0], both[1]], axis=1)
    gain_total = both[0]
    shared_total = both[1, :shared_size].reshape(5, states_width)
    tokens_all = tok_rows * dp_size
    gain_moment_new, norm_gain_new = small_update(norm_gain, gain_moment, gain_total, tokens_all)
    state_moment_new, state_proj_new = small_update(state_proj, state_moment, state_total, tokens_all)
    step_moment_new, step_proj_new = small_update(step_proj, step_moment, step_total, tokens_all)
    head_moment_new, head_params_new = small_update(head_params, head_moment, head_total, tokens_all)
    conv_moment_new, conv_params_new = small_update(conv_params, conv_moment, conv_total, tokens_all)
    state_conv_moment_new, state_conv_new = small_update(
        state_conv, state_conv_moment, shared_total, tokens_all
    )
    return (
        block_out,
        input_grad,
        moment_new.transpose(0, 2, 1),
        master_new.transpose(0, 2, 1),
        state_moment_new,
        state_proj_new,
        step_moment_new,
        step_proj_new,
        gain_moment_new,
        norm_gain_new,
        head_moment_new,
        head_params_new,
        conv_moment_new,
        conv_params_new,
        state_conv_moment_new,
        state_conv_new,
    )


def solution(mesh):
    in_specs = (
        P("dp", None),
        P("dp", None),
        P("dp", None),
        P(),
        P("dp", None, "tensor"),
        P("dp", None, "tensor"),
        P(),
        P(),
        P(None, "tensor"),
        P(None, "tensor"),
        P(),
        P(),
        P(None, "tensor"),
        P(None, "tensor"),
        P(None, "tensor"),
        P(None, "tensor"),
        P(),
        P(),
    )
    out_specs = (
        P("dp", None),
        P("dp", None),
        P("dp", None, "tensor"),
        P("dp", None, "tensor"),
        P(),
        P(),
        P(None, "tensor"),
        P(None, "tensor"),
        P(),
        P(),
        P(None, "tensor"),
        P(None, "tensor"),
        P(None, "tensor"),
        P(None, "tensor"),
        P(),
        P(),
    )
    return jax.shard_map(
        per_device, mesh=mesh, in_specs=in_specs, out_specs=out_specs, check_vma=False
    )
```

```python
import functools
import math

import jax
import jax.numpy as jnp
from jax import lax
from jax.experimental import pallas as pl
from jax.experimental.pallas import tpu as pltpu
from jax.sharding import PartitionSpec as P

HEADDIM = 64
NS_STEPS = 5
ROWS = 256
SUB = 128
LANES = 128
NARROW = 384
CHUNK = 384
GAIN_ROW, SHARED_ROW, HEAD_ROW = 19, 20, 21

exact_mode = lax.Precision.HIGHEST
norm_eps = 1e-05
schulz_coefs = (3.4445, -4.775, 2.0315)
muon_decay = 0.95
muon_rate = 0.02
small_decay = 0.9
small_rate = 2.0
log2_e = 1.4426950408889634
f32 = jnp.float32
bf16 = jnp.bfloat16
far_below = -1e30


def dot_nn(left, right, precision=None):
    return lax.dot_general(
        left, right, (((1,), (0,)), ((), ())), precision=precision, preferred_element_type=f32
    )


def dot_nt(left, right, precision=None):
    return lax.dot_general(
        left, right, (((1,), (1,)), ((), ())), precision=precision, preferred_element_type=f32
    )


def dot_tn(left, right, precision=None):
    return lax.dot_general(
        left, right, (((0,), (0,)), ((), ())), precision=precision, preferred_element_type=f32
    )


def sigmoid(values):
    return 0.5 * jnp.tanh(0.5 * values) + 0.5


def iota(shape, dim):
    return lax.broadcasted_iota(jnp.int32, shape, dim)


def segment_at(place, ends_ref, count):
    total = (place >= ends_ref[0]).astype(jnp.int32)
    for k in range(1, count):
        total = total + (place >= ends_ref[k]).astype(jnp.int32)
    return total


def step_terms(step_part, head_ref):
    shifted = step_part + head_ref[0:1, :]
    small = jnp.exp(-jnp.abs(shifted))
    tail = jnp.where(
        small < 0.01, small * (1.0 - small * (0.5 - small * (1.0 / 3.0))), jnp.log(1.0 + small)
    )
    step = jnp.maximum(shifted, 0.0) + tail
    decay = -jnp.exp(head_ref[1:2, :])
    log_rate = step * (decay * log2_e)
    lower = (iota((SUB, SUB), 0) >= iota((SUB, SUB), 1)).astype(f32)
    cum = dot_nn(lower, log_rate, exact_mode)
    source = cum - jnp.log(step) * log2_e
    return shifted, step, decay, cum, source


def expand(values, pair):
    shape = (values.shape[0], LANES)
    low = jnp.broadcast_to(values[:, 2 * pair : 2 * pair + 1], shape)
    high = jnp.broadcast_to(values[:, 2 * pair + 1 : 2 * pair + 2], shape)
    return jnp.where(iota(shape, 1) < HEADDIM, low, high)


def split_pair(values):
    low = iota(values.shape, 1) < HEADDIM
    zero = jnp.zeros_like(values)
    return jnp.where(low, values, zero), jnp.where(low, zero, values)


def lanes_of(pair):
    return slice(pair * LANES, (pair + 1) * LANES)


def shift_mask(place, shift, ends_ref, count, rows_all):
    other = place + shift
    inside = (other >= 0) & (other < rows_all)
    same = segment_at(place, ends_ref, count) == segment_at(other, ends_ref, count)
    return jnp.where(inside & same, 1.0, 0.0).astype(f32)


def conv_tile(buf_ref, first, lanes, taps, masks):
    total = taps[4:5, :] + taps[3:4, :] * buf_ref[first + 8 : first + 8 + SUB, lanes]
    for back in (1, 2, 3):
        rows = buf_ref[first + 8 - back : first + 8 - back + SUB, lanes]
        total = total + taps[3 - back : 4 - back, :] * (rows * masks[back - 1])
    return total


def block_terms(base, ends_ref, count):
    row_at = base + iota((SUB, SUB), 0)
    col_at = base + iota((SUB, SUB), 1)
    seg_row = segment_at(row_at, ends_ref, count)
    seg_col = segment_at(col_at, ends_ref, count)
    seg_last = segment_at(base + SUB - 1, ends_ref, count)
    seg_before = jnp.where(base == 0, -1, segment_at(base - 1, ends_ref, count))
    carried = jnp.where(seg_row == seg_before, 1.0, 0.0).astype(f32)
    tail_same = jnp.where(seg_row == seg_last, 1.0, 0.0).astype(f32)
    through = jnp.where(seg_last == seg_before, 1.0, 0.0).astype(f32)
    same = seg_row == seg_col
    return row_at, col_at, same, carried, tail_same, through


def store_half(values, block, blocks, core, mine_ref, other_ref):
    is_mine = block // (blocks // 2) == core

    @pl.when(is_mine)
    def _():
        mine_ref[...] = values

    @pl.when(jnp.logical_not(is_mine))
    def _():
        other_ref[...] = values


def half_specs(width, blocks, seq_count, block_of):
    def index(half, block):
        return jnp.where(half == 0, jnp.minimum(block, blocks // 2 - 1), jnp.maximum(block - blocks // 2, 0))

    def mine(i, place, ends):
        return (index(ends[seq_count], block_of(i)), 0)

    def other(i, place, ends):
        return (index(1 - ends[seq_count], block_of(i)), 0)

    return [pl.BlockSpec((ROWS, width), mine), pl.BlockSpec((ROWS, width), other)]


def load_weights(stack_ref, place_ref, held_ref, sems, first, count):
    copies = []
    for m in range(count):
        copies.append(
            pltpu.make_async_copy(
                stack_ref.at[place_ref[first + m]],
                held_ref.at[pl.ds(m * HEADDIM, HEADDIM)],
                sems.at[m],
            )
        )
    for copy in copies:
        copy.start()
    return copies


def forward_kernel(
    heads, seq_count, rows_all,
    place_ref, ends_ref,
    hidden_ref, cot_ref, stack_ref, gain_ref, narrow_ref, head_ref, conv_ref, shared_ref,
    normed_ref, gate_ref, input_ref, mixed_ref, dscaled_ref, shared_in_ref, step_ref, state_ref,
    sums_ref, mine_ref, other_ref,
    weights, sems, in_buf, shared_buf, state, low_buf, tail_buf, across,
):
    block = pl.program_id(0)
    inner = heads * HEADDIM
    pairs = heads // 2

    @pl.when(block == 0)
    def _():
        copies = load_weights(stack_ref, place_ref, weights, sems, 0, 3 * heads)
        in_buf[0:8, :] = jnp.zeros((8, inner), f32)
        shared_buf[0:8, :] = jnp.zeros((8, 2 * LANES), f32)
        state[...] = jnp.zeros_like(state)
        for copy in copies:
            copy.wait()

    first_row = block * ROWS
    hidden = hidden_ref[...].astype(f32)
    inv_rms = lax.rsqrt(jnp.mean(hidden * hidden, axis=1, keepdims=True) + norm_eps)
    normed = (hidden * inv_rms * gain_ref[0:1, :]).astype(bf16)
    normed_ref[...] = normed
    in_buf[8:, :] = dot_nt(normed, weights[inner : 2 * inner, :])
    narrow = dot_nn(normed, narrow_ref[...])
    shared_buf[8:, :] = narrow[:, 0 : 2 * LANES]
    step_ref[...] = narrow[:, 2 * LANES : 3 * LANES]
    gate_ref[...] = dot_nt(normed, weights[0:inner, :])
    row_at = first_row + iota((ROWS, cot_ref.shape[1]), 0)
    cot = jnp.where(row_at < ends_ref[seq_count - 1], cot_ref[...].astype(f32), 0.0).astype(bf16)
    dscaled_ref[...] = dot_nt(cot, weights[2 * inner : 3 * inner, :])
    input_ref[...] = in_buf[8:, :]
    shared_in_ref[...] = shared_buf[8:, :]

    for sub in range(ROWS // SUB):
        first = sub * SUB
        base = first_row + first
        row_at, col_at, same, carried, tail_same, through = block_terms(base, ends_ref, seq_count)
        causal = jnp.where(same & (row_at >= col_at), 0.0, far_below).astype(f32)
        masks = [shift_mask(row_at, -back, ends_ref, seq_count, rows_all) for back in (1, 2, 3)]
        bc = []
        for part in range(2):
            lanes = lanes_of(part)
            u = conv_tile(shared_buf, first, lanes, shared_ref[:, lanes], masks)
            bc.append((u * sigmoid(u)).astype(bf16))
        b_low, c_low = bc
        _, _, _, cum, source = step_terms(step_ref[first : first + SUB, :], head_ref)
        source_row = source.T
        scores = dot_nt(c_low, b_low)
        cum_last = cum[SUB - 1 : SUB, :]
        entry = jnp.exp2(cum) * carried
        leave = jnp.exp2(cum_last - source) * tail_same
        pass_on = jnp.exp2(cum_last) * through
        state_ref[sub] = state[...]
        across[...] = dot_nn(c_low, state[...].astype(bf16))
        square = jnp.zeros((SUB, LANES), f32)
        inner_dot = jnp.zeros((SUB, LANES), f32)
        for pair in range(pairs):
            lanes = lanes_of(pair)
            u = conv_tile(in_buf, first, lanes, conv_ref[:, lanes], masks)
            x_low = (u * sigmoid(u)).astype(bf16)
            x = x_low.astype(f32)
            mats = []
            for h in (2 * pair, 2 * pair + 1):
                gap = cum[:, h : h + 1] - source_row[h : h + 1, :]
                mats.append((jnp.exp2(gap + causal) * scores).astype(bf16))
            x_a, x_b = split_pair(x_low)
            mixed = dot_nn(jnp.concatenate(mats, axis=1), jnp.concatenate([x_a, x_b], axis=0))
            mixed = mixed + across[:, lanes] * expand(entry, pair)
            mixed = mixed + expand(head_ref[2:3, :], pair) * x
            mixed_ref[first : first + SUB, lanes] = mixed
            gate = gate_ref[first : first + SUB, lanes]
            gated = mixed * (gate * sigmoid(gate))
            gated_gain = gated * conv_ref[5:6, lanes]
            low_buf[first : first + SUB, lanes] = gated_gain.astype(bf16)
            square = square + gated * gated
            inner_dot = inner_dot + dscaled_ref[first : first + SUB, lanes] * gated_gain
            tail_buf[:, lanes] = (x * expand(leave, pair)).astype(bf16)
        fresh = dot_tn(b_low, tail_buf[...])
        for pair in range(pairs):
            lanes = lanes_of(pair)
            state[:, lanes] = state[:, lanes] * expand(pass_on, pair) + fresh[:, lanes]
        sums_ref[0:1, first : first + SUB] = jnp.sum(square.T, axis=0, keepdims=True)
        sums_ref[1:2, first : first + SUB] = jnp.sum(inner_dot.T, axis=0, keepdims=True)
    sums_ref[2:8, :] = jnp.zeros((6, ROWS), f32)
    in_buf[0:8, :] = in_buf[ROWS : ROWS + 8, :]
    shared_buf[0:8, :] = shared_buf[ROWS : ROWS + 8, :]
    part = dot_nn(low_buf[...], weights[2 * inner : 3 * inner, :]).astype(bf16)
    store_half(part, block, pl.num_programs(0), ends_ref[seq_count], mine_ref, other_ref)


def forward_call(place, ends, hidden, cot, stack, gain, narrow, head_rows, conv_rows, shared_rows, heads):
    rows_all, width = hidden.shape
    inner = heads * HEADDIM
    blocks = rows_all // ROWS

    def rows(columns):
        return pl.BlockSpec((ROWS, columns), lambda i, *_: (i, 0))

    def whole(array):
        return pl.BlockSpec(array.shape, lambda i, *_: (0,) * array.ndim)

    state_shape = (ROWS // SUB, LANES, inner)
    out_shape = [
        jax.ShapeDtypeStruct((rows_all, width), bf16),
        jax.ShapeDtypeStruct((rows_all, inner), f32),
        jax.ShapeDtypeStruct((rows_all, inner), f32),
        jax.ShapeDtypeStruct((rows_all, inner), f32),
        jax.ShapeDtypeStruct((rows_all, inner), f32),
        jax.ShapeDtypeStruct((rows_all, 2 * LANES), f32),
        jax.ShapeDtypeStruct((rows_all, LANES), f32),
        jax.ShapeDtypeStruct((rows_all // SUB, LANES, inner), f32),
        jax.ShapeDtypeStruct((8, rows_all), f32),
        jax.ShapeDtypeStruct((rows_all // 2, width), bf16),
        jax.ShapeDtypeStruct((rows_all // 2, width), bf16),
    ]
    out_specs = [
        rows(width), rows(inner), rows(inner), rows(inner), rows(inner), rows(2 * LANES), rows(LANES),
        pl.BlockSpec(state_shape, lambda i, *_: (i, 0, 0)),
        pl.BlockSpec((8, ROWS), lambda i, *_: (0, i)),
        *half_specs(width, blocks, ends.shape[0] - 1, lambda i: i),
    ]
    return pl.pallas_call(
        functools.partial(forward_kernel, heads, ends.shape[0] - 1, rows_all),
        grid_spec=pltpu.PrefetchScalarGridSpec(
            num_scalar_prefetch=2,
            grid=(blocks,),
            in_specs=[
                rows(width), rows(width), pl.BlockSpec(memory_space=pl.ANY), whole(gain), whole(narrow),
                whole(head_rows), whole(conv_rows), whole(shared_rows),
            ],
            out_specs=out_specs,
            scratch_shapes=[
                pltpu.VMEM((3 * inner, width), bf16),
                pltpu.SemaphoreType.DMA((3 * heads,)),
                pltpu.VMEM((ROWS + 8, inner), f32),
                pltpu.VMEM((ROWS + 8, 2 * LANES), f32),
                pltpu.VMEM((LANES, inner), f32),
                pltpu.VMEM((ROWS, inner), bf16),
                pltpu.VMEM((SUB, inner), bf16),
                pltpu.VMEM((SUB, inner), f32),
            ],
        ),
        out_shape=out_shape,
        compiler_params=pltpu.CompilerParams(
            dimension_semantics=("arbitrary",), vmem_limit_bytes=56 * 2**20
        ),
        cost_estimate=pl.CostEstimate(
            flops=2 * rows_all * width * (4 * inner + NARROW), bytes_accessed=60 * 2**20, transcendentals=0
        ),
        name="mixer_forward",
    )(place, ends, hidden, cot, stack, gain, narrow, head_rows, conv_rows, shared_rows)


def backward_kernel(
    heads, seq_count, rows_all, inner_all,
    place_ref, ends_ref,
    hidden_ref, gate_ref, input_ref, before_ref, mixed_ref, dscaled_ref, shared_in_ref,
    shared_before_ref, step_ref, state_ref, sums_ref,
    stack_ref, narrow_ref, gain_ref, head_ref, conv_ref, shared_ref,
    dboth_ref, scaled_ref, mine_ref, other_ref, narrow_grad_ref, extra_ref,
    weights, sems, in_buf, shared_buf, du_buf, dshared_buf, dstate, state_after, from_state, terms,
    source_terms, tail_buf, entry_buf, dnarrow_ref, conv_grad_ref, shared_grad_ref, head_grad_ref,
    skip_grad_ref, gain_grad_ref,
):
    turn = pl.program_id(0)
    block = pl.num_programs(0) - 1 - turn
    inner = heads * HEADDIM
    pairs = heads // 2

    @pl.when(turn == 0)
    def _():
        copies = load_weights(stack_ref, place_ref, weights, sems, 0, 2 * heads)
        du_buf[ROWS:, :] = jnp.zeros((8, inner), f32)
        dshared_buf[ROWS:, :] = jnp.zeros((8, 2 * LANES), f32)
        dstate[...] = jnp.zeros_like(dstate)
        state_after[...] = jnp.zeros_like(state_after)
        conv_grad_ref[...] = jnp.zeros_like(conv_grad_ref)
        shared_grad_ref[...] = jnp.zeros_like(shared_grad_ref)
        head_grad_ref[...] = jnp.zeros_like(head_grad_ref)
        skip_grad_ref[...] = jnp.zeros_like(skip_grad_ref)
        gain_grad_ref[...] = jnp.zeros_like(gain_grad_ref)
        narrow_grad_ref[...] = jnp.zeros_like(narrow_grad_ref)
        for copy in copies:
            copy.wait()

    first_row = block * ROWS
    in_buf[0:8, :] = jnp.where(block == 0, 0.0, before_ref[...])
    in_buf[8:, :] = input_ref[...]
    shared_buf[0:8, :] = jnp.where(block == 0, 0.0, shared_before_ref[...])
    shared_buf[8:, :] = shared_in_ref[...]
    reduce_heads = (iota((inner, LANES), 0) // HEADDIM == iota((inner, LANES), 1)).astype(f32)
    upper = (iota((SUB, SUB), 0) <= iota((SUB, SUB), 1)).astype(f32)

    for sub in reversed(range(ROWS // SUB)):
        first = sub * SUB
        here = slice(first, first + SUB)
        base = first_row + first
        row_at, col_at, same, carried, tail_same, through = block_terms(base, ends_ref, seq_count)
        causal = jnp.where(same & (row_at <= col_at), 0.0, far_below).astype(f32)
        masks = [shift_mask(row_at, -back, ends_ref, seq_count, rows_all) for back in (1, 2, 3)]
        bc, bc_slope = [], []
        for part in range(2):
            lanes = lanes_of(part)
            u = conv_tile(shared_buf, first, lanes, shared_ref[:, lanes], masks)
            sig = sigmoid(u)
            bc.append((u * sig).astype(bf16))
            bc_slope.append(sig * (1.0 + u * (1.0 - sig)))
        b_low, c_low = bc
        shifted, step, decay, cum, source = step_terms(step_ref[here, :], head_ref)
        cum_row = cum.T
        scores = dot_nt(b_low, c_low)
        cum_last = cum[SUB - 1 : SUB, :]
        entry = jnp.exp2(cum) * carried
        leave = jnp.exp2(cum_last - source) * tail_same
        pass_on = jnp.exp2(cum_last) * through
        square = sums_ref[0:1, here]
        inner_dot = sums_ref[1:2, here]
        inv_row = lax.rsqrt(square * (1.0 / inner_all) + norm_eps)
        fix_row = inv_row * inv_row * inv_row * inner_dot * (1.0 / inner_all)
        inv = jnp.broadcast_to(inv_row, (SUB, SUB)).T
        fix = jnp.broadcast_to(fix_row, (SUB, SUB)).T
        dstate_low = dstate[...].astype(bf16)
        from_state[...] = dot_nn(b_low, dstate_low)
        dscores = jnp.zeros((SUB, SUB), f32)
        for pair in range(pairs):
            lanes = lanes_of(pair)
            u = conv_tile(in_buf, first, lanes, conv_ref[:, lanes], masks)
            sig = sigmoid(u)
            x_low = (u * sig).astype(bf16)
            x = x_low.astype(f32)
            slope = sig * (1.0 + u * (1.0 - sig))
            gate = gate_ref[here, lanes]
            gate_sig = sigmoid(gate)
            gate_silu = gate * gate_sig
            mixed = mixed_ref[here, lanes]
            gated = mixed * gate_silu
            gain = conv_ref[5:6, lanes]
            dscaled = dscaled_ref[here, lanes]
            normal = gated * inv
            scaled_ref[here, lanes] = (normal * gain).astype(bf16)
            conv_grad_ref[5:6, lanes] += jnp.sum(dscaled * normal, axis=0, keepdims=True)
            dgated = inv * (dscaled * gain) - gated * fix
            dgate = dgated * mixed * (gate_sig * (1.0 + gate * (1.0 - gate_sig)))
            dboth_ref[here, lanes] = dgate.astype(bf16)
            dmixed = dgated * gate_silu
            dy_low = dmixed.astype(bf16)
            dy = dy_low.astype(f32)
            skip = expand(head_ref[2:3, :], pair)
            skip_grad_ref[0:1, lanes] += jnp.sum(dmixed * x, axis=0, keepdims=True)
            x_parts = split_pair(x_low)
            dy_parts = split_pair(dy_low)
            mats = []
            for k in range(2):
                h = 2 * pair + k
                gap = cum_row[h : h + 1, :] - source[:, h : h + 1]
                decays = jnp.exp2(gap + causal)
                mats.append((decays * scores).astype(bf16))
                dscores = dscores + dot_nt(x_parts[k], dy_low) * decays
            dx = dot_nn(jnp.concatenate(mats, axis=1), jnp.concatenate(dy_parts, axis=0))
            leave_here = expand(leave, pair)
            dx = dx + leave_here * from_state[:, lanes]
            source_term = x * dx
            source_terms[:, lanes] = source_term
            terms[:, lanes] = dy * (mixed - skip * x) - source_term
            tail_buf[:, lanes] = (x * leave_here).astype(bf16)
            entry_buf[:, lanes] = (dy * expand(entry, pair)).astype(bf16)
            du_buf[here, lanes] = (dx + skip * dmixed) * slope
        state_low = state_ref[sub].astype(bf16)
        dscores_low = dscores.astype(bf16)
        db = dot_nn(dscores_low, c_low) + dot_nt(tail_buf[...], dstate_low)
        dc = dot_tn(dscores_low, b_low) + dot_nt(entry_buf[...], state_low)
        dshared_buf[here, 0:LANES] = db * bc_slope[0]
        dshared_buf[here, LANES : 2 * LANES] = dc * bc_slope[1]
        at_end = jnp.sum(dstate[...] * state_after[...], axis=0, keepdims=True)
        state_after[...] = state_ref[sub]
        fresh = dot_tn(c_low, entry_buf[...])
        for pair in range(pairs):
            lanes = lanes_of(pair)
            dstate[:, lanes] = dstate[:, lanes] * expand(pass_on, pair) + fresh[:, lanes]
        last = iota((SUB, inner), 0) == SUB - 1
        dcum = dot_nn(terms[...] + jnp.where(last, at_end, 0.0), reduce_heads, exact_mode)
        from_source = dot_nn(source_terms[...], reduce_heads, exact_mode)
        dlog = dot_nn(upper, dcum, exact_mode)
        sig = sigmoid(shifted)
        ratio = jnp.where(shifted < -15.0, 1.0, sig / step)
        dlog_decay = dlog * decay
        dstep = from_source * ratio + dlog_decay * sig
        dnarrow_ref[here, 2 * LANES : 3 * LANES] = dstep.astype(bf16)
        head_grad_ref[0:1, :] += jnp.sum(dstep, axis=0, keepdims=True)
        head_grad_ref[1:2, :] += jnp.sum(dlog_decay * step, axis=0, keepdims=True)

    for sub in range(ROWS // SUB):
        first = sub * SUB
        here = slice(first, first + SUB)
        row_at = first_row + first + iota((SUB, LANES), 0)
        ahead = [shift_mask(row_at, k, ends_ref, seq_count, rows_all) for k in (1, 2, 3)]
        groups = [(pair, True) for pair in range(pairs)] + [(0, False), (1, False)]
        for group, wide in groups:
            lanes = lanes_of(group)
            grads, held = (du_buf, in_buf) if wide else (dshared_buf, shared_buf)
            taps = conv_ref[:, lanes] if wide else shared_ref[:, lanes]
            sums = conv_grad_ref if wide else shared_grad_ref
            du = grads[here, lanes]
            v = held[first + 8 : first + 8 + SUB, lanes]
            dv = taps[3:4, :] * du
            sums[3:4, lanes] += jnp.sum(du * v, axis=0, keepdims=True)
            sums[4:5, lanes] += jnp.sum(du, axis=0, keepdims=True)
            for k in (1, 2, 3):
                moved = grads[first + k : first + k + SUB, lanes] * ahead[k - 1]
                dv = dv + taps[3 - k : 4 - k, :] * moved
                sums[3 - k : 4 - k, lanes] += jnp.sum(moved * v, axis=0, keepdims=True)
            if wide:
                dboth_ref[here, inner + group * LANES : inner + (group + 1) * LANES] = dv.astype(bf16)
            else:
                dnarrow_ref[here, lanes] = dv.astype(bf16)
    du_buf[ROWS:, :] = du_buf[0:8, :]
    dshared_buf[ROWS:, :] = dshared_buf[0:8, :]

    dnormed = dot_nn(dboth_ref[...], weights[...]) + dot_nt(dnarrow_ref[...], narrow_ref[...])
    hidden = hidden_ref[...].astype(f32)
    inv_rms = lax.rsqrt(jnp.mean(hidden * hidden, axis=1, keepdims=True) + norm_eps)
    unit = hidden * inv_rms
    gain_grad_ref[0:1, :] += jnp.sum(dnormed * unit, axis=0, keepdims=True)
    narrow_grad_ref[...] += dot_tn(dnarrow_ref[...], (unit * gain_ref[0:1, :]).astype(bf16))
    store_half(
        dnormed.astype(bf16), block, pl.num_programs(0), ends_ref[seq_count], mine_ref, other_ref
    )

    @pl.when(block == 0)
    def _():
        width = hidden.shape[1]
        extra_ref[...] = jnp.zeros_like(extra_ref)
        extra_ref[0:16, :] = narrow_grad_ref[2 * LANES : 2 * LANES + 16, :]
        per_line = width // inner
        for k in range(6):
            at = (k % per_line) * inner
            row = 16 + k // per_line
            extra_ref[row : row + 1, at : at + inner] = conv_grad_ref[k : k + 1, :]
        extra_ref[GAIN_ROW : GAIN_ROW + 1, :] = gain_grad_ref[0:1, :]
        for k in range(5):
            at = 2 * LANES * k
            extra_ref[SHARED_ROW : SHARED_ROW + 1, at : at + 2 * LANES] = shared_grad_ref[k : k + 1, :]
        extra_ref[HEAD_ROW : HEAD_ROW + 2, 0:LANES] = head_grad_ref[0:2, :]
        skip_sum = dot_nn(skip_grad_ref[...], reduce_heads, exact_mode)
        extra_ref[HEAD_ROW + 2 : HEAD_ROW + 3, 0:LANES] = skip_sum[0:1, :]


def backward_call(
    place, ends, hidden, gate, input_part, mixed, dscaled, shared_in, step_part, states, sums, stack,
    narrow, gain, head_rows, conv_rows, shared_rows, heads, inner_all, extra_rows,
):
    rows_all, width = hidden.shape
    inner = heads * HEADDIM
    blocks = rows_all // ROWS

    def rows(columns):
        return pl.BlockSpec((ROWS, columns), lambda i, *_: (blocks - 1 - i, 0))

    def before(columns):
        step = ROWS // 8
        return pl.BlockSpec(
            (8, columns), lambda i, *_: (jnp.maximum((blocks - 1 - i) * step - 1, 0), 0)
        )

    def whole(shape):
        return pl.BlockSpec(shape, lambda i, *_: (0,) * len(shape))

    out_shape = [
        jax.ShapeDtypeStruct((rows_all, 2 * inner), bf16),
        jax.ShapeDtypeStruct((rows_all, inner), bf16),
        jax.ShapeDtypeStruct((rows_all // 2, width), bf16),
        jax.ShapeDtypeStruct((rows_all // 2, width), bf16),
        jax.ShapeDtypeStruct((NARROW, width), f32),
        jax.ShapeDtypeStruct((extra_rows, width), f32),
    ]
    out_specs = [
        rows(2 * inner), rows(inner),
        *half_specs(width, blocks, ends.shape[0] - 1, lambda i: blocks - 1 - i),
        whole((NARROW, width)), whole((extra_rows, width)),
    ]
    return pl.pallas_call(
        functools.partial(backward_kernel, heads, ends.shape[0] - 1, rows_all, inner_all),
        grid_spec=pltpu.PrefetchScalarGridSpec(
            num_scalar_prefetch=2,
            grid=(blocks,),
            in_specs=[
                rows(width), rows(inner), rows(inner), before(inner), rows(inner), rows(inner),
                rows(2 * LANES), before(2 * LANES), rows(LANES),
                pl.BlockSpec((ROWS // SUB, LANES, inner), lambda i, *_: (blocks - 1 - i, 0, 0)),
                pl.BlockSpec((8, ROWS), lambda i, *_: (0, blocks - 1 - i)),
                pl.BlockSpec(memory_space=pl.ANY), whole(narrow.shape), whole(gain.shape),
                whole(head_rows.shape), whole(conv_rows.shape), whole(shared_rows.shape),
            ],
            out_specs=out_specs,
            scratch_shapes=[
                pltpu.VMEM((2 * inner, width), bf16),
                pltpu.SemaphoreType.DMA((2 * heads,)),
                pltpu.VMEM((ROWS + 8, inner), f32),
                pltpu.VMEM((ROWS + 8, 2 * LANES), f32),
                pltpu.VMEM((ROWS + 8, inner), f32),
                pltpu.VMEM((ROWS + 8, 2 * LANES), f32),
                pltpu.VMEM((LANES, inner), f32),
                pltpu.VMEM((LANES, inner), f32),
                pltpu.VMEM((SUB, inner), f32),
                pltpu.VMEM((SUB, inner), f32),
                pltpu.VMEM((SUB, inner), f32),
                pltpu.VMEM((SUB, inner), bf16),
                pltpu.VMEM((SUB, inner), bf16),
                pltpu.VMEM((ROWS, NARROW), bf16),
                pltpu.VMEM((8, inner), f32),
                pltpu.VMEM((8, 2 * LANES), f32),
                pltpu.VMEM((8, LANES), f32),
                pltpu.VMEM((8, inner), f32),
                pltpu.VMEM((8, width), f32),
            ],
        ),
        out_shape=out_shape,
        compiler_params=pltpu.CompilerParams(
            dimension_semantics=("arbitrary",), vmem_limit_bytes=56 * 2**20
        ),
        cost_estimate=pl.CostEstimate(
            flops=4 * rows_all * width * (2 * inner + NARROW), bytes_accessed=60 * 2**20, transcendentals=0
        ),
        name="mixer_backward",
    )(
        place, ends, hidden, gate, input_part, input_part, mixed, dscaled, shared_in, shared_in, step_part,
        states, sums, stack, narrow, gain, head_rows, conv_rows, shared_rows,
    )


def grads_kernel(
    first_matrix, count, seq_count, clear, mask_right, place_ref, ends_ref, free_ref, left_ref, right_ref,
    *rest,
):
    out_ref, held, sems, free_sems = rest[-4:]
    chunk = pl.program_id(0)
    width = right_ref.shape[1]
    right = right_ref[...]
    if mask_right:
        valid = iota(right.shape, 0) < ends_ref[seq_count - 1]
        right = jnp.where(valid, right.astype(f32), 0.0).astype(bf16)
    held[0 : count * HEADDIM, :] = dot_tn(left_ref[...], right).astype(bf16)
    columns = pl.ds(pl.multiple_of(chunk * width, width), width)
    copies = [
        pltpu.make_async_copy(
            held.at[pl.ds(m * HEADDIM, HEADDIM), :],
            out_ref.at[place_ref[first_matrix + m], :, columns],
            sems.at[m],
        )
        for m in range(count)
    ]
    for copy in copies:
        copy.start()
    if clear:
        held[count * HEADDIM :, :] = jnp.zeros((HEADDIM, width), bf16)

        def clear_copy(s):
            return pltpu.make_async_copy(
                held.at[pl.ds(count * HEADDIM, HEADDIM), :], out_ref.at[s, :, columns], free_sems.at[s]
            )

        for s in range(out_ref.shape[0]):

            @pl.when(free_ref[s] > 0)
            def _(s=s):
                clear_copy(s).start()

        for s in range(out_ref.shape[0]):

            @pl.when(free_ref[s] > 0)
            def _(s=s):
                clear_copy(s).wait()

    for copy in copies:
        copy.wait()


def grads_call(place, ends, free, left, right, first_matrix, mask_right, into):
    rows_all, width = right.shape
    slots = free.shape[0]
    count = left.shape[1] // HEADDIM
    clear = into is None
    held = pl.BlockSpec(memory_space=pl.ANY)
    return pl.pallas_call(
        functools.partial(grads_kernel, first_matrix, count, ends.shape[0] - 1, clear, mask_right),
        grid_spec=pltpu.PrefetchScalarGridSpec(
            num_scalar_prefetch=3,
            grid=(width // CHUNK,),
            in_specs=[
                pl.BlockSpec(left.shape, lambda i, *_: (0, 0), pipeline_mode=pl.Buffered(1)),
                pl.BlockSpec((rows_all, CHUNK), lambda i, *_: (0, i)),
            ]
            + ([] if clear else [held]),
            out_specs=held,
            scratch_shapes=[
                pltpu.VMEM(((count + 1) * HEADDIM, CHUNK), bf16),
                pltpu.SemaphoreType.DMA((count,)),
                pltpu.SemaphoreType.DMA((slots,)),
            ],
        ),
        out_shape=jax.ShapeDtypeStruct((slots, HEADDIM, width), bf16),
        input_output_aliases={} if clear else {5: 0},
        compiler_params=pltpu.CompilerParams(
            dimension_semantics=("arbitrary",), vmem_limit_bytes=56 * 2**20
        ),
        cost_estimate=pl.CostEstimate(
            flops=2 * rows_all * width * left.shape[1], bytes_accessed=30 * 2**20, transcendentals=0
        ),
        name="weight_grads",
    )(place, ends, free, left, right, *([] if clear else [into]))


def exchange_kernel(sums_ref, mine_ref, other_ref, total_ref, near_ref, sums_in, part_in, sum_sems, part_sems):
    here = lax.axis_index("dp")
    tensor = lax.axis_index("tensor")
    peers = [(here, (tensor + k) % 4) for k in range(1, 4)]
    other_core = (here, tensor + 1 - 2 * (tensor % 2))
    rows = mine_ref.shape[0]
    greet([(peer, None) for peer in peers])
    parts = [pl.ds(k * ROWS, ROWS) for k in range(rows // ROWS)]

    def part_copy(k):
        return remote(
            other_ref.at[parts[k]], part_in.at[parts[k]], part_sems.at[0, k], part_sems.at[1, k], other_core
        )

    def sum_copy(k):
        return remote(
            sums_ref.at[0:2], sums_in.at[tensor], sum_sems.at[0, k], sum_sems.at[1, k], peers[k]
        )

    for k in range(3):
        sum_copy(k).start()
    for k in range(len(parts)):
        part_copy(k).start()
    for k in range(3):
        sum_copy(k).wait()
    total = jnp.zeros((2, sums_ref.shape[1]), f32)
    for t in range(4):
        total = total + jnp.where(tensor == t, sums_ref[0:2, :], sums_in[t])
    total_ref[0:2, :] = total
    total_ref[2:8, :] = jnp.zeros((6, sums_ref.shape[1]), f32)
    for k in range(len(parts)):
        part_copy(k).wait()
        here_rows = parts[k]
        near_ref[here_rows, :] = (
            mine_ref[here_rows, :].astype(f32) + part_in[here_rows, :].astype(f32)
        ).astype(bf16)


def exchange_call(sums, mine, other):
    rows, width = mine.shape
    spec = pl.BlockSpec(memory_space=pltpu.VMEM)
    sems = pltpu.SemaphoreType.DMA
    return pl.pallas_call(
        exchange_kernel,
        in_specs=[spec, spec, pl.BlockSpec(memory_space=pl.ANY)],
        out_specs=[spec] * 2,
        out_shape=[jax.ShapeDtypeStruct(sums.shape, f32), jax.ShapeDtypeStruct(mine.shape, bf16)],
        scratch_shapes=[
            pltpu.VMEM((4, 2, sums.shape[1]), f32), pltpu.VMEM((rows, width), bf16),
            sems((2, 3)), sems((2, rows // ROWS)),
        ],
        compiler_params=pltpu.CompilerParams(
            collective_id=2, has_side_effects=True, vmem_limit_bytes=40 * 2**20
        ),
        name="exchange_sums",
    )(sums, mine, other)


def branch_kernel(inner_all, seq_count, ends_ref, near_ref, far_ref, hidden_ref, sums_ref, full_ref, half_ref):
    width = hidden_ref.shape[1]
    blocks = pl.num_programs(0)
    first_row = (ends_ref[seq_count] * blocks + pl.program_id(0)) * ROWS
    for sub in range(ROWS // SUB):
        here = slice(sub * SUB, (sub + 1) * SUB)
        inv_row = lax.rsqrt(sums_ref[0:1, here] * (1.0 / inner_all) + norm_eps)
        inv = jnp.broadcast_to(inv_row, (SUB, SUB)).T
        row_at = first_row + sub * SUB + iota((SUB, LANES), 0)
        valid = jnp.where(row_at < ends_ref[seq_count - 1], 1.0, 0.0).astype(f32)
        for group in range(width // LANES):
            lanes = lanes_of(group)
            branch = (near_ref[here, lanes].astype(f32) + far_ref[here, lanes].astype(f32)) * inv
            result = ((hidden_ref[here, lanes].astype(f32) + branch) * valid).astype(bf16)
            full_ref[here, lanes] = result
            half_ref[here, lanes] = result


def input_kernel(seq_count, ends_ref, near_ref, far_ref, hidden_ref, cot_ref, gain_ref, full_ref, half_ref):
    width = hidden_ref.shape[1]
    blocks = pl.num_programs(0)
    first_row = (ends_ref[seq_count] * blocks + pl.program_id(0)) * ROWS
    hidden = hidden_ref[...].astype(f32)
    inv_rms = lax.rsqrt(jnp.mean(hidden * hidden, axis=1, keepdims=True) + norm_eps)
    gain_part = (near_ref[...].astype(f32) + far_ref[...].astype(f32)) * gain_ref[0:1, :]
    fix = inv_rms * inv_rms * inv_rms * (jnp.sum(gain_part * hidden, axis=1, keepdims=True) / width)
    row_at = first_row + iota(hidden.shape, 0)
    cot = jnp.where(row_at < ends_ref[seq_count - 1], cot_ref[...].astype(f32), 0.0)
    result = (inv_rms * gain_part - hidden * fix + cot).astype(bf16)
    full_ref[...] = result
    half_ref[...] = result


def half_call(kernel, name, ends, halves, fulls, wholes):
    rows, width = halves[0].shape
    seq_count = ends.shape[0] - 1
    blocks = rows // ROWS

    def in_full(i, ends):
        return (ends[seq_count] * blocks + i, 0)

    own = pl.BlockSpec((ROWS, width), lambda i, ends: (i, 0))
    full = pl.BlockSpec((ROWS, width), in_full)
    return pl.pallas_call(
        kernel,
        grid_spec=pltpu.PrefetchScalarGridSpec(
            num_scalar_prefetch=1,
            grid=(blocks,),
            in_specs=[own] * len(halves) + [full] * len(fulls) + wholes[1],
            out_specs=[full, own],
        ),
        out_shape=[
            jax.ShapeDtypeStruct((2 * rows, width), bf16),
            jax.ShapeDtypeStruct((rows, width), bf16),
        ],
        compiler_params=pltpu.CompilerParams(
            dimension_semantics=("arbitrary",), vmem_limit_bytes=40 * 2**20
        ),
        cost_estimate=pl.CostEstimate(flops=0, bytes_accessed=16 * 2**20, transcendentals=0),
        name=name,
    )(ends, *halves, *fulls, *wholes[0])


def remote(src, dst, send_sem, recv_sem, target):
    return pltpu.make_async_remote_copy(
        src_ref=src,
        dst_ref=dst,
        send_sem=send_sem,
        recv_sem=recv_sem,
        device_id=target,
        device_id_type=pl.DeviceIdType.MESH,
    )


def greet(targets):
    barrier = pltpu.get_barrier_semaphore()
    for target, condition in targets:
        if condition is None:
            pl.semaphore_signal(barrier, inc=1, device_id=target, device_id_type=pl.DeviceIdType.MESH)
        else:

            @pl.when(condition)
            def _(target=target):
                pl.semaphore_signal(
                    barrier, inc=1, device_id=target, device_id_type=pl.DeviceIdType.MESH
                )

    peers = sum(1 if condition is None else condition.astype(jnp.int32) for _, condition in targets)
    pl.semaphore_wait(barrier, peers)


def gather_kernel(
    lines, own_ref, out_ref, local_sem, x_send, x_recv, up_send, up_recv, down_send, down_recv
):
    here = lax.axis_index("dp")
    tensor = lax.axis_index("tensor")
    line, side = here // 2, here % 2
    partner = here + 1 - 2 * side
    slots = own_ref.shape[0]
    most = slots - 1
    has_up, has_down = line < lines - 1, line > 0
    across, above, below = (partner, tensor), (here + 2, tensor), (here - 2, tensor)

    greet([(across, None), (above, has_up), (below, has_down)])
    local = pltpu.make_async_copy(own_ref, out_ref.at[pl.ds(here * slots, slots)], local_sem)
    local.start()
    order = [most] + list(range(min(2, most))) + [slots] + list(range(min(2, most), most))

    def place(at, part):
        device = 2 * at + 1 - side if part == slots else 2 * at + side
        return device * slots + min(part, most)

    def line_copy(step, at, part, upward):
        own = step == 0 and part < slots
        to = out_ref.at[place(at, part)]
        src = own_ref.at[part] if own else to
        if upward:
            return remote(src, to, up_send.at[step, part], up_recv.at[step, part], above)
        return remote(src, to, down_send.at[step, part], down_recv.at[step, part], below)

    def x_copy(device, index, part, own=False):
        to = out_ref.at[device * slots + part]
        return remote(
            own_ref.at[part] if own else to, to, x_send.at[index, part], x_recv.at[index, part], across
        )

    x_copy(here, 0, most, True).start()
    for part in order:
        if part == slots:
            x_copy(partner, 0, most).wait_recv()

        @pl.when(has_up)
        def _(part=part):
            line_copy(0, line, part, True).start()

        @pl.when(has_down)
        def _(part=part):
            line_copy(0, line, part, False).start()

        if part < most:
            x_copy(here, 0, part, True).start()

    for k in range(1, lines):
        for part in order:

            @pl.when(line >= k)
            def _(k=k, part=part):
                line_copy(k - 1, line - k, part, True).wait_recv()
                if k < lines - 1:

                    @pl.when(has_up)
                    def _():
                        line_copy(k, line - k, part, True).start()

                if part < most:
                    x_copy(2 * (line - k) + side, k, part).start()

            @pl.when(line + k < lines)
            def _(k=k, part=part):
                line_copy(k - 1, line + k, part, False).wait_recv()
                if k < lines - 1:

                    @pl.when(has_down)
                    def _():
                        line_copy(k, line + k, part, False).start()

                if part < most:
                    x_copy(2 * (line + k) + side, lines - 1 + k, part).start()

    local.wait()
    x_copy(partner, 0, most).wait_send()
    for part in range(most):
        x_copy(partner, 0, part).wait()
    for k in range(1, lines):
        for part in range(most):

            @pl.when(line >= k)
            def _(k=k, part=part):
                x_copy(2 * (line - k) + 1 - side, k, part).wait()

            @pl.when(line + k < lines)
            def _(k=k, part=part):
                x_copy(2 * (line + k) + 1 - side, lines - 1 + k, part).wait()

    for k in range(lines - 1):
        for part in order:

            @pl.when(has_up & (line >= k))
            def _(k=k, part=part):
                line_copy(k, line - k, part, True).wait_send()

            @pl.when(has_down & (line + k < lines))
            def _(k=k, part=part):
                line_copy(k, line + k, part, False).wait_send()


def gather_call(own, dp_size):
    slots, side, width = own.shape
    lines = dp_size // 2
    step_sems = pltpu.SemaphoreType.DMA((lines - 1, slots + 1))
    x_sems = pltpu.SemaphoreType.DMA((2 * lines - 1, slots))
    return pl.pallas_call(
        functools.partial(gather_kernel, lines),
        in_specs=[pl.BlockSpec(memory_space=pl.ANY)],
        out_specs=pl.BlockSpec(memory_space=pl.ANY),
        out_shape=jax.ShapeDtypeStruct((slots * dp_size, side, width), own.dtype),
        scratch_shapes=[
            pltpu.SemaphoreType.DMA, x_sems, x_sems, step_sems, step_sems, step_sems, step_sems,
        ],
        compiler_params=pltpu.CompilerParams(collective_id=0, has_side_effects=True),
        name="gather_weights",
    )(own)


def reduce_kernel(
    lines,
    grads, near_ref, far_ref, extra_ref, owned_ref, totals_ref,
    x_in, up_in, down_in, last_out, last_in, halves, half_in, group_in, group_out, group_back,
    x_send, x_recv, up_send, up_recv, down_send, down_recv, last_sems, small_sems, group_sems, back_sems,
):
    here = lax.axis_index("dp")
    tensor = lax.axis_index("tensor")
    line, side = here // 2, here % 2
    core = tensor % 2
    slots = owned_ref.shape[0]
    most = slots - 1
    width = near_ref.shape[1]
    half = width // 2
    group = halves.shape[1] // lines
    has_up, has_down = line < lines - 1, line > 0
    across = (here + 1 - 2 * side, tensor)
    above, below = (here + 2, tensor), (here - 2, tensor)
    other_core = (here, tensor + 1 - 2 * core)
    other_chip = (here, (tensor + 2) % 4)
    on_line = [(2 * ((line + k) % lines) + side, tensor) for k in range(1, lines)]

    greet([(target, None) for target in [across, other_core, other_chip] + on_line])

    def add(*parts):
        total = parts[0].astype(f32)
        for part in parts[1:]:
            total = total + part.astype(f32)
        return total

    half_copy = remote(halves.at[1 - side], half_in, small_sems.at[0, 0], small_sems.at[1, 0], across)

    def group_copy(k):
        to = (line + k) % lines
        rows = pl.ds(pl.multiple_of(to * group, group), group)
        return remote(
            halves.at[side, rows], group_in.at[k - 1], group_sems.at[0, k - 1], group_sems.at[1, k - 1],
            on_line[k - 1],
        )

    def back_copy(k):
        return remote(
            group_out, group_back.at[k - 1], back_sems.at[0, k - 1], back_sems.at[1, k - 1], on_line[k - 1]
        )

    total_half = remote(
        totals_ref.at[tensor, side], totals_ref.at[tensor, side], small_sems.at[0, 1], small_sems.at[1, 1],
        across,
    )
    total_chip = remote(
        totals_ref.at[tensor], totals_ref.at[tensor], small_sems.at[0, 2], small_sems.at[1, 2], other_chip
    )

    def total_core(k):
        at = core + 2 * k
        return remote(
            totals_ref.at[at], totals_ref.at[at], small_sems.at[0, 3 + k], small_sems.at[1, 3 + k], other_core
        )

    def small_start():
        mine = near_ref[...] + far_ref[...]
        rest = extra_ref[...]
        for k in range(2):
            columns = slice(k * half, (k + 1) * half)
            halves[k, 0:HEADDIM, :] = mine[:, columns]
            halves[k, HEADDIM:, :] = rest[:, columns]
        half_copy.start()

    def small_group():
        half_copy.wait()
        halves[side] = halves[side] + half_in[...]
        for k in range(1, lines):
            group_copy(k).start()

    def small_back():
        for k in range(1, lines):
            group_copy(k).wait()
        rows = pl.ds(pl.multiple_of(line * group, group), group)
        total = halves[side, rows, :]
        for k in range(1, lines):
            total = total + group_in[k - 1]
        group_out[...] = total
        for k in range(1, lines):
            back_copy(k).start()

    def small_half():
        for k in range(1, lines):
            back_copy(k).wait()
        rows = pl.ds(pl.multiple_of(line * group, group), group)
        totals_ref[tensor, side, rows, :] = group_out[...]
        for k in range(1, lines):
            source = (line + lines - k) % lines
            rows = pl.ds(pl.multiple_of(source * group, group), group)
            totals_ref[tensor, side, rows, :] = group_back[k - 1]
        total_half.start()

    def small_chip():
        total_half.wait()
        total_chip.start()

    def small_core():
        total_chip.wait()
        for k in range(2):
            total_core(k).start()

    def small_end():
        for k in range(2):
            total_core(k).wait()

    small = [(1, small_group), (3, small_back), (5, small_half), (8, small_chip), (13, small_core)]
    events = []

    def event():
        events.append(None)
        while small and small[0][0] <= len(events):
            small.pop(0)[1]()

    def x_copy(at, i):
        return remote(
            grads.at[(2 * at + 1 - side) * slots + i], x_in.at[at, i], x_send.at[at, i], x_recv.at[at, i], across
        )

    def x_needed(turn):
        step, i = turn // most, turn % most
        if step < lines - 1:
            each_way(step, lambda at, upward: x_copy(at, i).start())
        elif step == lines - 1:
            x_copy(line, i).start()

    def line_copy(src, at, i, upward):
        if upward:
            return remote(src, up_in.at[at, i], up_send.at[at, i], up_recv.at[at, i], above)
        return remote(src, down_in.at[at, i], down_send.at[at, i], down_recv.at[at, i], below)

    def line_most(at, i, upward):
        arrived = up_in if upward else down_in
        x_copy(at, i).wait_recv()
        own = add(grads[(2 * at + side) * slots + i], x_in[at, i])

        @pl.when(has_down if upward else has_up)
        def _():
            line_copy(x_in.at[at, i], at, i, upward).wait_recv()
            x_in[at, i] = add(own, arrived[at, i]).astype(bf16)

        @pl.when(jnp.logical_not(has_down if upward else has_up))
        def _():
            x_in[at, i] = own.astype(bf16)

        line_copy(x_in.at[at, i], at, i, upward).start()

    def line_last(at, k, upward):
        arrived = up_in if upward else down_in
        own = grads.at[(2 * at + k) * slots + most]

        @pl.when(has_down if upward else has_up)
        def _():
            line_copy(own, at, most + k, upward).wait_recv()
            arrived[at, most + k] = add(own[...], arrived[at, most + k]).astype(bf16)
            line_copy(arrived.at[at, most + k], at, most + k, upward).start()

        @pl.when(jnp.logical_not(has_down if upward else has_up))
        def _():
            line_copy(own, at, most + k, upward).start()

    def each_way(step, work):
        @pl.when(lines - 1 - step > line)
        def _():
            work(lines - 1 - step, True)

        @pl.when(step < line)
        def _():
            work(step, False)

    small_start()
    x_needed(0)
    x_needed(1)
    for step in range(lines - 1):
        for k in range(2):
            each_way(step, lambda at, upward, k=k: line_last(at, k, upward))
        event()
        for i in range(most):
            x_needed(step * most + i + 2)
            each_way(step, lambda at, upward, i=i: line_most(at, i, upward))
            event()

    def gathered_last(k):
        return grads[(2 * line + k) * slots + most].astype(f32)

    owned_ref[most] = gathered_last(side)
    to_send = gathered_last(1 - side)
    last_out[...] = to_send

    @pl.when(has_down)
    def _():
        for k in range(2):
            line_copy(last_in, line, most + k, True).wait_recv()
        owned_ref[most] = owned_ref[most] + up_in[line, most + side].astype(f32)
        last_out[...] = last_out[...] + up_in[line, most + 1 - side].astype(f32)

    @pl.when(has_up)
    def _():
        for k in range(2):
            line_copy(last_in, line, most + k, False).wait_recv()
        owned_ref[most] = owned_ref[most] + down_in[line, most + side].astype(f32)
        last_out[...] = last_out[...] + down_in[line, most + 1 - side].astype(f32)

    x_in[line, most] = last_out[...].astype(bf16)
    last_copy = remote(x_in.at[line, most], last_in, last_sems.at[0], last_sems.at[1], across)
    last_copy.start()
    for turn in range((lines - 1) * most + 2, lines * most):
        x_needed(turn)
    while small:
        small.pop(0)[1]()

    def finish(i, carry):
        x_copy(line, i).wait_recv()
        owned_ref[i] = add(grads[(2 * line + side) * slots + i], x_in[line, i])

        @pl.when(has_down)
        def _():
            line_copy(last_in, line, i, True).wait_recv()
            owned_ref[i] = owned_ref[i] + up_in[line, i].astype(f32)

        @pl.when(has_up)
        def _():
            line_copy(last_in, line, i, False).wait_recv()
            owned_ref[i] = owned_ref[i] + down_in[line, i].astype(f32)

        return carry

    lax.fori_loop(0, most, finish, 0)
    last_copy.wait()
    owned_ref[most] = owned_ref[most] + last_in[...].astype(f32)
    small_end()

    def x_sent(at):
        def one(i, carry):
            x_copy(at, i).wait_send()
            return carry

        lax.fori_loop(0, most, one, 0)

    def line_sent(at, upward):
        def one(i, carry):
            line_copy(last_in, at, i, upward).wait_send()
            return carry

        lax.fori_loop(0, slots + 1, one, 0)

    x_sent(line)
    for step in range(lines - 1):
        each_way(step, lambda at, upward: x_sent(at))
        each_way(step, line_sent)


def reduce_call(grads, near, far, extra, dp_size):
    slots_all, side, width = grads.shape
    slots = slots_all // dp_size
    lines = dp_size // 2
    small_rows = HEADDIM + extra.shape[0]
    group = small_rows // lines
    spec = pl.BlockSpec(memory_space=pltpu.VMEM)
    sems = pltpu.SemaphoreType.DMA
    return pl.pallas_call(
        functools.partial(reduce_kernel, lines),
        in_specs=[spec] * 4,
        out_specs=[spec] * 2,
        out_shape=[
            jax.ShapeDtypeStruct((slots, side, width), f32),
            jax.ShapeDtypeStruct((4, 2, small_rows, width // 2), f32),
        ],
        scratch_shapes=[
            pltpu.VMEM((lines, slots, side, width), bf16),
            pltpu.VMEM((lines, slots + 1, side, width), bf16),
            pltpu.VMEM((lines, slots + 1, side, width), bf16),
            pltpu.VMEM((side, width), f32),
            pltpu.VMEM((side, width), bf16),
            pltpu.VMEM((2, small_rows, width // 2), f32),
            pltpu.VMEM((small_rows, width // 2), f32),
            pltpu.VMEM((lines - 1, group, width // 2), f32),
            pltpu.VMEM((group, width // 2), f32),
            pltpu.VMEM((lines - 1, group, width // 2), f32),
            sems((lines, slots)), sems((lines, slots)),
            sems((lines, slots + 1)), sems((lines, slots + 1)),
            sems((lines, slots + 1)), sems((lines, slots + 1)),
            sems((2,)), sems((2, 5)), sems((2, lines - 1)), sems((2, lines - 1)),
        ],
        compiler_params=pltpu.CompilerParams(
            collective_id=1, has_side_effects=True, vmem_limit_bytes=56 * 2**20
        ),
        cost_estimate=pl.CostEstimate(flops=10**11, bytes_accessed=40 * 2**20, transcendentals=0),
        name="reduce_grads",
    )(grads, near, far, extra)


def small_rule(rate, weight, moment, gradient):
    moment_new = small_decay * moment + (1.0 - small_decay) * gradient
    return moment_new, weight - rate * moment_new


def muon_kernel(
    rate, small_rate_now,
    grad_ref, totals_ref, moment_ref, master_ref,
    state_moment, state_proj, step_moment, step_proj, gain_moment, gain, head_moment, head, conv_moment, conv,
    shared_moment, shared,
    moment_out, master_out,
    state_moment_out, state_out, step_moment_out, step_out, gain_moment_out, gain_out, head_moment_out,
    head_out, conv_moment_out, conv_out, shared_moment_out, shared_out,
):
    tensor = lax.axis_index("tensor")
    rule = functools.partial(small_rule, small_rate_now)

    def row(at, row_at):
        return jnp.concatenate(
            [totals_ref[at, k, row_at : row_at + 1, :] for k in range(2)], axis=1
        )

    def over_tensor(row_at):
        return row(0, row_at) + row(1, row_at) + row(2, row_at) + row(3, row_at)

    for k in range(2):
        parts = [
            jnp.concatenate([totals_ref[2 * k + j, c, 0:HEADDIM, :] for c in range(2)], axis=1)
            for j in range(2)
        ]
        lanes = lanes_of(k)
        state_moment_out[:, lanes], state_out[:, lanes] = rule(
            state_proj[:, lanes], state_moment[:, lanes], jnp.concatenate(parts, axis=0).T
        )
    heads = step_proj.shape[0]
    extra = HEADDIM
    own = [totals_ref[tensor, k, extra : extra + 32, :] for k in range(2)]
    step_moment_out[...], step_out[...] = rule(
        step_proj[...], step_moment[...], jnp.concatenate(own, axis=1)[0:heads]
    )
    gain_moment_out[...], gain_out[...] = rule(gain[...], gain_moment[...], over_tensor(extra + GAIN_ROW))
    head_moment_out[...], head_out[...] = rule(
        head[...], head_moment[...], own[0][HEAD_ROW : HEAD_ROW + 3, 0:heads]
    )
    inner = conv.shape[1]
    per_line = 2 * own[0].shape[1] // inner
    conv_total = jnp.concatenate(own, axis=1)
    for k in range(6):
        at = (k % per_line) * inner
        line = 16 + k // per_line
        one = slice(k, k + 1)
        conv_moment_out[one, :], conv_out[one, :] = rule(
            conv[one, :], conv_moment[one, :], conv_total[line : line + 1, at : at + inner]
        )
    shared_total = over_tensor(extra + SHARED_ROW)
    for k in range(5):
        one = slice(k, k + 1)
        shared_moment_out[one, :], shared_out[one, :] = rule(
            shared[one, :], shared_moment[one, :], shared_total[:, 2 * LANES * k : 2 * LANES * (k + 1)]
        )

    first_coef, second_coef, third_coef = schulz_coefs
    side = HEADDIM
    same = iota((side, side), 0) == iota((side, side), 1)
    eye = jnp.where(same, 1.0, 0.0).astype(f32)
    slots = grad_ref.shape[0]
    grams, totals, scales = [], [], []
    for s in range(slots):
        moment = muon_decay * moment_ref[s] + grad_ref[s].astype(f32)
        moment_out[s] = moment
        square = jnp.sum(jnp.sum(moment * moment, axis=1, keepdims=True), axis=0, keepdims=True)
        scale = 1.0 / (jnp.sqrt(square) + 1e-07)
        scaled = moment * scale
        grams.append(dot_nt(scaled, scaled, exact_mode))
        totals.append(eye)
        scales.append(scale)
    for _ in range(NS_STEPS):
        for s in range(slots):
            gram = grams[s]
            factor = (
                first_coef * eye + second_coef * gram + third_coef * dot_nn(gram, gram, exact_mode)
            )
            totals[s] = dot_nn(factor, totals[s], exact_mode)
            grams[s] = dot_nn(dot_nn(factor, gram, exact_mode), factor, exact_mode)
    for s in range(slots):
        ortho = dot_nn(totals[s], moment_out[s] * scales[s], exact_mode)
        master_out[s] = master_ref[s] - rate * ortho


def muon_call(grad, totals, moment, master, small, tokens_all):
    slots, side, width = moment.shape
    spec = pl.BlockSpec(memory_space=pltpu.VMEM)
    return pl.pallas_call(
        functools.partial(
            muon_kernel, muon_rate * math.sqrt(max(width, side)), small_rate / math.sqrt(tokens_all)
        ),
        in_specs=[spec] * (4 + len(small)),
        out_specs=[spec] * (2 + len(small)),
        out_shape=[jax.ShapeDtypeStruct(moment.shape, f32)] * 2
        + [jax.ShapeDtypeStruct(array.shape, f32) for array in small],
        compiler_params=pltpu.CompilerParams(vmem_limit_bytes=56 * 2**20),
        name="muon",
    )(grad, totals, moment, master, *small)


def pad_to(array, rows, columns):
    return jnp.pad(array, ((0, rows - array.shape[0]), (0, columns - array.shape[1])))


def swap(values, bit):
    return lax.ppermute(values, "tensor", [(t, t ^ bit) for t in range(4)])


def place_half(full, half):
    core = lax.axis_index("tensor") % 2
    return lax.dynamic_update_slice(full, swap(half, 1), ((1 - core) * half.shape[0], 0))


def per_device(
    hidden_in,
    out_grad,
    seq_lengths,
    owner_map,
    muon_master,
    muon_moment,
    state_proj,
    state_moment,
    step_proj,
    step_moment,
    norm_gain,
    gain_moment,
    head_params,
    head_moment,
    conv_params,
    conv_moment,
    state_conv,
    state_conv_moment,
):
    tok_rows, width = hidden_in.shape
    heads = step_proj.shape[1]
    inner = conv_params.shape[1]
    dp_size = lax.axis_size("dp")
    inner_all = inner * lax.axis_size("tensor")
    slots = muon_master.shape[0] * dp_size
    core = lax.axis_index("tensor") % 2
    chip = lax.axis_index("tensor") // 2
    ends = jnp.concatenate([jnp.cumsum(seq_lengths[0], dtype=jnp.int32), core[None].astype(jnp.int32)])
    seq_count = seq_lengths.shape[1]
    master = muon_master.transpose(0, 2, 1)
    moment = muon_moment.transpose(0, 2, 1)
    stack = gather_call(master.astype(bf16), dp_size)
    narrow = pad_to(jnp.concatenate([state_proj, step_proj], axis=1), width, NARROW).astype(bf16)
    gain = norm_gain[None, :]
    head_rows = pad_to(head_params, 8, LANES)
    conv_rows = pad_to(conv_params, 8, inner)
    shared_rows = pad_to(state_conv, 8, state_conv.shape[1])
    free = jnp.all(owner_map[None, :] != jnp.arange(slots, dtype=jnp.int32)[:, None], axis=1)
    free = free.astype(jnp.int32)
    group_rows = 8 * (dp_size // 2)
    extra_rows = -(-(HEADDIM + 32) // group_rows) * group_rows - HEADDIM

    normed, gate, input_part, mixed, dscaled, shared_in, step_part, states, sums, mine, other = forward_call(
        owner_map, ends, hidden_in, out_grad, stack, gain, narrow, head_rows, conv_rows, shared_rows, heads
    )
    sums, near = exchange_call(sums, mine, other)
    far = swap(near, 2)
    dboth, scaled, mine, other, narrow_grad, extra = backward_call(
        owner_map, ends, hidden_in, gate, input_part, mixed, dscaled, shared_in, step_part, states, sums,
        stack, narrow, gain, head_rows, conv_rows, shared_rows, heads, inner_all, extra_rows,
    )

    quarters = narrow_grad[: 4 * HEADDIM].reshape(2, 2, HEADDIM, width)
    got = swap(other, 1)
    got_narrow = swap(lax.dynamic_index_in_dim(quarters, 1 - core, 1, keepdims=False), 1)
    mine_narrow = lax.dynamic_index_in_dim(quarters, core, 1, keepdims=False)
    far, scaled = lax.optimization_barrier((far, scaled))
    rows_spec = pl.BlockSpec((8, ROWS), lambda i, ends: (0, ends[seq_count] * (tok_rows // ROWS // 2) + i))
    block_full, block_half = half_call(
        functools.partial(branch_kernel, inner_all, seq_count), "block_out", ends, [near, far], [hidden_in],
        ([sums], [rows_spec]),
    )
    block_out = place_half(block_full, block_half)
    scaled, block_half = lax.optimization_barrier((scaled, block_half))
    slotted = grads_call(owner_map, ends, free, scaled, out_grad, 2 * heads, True, None)
    slotted, got, got_narrow = lax.optimization_barrier((slotted, got, got_narrow))
    pair = mine_narrow + got_narrow
    near_narrow = lax.dynamic_index_in_dim(pair, chip, 0, keepdims=False)
    send_narrow = lax.dynamic_index_in_dim(pair, 1 - chip, 0, keepdims=False)
    far_narrow = swap(send_narrow, 2)
    send_narrow, got = lax.optimization_barrier((send_narrow, got))
    near_grad = (mine.astype(f32) + got.astype(f32)).astype(bf16)
    far_grad = swap(near_grad, 2)
    near_grad, near_narrow, dboth = lax.optimization_barrier((near_grad, near_narrow, dboth))
    slotted = grads_call(owner_map, ends, free, dboth, normed, 0, False, slotted)
    owned, totals = reduce_call(slotted, near_narrow, far_narrow, extra, dp_size)
    owned, totals, far_grad = lax.optimization_barrier((owned, totals, far_grad))
    gain_spec = pl.BlockSpec(gain.shape, lambda i, ends: (0, 0))
    input_full, input_half = half_call(
        functools.partial(input_kernel, seq_count), "input_grad", ends, [near_grad, far_grad],
        [hidden_in, out_grad], ([gain], [gain_spec]),
    )
    input_grad = place_half(input_full, input_half)
    owned, input_half = lax.optimization_barrier((owned, input_half))
    small = [
        state_moment, state_proj, step_moment.T, step_proj.T, gain_moment[None, :], gain, head_moment,
        head_params, conv_moment, conv_params, state_conv_moment, state_conv,
    ]
    moment_new, master_new, *small_new = muon_call(owned, totals, moment, master, small, tok_rows * dp_size)
    state_moment_new, state_proj_new, step_moment_new, step_proj_new = small_new[:4]
    gain_moment_new, norm_gain_new, head_moment_new, head_params_new = small_new[4:8]
    conv_moment_new, conv_params_new, state_conv_moment_new, state_conv_new = small_new[8:]
    step_moment_new, step_proj_new = step_moment_new.T, step_proj_new.T
    gain_moment_new, norm_gain_new = gain_moment_new[0], norm_gain_new[0]
    return (
        block_out,
        input_grad,
        moment_new.transpose(0, 2, 1),
        master_new.transpose(0, 2, 1),
        state_moment_new,
        state_proj_new,
        step_moment_new,
        step_proj_new,
        gain_moment_new,
        norm_gain_new,
        head_moment_new,
        head_params_new,
        conv_moment_new,
        conv_params_new,
        state_conv_moment_new,
        state_conv_new,
    )


def solution(mesh):
    in_specs = (
        P("dp", None),
        P("dp", None),
        P("dp", None),
        P(),
        P("dp", None, "tensor"),
        P("dp", None, "tensor"),
        P(),
        P(),
        P(None, "tensor"),
        P(None, "tensor"),
        P(),
        P(),
        P(None, "tensor"),
        P(None, "tensor"),
        P(None, "tensor"),
        P(None, "tensor"),
        P(),
        P(),
    )
    out_specs = (
        P("dp", None),
        P("dp", None),
        P("dp", None, "tensor"),
        P("dp", None, "tensor"),
        P(),
        P(),
        P(None, "tensor"),
        P(None, "tensor"),
        P(),
        P(),
        P(None, "tensor"),
        P(None, "tensor"),
        P(None, "tensor"),
        P(None, "tensor"),
        P(),
        P(),
    )
    return jax.shard_map(
        per_device, mesh=mesh, in_specs=in_specs, out_specs=out_specs, check_vma=False
    )
```

```python
import functools
import math

import jax
import jax.numpy as jnp
from jax import lax
from jax.experimental import pallas as pl
from jax.experimental.pallas import tpu as pltpu
from jax.sharding import PartitionSpec as P

HEADDIM = 64
NS_STEPS = 5
ROWS = 256
SUB = 128
LANES = 128
NARROW = 384
CHUNK = 768
GAIN_ROW, SHARED_ROW, HEAD_ROW = 19, 20, 21

exact_mode = lax.Precision.HIGHEST
norm_eps = 1e-05
schulz_coefs = (3.4445, -4.775, 2.0315)
muon_decay = 0.95
muon_rate = 0.02
small_decay = 0.9
small_rate = 2.0
log2_e = 1.4426950408889634
f32 = jnp.float32
bf16 = jnp.bfloat16
far_below = -1e30


def dot_nn(left, right, precision=None):
    return lax.dot_general(
        left, right, (((1,), (0,)), ((), ())), precision=precision, preferred_element_type=f32
    )


def dot_nt(left, right, precision=None):
    return lax.dot_general(
        left, right, (((1,), (1,)), ((), ())), precision=precision, preferred_element_type=f32
    )


def dot_tn(left, right, precision=None):
    return lax.dot_general(
        left, right, (((0,), (0,)), ((), ())), precision=precision, preferred_element_type=f32
    )


def sigmoid(values):
    return 0.5 * jnp.tanh(0.5 * values) + 0.5


def iota(shape, dim):
    return lax.broadcasted_iota(jnp.int32, shape, dim)


def segment_at(place, ends_ref, count):
    total = (place >= ends_ref[0]).astype(jnp.int32)
    for k in range(1, count):
        total = total + (place >= ends_ref[k]).astype(jnp.int32)
    return total


def step_terms(step_part, head_ref):
    shifted = step_part + head_ref[0:1, :]
    small = jnp.exp(-jnp.abs(shifted))
    tail = jnp.where(
        small < 0.01, small * (1.0 - small * (0.5 - small * (1.0 / 3.0))), jnp.log(1.0 + small)
    )
    step = jnp.maximum(shifted, 0.0) + tail
    decay = -jnp.exp(head_ref[1:2, :])
    log_rate = step * (decay * log2_e)
    lower = (iota((SUB, SUB), 0) >= iota((SUB, SUB), 1)).astype(f32)
    cum = dot_nn(lower, log_rate, exact_mode)
    source = cum - jnp.log(step) * log2_e
    return shifted, step, decay, cum, source


def expand(values, pair):
    shape = (values.shape[0], LANES)
    low = jnp.broadcast_to(values[:, 2 * pair : 2 * pair + 1], shape)
    high = jnp.broadcast_to(values[:, 2 * pair + 1 : 2 * pair + 2], shape)
    return jnp.where(iota(shape, 1) < HEADDIM, low, high)


def split_pair(values):
    low = iota(values.shape, 1) < HEADDIM
    zero = jnp.zeros_like(values)
    return jnp.where(low, values, zero), jnp.where(low, zero, values)


def lanes_of(pair):
    return slice(pair * LANES, (pair + 1) * LANES)


def shift_mask(place, shift, ends_ref, count, rows_all):
    other = place + shift
    inside = (other >= 0) & (other < rows_all)
    same = segment_at(place, ends_ref, count) == segment_at(other, ends_ref, count)
    return jnp.where(inside & same, 1.0, 0.0).astype(f32)


def conv_tile(buf_ref, first, lanes, taps, masks):
    total = taps[4:5, :] + taps[3:4, :] * buf_ref[first + 8 : first + 8 + SUB, lanes]
    for back in (1, 2, 3):
        rows = buf_ref[first + 8 - back : first + 8 - back + SUB, lanes]
        total = total + taps[3 - back : 4 - back, :] * (rows * masks[back - 1])
    return total


def block_terms(base, ends_ref, count):
    row_at = base + iota((SUB, SUB), 0)
    col_at = base + iota((SUB, SUB), 1)
    seg_row = segment_at(row_at, ends_ref, count)
    seg_col = segment_at(col_at, ends_ref, count)
    seg_last = segment_at(base + SUB - 1, ends_ref, count)
    seg_before = jnp.where(base == 0, -1, segment_at(base - 1, ends_ref, count))
    carried = jnp.where(seg_row == seg_before, 1.0, 0.0).astype(f32)
    tail_same = jnp.where(seg_row == seg_last, 1.0, 0.0).astype(f32)
    through = jnp.where(seg_last == seg_before, 1.0, 0.0).astype(f32)
    same = seg_row == seg_col
    return row_at, col_at, same, carried, tail_same, through


def store_half(values, block, blocks, core, mine_ref, other_ref):
    is_mine = block // (blocks // 2) == core

    @pl.when(is_mine)
    def _():
        mine_ref[...] = values

    @pl.when(jnp.logical_not(is_mine))
    def _():
        other_ref[...] = values


def half_specs(width, blocks, seq_count, block_of):
    def index(half, block):
        return jnp.where(half == 0, jnp.minimum(block, blocks // 2 - 1), jnp.maximum(block - blocks // 2, 0))

    def mine(i, place, ends):
        return (index(ends[seq_count], block_of(i)), 0)

    def other(i, place, ends):
        return (index(1 - ends[seq_count], block_of(i)), 0)

    return [pl.BlockSpec((ROWS, width), mine), pl.BlockSpec((ROWS, width), other)]


def load_weights(stack_ref, place_ref, held_ref, sems, first, count):
    copies = []
    for m in range(count):
        copies.append(
            pltpu.make_async_copy(
                stack_ref.at[place_ref[first + m]],
                held_ref.at[pl.ds(m * HEADDIM, HEADDIM)],
                sems.at[m],
            )
        )
    for copy in copies:
        copy.start()
    return copies


def fold_rows(values):
    return jnp.sum(values.reshape(values.shape[0] // 8, 8, values.shape[1]), axis=0)


def project_units(normed_ref, cot_ref, narrow_ref, weights, targets, row_at, last_end, inner):
    next_gate, next_in, next_scaled, next_narrow = targets
    units = []

    def one(target, at, weight_row, left_ref, masked):
        def unit():
            part = dot_nt(left_ref[...], weights[weight_row + at : weight_row + at + 2 * LANES, :])
            if masked:
                part = jnp.where(row_at < last_end, part, 0.0)
            target[:, at : at + 2 * LANES] = part

        return unit

    for at in range(0, inner, 2 * LANES):
        units.append(one(next_in, at, inner, normed_ref, False))
    units.append(lambda: next_narrow.__setitem__(Ellipsis, dot_nn(normed_ref[...], narrow_ref[...])))
    for at in range(0, inner, 2 * LANES):
        units.append(one(next_gate, at, 0, normed_ref, False))
        units.append(one(next_scaled, at, 2 * inner, cot_ref, True))
    return units


def forward_kernel(
    heads, seq_count, rows_all,
    place_ref, ends_ref,
    hidden_ref, cot_ref, stack_ref, gain_ref, narrow_ref, head_ref, conv_ref, shared_ref,
    normed_ref, gate_ref, input_ref, x_ref, slope_ref, mixed_ref, dscaled_ref, shared_in_ref, bc_ref,
    bc_slope_ref, step_ref, state_ref, sums_ref, mine_ref, other_ref,
    weights, sems, in_buf, shared_buf, gate_buf, scaled_buf, step_buf, next_gate, next_in, next_scaled,
    next_narrow, state, low_buf, tail_buf, across,
):
    turn = pl.program_id(0)
    blocks = pl.num_programs(0) - 1
    block = turn - 1
    inner = heads * HEADDIM
    pairs = heads // 2

    def normalize():
        hidden = hidden_ref[...].astype(f32)
        inv_rms = lax.rsqrt(jnp.mean(hidden * hidden, axis=1, keepdims=True) + norm_eps)
        normed_ref[...] = (hidden * inv_rms * gain_ref[0:1, :]).astype(bf16)

    row_here = jnp.minimum(turn, blocks - 1) * ROWS + iota((ROWS, 2 * LANES), 0)
    targets = (next_gate, next_in, next_scaled, next_narrow)
    units = project_units(
        normed_ref, cot_ref, narrow_ref, weights, targets, row_here, ends_ref[seq_count - 1], inner
    )

    def take_next():
        in_buf[0:8, :] = in_buf[ROWS : ROWS + 8, :]
        shared_buf[0:8, :] = shared_buf[ROWS : ROWS + 8, :]
        in_buf[8:, :] = next_in[...]
        gate_buf[...] = next_gate[...]
        scaled_buf[...] = next_scaled[...]
        shared_buf[8:, :] = next_narrow[:, 0 : 2 * LANES]
        step_buf[...] = next_narrow[:, 2 * LANES : 3 * LANES]

    @pl.when(turn == 0)
    def _():
        copies = load_weights(stack_ref, place_ref, weights, sems, 0, 3 * heads)
        in_buf[ROWS : ROWS + 8, :] = jnp.zeros((8, inner), f32)
        shared_buf[ROWS : ROWS + 8, :] = jnp.zeros((8, 2 * LANES), f32)
        state[...] = jnp.zeros_like(state)
        normalize()
        for copy in copies:
            copy.wait()
        for unit in units:
            unit()
        take_next()

    @pl.when(turn > 0)
    def _():
        normalize()
        pending = list(units)
        first_row = block * ROWS
        input_ref[...] = in_buf[8:, :].astype(bf16)
        gate_ref[...] = gate_buf[...].astype(bf16)
        dscaled_ref[...] = scaled_buf[...].astype(bf16)
        shared_in_ref[...] = shared_buf[8:, :].astype(bf16)
        step_ref[...] = step_buf[...]
        for sub in range(ROWS // SUB):
            first = sub * SUB
            here = slice(first, first + SUB)
            base = first_row + first
            row_at, col_at, same, carried, tail_same, through = block_terms(base, ends_ref, seq_count)
            causal = jnp.where(same & (row_at >= col_at), 0.0, far_below).astype(f32)
            masks = [shift_mask(row_at, -back, ends_ref, seq_count, rows_all) for back in (1, 2, 3)]
            bc = []
            for part in range(2):
                lanes = lanes_of(part)
                u = conv_tile(shared_buf, first, lanes, shared_ref[:, lanes], masks)
                sig = sigmoid(u)
                bc.append((u * sig).astype(bf16))
                bc_ref[here, lanes] = bc[part]
                bc_slope_ref[here, lanes] = (sig * (1.0 + u * (1.0 - sig))).astype(bf16)
            b_low, c_low = bc
            _, _, _, cum, source = step_terms(step_buf[here, :], head_ref)
            source_row = source.T
            scores = dot_nt(c_low, b_low)
            cum_last = cum[SUB - 1 : SUB, :]
            entry = jnp.exp2(cum) * carried
            leave = jnp.exp2(cum_last - source) * tail_same
            pass_on = jnp.exp2(cum_last) * through
            state_low = state[...].astype(bf16)
            state_ref[sub] = state_low
            across[...] = dot_nn(c_low, state_low)
            square = jnp.zeros((SUB, LANES), f32)
            inner_dot = jnp.zeros((SUB, LANES), f32)
            for pair in range(pairs):
                if pending:
                    pending.pop(0)()
                lanes = lanes_of(pair)
                u = conv_tile(in_buf, first, lanes, conv_ref[:, lanes], masks)
                sig = sigmoid(u)
                x_low = (u * sig).astype(bf16)
                x_ref[here, lanes] = x_low
                slope_ref[here, lanes] = (sig * (1.0 + u * (1.0 - sig))).astype(bf16)
                x = x_low.astype(f32)
                mats = []
                for h in (2 * pair, 2 * pair + 1):
                    gap = cum[:, h : h + 1] - source_row[h : h + 1, :]
                    mats.append((jnp.exp2(gap + causal) * scores).astype(bf16))
                x_a, x_b = split_pair(x_low)
                mixed = dot_nn(jnp.concatenate(mats, axis=1), jnp.concatenate([x_a, x_b], axis=0))
                mixed = mixed + across[:, lanes] * expand(entry, pair)
                mixed = mixed + expand(head_ref[2:3, :], pair) * x
                mixed_ref[here, lanes] = mixed
                gate = gate_buf[here, lanes]
                gated = mixed * (gate * sigmoid(gate))
                gated_gain = gated * conv_ref[5:6, lanes]
                low_buf[here, lanes] = gated_gain.astype(bf16)
                square = square + gated * gated
                inner_dot = inner_dot + scaled_buf[here, lanes] * gated_gain
                tail_buf[:, lanes] = (x * expand(leave, pair)).astype(bf16)
            fresh = dot_tn(b_low, tail_buf[...])
            for pair in range(pairs):
                lanes = lanes_of(pair)
                state[:, lanes] = state[:, lanes] * expand(pass_on, pair) + fresh[:, lanes]
            sums_ref[0:1, here] = jnp.sum(square.T, axis=0, keepdims=True)
            sums_ref[1:2, here] = jnp.sum(inner_dot.T, axis=0, keepdims=True)
        while pending:
            pending.pop(0)()
        sums_ref[2:8, :] = jnp.zeros((6, ROWS), f32)
        part = dot_nn(low_buf[...], weights[2 * inner : 3 * inner, :]).astype(bf16)
        store_half(part, block, blocks, ends_ref[seq_count], mine_ref, other_ref)
        take_next()


def forward_call(place, ends, hidden, cot, stack, gain, narrow, head_rows, conv_rows, shared_rows, heads):
    rows_all, width = hidden.shape
    inner = heads * HEADDIM
    blocks = rows_all // ROWS

    def ahead(columns):
        return pl.BlockSpec((ROWS, columns), lambda i, *_: (jnp.minimum(i, blocks - 1), 0))

    def rows(columns):
        return pl.BlockSpec((ROWS, columns), lambda i, *_: (jnp.maximum(i - 1, 0), 0))

    def whole(array):
        return pl.BlockSpec(array.shape, lambda i, *_: (0,) * array.ndim)

    columns = [
        (inner, bf16), (inner, bf16), (inner, bf16), (inner, bf16), (inner, f32), (inner, bf16),
        (2 * LANES, bf16), (2 * LANES, bf16), (2 * LANES, bf16), (LANES, f32),
    ]
    out_shape = [
        jax.ShapeDtypeStruct((rows_all, width), bf16),
        *[jax.ShapeDtypeStruct((rows_all, count), kind) for count, kind in columns],
        jax.ShapeDtypeStruct((rows_all // SUB, LANES, inner), bf16),
        jax.ShapeDtypeStruct((8, rows_all), f32),
        jax.ShapeDtypeStruct((rows_all // 2, width), bf16),
        jax.ShapeDtypeStruct((rows_all // 2, width), bf16),
    ]
    out_specs = [
        ahead(width),
        *[rows(count) for count, _ in columns],
        pl.BlockSpec((ROWS // SUB, LANES, inner), lambda i, *_: (jnp.maximum(i - 1, 0), 0, 0)),
        pl.BlockSpec((8, ROWS), lambda i, *_: (0, jnp.maximum(i - 1, 0))),
        *half_specs(width, blocks, ends.shape[0] - 1, lambda i: jnp.maximum(i - 1, 0)),
    ]
    return pl.pallas_call(
        functools.partial(forward_kernel, heads, ends.shape[0] - 1, rows_all),
        grid_spec=pltpu.PrefetchScalarGridSpec(
            num_scalar_prefetch=2,
            grid=(blocks + 1,),
            in_specs=[
                ahead(width), ahead(width), pl.BlockSpec(memory_space=pl.ANY), whole(gain), whole(narrow),
                whole(head_rows), whole(conv_rows), whole(shared_rows),
            ],
            out_specs=out_specs,
            scratch_shapes=[
                pltpu.VMEM((3 * inner, width), bf16),
                pltpu.SemaphoreType.DMA((3 * heads,)),
                pltpu.VMEM((ROWS + 8, inner), f32),
                pltpu.VMEM((ROWS + 8, 2 * LANES), f32),
                pltpu.VMEM((ROWS, inner), f32),
                pltpu.VMEM((ROWS, inner), f32),
                pltpu.VMEM((ROWS, LANES), f32),
                pltpu.VMEM((ROWS, inner), f32),
                pltpu.VMEM((ROWS, inner), f32),
                pltpu.VMEM((ROWS, inner), f32),
                pltpu.VMEM((ROWS, NARROW), f32),
                pltpu.VMEM((LANES, inner), f32),
                pltpu.VMEM((ROWS, inner), bf16),
                pltpu.VMEM((SUB, inner), bf16),
                pltpu.VMEM((SUB, inner), f32),
            ],
        ),
        out_shape=out_shape,
        compiler_params=pltpu.CompilerParams(
            dimension_semantics=("arbitrary",), vmem_limit_bytes=56 * 2**20
        ),
        cost_estimate=pl.CostEstimate(
            flops=2 * rows_all * width * (4 * inner + NARROW), bytes_accessed=60 * 2**20, transcendentals=0
        ),
        name="mixer_forward",
    )(place, ends, hidden, cot, stack, gain, narrow, head_rows, conv_rows, shared_rows)


def backward_kernel(
    heads, seq_count, rows_all, inner_all,
    place_ref, ends_ref,
    hidden_ref, gate_ref, input_ref, x_ref, slope_ref, mixed_ref, dscaled_ref, shared_in_ref, bc_ref,
    bc_slope_ref, step_ref, state_ref, sums_ref,
    stack_ref, narrow_ref, gain_ref, head_ref, conv_ref, shared_ref,
    dboth_ref, scaled_ref, mine_ref, other_ref, narrow_grad_ref, extra_ref,
    weights, sems, du_buf, dshared_buf, dstate, state_after, from_state, terms, source_terms, tail_buf,
    entry_buf, dnarrow_buf, last_both, last_narrow, dn_buf, conv_grad, shared_grad, head_grad, skip_grad,
    gain_grad,
):
    turn = pl.program_id(0)
    blocks = pl.num_programs(0) - 1
    block = blocks - 1 - turn
    inner = heads * HEADDIM
    pairs = heads // 2
    width = hidden_ref.shape[1]
    wide = 2 * LANES

    @pl.when(turn == 0)
    def _():
        copies = load_weights(stack_ref, place_ref, weights, sems, 0, 2 * heads)
        du_buf[ROWS:, :] = jnp.zeros((8, inner), f32)
        dshared_buf[ROWS:, :] = jnp.zeros((8, 2 * LANES), f32)
        for ref in (
            dstate, state_after, last_both, last_narrow, conv_grad, shared_grad, head_grad, skip_grad,
            gain_grad, narrow_grad_ref,
        ):
            ref[...] = jnp.zeros_like(ref)
        for copy in copies:
            copy.wait()

    def row_units():
        hidden = hidden_ref[...].astype(f32)
        inv_rms = lax.rsqrt(jnp.mean(hidden * hidden, axis=1, keepdims=True) + norm_eps)

        def one(at):
            columns = slice(at, at + wide)

            def unit():
                part = dot_nn(last_both[...], weights[:, columns])
                part = part + dot_nt(last_narrow[...], narrow_ref[columns, :])
                dn_buf[:, columns] = part.astype(bf16)
                unit_rows = hidden_ref[:, columns].astype(f32) * inv_rms
                gain_grad[:, columns] += fold_rows(part * unit_rows)
                normed = (unit_rows * gain_ref[0:1, columns]).astype(bf16)
                narrow_grad_ref[:, columns] += dot_tn(last_narrow[...], normed)

            return unit

        return [one(at) for at in range(0, width, wide)]

    def finish_rows():
        store_half(dn_buf[...], block + 1, blocks, ends_ref[seq_count], mine_ref, other_ref)

    @pl.when(turn < blocks)
    def _():
        pending = row_units()
        reduce_heads = (iota((inner, LANES), 0) // HEADDIM == iota((inner, LANES), 1)).astype(bf16)
        first_row = block * ROWS
        kept = []
        for sub in reversed(range(ROWS // SUB)):
            first = sub * SUB
            here = slice(first, first + SUB)
            base = first_row + first
            row_at, col_at, same, carried, tail_same, through = block_terms(base, ends_ref, seq_count)
            causal = jnp.where(same & (row_at <= col_at), 0.0, far_below).astype(f32)
            b_low, c_low = bc_ref[here, 0:LANES], bc_ref[here, LANES : 2 * LANES]
            shifted, step, decay, cum, source = step_terms(step_ref[here, :], head_ref)
            kept.append((here, shifted, step, decay))
            cum_row = cum.T
            scores = dot_nt(b_low, c_low)
            cum_last = cum[SUB - 1 : SUB, :]
            entry = jnp.exp2(cum) * carried
            leave = jnp.exp2(cum_last - source) * tail_same
            pass_on = jnp.exp2(cum_last) * through
            inv_row = lax.rsqrt(sums_ref[0:1, here] * (1.0 / inner_all) + norm_eps)
            fix_row = inv_row * inv_row * inv_row * sums_ref[1:2, here] * (1.0 / inner_all)
            inv = jnp.broadcast_to(inv_row, (SUB, SUB)).T
            fix = jnp.broadcast_to(fix_row, (SUB, SUB)).T
            dstate_low = dstate[...].astype(bf16)
            from_state[...] = dot_nn(b_low, dstate_low)
            dscores = jnp.zeros((SUB, SUB), f32)
            for pair in range(pairs):
                if pending and pair % 2 == 1:
                    pending.pop(0)()
                lanes = lanes_of(pair)
                x_low = x_ref[here, lanes]
                x = x_low.astype(f32)
                slope = slope_ref[here, lanes].astype(f32)
                gate = gate_ref[here, lanes].astype(f32)
                gate_sig = sigmoid(gate)
                gate_silu = gate * gate_sig
                mixed = mixed_ref[here, lanes]
                gated = mixed * gate_silu
                gain = conv_ref[5:6, lanes]
                dscaled = dscaled_ref[here, lanes].astype(f32)
                normal = gated * inv
                scaled_ref[here, lanes] = (normal * gain).astype(bf16)
                conv_grad[5, :, lanes] += fold_rows(dscaled * normal)
                dgated = inv * (dscaled * gain) - gated * fix
                dgate = dgated * mixed * (gate_sig * (1.0 + gate * (1.0 - gate_sig)))
                dboth_ref[here, lanes] = dgate.astype(bf16)
                dmixed = dgated * gate_silu
                dy_low = dmixed.astype(bf16)
                dy = dy_low.astype(f32)
                skip = expand(head_ref[2:3, :], pair)
                skip_grad[:, lanes] += fold_rows(dmixed * x)
                x_parts = split_pair(x_low)
                dy_parts = split_pair(dy_low)
                mats = []
                for k in range(2):
                    h = 2 * pair + k
                    gap = cum_row[h : h + 1, :] - source[:, h : h + 1]
                    decays = jnp.exp2(gap + causal)
                    mats.append((decays * scores).astype(bf16))
                    dscores = dscores + dot_nt(x_parts[k], dy_low) * decays
                dx = dot_nn(jnp.concatenate(mats, axis=1), jnp.concatenate(dy_parts, axis=0))
                leave_here = expand(leave, pair)
                dx = dx + leave_here * from_state[:, lanes]
                source_term = x * dx
                source_terms[here, lanes] = source_term
                terms[here, lanes] = dy * (mixed - skip * x) - source_term
                tail_buf[:, lanes] = (x * leave_here).astype(bf16)
                entry_buf[:, lanes] = (dy * expand(entry, pair)).astype(bf16)
                du_buf[here, lanes] = (dx + skip * dmixed) * slope
            state_low = state_ref[sub]
            dscores_low = dscores.astype(bf16)
            db = dot_nn(dscores_low, c_low) + dot_nt(tail_buf[...], dstate_low)
            dc = dot_tn(dscores_low, b_low) + dot_nt(entry_buf[...], state_low)
            dshared_buf[here, 0:LANES] = db * bc_slope_ref[here, 0:LANES].astype(f32)
            dshared_buf[here, LANES:wide] = dc * bc_slope_ref[here, LANES:wide].astype(f32)
            at_end = jnp.sum(dstate[...] * state_after[...].astype(f32), axis=0, keepdims=True)
            terms[first + SUB - 1 : first + SUB, :] += at_end
            state_after[...] = state_low
            fresh = dot_tn(c_low, entry_buf[...])
            for pair in range(pairs):
                lanes = lanes_of(pair)
                dstate[:, lanes] = dstate[:, lanes] * expand(pass_on, pair) + fresh[:, lanes]
        while pending:
            pending.pop(0)()

        both = jnp.concatenate([terms[...], source_terms[...]], axis=0)
        high = both.astype(bf16)
        low = (both - high.astype(f32)).astype(bf16)
        reduced = dot_nn(high, reduce_heads) + dot_nn(low, reduce_heads)
        upper = (iota((SUB, SUB), 0) <= iota((SUB, SUB), 1)).astype(f32)

        for sub in range(ROWS // SUB):
            first = sub * SUB
            here = slice(first, first + SUB)
            row_at = first_row + first + iota((SUB, LANES), 0)
            ahead = [shift_mask(row_at, k, ends_ref, seq_count, rows_all) for k in (1, 2, 3)]
            groups = [(pair, True) for pair in range(pairs)] + [(0, False), (1, False)]
            for group, is_wide in groups:
                lanes = lanes_of(group)
                grads, held = (du_buf, input_ref) if is_wide else (dshared_buf, shared_in_ref)
                taps = conv_ref[:, lanes] if is_wide else shared_ref[:, lanes]
                sums = conv_grad if is_wide else shared_grad
                du = grads[here, lanes]
                v = held[here, lanes].astype(f32)
                dv = taps[3:4, :] * du
                sums[3, :, lanes] += fold_rows(du * v)
                sums[4, :, lanes] += fold_rows(du)
                for k in (1, 2, 3):
                    moved = grads[first + k : first + k + SUB, lanes] * ahead[k - 1]
                    dv = dv + taps[3 - k : 4 - k, :] * moved
                    sums[3 - k, :, lanes] += fold_rows(moved * v)
                if is_wide:
                    dboth_ref[here, inner + group * LANES : inner + (group + 1) * LANES] = dv.astype(bf16)
                else:
                    dnarrow_buf[here, lanes] = dv.astype(bf16)
        for here, shifted, step, decay in kept:
            dcum = reduced[here]
            from_source = reduced[ROWS + here.start : ROWS + here.stop]
            dlog = dot_nn(upper, dcum, exact_mode)
            sig = sigmoid(shifted)
            ratio = jnp.where(shifted < -15.0, 1.0, sig / step)
            dlog_decay = dlog * decay
            dstep = from_source * ratio + dlog_decay * sig
            dnarrow_buf[here, wide:NARROW] = dstep.astype(bf16)
            head_grad[0] += fold_rows(dstep)
            head_grad[1] += fold_rows(dlog_decay * step)
        du_buf[ROWS:, :] = du_buf[0:8, :]
        dshared_buf[ROWS:, :] = dshared_buf[0:8, :]

        @pl.when(turn > 0)
        def _():
            finish_rows()

        last_both[...] = dboth_ref[...]
        last_narrow[...] = dnarrow_buf[...]

    @pl.when(turn == blocks)
    def _():
        for unit in row_units():
            unit()
        finish_rows()
        extra_ref[...] = jnp.zeros_like(extra_ref)
        extra_ref[0:16, :] = narrow_grad_ref[wide : wide + 16, :]
        per_line = width // inner

        def total(values):
            return jnp.sum(values, axis=0, keepdims=True)

        for k in range(6):
            at = (k % per_line) * inner
            row = 16 + k // per_line
            extra_ref[row : row + 1, at : at + inner] = total(conv_grad[k])
        extra_ref[GAIN_ROW : GAIN_ROW + 1, :] = total(gain_grad[...])
        for k in range(5):
            extra_ref[SHARED_ROW : SHARED_ROW + 1, wide * k : wide * (k + 1)] = total(shared_grad[k])
        for k in range(2):
            extra_ref[HEAD_ROW + k : HEAD_ROW + k + 1, 0:LANES] = total(head_grad[k])
        reduce_all = (iota((inner, LANES), 0) // HEADDIM == iota((inner, LANES), 1)).astype(f32)
        skip_sum = dot_nn(skip_grad[...], reduce_all, exact_mode)
        extra_ref[HEAD_ROW + 2 : HEAD_ROW + 3, 0:LANES] = total(skip_sum)


def backward_call(
    place, ends, hidden, saved, sums, stack, narrow, gain, head_rows, conv_rows, shared_rows, heads,
    inner_all, extra_rows,
):
    rows_all, width = hidden.shape
    inner = heads * HEADDIM
    blocks = rows_all // ROWS

    def rows(columns):
        return pl.BlockSpec((ROWS, columns), lambda i, *_: (jnp.maximum(blocks - 1 - i, 0), 0))

    def behind(i):
        return jnp.minimum(blocks - i, blocks - 1)

    def whole(shape):
        return pl.BlockSpec(shape, lambda i, *_: (0,) * len(shape))

    out_shape = [
        jax.ShapeDtypeStruct((rows_all, 2 * inner), bf16),
        jax.ShapeDtypeStruct((rows_all, inner), bf16),
        jax.ShapeDtypeStruct((rows_all // 2, width), bf16),
        jax.ShapeDtypeStruct((rows_all // 2, width), bf16),
        jax.ShapeDtypeStruct((NARROW, width), f32),
        jax.ShapeDtypeStruct((extra_rows, width), f32),
    ]
    out_specs = [
        rows(2 * inner), rows(inner),
        *half_specs(width, blocks, ends.shape[0] - 1, behind),
        whole((NARROW, width)), whole((extra_rows, width)),
    ]
    return pl.pallas_call(
        functools.partial(backward_kernel, heads, ends.shape[0] - 1, rows_all, inner_all),
        grid_spec=pltpu.PrefetchScalarGridSpec(
            num_scalar_prefetch=2,
            grid=(blocks + 1,),
            in_specs=[
                pl.BlockSpec((ROWS, width), lambda i, *_: (behind(i), 0)),
                *[rows(array.shape[1]) for array in saved[:-1]],
                pl.BlockSpec(
                    (ROWS // SUB, LANES, inner), lambda i, *_: (jnp.maximum(blocks - 1 - i, 0), 0, 0)
                ),
                pl.BlockSpec((8, ROWS), lambda i, *_: (0, jnp.maximum(blocks - 1 - i, 0))),
                pl.BlockSpec(memory_space=pl.ANY), whole(narrow.shape), whole(gain.shape),
                whole(head_rows.shape), whole(conv_rows.shape), whole(shared_rows.shape),
            ],
            out_specs=out_specs,
            scratch_shapes=[
                pltpu.VMEM((2 * inner, width), bf16),
                pltpu.SemaphoreType.DMA((2 * heads,)),
                pltpu.VMEM((ROWS + 8, inner), f32),
                pltpu.VMEM((ROWS + 8, 2 * LANES), f32),
                pltpu.VMEM((LANES, inner), f32),
                pltpu.VMEM((LANES, inner), bf16),
                pltpu.VMEM((SUB, inner), f32),
                pltpu.VMEM((ROWS, inner), f32),
                pltpu.VMEM((ROWS, inner), f32),
                pltpu.VMEM((SUB, inner), bf16),
                pltpu.VMEM((SUB, inner), bf16),
                pltpu.VMEM((ROWS, NARROW), bf16),
                pltpu.VMEM((ROWS, 2 * inner), bf16),
                pltpu.VMEM((ROWS, NARROW), bf16),
                pltpu.VMEM((ROWS, width), bf16),
                pltpu.VMEM((6, 8, inner), f32),
                pltpu.VMEM((5, 8, 2 * LANES), f32),
                pltpu.VMEM((2, 8, LANES), f32),
                pltpu.VMEM((8, inner), f32),
                pltpu.VMEM((8, width), f32),
            ],
        ),
        out_shape=out_shape,
        compiler_params=pltpu.CompilerParams(
            dimension_semantics=("arbitrary",), vmem_limit_bytes=56 * 2**20
        ),
        cost_estimate=pl.CostEstimate(
            flops=4 * rows_all * width * (2 * inner + NARROW), bytes_accessed=60 * 2**20, transcendentals=0
        ),
        name="mixer_backward",
    )(place, ends, hidden, *saved, sums, stack, narrow, gain, head_rows, conv_rows, shared_rows)


def grads_kernel(
    first_matrix, count, seq_count, clear, mask_right, place_ref, ends_ref, free_ref, left_ref, right_ref,
    *rest,
):
    out_ref, held, sems, free_sems = rest[-4:]
    chunk = pl.program_id(0)
    width = right_ref.shape[1]
    right = right_ref[...]
    if mask_right:
        valid = iota(right.shape, 0) < ends_ref[seq_count - 1]
        right = jnp.where(valid, right.astype(f32), 0.0).astype(bf16)
    held[0 : count * HEADDIM, :] = dot_tn(left_ref[...], right).astype(bf16)
    columns = pl.ds(pl.multiple_of(chunk * width, width), width)
    copies = [
        pltpu.make_async_copy(
            held.at[pl.ds(m * HEADDIM, HEADDIM), :],
            out_ref.at[place_ref[first_matrix + m], :, columns],
            sems.at[m],
        )
        for m in range(count)
    ]
    for copy in copies:
        copy.start()
    if clear:
        held[count * HEADDIM :, :] = jnp.zeros((HEADDIM, width), bf16)

        def clear_copy(s):
            return pltpu.make_async_copy(
                held.at[pl.ds(count * HEADDIM, HEADDIM), :], out_ref.at[s, :, columns], free_sems.at[s]
            )

        for s in range(out_ref.shape[0]):

            @pl.when(free_ref[s] > 0)
            def _(s=s):
                clear_copy(s).start()

        for s in range(out_ref.shape[0]):

            @pl.when(free_ref[s] > 0)
            def _(s=s):
                clear_copy(s).wait()

    for copy in copies:
        copy.wait()


def grads_call(place, ends, free, left, right, first_matrix, mask_right, into):
    rows_all, width = right.shape
    slots = free.shape[0]
    count = left.shape[1] // HEADDIM
    clear = into is None
    held = pl.BlockSpec(memory_space=pl.ANY)
    return pl.pallas_call(
        functools.partial(grads_kernel, first_matrix, count, ends.shape[0] - 1, clear, mask_right),
        grid_spec=pltpu.PrefetchScalarGridSpec(
            num_scalar_prefetch=3,
            grid=(width // CHUNK,),
            in_specs=[
                pl.BlockSpec(left.shape, lambda i, *_: (0, 0), pipeline_mode=pl.Buffered(1)),
                pl.BlockSpec((rows_all, CHUNK), lambda i, *_: (0, i)),
            ]
            + ([] if clear else [held]),
            out_specs=held,
            scratch_shapes=[
                pltpu.VMEM(((count + 1) * HEADDIM, CHUNK), bf16),
                pltpu.SemaphoreType.DMA((count,)),
                pltpu.SemaphoreType.DMA((slots,)),
            ],
        ),
        out_shape=jax.ShapeDtypeStruct((slots, HEADDIM, width), bf16),
        input_output_aliases={} if clear else {5: 0},
        compiler_params=pltpu.CompilerParams(
            dimension_semantics=("arbitrary",), vmem_limit_bytes=56 * 2**20
        ),
        cost_estimate=pl.CostEstimate(
            flops=2 * rows_all * width * left.shape[1], bytes_accessed=30 * 2**20, transcendentals=0
        ),
        name="weight_grads",
    )(place, ends, free, left, right, *([] if clear else [into]))


def exchange_kernel(sums_ref, mine_ref, other_ref, total_ref, near_ref, sums_in, part_in, sum_sems, part_sems):
    here = lax.axis_index("dp")
    tensor = lax.axis_index("tensor")
    peers = [(here, (tensor + k) % 4) for k in range(1, 4)]
    other_core = (here, tensor + 1 - 2 * (tensor % 2))
    rows = mine_ref.shape[0]
    greet([(peer, None) for peer in peers])
    parts = [pl.ds(k * ROWS, ROWS) for k in range(rows // ROWS)]

    def part_copy(k):
        return remote(
            other_ref.at[parts[k]], part_in.at[parts[k]], part_sems.at[0, k], part_sems.at[1, k], other_core
        )

    def sum_copy(k):
        return remote(
            sums_ref.at[0:2], sums_in.at[tensor], sum_sems.at[0, k], sum_sems.at[1, k], peers[k]
        )

    for k in range(3):
        sum_copy(k).start()
    for k in range(len(parts)):
        part_copy(k).start()
    for k in range(3):
        sum_copy(k).wait()
    total = jnp.zeros((2, sums_ref.shape[1]), f32)
    for t in range(4):
        total = total + jnp.where(tensor == t, sums_ref[0:2, :], sums_in[t])
    total_ref[0:2, :] = total
    total_ref[2:8, :] = jnp.zeros((6, sums_ref.shape[1]), f32)
    for k in range(len(parts)):
        part_copy(k).wait()
        here_rows = parts[k]
        near_ref[here_rows, :] = (
            mine_ref[here_rows, :].astype(f32) + part_in[here_rows, :].astype(f32)
        ).astype(bf16)


def exchange_call(sums, mine, other):
    rows, width = mine.shape
    spec = pl.BlockSpec(memory_space=pltpu.VMEM)
    sems = pltpu.SemaphoreType.DMA
    return pl.pallas_call(
        exchange_kernel,
        in_specs=[spec, spec, pl.BlockSpec(memory_space=pl.ANY)],
        out_specs=[spec] * 2,
        out_shape=[jax.ShapeDtypeStruct(sums.shape, f32), jax.ShapeDtypeStruct(mine.shape, bf16)],
        scratch_shapes=[
            pltpu.VMEM((4, 2, sums.shape[1]), f32), pltpu.VMEM((rows, width), bf16),
            sems((2, 3)), sems((2, rows // ROWS)),
        ],
        compiler_params=pltpu.CompilerParams(
            collective_id=2, has_side_effects=True, vmem_limit_bytes=40 * 2**20
        ),
        name="exchange_sums",
    )(sums, mine, other)


def branch_kernel(inner_all, seq_count, ends_ref, near_ref, far_ref, hidden_ref, sums_ref, full_ref, half_ref):
    width = hidden_ref.shape[1]
    blocks = pl.num_programs(0)
    first_row = (ends_ref[seq_count] * blocks + pl.program_id(0)) * ROWS
    for sub in range(ROWS // SUB):
        here = slice(sub * SUB, (sub + 1) * SUB)
        inv_row = lax.rsqrt(sums_ref[0:1, here] * (1.0 / inner_all) + norm_eps)
        inv = jnp.broadcast_to(inv_row, (SUB, SUB)).T
        row_at = first_row + sub * SUB + iota((SUB, LANES), 0)
        valid = jnp.where(row_at < ends_ref[seq_count - 1], 1.0, 0.0).astype(f32)
        for group in range(width // LANES):
            lanes = lanes_of(group)
            branch = (near_ref[here, lanes].astype(f32) + far_ref[here, lanes].astype(f32)) * inv
            result = ((hidden_ref[here, lanes].astype(f32) + branch) * valid).astype(bf16)
            full_ref[here, lanes] = result
            half_ref[here, lanes] = result


def input_kernel(seq_count, ends_ref, near_ref, far_ref, hidden_ref, cot_ref, gain_ref, full_ref, half_ref):
    width = hidden_ref.shape[1]
    blocks = pl.num_programs(0)
    first_row = (ends_ref[seq_count] * blocks + pl.program_id(0)) * ROWS
    hidden = hidden_ref[...].astype(f32)
    inv_rms = lax.rsqrt(jnp.mean(hidden * hidden, axis=1, keepdims=True) + norm_eps)
    gain_part = (near_ref[...].astype(f32) + far_ref[...].astype(f32)) * gain_ref[0:1, :]
    fix = inv_rms * inv_rms * inv_rms * (jnp.sum(gain_part * hidden, axis=1, keepdims=True) / width)
    row_at = first_row + iota(hidden.shape, 0)
    cot = jnp.where(row_at < ends_ref[seq_count - 1], cot_ref[...].astype(f32), 0.0)
    result = (inv_rms * gain_part - hidden * fix + cot).astype(bf16)
    full_ref[...] = result
    half_ref[...] = result


def half_call(kernel, name, ends, halves, fulls, wholes):
    rows, width = halves[0].shape
    seq_count = ends.shape[0] - 1
    blocks = rows // ROWS

    def in_full(i, ends):
        return (ends[seq_count] * blocks + i, 0)

    own = pl.BlockSpec((ROWS, width), lambda i, ends: (i, 0))
    full = pl.BlockSpec((ROWS, width), in_full)
    return pl.pallas_call(
        kernel,
        grid_spec=pltpu.PrefetchScalarGridSpec(
            num_scalar_prefetch=1,
            grid=(blocks,),
            in_specs=[own] * len(halves) + [full] * len(fulls) + wholes[1],
            out_specs=[full, own],
        ),
        out_shape=[
            jax.ShapeDtypeStruct((2 * rows, width), bf16),
            jax.ShapeDtypeStruct((rows, width), bf16),
        ],
        compiler_params=pltpu.CompilerParams(
            dimension_semantics=("arbitrary",), vmem_limit_bytes=40 * 2**20
        ),
        cost_estimate=pl.CostEstimate(flops=0, bytes_accessed=16 * 2**20, transcendentals=0),
        name=name,
    )(ends, *halves, *fulls, *wholes[0])


def remote(src, dst, send_sem, recv_sem, target):
    return pltpu.make_async_remote_copy(
        src_ref=src,
        dst_ref=dst,
        send_sem=send_sem,
        recv_sem=recv_sem,
        device_id=target,
        device_id_type=pl.DeviceIdType.MESH,
    )


def greet(targets):
    barrier = pltpu.get_barrier_semaphore()
    for target, condition in targets:
        if condition is None:
            pl.semaphore_signal(barrier, inc=1, device_id=target, device_id_type=pl.DeviceIdType.MESH)
        else:

            @pl.when(condition)
            def _(target=target):
                pl.semaphore_signal(
                    barrier, inc=1, device_id=target, device_id_type=pl.DeviceIdType.MESH
                )

    peers = sum(1 if condition is None else condition.astype(jnp.int32) for _, condition in targets)
    pl.semaphore_wait(barrier, peers)


def gather_kernel(
    lines, own_ref, out_ref, local_sem, x_send, x_recv, up_send, up_recv, down_send, down_recv
):
    here = lax.axis_index("dp")
    tensor = lax.axis_index("tensor")
    line, side = here // 2, here % 2
    partner = here + 1 - 2 * side
    slots = own_ref.shape[0]
    most = slots - 1
    has_up, has_down = line < lines - 1, line > 0
    across, above, below = (partner, tensor), (here + 2, tensor), (here - 2, tensor)

    greet([(across, None), (above, has_up), (below, has_down)])
    local = pltpu.make_async_copy(own_ref, out_ref.at[pl.ds(here * slots, slots)], local_sem)
    local.start()
    order = [most] + list(range(min(2, most))) + [slots] + list(range(min(2, most), most))

    def place(at, part):
        device = 2 * at + 1 - side if part == slots else 2 * at + side
        return device * slots + min(part, most)

    def line_copy(step, at, part, upward):
        own = step == 0 and part < slots
        to = out_ref.at[place(at, part)]
        src = own_ref.at[part] if own else to
        if upward:
            return remote(src, to, up_send.at[step, part], up_recv.at[step, part], above)
        return remote(src, to, down_send.at[step, part], down_recv.at[step, part], below)

    def x_copy(device, index, part, own=False):
        to = out_ref.at[device * slots + part]
        return remote(
            own_ref.at[part] if own else to, to, x_send.at[index, part], x_recv.at[index, part], across
        )

    x_copy(here, 0, most, True).start()
    for part in order:
        if part == slots:
            x_copy(partner, 0, most).wait_recv()

        @pl.when(has_up)
        def _(part=part):
            line_copy(0, line, part, True).start()

        @pl.when(has_down)
        def _(part=part):
            line_copy(0, line, part, False).start()

        if part < most:
            x_copy(here, 0, part, True).start()

    for k in range(1, lines):
        for part in order:

            @pl.when(line >= k)
            def _(k=k, part=part):
                line_copy(k - 1, line - k, part, True).wait_recv()
                if k < lines - 1:

                    @pl.when(has_up)
                    def _():
                        line_copy(k, line - k, part, True).start()

                if part < most:
                    x_copy(2 * (line - k) + side, k, part).start()

            @pl.when(line + k < lines)
            def _(k=k, part=part):
                line_copy(k - 1, line + k, part, False).wait_recv()
                if k < lines - 1:

                    @pl.when(has_down)
                    def _():
                        line_copy(k, line + k, part, False).start()

                if part < most:
                    x_copy(2 * (line + k) + side, lines - 1 + k, part).start()

    local.wait()
    x_copy(partner, 0, most).wait_send()
    for part in range(most):
        x_copy(partner, 0, part).wait()
    for k in range(1, lines):
        for part in range(most):

            @pl.when(line >= k)
            def _(k=k, part=part):
                x_copy(2 * (line - k) + 1 - side, k, part).wait()

            @pl.when(line + k < lines)
            def _(k=k, part=part):
                x_copy(2 * (line + k) + 1 - side, lines - 1 + k, part).wait()

    for k in range(lines - 1):
        for part in order:

            @pl.when(has_up & (line >= k))
            def _(k=k, part=part):
                line_copy(k, line - k, part, True).wait_send()

            @pl.when(has_down & (line + k < lines))
            def _(k=k, part=part):
                line_copy(k, line + k, part, False).wait_send()


def gather_call(own, dp_size):
    slots, side, width = own.shape
    lines = dp_size // 2
    step_sems = pltpu.SemaphoreType.DMA((lines - 1, slots + 1))
    x_sems = pltpu.SemaphoreType.DMA((2 * lines - 1, slots))
    return pl.pallas_call(
        functools.partial(gather_kernel, lines),
        in_specs=[pl.BlockSpec(memory_space=pl.ANY)],
        out_specs=pl.BlockSpec(memory_space=pl.ANY),
        out_shape=jax.ShapeDtypeStruct((slots * dp_size, side, width), own.dtype),
        scratch_shapes=[
            pltpu.SemaphoreType.DMA, x_sems, x_sems, step_sems, step_sems, step_sems, step_sems,
        ],
        compiler_params=pltpu.CompilerParams(collective_id=0, has_side_effects=True),
        name="gather_weights",
    )(own)


def reduce_kernel(
    lines,
    grads, near_ref, far_ref, extra_ref, owned_ref, totals_ref,
    x_in, up_in, down_in, last_out, last_in, halves, half_in, group_in, group_out, group_back,
    x_send, x_recv, up_send, up_recv, down_send, down_recv, last_sems, small_sems, group_sems, back_sems,
):
    here = lax.axis_index("dp")
    tensor = lax.axis_index("tensor")
    line, side = here // 2, here % 2
    core = tensor % 2
    slots = owned_ref.shape[0]
    most = slots - 1
    width = near_ref.shape[1]
    half = width // 2
    group = halves.shape[1] // lines
    has_up, has_down = line < lines - 1, line > 0
    across = (here + 1 - 2 * side, tensor)
    above, below = (here + 2, tensor), (here - 2, tensor)
    other_core = (here, tensor + 1 - 2 * core)
    other_chip = (here, (tensor + 2) % 4)
    on_line = [(2 * ((line + k) % lines) + side, tensor) for k in range(1, lines)]

    greet([(target, None) for target in [across, other_core, other_chip] + on_line])

    def add(*parts):
        total = parts[0].astype(f32)
        for part in parts[1:]:
            total = total + part.astype(f32)
        return total

    half_copy = remote(halves.at[1 - side], half_in, small_sems.at[0, 0], small_sems.at[1, 0], across)

    def group_copy(k):
        to = (line + k) % lines
        rows = pl.ds(pl.multiple_of(to * group, group), group)
        return remote(
            halves.at[side, rows], group_in.at[k - 1], group_sems.at[0, k - 1], group_sems.at[1, k - 1],
            on_line[k - 1],
        )

    def back_copy(k):
        return remote(
            group_out, group_back.at[k - 1], back_sems.at[0, k - 1], back_sems.at[1, k - 1], on_line[k - 1]
        )

    total_half = remote(
        totals_ref.at[tensor, side], totals_ref.at[tensor, side], small_sems.at[0, 1], small_sems.at[1, 1],
        across,
    )
    total_chip = remote(
        totals_ref.at[tensor], totals_ref.at[tensor], small_sems.at[0, 2], small_sems.at[1, 2], other_chip
    )

    def total_core(k):
        at = core + 2 * k
        return remote(
            totals_ref.at[at], totals_ref.at[at], small_sems.at[0, 3 + k], small_sems.at[1, 3 + k], other_core
        )

    def small_start():
        mine = near_ref[...] + far_ref[...]
        rest = extra_ref[...]
        for k in range(2):
            columns = slice(k * half, (k + 1) * half)
            halves[k, 0:HEADDIM, :] = mine[:, columns]
            halves[k, HEADDIM:, :] = rest[:, columns]
        half_copy.start()

    def small_group():
        half_copy.wait()
        halves[side] = halves[side] + half_in[...]
        for k in range(1, lines):
            group_copy(k).start()

    def small_back():
        for k in range(1, lines):
            group_copy(k).wait()
        rows = pl.ds(pl.multiple_of(line * group, group), group)
        total = halves[side, rows, :]
        for k in range(1, lines):
            total = total + group_in[k - 1]
        group_out[...] = total
        for k in range(1, lines):
            back_copy(k).start()

    def small_half():
        for k in range(1, lines):
            back_copy(k).wait()
        rows = pl.ds(pl.multiple_of(line * group, group), group)
        totals_ref[tensor, side, rows, :] = group_out[...]
        for k in range(1, lines):
            source = (line + lines - k) % lines
            rows = pl.ds(pl.multiple_of(source * group, group), group)
            totals_ref[tensor, side, rows, :] = group_back[k - 1]
        total_half.start()

    def small_chip():
        total_half.wait()
        total_chip.start()

    def small_core():
        total_chip.wait()
        for k in range(2):
            total_core(k).start()

    def small_end():
        for k in range(2):
            total_core(k).wait()

    small = [(1, small_group), (3, small_back), (5, small_half), (8, small_chip), (13, small_core)]
    events = []

    def event():
        events.append(None)
        while small and small[0][0] <= len(events):
            small.pop(0)[1]()

    def x_copy(at, i):
        return remote(
            grads.at[(2 * at + 1 - side) * slots + i], x_in.at[at, i], x_send.at[at, i], x_recv.at[at, i], across
        )

    def x_needed(turn):
        step, i = turn // most, turn % most
        if step < lines - 1:
            each_way(step, lambda at, upward: x_copy(at, i).start())
        elif step == lines - 1:
            x_copy(line, i).start()

    def line_copy(src, at, i, upward):
        if upward:
            return remote(src, up_in.at[at, i], up_send.at[at, i], up_recv.at[at, i], above)
        return remote(src, down_in.at[at, i], down_send.at[at, i], down_recv.at[at, i], below)

    def line_most(at, i, upward):
        arrived = up_in if upward else down_in
        x_copy(at, i).wait_recv()
        own = add(grads[(2 * at + side) * slots + i], x_in[at, i])

        @pl.when(has_down if upward else has_up)
        def _():
            line_copy(x_in.at[at, i], at, i, upward).wait_recv()
            x_in[at, i] = add(own, arrived[at, i]).astype(bf16)

        @pl.when(jnp.logical_not(has_down if upward else has_up))
        def _():
            x_in[at, i] = own.astype(bf16)

        line_copy(x_in.at[at, i], at, i, upward).start()

    def line_last(at, k, upward):
        arrived = up_in if upward else down_in
        own = grads.at[(2 * at + k) * slots + most]

        @pl.when(has_down if upward else has_up)
        def _():
            line_copy(own, at, most + k, upward).wait_recv()
            arrived[at, most + k] = add(own[...], arrived[at, most + k]).astype(bf16)
            line_copy(arrived.at[at, most + k], at, most + k, upward).start()

        @pl.when(jnp.logical_not(has_down if upward else has_up))
        def _():
            line_copy(own, at, most + k, upward).start()

    def each_way(step, work):
        @pl.when(lines - 1 - step > line)
        def _():
            work(lines - 1 - step, True)

        @pl.when(step < line)
        def _():
            work(step, False)

    small_start()
    x_needed(0)
    x_needed(1)
    for step in range(lines - 1):
        for k in range(2):
            each_way(step, lambda at, upward, k=k: line_last(at, k, upward))
        event()
        for i in range(most):
            x_needed(step * most + i + 2)
            each_way(step, lambda at, upward, i=i: line_most(at, i, upward))
            event()

    def gathered_last(k):
        return grads[(2 * line + k) * slots + most].astype(f32)

    owned_ref[most] = gathered_last(side)
    to_send = gathered_last(1 - side)
    last_out[...] = to_send

    @pl.when(has_down)
    def _():
        for k in range(2):
            line_copy(last_in, line, most + k, True).wait_recv()
        owned_ref[most] = owned_ref[most] + up_in[line, most + side].astype(f32)
        last_out[...] = last_out[...] + up_in[line, most + 1 - side].astype(f32)

    @pl.when(has_up)
    def _():
        for k in range(2):
            line_copy(last_in, line, most + k, False).wait_recv()
        owned_ref[most] = owned_ref[most] + down_in[line, most + side].astype(f32)
        last_out[...] = last_out[...] + down_in[line, most + 1 - side].astype(f32)

    x_in[line, most] = last_out[...].astype(bf16)
    last_copy = remote(x_in.at[line, most], last_in, last_sems.at[0], last_sems.at[1], across)
    last_copy.start()
    for turn in range((lines - 1) * most + 2, lines * most):
        x_needed(turn)
    while small:
        small.pop(0)[1]()

    def finish(i, carry):
        x_copy(line, i).wait_recv()
        owned_ref[i] = add(grads[(2 * line + side) * slots + i], x_in[line, i])

        @pl.when(has_down)
        def _():
            line_copy(last_in, line, i, True).wait_recv()
            owned_ref[i] = owned_ref[i] + up_in[line, i].astype(f32)

        @pl.when(has_up)
        def _():
            line_copy(last_in, line, i, False).wait_recv()
            owned_ref[i] = owned_ref[i] + down_in[line, i].astype(f32)

        return carry

    lax.fori_loop(0, most, finish, 0)
    last_copy.wait()
    owned_ref[most] = owned_ref[most] + last_in[...].astype(f32)
    small_end()

    def x_sent(at):
        def one(i, carry):
            x_copy(at, i).wait_send()
            return carry

        lax.fori_loop(0, most, one, 0)

    def line_sent(at, upward):
        def one(i, carry):
            line_copy(last_in, at, i, upward).wait_send()
            return carry

        lax.fori_loop(0, slots + 1, one, 0)

    x_sent(line)
    for step in range(lines - 1):
        each_way(step, lambda at, upward: x_sent(at))
        each_way(step, line_sent)


def reduce_call(grads, near, far, extra, dp_size):
    slots_all, side, width = grads.shape
    slots = slots_all // dp_size
    lines = dp_size // 2
    small_rows = HEADDIM + extra.shape[0]
    group = small_rows // lines
    spec = pl.BlockSpec(memory_space=pltpu.VMEM)
    sems = pltpu.SemaphoreType.DMA
    return pl.pallas_call(
        functools.partial(reduce_kernel, lines),
        in_specs=[spec] * 4,
        out_specs=[spec] * 2,
        out_shape=[
            jax.ShapeDtypeStruct((slots, side, width), f32),
            jax.ShapeDtypeStruct((4, 2, small_rows, width // 2), f32),
        ],
        scratch_shapes=[
            pltpu.VMEM((lines, slots, side, width), bf16),
            pltpu.VMEM((lines, slots + 1, side, width), bf16),
            pltpu.VMEM((lines, slots + 1, side, width), bf16),
            pltpu.VMEM((side, width), f32),
            pltpu.VMEM((side, width), bf16),
            pltpu.VMEM((2, small_rows, width // 2), f32),
            pltpu.VMEM((small_rows, width // 2), f32),
            pltpu.VMEM((lines - 1, group, width // 2), f32),
            pltpu.VMEM((group, width // 2), f32),
            pltpu.VMEM((lines - 1, group, width // 2), f32),
            sems((lines, slots)), sems((lines, slots)),
            sems((lines, slots + 1)), sems((lines, slots + 1)),
            sems((lines, slots + 1)), sems((lines, slots + 1)),
            sems((2,)), sems((2, 5)), sems((2, lines - 1)), sems((2, lines - 1)),
        ],
        compiler_params=pltpu.CompilerParams(
            collective_id=1, has_side_effects=True, vmem_limit_bytes=56 * 2**20
        ),
        cost_estimate=pl.CostEstimate(flops=10**11, bytes_accessed=40 * 2**20, transcendentals=0),
        name="reduce_grads",
    )(grads, near, far, extra)


def small_rule(rate, weight, moment, gradient):
    moment_new = small_decay * moment + (1.0 - small_decay) * gradient
    return moment_new, weight - rate * moment_new


def muon_kernel(
    rate, small_rate_now,
    grad_ref, totals_ref, moment_ref, master_ref,
    state_moment, state_proj, step_moment, step_proj, gain_moment, gain, head_moment, head, conv_moment, conv,
    shared_moment, shared,
    moment_out, master_out,
    state_moment_out, state_out, step_moment_out, step_out, gain_moment_out, gain_out, head_moment_out,
    head_out, conv_moment_out, conv_out, shared_moment_out, shared_out,
):
    tensor = lax.axis_index("tensor")
    rule = functools.partial(small_rule, small_rate_now)

    def row(at, row_at):
        return jnp.concatenate(
            [totals_ref[at, k, row_at : row_at + 1, :] for k in range(2)], axis=1
        )

    def over_tensor(row_at):
        return row(0, row_at) + row(1, row_at) + row(2, row_at) + row(3, row_at)

    for k in range(2):
        parts = [
            jnp.concatenate([totals_ref[2 * k + j, c, 0:HEADDIM, :] for c in range(2)], axis=1)
            for j in range(2)
        ]
        lanes = lanes_of(k)
        state_moment_out[:, lanes], state_out[:, lanes] = rule(
            state_proj[:, lanes], state_moment[:, lanes], jnp.concatenate(parts, axis=0).T
        )
    heads = step_proj.shape[0]
    extra = HEADDIM
    own = [totals_ref[tensor, k, extra : extra + 32, :] for k in range(2)]
    step_moment_out[...], step_out[...] = rule(
        step_proj[...], step_moment[...], jnp.concatenate(own, axis=1)[0:heads]
    )
    gain_moment_out[...], gain_out[...] = rule(gain[...], gain_moment[...], over_tensor(extra + GAIN_ROW))
    head_moment_out[...], head_out[...] = rule(
        head[...], head_moment[...], own[0][HEAD_ROW : HEAD_ROW + 3, 0:heads]
    )
    inner = conv.shape[1]
    per_line = 2 * own[0].shape[1] // inner
    conv_total = jnp.concatenate(own, axis=1)
    for k in range(6):
        at = (k % per_line) * inner
        line = 16 + k // per_line
        one = slice(k, k + 1)
        conv_moment_out[one, :], conv_out[one, :] = rule(
            conv[one, :], conv_moment[one, :], conv_total[line : line + 1, at : at + inner]
        )
    shared_total = over_tensor(extra + SHARED_ROW)
    for k in range(5):
        one = slice(k, k + 1)
        shared_moment_out[one, :], shared_out[one, :] = rule(
            shared[one, :], shared_moment[one, :], shared_total[:, 2 * LANES * k : 2 * LANES * (k + 1)]
        )

    first_coef, second_coef, third_coef = schulz_coefs
    side = HEADDIM
    same = iota((side, side), 0) == iota((side, side), 1)
    eye = jnp.where(same, 1.0, 0.0).astype(f32)
    slots = grad_ref.shape[0]
    grams, totals, scales = [], [], []
    for s in range(slots):
        moment = muon_decay * moment_ref[s] + grad_ref[s].astype(f32)
        moment_out[s] = moment
        square = jnp.sum(jnp.sum(moment * moment, axis=1, keepdims=True), axis=0, keepdims=True)
        scale = 1.0 / (jnp.sqrt(square) + 1e-07)
        scaled = moment * scale
        grams.append(dot_nt(scaled, scaled, exact_mode))
        totals.append(eye)
        scales.append(scale)
    for _ in range(NS_STEPS):
        for s in range(slots):
            gram = grams[s]
            factor = (
                first_coef * eye + second_coef * gram + third_coef * dot_nn(gram, gram, exact_mode)
            )
            totals[s] = dot_nn(factor, totals[s], exact_mode)
            grams[s] = dot_nn(dot_nn(factor, gram, exact_mode), factor, exact_mode)
    for s in range(slots):
        ortho = dot_nn(totals[s], moment_out[s] * scales[s], exact_mode)
        master_out[s] = master_ref[s] - rate * ortho


def muon_call(grad, totals, moment, master, small, tokens_all):
    slots, side, width = moment.shape
    spec = pl.BlockSpec(memory_space=pltpu.VMEM)
    return pl.pallas_call(
        functools.partial(
            muon_kernel, muon_rate * math.sqrt(max(width, side)), small_rate / math.sqrt(tokens_all)
        ),
        in_specs=[spec] * (4 + len(small)),
        out_specs=[spec] * (2 + len(small)),
        out_shape=[jax.ShapeDtypeStruct(moment.shape, f32)] * 2
        + [jax.ShapeDtypeStruct(array.shape, f32) for array in small],
        compiler_params=pltpu.CompilerParams(vmem_limit_bytes=56 * 2**20),
        name="muon",
    )(grad, totals, moment, master, *small)


def pad_to(array, rows, columns):
    return jnp.pad(array, ((0, rows - array.shape[0]), (0, columns - array.shape[1])))


def swap(values, bit):
    return lax.ppermute(values, "tensor", [(t, t ^ bit) for t in range(4)])


def place_half(full, half):
    core = lax.axis_index("tensor") % 2
    return lax.dynamic_update_slice(full, swap(half, 1), ((1 - core) * half.shape[0], 0))


def per_device(
    hidden_in,
    out_grad,
    seq_lengths,
    owner_map,
    muon_master,
    muon_moment,
    state_proj,
    state_moment,
    step_proj,
    step_moment,
    norm_gain,
    gain_moment,
    head_params,
    head_moment,
    conv_params,
    conv_moment,
    state_conv,
    state_conv_moment,
):
    tok_rows, width = hidden_in.shape
    heads = step_proj.shape[1]
    inner = conv_params.shape[1]
    dp_size = lax.axis_size("dp")
    inner_all = inner * lax.axis_size("tensor")
    slots = muon_master.shape[0] * dp_size
    core = lax.axis_index("tensor") % 2
    chip = lax.axis_index("tensor") // 2
    ends = jnp.concatenate([jnp.cumsum(seq_lengths[0], dtype=jnp.int32), core[None].astype(jnp.int32)])
    seq_count = seq_lengths.shape[1]
    master = muon_master.transpose(0, 2, 1)
    moment = muon_moment.transpose(0, 2, 1)
    stack = gather_call(master.astype(bf16), dp_size)
    narrow = pad_to(jnp.concatenate([state_proj, step_proj], axis=1), width, NARROW).astype(bf16)
    gain = norm_gain[None, :]
    head_rows = pad_to(head_params, 8, LANES)
    conv_rows = pad_to(conv_params, 8, inner)
    shared_rows = pad_to(state_conv, 8, state_conv.shape[1])
    free = jnp.all(owner_map[None, :] != jnp.arange(slots, dtype=jnp.int32)[:, None], axis=1)
    free = free.astype(jnp.int32)
    group_rows = 8 * (dp_size // 2)
    extra_rows = -(-(HEADDIM + 32) // group_rows) * group_rows - HEADDIM

    normed, *saved, sums, mine, other = forward_call(
        owner_map, ends, hidden_in, out_grad, stack, gain, narrow, head_rows, conv_rows, shared_rows, heads
    )
    sums, near = exchange_call(sums, mine, other)
    far = swap(near, 2)
    dboth, scaled, mine, other, narrow_grad, extra = backward_call(
        owner_map, ends, hidden_in, saved, sums, stack, narrow, gain, head_rows, conv_rows, shared_rows, heads,
        inner_all, extra_rows,
    )

    quarters = narrow_grad[: 4 * HEADDIM].reshape(2, 2, HEADDIM, width)
    got = swap(other, 1)
    got_narrow = swap(lax.dynamic_index_in_dim(quarters, 1 - core, 1, keepdims=False), 1)
    mine_narrow = lax.dynamic_index_in_dim(quarters, core, 1, keepdims=False)
    far, scaled = lax.optimization_barrier((far, scaled))
    rows_spec = pl.BlockSpec((8, ROWS), lambda i, ends: (0, ends[seq_count] * (tok_rows // ROWS // 2) + i))
    block_full, block_half = half_call(
        functools.partial(branch_kernel, inner_all, seq_count), "block_out", ends, [near, far], [hidden_in],
        ([sums], [rows_spec]),
    )
    block_out = place_half(block_full, block_half)
    scaled, block_half = lax.optimization_barrier((scaled, block_half))
    slotted = grads_call(owner_map, ends, free, scaled, out_grad, 2 * heads, True, None)
    slotted, got, got_narrow = lax.optimization_barrier((slotted, got, got_narrow))
    pair = mine_narrow + got_narrow
    near_narrow = lax.dynamic_index_in_dim(pair, chip, 0, keepdims=False)
    send_narrow = lax.dynamic_index_in_dim(pair, 1 - chip, 0, keepdims=False)
    far_narrow = swap(send_narrow, 2)
    send_narrow, got = lax.optimization_barrier((send_narrow, got))
    near_grad = (mine.astype(f32) + got.astype(f32)).astype(bf16)
    far_grad = swap(near_grad, 2)
    near_grad, near_narrow, dboth = lax.optimization_barrier((near_grad, near_narrow, dboth))
    slotted = grads_call(owner_map, ends, free, dboth, normed, 0, False, slotted)
    owned, totals = reduce_call(slotted, near_narrow, far_narrow, extra, dp_size)
    owned, totals, far_grad = lax.optimization_barrier((owned, totals, far_grad))
    gain_spec = pl.BlockSpec(gain.shape, lambda i, ends: (0, 0))
    input_full, input_half = half_call(
        functools.partial(input_kernel, seq_count), "input_grad", ends, [near_grad, far_grad],
        [hidden_in, out_grad], ([gain], [gain_spec]),
    )
    input_grad = place_half(input_full, input_half)
    owned, input_half = lax.optimization_barrier((owned, input_half))
    small = [
        state_moment, state_proj, step_moment.T, step_proj.T, gain_moment[None, :], gain, head_moment,
        head_params, conv_moment, conv_params, state_conv_moment, state_conv,
    ]
    moment_new, master_new, *small_new = muon_call(owned, totals, moment, master, small, tok_rows * dp_size)
    state_moment_new, state_proj_new, step_moment_new, step_proj_new = small_new[:4]
    gain_moment_new, norm_gain_new, head_moment_new, head_params_new = small_new[4:8]
    conv_moment_new, conv_params_new, state_conv_moment_new, state_conv_new = small_new[8:]
    step_moment_new, step_proj_new = step_moment_new.T, step_proj_new.T
    gain_moment_new, norm_gain_new = gain_moment_new[0], norm_gain_new[0]
    return (
        block_out,
        input_grad,
        moment_new.transpose(0, 2, 1),
        master_new.transpose(0, 2, 1),
        state_moment_new,
        state_proj_new,
        step_moment_new,
        step_proj_new,
        gain_moment_new,
        norm_gain_new,
        head_moment_new,
        head_params_new,
        conv_moment_new,
        conv_params_new,
        state_conv_moment_new,
        state_conv_new,
    )


def solution(mesh):
    in_specs = (
        P("dp", None),
        P("dp", None),
        P("dp", None),
        P(),
        P("dp", None, "tensor"),
        P("dp", None, "tensor"),
        P(),
        P(),
        P(None, "tensor"),
        P(None, "tensor"),
        P(),
        P(),
        P(None, "tensor"),
        P(None, "tensor"),
        P(None, "tensor"),
        P(None, "tensor"),
        P(),
        P(),
    )
    out_specs = (
        P("dp", None),
        P("dp", None),
        P("dp", None, "tensor"),
        P("dp", None, "tensor"),
        P(),
        P(),
        P(None, "tensor"),
        P(None, "tensor"),
        P(),
        P(),
        P(None, "tensor"),
        P(None, "tensor"),
        P(None, "tensor"),
        P(None, "tensor"),
        P(),
        P(),
    )
    return jax.shard_map(
        per_device, mesh=mesh, in_specs=in_specs, out_specs=out_specs, check_vma=False
    )
```

```python
import functools
import math

import jax
import jax.numpy as jnp
from jax import lax
from jax.experimental import pallas as pl
from jax.experimental.pallas import tpu as pltpu
from jax.sharding import PartitionSpec as P

HEADDIM = 64
NS_STEPS = 5
ROWS = 256
SUB = 128
LANES = 128
NARROW = 384
CHUNK = 768
GAIN_ROW, SHARED_ROW, HEAD_ROW = 19, 20, 21
AHEAD = 5

exact_mode = lax.Precision.HIGHEST
norm_eps = 1e-05
schulz_coefs = (3.4445, -4.775, 2.0315)
muon_decay = 0.95
muon_rate = 0.02
small_decay = 0.9
small_rate = 2.0
log2_e = 1.4426950408889634
f32 = jnp.float32
bf16 = jnp.bfloat16
far_below = -1e30


def dot_nn(left, right, precision=None):
    return lax.dot_general(
        left, right, (((1,), (0,)), ((), ())), precision=precision, preferred_element_type=f32
    )


def dot_nt(left, right, precision=None):
    return lax.dot_general(
        left, right, (((1,), (1,)), ((), ())), precision=precision, preferred_element_type=f32
    )


def dot_tn(left, right, precision=None):
    return lax.dot_general(
        left, right, (((0,), (0,)), ((), ())), precision=precision, preferred_element_type=f32
    )


def sigmoid(values):
    return 0.5 * jnp.tanh(0.5 * values) + 0.5


def iota(shape, dim):
    return lax.broadcasted_iota(jnp.int32, shape, dim)


def segment_at(place, ends_ref, count):
    total = (place >= ends_ref[0]).astype(jnp.int32)
    for k in range(1, count):
        total = total + (place >= ends_ref[k]).astype(jnp.int32)
    return total


def step_terms(step_part, head_ref):
    shifted = step_part + head_ref[0:1, :]
    small = jnp.exp(-jnp.abs(shifted))
    tail = jnp.where(
        small < 0.01, small * (1.0 - small * (0.5 - small * (1.0 / 3.0))), jnp.log(1.0 + small)
    )
    step = jnp.maximum(shifted, 0.0) + tail
    decay = -jnp.exp(head_ref[1:2, :])
    log_rate = step * (decay * log2_e)
    lower = (iota((SUB, SUB), 0) >= iota((SUB, SUB), 1)).astype(f32)
    cum = dot_nn(lower, log_rate, exact_mode)
    source = cum - jnp.log(step) * log2_e
    return shifted, step, decay, cum, source


def expand(values, pair):
    shape = (values.shape[0], LANES)
    low = jnp.broadcast_to(values[:, 2 * pair : 2 * pair + 1], shape)
    high = jnp.broadcast_to(values[:, 2 * pair + 1 : 2 * pair + 2], shape)
    return jnp.where(iota(shape, 1) < HEADDIM, low, high)


def split_pair(values):
    low = iota(values.shape, 1) < HEADDIM
    zero = jnp.zeros_like(values)
    return jnp.where(low, values, zero), jnp.where(low, zero, values)


def lanes_of(pair):
    return slice(pair * LANES, (pair + 1) * LANES)


def shift_mask(place, shift, ends_ref, count, rows_all):
    other = place + shift
    inside = (other >= 0) & (other < rows_all)
    same = segment_at(place, ends_ref, count) == segment_at(other, ends_ref, count)
    return jnp.where(inside & same, 1.0, 0.0).astype(f32)


def conv_tile(buf_ref, first, lanes, taps, masks):
    total = taps[4:5, :] + taps[3:4, :] * buf_ref[first + 8 : first + 8 + SUB, lanes]
    for back in (1, 2, 3):
        rows = buf_ref[first + 8 - back : first + 8 - back + SUB, lanes]
        total = total + taps[3 - back : 4 - back, :] * (rows * masks[back - 1])
    return total


def block_terms(base, ends_ref, count):
    row_at = base + iota((SUB, SUB), 0)
    col_at = base + iota((SUB, SUB), 1)
    seg_row = segment_at(row_at, ends_ref, count)
    seg_col = segment_at(col_at, ends_ref, count)
    seg_last = segment_at(base + SUB - 1, ends_ref, count)
    seg_before = jnp.where(base == 0, -1, segment_at(base - 1, ends_ref, count))
    carried = jnp.where(seg_row == seg_before, 1.0, 0.0).astype(f32)
    tail_same = jnp.where(seg_row == seg_last, 1.0, 0.0).astype(f32)
    through = jnp.where(seg_last == seg_before, 1.0, 0.0).astype(f32)
    same = seg_row == seg_col
    return row_at, col_at, same, carried, tail_same, through


def store_half(values, block, blocks, core, mine_ref, other_ref):
    is_mine = block // (blocks // 2) == core

    @pl.when(is_mine)
    def _():
        mine_ref[...] = values

    @pl.when(jnp.logical_not(is_mine))
    def _():
        other_ref[...] = values


def half_specs(width, blocks, seq_count, block_of):
    def index(half, block):
        return jnp.where(half == 0, jnp.minimum(block, blocks // 2 - 1), jnp.maximum(block - blocks // 2, 0))

    def mine(i, place, ends):
        return (index(ends[seq_count], block_of(i)), 0)

    def other(i, place, ends):
        return (index(1 - ends[seq_count], block_of(i)), 0)

    return [pl.BlockSpec((ROWS, width), mine), pl.BlockSpec((ROWS, width), other)]


def load_weights(stack_ref, place_ref, held_ref, sems, first, count):
    copies = []
    for m in range(count):
        copies.append(
            pltpu.make_async_copy(
                stack_ref.at[place_ref[first + m]],
                held_ref.at[pl.ds(m * HEADDIM, HEADDIM)],
                sems.at[m],
            )
        )
    for copy in copies:
        copy.start()
    return copies


def fold_rows(values):
    return jnp.sum(values.reshape(values.shape[0] // 8, 8, values.shape[1]), axis=0)


def saved_views(low_ref, high_ref, inner):
    wide = [low_ref.at[:, k * inner : (k + 1) * inner] for k in range(5)]
    shared = [
        low_ref.at[:, 5 * inner + 2 * LANES * k : 5 * inner + 2 * LANES * (k + 1)] for k in range(3)
    ]
    return (*wide, *shared, high_ref.at[:, 0:inner], high_ref.at[:, inner : inner + LANES])


def project_units(normed_ref, cot_ref, narrow_ref, weights, targets, row_at, last_end, inner):
    next_gate, next_in, next_scaled, next_narrow = targets
    units = []

    def one(target, at, weight_row, left_ref, masked):
        def unit():
            part = dot_nt(left_ref[...], weights[weight_row + at : weight_row + at + 2 * LANES, :])
            if masked:
                part = jnp.where(row_at < last_end, part, 0.0)
            target[:, at : at + 2 * LANES] = part.astype(bf16)

        return unit

    for at in range(0, inner, 2 * LANES):
        units.append(one(next_in, at, inner, normed_ref, False))
    units.append(lambda: next_narrow.__setitem__(Ellipsis, dot_nn(normed_ref[...], narrow_ref[...])))
    for at in range(0, inner, 2 * LANES):
        units.append(one(next_gate, at, 0, normed_ref, False))
        units.append(one(next_scaled, at, 2 * inner, cot_ref, True))
    return units


def forward_kernel(
    heads, seq_count, rows_all,
    place_ref, ends_ref,
    hidden_ref, cot_ref, stack_ref, gain_ref, narrow_ref, head_ref, conv_ref, shared_ref,
    normed_ref, low_ref, high_ref, state_ref, sums_ref, mine_ref, other_ref,
    weights, sems, in_buf, shared_buf, next_gate, next_in, next_scaled,
    next_narrow, state, low_buf, tail_buf, across,
):
    gate_ref, input_ref, x_ref, slope_ref, dscaled_ref, shared_in_ref, bc_ref, bc_slope_ref, mixed_ref, step_ref = (
        saved_views(low_ref, high_ref, heads * HEADDIM)
    )
    turn = pl.program_id(0)
    blocks = pl.num_programs(0) - 1
    block = turn - 1
    inner = heads * HEADDIM
    pairs = heads // 2

    def normalize():
        hidden = hidden_ref[...].astype(f32)
        inv_rms = lax.rsqrt(jnp.mean(hidden * hidden, axis=1, keepdims=True) + norm_eps)
        normed_ref[...] = (hidden * inv_rms * gain_ref[0:1, :]).astype(bf16)

    row_here = jnp.minimum(turn, blocks - 1) * ROWS + iota((ROWS, 2 * LANES), 0)
    targets = (next_gate, next_in, next_scaled, next_narrow)
    units = project_units(
        normed_ref, cot_ref, narrow_ref, weights, targets, row_here, ends_ref[seq_count - 1], inner
    )

    def take_next():
        in_buf[0:8, :] = in_buf[ROWS : ROWS + 8, :]
        shared_buf[0:8, :] = shared_buf[ROWS : ROWS + 8, :]
        in_buf[8:, :] = next_in[...].astype(f32)
        input_ref[...] = next_in[...]
        gate_ref[...] = next_gate[...]
        dscaled_ref[...] = next_scaled[...]
        shared_buf[8:, :] = next_narrow[:, 0 : 2 * LANES]
        shared_in_ref[...] = next_narrow[:, 0 : 2 * LANES].astype(bf16)
        step_ref[...] = next_narrow[:, 2 * LANES : 3 * LANES]

    @pl.when(turn == 0)
    def _():
        copies = load_weights(stack_ref, place_ref, weights, sems, 0, 3 * heads)
        in_buf[ROWS : ROWS + 8, :] = jnp.zeros((8, inner), f32)
        shared_buf[ROWS : ROWS + 8, :] = jnp.zeros((8, 2 * LANES), f32)
        state[...] = jnp.zeros_like(state)
        normalize()
        for copy in copies:
            copy.wait()
        for unit in units:
            unit()

    @pl.when(turn > 0)
    def _():
        take_next()
        normalize()
        pending = list(units)
        first_row = block * ROWS
        for sub in range(ROWS // SUB):
            first = sub * SUB
            here = slice(first, first + SUB)
            base = first_row + first
            row_at, col_at, same, carried, tail_same, through = block_terms(base, ends_ref, seq_count)
            causal = jnp.where(same & (row_at >= col_at), 0.0, far_below).astype(f32)
            masks = [shift_mask(row_at, -back, ends_ref, seq_count, rows_all) for back in (1, 2, 3)]
            bc = []
            for part in range(2):
                lanes = lanes_of(part)
                u = conv_tile(shared_buf, first, lanes, shared_ref[:, lanes], masks)
                sig = sigmoid(u)
                bc.append((u * sig).astype(bf16))
                bc_ref[here, lanes] = bc[part]
                bc_slope_ref[here, lanes] = (sig * (1.0 + u * (1.0 - sig))).astype(bf16)
            b_low, c_low = bc
            _, _, _, cum, source = step_terms(step_ref[here, :], head_ref)
            source_row = source.T
            scores = dot_nt(c_low, b_low)
            cum_last = cum[SUB - 1 : SUB, :]
            entry = jnp.exp2(cum) * carried
            leave = jnp.exp2(cum_last - source) * tail_same
            pass_on = jnp.exp2(cum_last) * through
            state_low = state[...].astype(bf16)
            state_ref[sub] = state_low
            across[...] = dot_nn(c_low, state_low)
            square = jnp.zeros((SUB, LANES), f32)
            inner_dot = jnp.zeros((SUB, LANES), f32)
            for pair in range(pairs):
                if pending:
                    pending.pop(0)()
                lanes = lanes_of(pair)
                u = conv_tile(in_buf, first, lanes, conv_ref[:, lanes], masks)
                sig = sigmoid(u)
                x_low = (u * sig).astype(bf16)
                x_ref[here, lanes] = x_low
                slope_ref[here, lanes] = (sig * (1.0 + u * (1.0 - sig))).astype(bf16)
                x = x_low.astype(f32)
                mats = []
                for h in (2 * pair, 2 * pair + 1):
                    gap = cum[:, h : h + 1] - source_row[h : h + 1, :]
                    mats.append((jnp.exp2(gap + causal) * scores).astype(bf16))
                x_a, x_b = split_pair(x_low)
                mixed = dot_nn(jnp.concatenate(mats, axis=1), jnp.concatenate([x_a, x_b], axis=0))
                mixed = mixed + across[:, lanes] * expand(entry, pair)
                mixed = mixed + expand(head_ref[2:3, :], pair) * x
                mixed_ref[here, lanes] = mixed
                gate = gate_ref[here, lanes].astype(f32)
                gated = mixed * (gate * sigmoid(gate))
                gated_gain = gated * conv_ref[5:6, lanes]
                low_buf[here, lanes] = gated_gain.astype(bf16)
                square = square + gated * gated
                inner_dot = inner_dot + dscaled_ref[here, lanes].astype(f32) * gated_gain
                tail_buf[:, lanes] = (x * expand(leave, pair)).astype(bf16)
            fresh = dot_tn(b_low, tail_buf[...])
            for pair in range(pairs):
                lanes = lanes_of(pair)
                state[:, lanes] = state[:, lanes] * expand(pass_on, pair) + fresh[:, lanes]
            sums_ref[0:1, here] = jnp.sum(square.T, axis=0, keepdims=True)
            sums_ref[1:2, here] = jnp.sum(inner_dot.T, axis=0, keepdims=True)
        while pending:
            pending.pop(0)()
        sums_ref[2:8, :] = jnp.zeros((6, ROWS), f32)
        part = dot_nn(low_buf[...], weights[2 * inner : 3 * inner, :]).astype(bf16)
        store_half(part, block, blocks, ends_ref[seq_count], mine_ref, other_ref)


def forward_call(place, ends, hidden, cot, stack, gain, narrow, head_rows, conv_rows, shared_rows, heads):
    rows_all, width = hidden.shape
    inner = heads * HEADDIM
    blocks = rows_all // ROWS

    def ahead(columns):
        return pl.BlockSpec((ROWS, columns), lambda i, *_: (jnp.minimum(i, blocks - 1), 0))

    def rows(columns):
        return pl.BlockSpec((ROWS, columns), lambda i, *_: (jnp.maximum(i - 1, 0), 0))

    whole = pl.BlockSpec(memory_space=pltpu.VMEM)
    columns = [(5 * inner + 6 * LANES, bf16), (inner + LANES, f32)]
    out_shape = [
        jax.ShapeDtypeStruct((rows_all, width), bf16),
        *[jax.ShapeDtypeStruct((rows_all, count), kind) for count, kind in columns],
        jax.ShapeDtypeStruct((rows_all // SUB, LANES, inner), bf16),
        jax.ShapeDtypeStruct((8, rows_all), f32),
        jax.ShapeDtypeStruct((rows_all // 2, width), bf16),
        jax.ShapeDtypeStruct((rows_all // 2, width), bf16),
    ]
    out_specs = [
        ahead(width),
        *[rows(count) for count, _ in columns],
        pl.BlockSpec((ROWS // SUB, LANES, inner), lambda i, *_: (jnp.maximum(i - 1, 0), 0, 0)),
        pl.BlockSpec((8, ROWS), lambda i, *_: (0, jnp.maximum(i - 1, 0))),
        *half_specs(width, blocks, ends.shape[0] - 1, lambda i: jnp.maximum(i - 1, 0)),
    ]
    return pl.pallas_call(
        functools.partial(forward_kernel, heads, ends.shape[0] - 1, rows_all),
        grid_spec=pltpu.PrefetchScalarGridSpec(
            num_scalar_prefetch=2,
            grid=(blocks + 1,),
            in_specs=[
                ahead(width), ahead(width), pl.BlockSpec(memory_space=pl.ANY), whole, whole, whole, whole, whole,
            ],
            out_specs=out_specs,
            scratch_shapes=[
                pltpu.VMEM((3 * inner, width), bf16),
                pltpu.SemaphoreType.DMA((3 * heads,)),
                pltpu.VMEM((ROWS + 8, inner), f32),
                pltpu.VMEM((ROWS + 8, 2 * LANES), f32),
                pltpu.VMEM((ROWS, inner), bf16),
                pltpu.VMEM((ROWS, inner), bf16),
                pltpu.VMEM((ROWS, inner), bf16),
                pltpu.VMEM((ROWS, NARROW), f32),
                pltpu.VMEM((LANES, inner), f32),
                pltpu.VMEM((ROWS, inner), bf16),
                pltpu.VMEM((SUB, inner), bf16),
                pltpu.VMEM((SUB, inner), f32),
            ],
        ),
        out_shape=out_shape,
        compiler_params=pltpu.CompilerParams(
            dimension_semantics=("arbitrary",), vmem_limit_bytes=56 * 2**20
        ),
        cost_estimate=pl.CostEstimate(
            flops=2 * rows_all * width * (4 * inner + NARROW), bytes_accessed=60 * 2**20, transcendentals=0
        ),
        name="mixer_forward",
    )(place, ends, hidden, cot, stack, gain, narrow, head_rows, conv_rows, shared_rows)


def backward_kernel(
    heads, seq_count, rows_all, inner_all,
    place_ref, ends_ref,
    hidden_ref, low_ref, high_ref, state_ref, sums_ref,
    stack_ref, narrow_ref, gain_ref, head_ref, conv_ref, shared_ref,
    dboth_ref, scaled_ref, mine_ref, other_ref, mine_narrow_ref, other_narrow_ref, extra_ref,
    weights, sems, du_buf, dshared_buf, dstate, state_after, from_state, terms, source_terms, tail_buf,
    entry_buf, dnarrow_buf, last_both, last_narrow, dn_buf, conv_grad, shared_grad, head_grad, skip_grad,
    gain_grad, narrow_grad_ref,
):
    gate_ref, input_ref, x_ref, slope_ref, dscaled_ref, shared_in_ref, bc_ref, bc_slope_ref, mixed_ref, step_ref = (
        saved_views(low_ref, high_ref, heads * HEADDIM)
    )
    turn = pl.program_id(0)
    blocks = pl.num_programs(0) - 1
    block = blocks - 1 - turn
    inner = heads * HEADDIM
    pairs = heads // 2
    width = hidden_ref.shape[1]
    wide = 2 * LANES

    @pl.when(turn == 0)
    def _():
        copies = load_weights(stack_ref, place_ref, weights, sems, 0, 2 * heads)
        du_buf[ROWS:, :] = jnp.zeros((8, inner), f32)
        dshared_buf[ROWS:, :] = jnp.zeros((8, 2 * LANES), f32)
        for ref in (
            dstate, state_after, last_both, last_narrow, conv_grad, shared_grad, head_grad, skip_grad,
            gain_grad, narrow_grad_ref,
        ):
            ref[...] = jnp.zeros_like(ref)
        for copy in copies:
            copy.wait()

    def row_units():
        hidden = hidden_ref[...].astype(f32)
        inv_rms = lax.rsqrt(jnp.mean(hidden * hidden, axis=1, keepdims=True) + norm_eps)

        def one(at):
            columns = slice(at, at + wide)

            def unit():
                part = dot_nn(last_both[...], weights[:, columns])
                part = part + dot_nt(last_narrow[...], narrow_ref[columns, :])
                dn_buf[:, columns] = part.astype(bf16)
                unit_rows = hidden_ref[:, columns].astype(f32) * inv_rms
                gain_grad[:, columns] += fold_rows(part * unit_rows)
                normed = (unit_rows * gain_ref[0:1, columns]).astype(bf16)
                narrow_grad_ref[:, columns] += dot_tn(last_narrow[...], normed)

            return unit

        return [one(at) for at in range(0, width, wide)]

    def finish_rows():
        store_half(dn_buf[...], block + 1, blocks, ends_ref[seq_count], mine_ref, other_ref)

    @pl.when(turn < blocks)
    def _():
        pending = row_units()
        reduce_heads = (iota((inner, LANES), 0) // HEADDIM == iota((inner, LANES), 1)).astype(bf16)
        first_row = block * ROWS
        kept = []
        for sub in reversed(range(ROWS // SUB)):
            first = sub * SUB
            here = slice(first, first + SUB)
            base = first_row + first
            row_at, col_at, same, carried, tail_same, through = block_terms(base, ends_ref, seq_count)
            causal = jnp.where(same & (row_at <= col_at), 0.0, far_below).astype(f32)
            b_low, c_low = bc_ref[here, 0:LANES], bc_ref[here, LANES : 2 * LANES]
            shifted, step, decay, cum, source = step_terms(step_ref[here, :], head_ref)
            kept.append((here, shifted, step, decay))
            cum_row = cum.T
            scores = dot_nt(b_low, c_low)
            cum_last = cum[SUB - 1 : SUB, :]
            entry = jnp.exp2(cum) * carried
            leave = jnp.exp2(cum_last - source) * tail_same
            pass_on = jnp.exp2(cum_last) * through
            inv_row = lax.rsqrt(sums_ref[0:1, here] * (1.0 / inner_all) + norm_eps)
            fix_row = inv_row * inv_row * inv_row * sums_ref[1:2, here] * (1.0 / inner_all)
            inv = jnp.broadcast_to(inv_row, (SUB, SUB)).T
            fix = jnp.broadcast_to(fix_row, (SUB, SUB)).T
            dstate_low = dstate[...].astype(bf16)
            from_state[...] = dot_nn(b_low, dstate_low)
            dscores = jnp.zeros((SUB, SUB), f32)
            for pair in range(pairs):
                if pending and pair % 2 == 1:
                    pending.pop(0)()
                lanes = lanes_of(pair)
                x_low = x_ref[here, lanes]
                x = x_low.astype(f32)
                slope = slope_ref[here, lanes].astype(f32)
                gate = gate_ref[here, lanes].astype(f32)
                gate_sig = sigmoid(gate)
                gate_silu = gate * gate_sig
                mixed = mixed_ref[here, lanes]
                gated = mixed * gate_silu
                gain = conv_ref[5:6, lanes]
                dscaled = dscaled_ref[here, lanes].astype(f32)
                normal = gated * inv
                scaled_ref[here, lanes] = (normal * gain).astype(bf16)
                conv_grad[5, :, lanes] += fold_rows(dscaled * normal)
                dgated = inv * (dscaled * gain) - gated * fix
                dgate = dgated * mixed * (gate_sig * (1.0 + gate * (1.0 - gate_sig)))
                dboth_ref[here, lanes] = dgate.astype(bf16)
                dmixed = dgated * gate_silu
                dy_low = dmixed.astype(bf16)
                dy = dy_low.astype(f32)
                skip = expand(head_ref[2:3, :], pair)
                skip_grad[:, lanes] += fold_rows(dmixed * x)
                x_parts = split_pair(x_low)
                dy_parts = split_pair(dy_low)
                mats = []
                for k in range(2):
                    h = 2 * pair + k
                    gap = cum_row[h : h + 1, :] - source[:, h : h + 1]
                    decays = jnp.exp2(gap + causal)
                    mats.append((decays * scores).astype(bf16))
                    dscores = dscores + dot_nt(x_parts[k], dy_low) * decays
                dx = dot_nn(jnp.concatenate(mats, axis=1), jnp.concatenate(dy_parts, axis=0))
                leave_here = expand(leave, pair)
                dx = dx + leave_here * from_state[:, lanes]
                source_term = x * dx
                source_terms[here, lanes] = source_term
                terms[here, lanes] = dy * (mixed - skip * x) - source_term
                tail_buf[:, lanes] = (x * leave_here).astype(bf16)
                entry_buf[:, lanes] = (dy * expand(entry, pair)).astype(bf16)
                du_buf[here, lanes] = (dx + skip * dmixed) * slope
            state_low = state_ref[sub]
            dscores_low = dscores.astype(bf16)
            db = dot_nn(dscores_low, c_low) + dot_nt(tail_buf[...], dstate_low)
            dc = dot_tn(dscores_low, b_low) + dot_nt(entry_buf[...], state_low)
            dshared_buf[here, 0:LANES] = db * bc_slope_ref[here, 0:LANES].astype(f32)
            dshared_buf[here, LANES:wide] = dc * bc_slope_ref[here, LANES:wide].astype(f32)
            at_end = jnp.sum(dstate[...] * state_after[...].astype(f32), axis=0, keepdims=True)
            terms[first + SUB - 1 : first + SUB, :] += at_end
            state_after[...] = state_low
            fresh = dot_tn(c_low, entry_buf[...])
            for pair in range(pairs):
                lanes = lanes_of(pair)
                dstate[:, lanes] = dstate[:, lanes] * expand(pass_on, pair) + fresh[:, lanes]
        while pending:
            pending.pop(0)()

        both = jnp.concatenate([terms[...], source_terms[...]], axis=0)
        high = both.astype(bf16)
        low = (both - high.astype(f32)).astype(bf16)
        reduced = dot_nn(high, reduce_heads) + dot_nn(low, reduce_heads)
        upper = (iota((SUB, SUB), 0) <= iota((SUB, SUB), 1)).astype(f32)

        for sub in range(ROWS // SUB):
            first = sub * SUB
            here = slice(first, first + SUB)
            row_at = first_row + first + iota((SUB, LANES), 0)
            ahead = [shift_mask(row_at, k, ends_ref, seq_count, rows_all) for k in (1, 2, 3)]
            groups = [(pair, True) for pair in range(pairs)] + [(0, False), (1, False)]
            for group, is_wide in groups:
                lanes = lanes_of(group)
                grads, held = (du_buf, input_ref) if is_wide else (dshared_buf, shared_in_ref)
                taps = conv_ref[:, lanes] if is_wide else shared_ref[:, lanes]
                sums = conv_grad if is_wide else shared_grad
                du = grads[here, lanes]
                v = held[here, lanes].astype(f32)
                dv = taps[3:4, :] * du
                sums[3, :, lanes] += fold_rows(du * v)
                sums[4, :, lanes] += fold_rows(du)
                for k in (1, 2, 3):
                    moved = grads[first + k : first + k + SUB, lanes] * ahead[k - 1]
                    dv = dv + taps[3 - k : 4 - k, :] * moved
                    sums[3 - k, :, lanes] += fold_rows(moved * v)
                if is_wide:
                    dboth_ref[here, inner + group * LANES : inner + (group + 1) * LANES] = dv.astype(bf16)
                else:
                    dnarrow_buf[here, lanes] = dv.astype(bf16)
        for here, shifted, step, decay in kept:
            dcum = reduced[here]
            from_source = reduced[ROWS + here.start : ROWS + here.stop]
            dlog = dot_nn(upper, dcum, exact_mode)
            sig = sigmoid(shifted)
            ratio = jnp.where(shifted < -15.0, 1.0, sig / step)
            dlog_decay = dlog * decay
            dstep = from_source * ratio + dlog_decay * sig
            dnarrow_buf[here, wide:NARROW] = dstep.astype(bf16)
            head_grad[0] += fold_rows(dstep)
            head_grad[1] += fold_rows(dlog_decay * step)
        du_buf[ROWS:, :] = du_buf[0:8, :]
        dshared_buf[ROWS:, :] = dshared_buf[0:8, :]

        @pl.when(turn > 0)
        def _():
            finish_rows()

        last_both[...] = dboth_ref[...]
        last_narrow[...] = dnarrow_buf[...]

    @pl.when(turn == blocks)
    def _():
        for unit in row_units():
            unit()
        finish_rows()
        extra_ref[...] = jnp.zeros_like(extra_ref)
        extra_ref[0:16, :] = narrow_grad_ref[wide : wide + 16, :]
        core = ends_ref[seq_count]
        for k in range(2):
            near = pl.multiple_of((2 * k + core) * HEADDIM, HEADDIM)
            far = pl.multiple_of((2 * k + 1 - core) * HEADDIM, HEADDIM)
            mine_narrow_ref[k] = narrow_grad_ref[pl.ds(near, HEADDIM), :]
            other_narrow_ref[k] = narrow_grad_ref[pl.ds(far, HEADDIM), :]
        per_line = width // inner

        def total(values):
            return jnp.sum(values, axis=0, keepdims=True)

        for k in range(6):
            at = (k % per_line) * inner
            row = 16 + k // per_line
            extra_ref[row : row + 1, at : at + inner] = total(conv_grad[k])
        extra_ref[GAIN_ROW : GAIN_ROW + 1, :] = total(gain_grad[...])
        for k in range(5):
            extra_ref[SHARED_ROW : SHARED_ROW + 1, wide * k : wide * (k + 1)] = total(shared_grad[k])
        for k in range(2):
            extra_ref[HEAD_ROW + k : HEAD_ROW + k + 1, 0:LANES] = total(head_grad[k])
        reduce_all = (iota((inner, LANES), 0) // HEADDIM == iota((inner, LANES), 1)).astype(f32)
        skip_sum = dot_nn(skip_grad[...], reduce_all, exact_mode)
        extra_ref[HEAD_ROW + 2 : HEAD_ROW + 3, 0:LANES] = total(skip_sum)


def backward_call(
    place, ends, hidden, saved, sums, stack, narrow, gain, head_rows, conv_rows, shared_rows, heads,
    inner_all, extra_rows,
):
    rows_all, width = hidden.shape
    inner = heads * HEADDIM
    blocks = rows_all // ROWS

    def rows(columns):
        return pl.BlockSpec((ROWS, columns), lambda i, *_: (jnp.maximum(blocks - 1 - i, 0), 0))

    def behind(i):
        return jnp.minimum(blocks - i, blocks - 1)

    whole = pl.BlockSpec(memory_space=pltpu.VMEM)
    out_shape = [
        jax.ShapeDtypeStruct((rows_all, 2 * inner), bf16),
        jax.ShapeDtypeStruct((rows_all, inner), bf16),
        jax.ShapeDtypeStruct((rows_all // 2, width), bf16),
        jax.ShapeDtypeStruct((rows_all // 2, width), bf16),
        jax.ShapeDtypeStruct((2, HEADDIM, width), f32),
        jax.ShapeDtypeStruct((2, HEADDIM, width), f32),
        jax.ShapeDtypeStruct((extra_rows, width), f32),
    ]
    out_specs = [
        rows(2 * inner), rows(inner),
        *half_specs(width, blocks, ends.shape[0] - 1, behind),
        whole, whole, whole,
    ]
    return pl.pallas_call(
        functools.partial(backward_kernel, heads, ends.shape[0] - 1, rows_all, inner_all),
        grid_spec=pltpu.PrefetchScalarGridSpec(
            num_scalar_prefetch=2,
            grid=(blocks + 1,),
            in_specs=[
                pl.BlockSpec((ROWS, width), lambda i, *_: (behind(i), 0)),
                *[rows(array.shape[1]) for array in saved[:-1]],
                pl.BlockSpec(
                    (ROWS // SUB, LANES, inner), lambda i, *_: (jnp.maximum(blocks - 1 - i, 0), 0, 0)
                ),
                pl.BlockSpec((8, ROWS), lambda i, *_: (0, jnp.maximum(blocks - 1 - i, 0))),
                pl.BlockSpec(memory_space=pl.ANY), whole, whole, whole, whole, whole,
            ],
            out_specs=out_specs,
            scratch_shapes=[
                pltpu.VMEM((2 * inner, width), bf16),
                pltpu.SemaphoreType.DMA((2 * heads,)),
                pltpu.VMEM((ROWS + 8, inner), f32),
                pltpu.VMEM((ROWS + 8, 2 * LANES), f32),
                pltpu.VMEM((LANES, inner), f32),
                pltpu.VMEM((LANES, inner), bf16),
                pltpu.VMEM((SUB, inner), f32),
                pltpu.VMEM((ROWS, inner), f32),
                pltpu.VMEM((ROWS, inner), f32),
                pltpu.VMEM((SUB, inner), bf16),
                pltpu.VMEM((SUB, inner), bf16),
                pltpu.VMEM((ROWS, NARROW), bf16),
                pltpu.VMEM((ROWS, 2 * inner), bf16),
                pltpu.VMEM((ROWS, NARROW), bf16),
                pltpu.VMEM((ROWS, width), bf16),
                pltpu.VMEM((6, 8, inner), f32),
                pltpu.VMEM((5, 8, 2 * LANES), f32),
                pltpu.VMEM((2, 8, LANES), f32),
                pltpu.VMEM((8, inner), f32),
                pltpu.VMEM((8, width), f32),
                pltpu.VMEM((NARROW, width), f32),
            ],
        ),
        out_shape=out_shape,
        compiler_params=pltpu.CompilerParams(
            dimension_semantics=("arbitrary",), vmem_limit_bytes=56 * 2**20
        ),
        cost_estimate=pl.CostEstimate(
            flops=4 * rows_all * width * (2 * inner + NARROW), bytes_accessed=60 * 2**20, transcendentals=0
        ),
        name="mixer_backward",
    )(place, ends, hidden, *saved, sums, stack, narrow, gain, head_rows, conv_rows, shared_rows)


def grads_kernel(
    first_matrix, count, seq_count, clear, mask_right, place_ref, ends_ref, free_ref, left_ref, right_ref,
    *rest,
):
    out_ref, held, sems, free_sems = rest[-4:]
    chunk = pl.program_id(0)
    width = right_ref.shape[1]
    right = right_ref[...]
    if mask_right:
        valid = iota(right.shape, 0) < ends_ref[seq_count - 1]
        right = jnp.where(valid, right.astype(f32), 0.0).astype(bf16)
    held[0 : count * HEADDIM, :] = dot_tn(left_ref[...], right).astype(bf16)
    columns = pl.ds(pl.multiple_of(chunk * width, width), width)
    copies = [
        pltpu.make_async_copy(
            held.at[pl.ds(m * HEADDIM, HEADDIM), :],
            out_ref.at[place_ref[first_matrix + m], :, columns],
            sems.at[m],
        )
        for m in range(count)
    ]
    for copy in copies:
        copy.start()
    if clear:
        held[count * HEADDIM :, :] = jnp.zeros((HEADDIM, width), bf16)

        def clear_copy(s):
            return pltpu.make_async_copy(
                held.at[pl.ds(count * HEADDIM, HEADDIM), :], out_ref.at[s, :, columns], free_sems.at[s]
            )

        for s in range(out_ref.shape[0]):

            @pl.when(free_ref[s] > 0)
            def _(s=s):
                clear_copy(s).start()

        for s in range(out_ref.shape[0]):

            @pl.when(free_ref[s] > 0)
            def _(s=s):
                clear_copy(s).wait()

    for copy in copies:
        copy.wait()


def grads_call(place, ends, free, left, right, first_matrix, mask_right, into):
    rows_all, width = right.shape
    slots = free.shape[0]
    count = left.shape[1] // HEADDIM
    clear = into is None
    held = pl.BlockSpec(memory_space=pl.ANY)
    return pl.pallas_call(
        functools.partial(grads_kernel, first_matrix, count, ends.shape[0] - 1, clear, mask_right),
        grid_spec=pltpu.PrefetchScalarGridSpec(
            num_scalar_prefetch=3,
            grid=(width // CHUNK,),
            in_specs=[
                pl.BlockSpec(left.shape, lambda i, *_: (0, 0), pipeline_mode=pl.Buffered(1)),
                pl.BlockSpec((rows_all, CHUNK), lambda i, *_: (0, i)),
            ]
            + ([] if clear else [held]),
            out_specs=held,
            scratch_shapes=[
                pltpu.VMEM(((count + 1) * HEADDIM, CHUNK), bf16),
                pltpu.SemaphoreType.DMA((count,)),
                pltpu.SemaphoreType.DMA((slots,)),
            ],
        ),
        out_shape=jax.ShapeDtypeStruct((slots, HEADDIM, width), bf16),
        input_output_aliases={} if clear else {5: 0},
        compiler_params=pltpu.CompilerParams(
            dimension_semantics=("arbitrary",), vmem_limit_bytes=56 * 2**20
        ),
        cost_estimate=pl.CostEstimate(
            flops=2 * rows_all * width * left.shape[1], bytes_accessed=30 * 2**20, transcendentals=0
        ),
        name="weight_grads",
    )(place, ends, free, left, right, *([] if clear else [into]))


def exchange_kernel(
    sums_ref, mine_ref, other_ref, total_ref, near_ref, sums_in, part_in, mine_in, sum_sems, part_sems, mine_sems
):
    here = lax.axis_index("dp")
    tensor = lax.axis_index("tensor")
    peers = [(here, (tensor + k) % 4) for k in range(1, 4)]
    other_core = (here, tensor + 1 - 2 * (tensor % 2))
    rows = mine_ref.shape[0]
    greet([(peer, None) for peer in peers])
    parts = [pl.ds(k * ROWS, ROWS) for k in range(rows // ROWS)]

    def part_copy(k):
        return remote(
            other_ref.at[parts[k]], part_in.at[parts[k]], part_sems.at[0, k], part_sems.at[1, k], other_core
        )

    def sum_copy(k):
        return remote(
            sums_ref.at[0:2], sums_in.at[tensor], sum_sems.at[0, k], sum_sems.at[1, k], peers[k]
        )

    def mine_copy(k):
        return pltpu.make_async_copy(mine_ref.at[parts[k]], mine_in.at[parts[k]], mine_sems.at[k])

    for k in range(3):
        sum_copy(k).start()
    for k in range(len(parts)):
        part_copy(k).start()
    for k in range(len(parts)):
        mine_copy(k).start()
    for k in range(3):
        sum_copy(k).wait()
    total = jnp.zeros((2, sums_ref.shape[1]), f32)
    for t in range(4):
        total = total + jnp.where(tensor == t, sums_ref[0:2, :], sums_in[t])
    total_ref[0:2, :] = total
    total_ref[2:8, :] = jnp.zeros((6, sums_ref.shape[1]), f32)
    for k in range(len(parts)):
        mine_copy(k).wait()
        part_copy(k).wait()
        here_rows = parts[k]
        near_ref[here_rows, :] = (
            mine_in[here_rows, :].astype(f32) + part_in[here_rows, :].astype(f32)
        ).astype(bf16)


def exchange_call(sums, mine, other):
    rows, width = mine.shape
    spec = pl.BlockSpec(memory_space=pltpu.VMEM)
    sems = pltpu.SemaphoreType.DMA
    return pl.pallas_call(
        exchange_kernel,
        in_specs=[spec] + [pl.BlockSpec(memory_space=pltpu.HBM)] * 2,
        out_specs=[spec] * 2,
        out_shape=[jax.ShapeDtypeStruct(sums.shape, f32), jax.ShapeDtypeStruct(mine.shape, bf16)],
        scratch_shapes=[
            pltpu.VMEM((4, 2, sums.shape[1]), f32), pltpu.VMEM((rows, width), bf16),
            pltpu.VMEM((rows, width), bf16),
            sems((2, 3)), sems((2, rows // ROWS)), sems((rows // ROWS,)),
        ],
        compiler_params=pltpu.CompilerParams(
            collective_id=2, has_side_effects=True, vmem_limit_bytes=40 * 2**20
        ),
        name="exchange_sums",
    )(sums, mine, other)


def branch_kernel(inner_all, seq_count, ends_ref, near_ref, far_ref, hidden_ref, sums_ref, full_ref, half_ref):
    width = hidden_ref.shape[1]
    blocks = pl.num_programs(0)
    first_row = (ends_ref[seq_count] * blocks + pl.program_id(0)) * SUB
    inv_row = lax.rsqrt(sums_ref[0:1, :] * (1.0 / inner_all) + norm_eps)
    inv = jnp.broadcast_to(inv_row, (SUB, SUB)).T
    row_at = first_row + iota((SUB, LANES), 0)
    valid = jnp.where(row_at < ends_ref[seq_count - 1], 1.0, 0.0).astype(f32)
    for group in range(width // LANES):
        lanes = lanes_of(group)
        branch = (near_ref[:, lanes].astype(f32) + far_ref[:, lanes].astype(f32)) * inv
        result = ((hidden_ref[:, lanes].astype(f32) + branch) * valid).astype(bf16)
        full_ref[:, lanes] = result
        half_ref[:, lanes] = result


def input_kernel(seq_count, ends_ref, near_ref, far_ref, hidden_ref, cot_ref, gain_ref, full_ref, half_ref):
    width = hidden_ref.shape[1]
    blocks = pl.num_programs(0)
    first_row = (ends_ref[seq_count] * blocks + pl.program_id(0)) * SUB
    hidden = hidden_ref[...].astype(f32)
    inv_rms = lax.rsqrt(jnp.mean(hidden * hidden, axis=1, keepdims=True) + norm_eps)
    gain_part = (near_ref[...].astype(f32) + far_ref[...].astype(f32)) * gain_ref[0:1, :]
    fix = inv_rms * inv_rms * inv_rms * (jnp.sum(gain_part * hidden, axis=1, keepdims=True) / width)
    row_at = first_row + iota(hidden.shape, 0)
    cot = jnp.where(row_at < ends_ref[seq_count - 1], cot_ref[...].astype(f32), 0.0)
    result = (inv_rms * gain_part - hidden * fix + cot).astype(bf16)
    full_ref[...] = result
    half_ref[...] = result


def half_call(kernel, name, ends, halves, fulls, wholes):
    rows, width = halves[0].shape
    seq_count = ends.shape[0] - 1
    blocks = rows // SUB

    def in_full(i, ends):
        return (ends[seq_count] * blocks + i, 0)

    own = pl.BlockSpec((SUB, width), lambda i, ends: (i, 0))
    full = pl.BlockSpec((SUB, width), in_full)
    return pl.pallas_call(
        kernel,
        grid_spec=pltpu.PrefetchScalarGridSpec(
            num_scalar_prefetch=1,
            grid=(blocks,),
            in_specs=[own] * len(halves) + [full] * len(fulls) + wholes[1],
            out_specs=[full, own],
        ),
        out_shape=[
            jax.ShapeDtypeStruct((2 * rows, width), bf16),
            jax.ShapeDtypeStruct((rows, width), bf16),
        ],
        compiler_params=pltpu.CompilerParams(
            dimension_semantics=("arbitrary",), vmem_limit_bytes=40 * 2**20
        ),
        cost_estimate=pl.CostEstimate(flops=0, bytes_accessed=16 * 2**20, transcendentals=0),
        name=name,
    )(ends, *halves, *fulls, *wholes[0])


def remote(src, dst, send_sem, recv_sem, target):
    return pltpu.make_async_remote_copy(
        src_ref=src,
        dst_ref=dst,
        send_sem=send_sem,
        recv_sem=recv_sem,
        device_id=target,
        device_id_type=pl.DeviceIdType.MESH,
    )


def greet(targets):
    barrier = pltpu.get_barrier_semaphore()
    for target, condition in targets:
        if condition is None:
            pl.semaphore_signal(barrier, inc=1, device_id=target, device_id_type=pl.DeviceIdType.MESH)
        else:

            @pl.when(condition)
            def _(target=target):
                pl.semaphore_signal(
                    barrier, inc=1, device_id=target, device_id_type=pl.DeviceIdType.MESH
                )

    peers = sum(1 if condition is None else condition.astype(jnp.int32) for _, condition in targets)
    pl.semaphore_wait(barrier, peers)


def gather_kernel(
    lines, own_ref, out_ref, local_sem, x_send, x_recv, up_send, up_recv, down_send, down_recv
):
    here = lax.axis_index("dp")
    tensor = lax.axis_index("tensor")
    line, side = here // 2, here % 2
    partner = here + 1 - 2 * side
    slots = own_ref.shape[0]
    most = slots - 1
    has_up, has_down = line < lines - 1, line > 0
    across, above, below = (partner, tensor), (here + 2, tensor), (here - 2, tensor)

    greet([(across, None), (above, has_up), (below, has_down)])
    local = pltpu.make_async_copy(own_ref, out_ref.at[pl.ds(here * slots, slots)], local_sem)
    local.start()
    order = [most] + list(range(min(2, most))) + [slots] + list(range(min(2, most), most))

    def place(at, part):
        device = 2 * at + 1 - side if part == slots else 2 * at + side
        return device * slots + min(part, most)

    def line_copy(step, at, part, upward):
        own = step == 0 and part < slots
        to = out_ref.at[place(at, part)]
        src = own_ref.at[part] if own else to
        if upward:
            return remote(src, to, up_send.at[step, part], up_recv.at[step, part], above)
        return remote(src, to, down_send.at[step, part], down_recv.at[step, part], below)

    def x_copy(device, index, part, own=False):
        to = out_ref.at[device * slots + part]
        return remote(
            own_ref.at[part] if own else to, to, x_send.at[index, part], x_recv.at[index, part], across
        )

    x_copy(here, 0, most, True).start()
    for part in order:
        if part == slots:
            x_copy(partner, 0, most).wait_recv()

        @pl.when(has_up)
        def _(part=part):
            line_copy(0, line, part, True).start()

        @pl.when(has_down)
        def _(part=part):
            line_copy(0, line, part, False).start()

        if part < most:
            x_copy(here, 0, part, True).start()

    for k in range(1, lines):
        for part in order:

            @pl.when(line >= k)
            def _(k=k, part=part):
                line_copy(k - 1, line - k, part, True).wait_recv()
                if k < lines - 1:

                    @pl.when(has_up)
                    def _():
                        line_copy(k, line - k, part, True).start()

                if part < most:
                    x_copy(2 * (line - k) + side, k, part).start()

            @pl.when(line + k < lines)
            def _(k=k, part=part):
                line_copy(k - 1, line + k, part, False).wait_recv()
                if k < lines - 1:

                    @pl.when(has_down)
                    def _():
                        line_copy(k, line + k, part, False).start()

                if part < most:
                    x_copy(2 * (line + k) + side, lines - 1 + k, part).start()

    local.wait()
    x_copy(partner, 0, most).wait_send()
    for part in range(most):
        x_copy(partner, 0, part).wait()
    for k in range(1, lines):
        for part in range(most):

            @pl.when(line >= k)
            def _(k=k, part=part):
                x_copy(2 * (line - k) + 1 - side, k, part).wait()

            @pl.when(line + k < lines)
            def _(k=k, part=part):
                x_copy(2 * (line + k) + 1 - side, lines - 1 + k, part).wait()

    for k in range(lines - 1):
        for part in order:

            @pl.when(has_up & (line >= k))
            def _(k=k, part=part):
                line_copy(k, line - k, part, True).wait_send()

            @pl.when(has_down & (line + k < lines))
            def _(k=k, part=part):
                line_copy(k, line + k, part, False).wait_send()


def gather_call(own, dp_size):
    slots, side, width = own.shape
    lines = dp_size // 2
    step_sems = pltpu.SemaphoreType.DMA((lines - 1, slots + 1))
    x_sems = pltpu.SemaphoreType.DMA((2 * lines - 1, slots))
    return pl.pallas_call(
        functools.partial(gather_kernel, lines),
        in_specs=[pl.BlockSpec(memory_space=pl.ANY)],
        out_specs=pl.BlockSpec(memory_space=pl.ANY),
        out_shape=jax.ShapeDtypeStruct((slots * dp_size, side, width), own.dtype),
        scratch_shapes=[
            pltpu.SemaphoreType.DMA, x_sems, x_sems, step_sems, step_sems, step_sems, step_sems,
        ],
        compiler_params=pltpu.CompilerParams(collective_id=0, has_side_effects=True),
        name="gather_weights",
    )(own)


def reduce_kernel(
    lines,
    grads, near_ref, far_ref, extra_ref, owned_ref, totals_ref,
    x_in, up_in, down_in, last_out, last_in, halves, half_in, group_in, group_out, group_back,
    x_send, x_recv, up_send, up_recv, down_send, down_recv, last_sems, small_sems, group_sems, back_sems,
):
    here = lax.axis_index("dp")
    tensor = lax.axis_index("tensor")
    line, side = here // 2, here % 2
    core = tensor % 2
    slots = owned_ref.shape[0]
    most = slots - 1
    width = near_ref.shape[1]
    half = width // 2
    group = halves.shape[1] // lines
    has_up, has_down = line < lines - 1, line > 0
    across = (here + 1 - 2 * side, tensor)
    above, below = (here + 2, tensor), (here - 2, tensor)
    other_core = (here, tensor + 1 - 2 * core)
    other_chip = (here, (tensor + 2) % 4)
    on_line = [(2 * ((line + k) % lines) + side, tensor) for k in range(1, lines)]

    greet([(target, None) for target in [across, other_core, other_chip] + on_line])

    def add(*parts):
        total = parts[0].astype(f32)
        for part in parts[1:]:
            total = total + part.astype(f32)
        return total

    half_copy = remote(halves.at[1 - side], half_in, small_sems.at[0, 0], small_sems.at[1, 0], across)

    def group_copy(k):
        to = (line + k) % lines
        rows = pl.ds(pl.multiple_of(to * group, group), group)
        return remote(
            halves.at[side, rows], group_in.at[k - 1], group_sems.at[0, k - 1], group_sems.at[1, k - 1],
            on_line[k - 1],
        )

    def back_copy(k):
        return remote(
            group_out, group_back.at[k - 1], back_sems.at[0, k - 1], back_sems.at[1, k - 1], on_line[k - 1]
        )

    total_half = remote(
        totals_ref.at[tensor, side], totals_ref.at[tensor, side], small_sems.at[0, 1], small_sems.at[1, 1],
        across,
    )
    total_chip = remote(
        totals_ref.at[tensor], totals_ref.at[tensor], small_sems.at[0, 2], small_sems.at[1, 2], other_chip
    )

    def total_core(k):
        at = core + 2 * k
        return remote(
            totals_ref.at[at], totals_ref.at[at], small_sems.at[0, 3 + k], small_sems.at[1, 3 + k], other_core
        )

    def small_start():
        mine = near_ref[...] + far_ref[...]
        rest = extra_ref[...]
        for k in range(2):
            columns = slice(k * half, (k + 1) * half)
            halves[k, 0:HEADDIM, :] = mine[:, columns]
            halves[k, HEADDIM:, :] = rest[:, columns]
        half_copy.start()

    def small_group():
        half_copy.wait()
        halves[side] = halves[side] + half_in[...]
        for k in range(1, lines):
            group_copy(k).start()

    def small_back():
        for k in range(1, lines):
            group_copy(k).wait()
        rows = pl.ds(pl.multiple_of(line * group, group), group)
        total = halves[side, rows, :]
        for k in range(1, lines):
            total = total + group_in[k - 1]
        group_out[...] = total
        for k in range(1, lines):
            back_copy(k).start()

    def small_half():
        for k in range(1, lines):
            back_copy(k).wait()
        rows = pl.ds(pl.multiple_of(line * group, group), group)
        totals_ref[tensor, side, rows, :] = group_out[...]
        for k in range(1, lines):
            source = (line + lines - k) % lines
            rows = pl.ds(pl.multiple_of(source * group, group), group)
            totals_ref[tensor, side, rows, :] = group_back[k - 1]
        total_half.start()

    def small_chip():
        total_half.wait()
        total_chip.start()

    def small_core():
        total_chip.wait()
        for k in range(2):
            total_core(k).start()

    def small_end():
        for k in range(2):
            total_core(k).wait()

    small = [(1, small_group), (3, small_back), (5, small_half), (8, small_chip), (13, small_core)]
    events = []

    def event():
        events.append(None)
        while small and small[0][0] <= len(events):
            small.pop(0)[1]()

    def x_copy(at, i):
        return remote(
            grads.at[(2 * at + 1 - side) * slots + i], x_in.at[at, i], x_send.at[at, i], x_recv.at[at, i], across
        )

    def x_needed(turn):
        step, i = turn // most, turn % most
        if step < lines - 1:
            each_way(step, lambda at, upward: x_copy(at, i).start())
        elif step == lines - 1:
            x_copy(line, i).start()

    def line_copy(src, at, i, upward):
        if upward:
            return remote(src, up_in.at[at, i], up_send.at[at, i], up_recv.at[at, i], above)
        return remote(src, down_in.at[at, i], down_send.at[at, i], down_recv.at[at, i], below)

    def line_most(at, i, upward):
        arrived = up_in if upward else down_in
        x_copy(at, i).wait_recv()
        own = add(grads[(2 * at + side) * slots + i], x_in[at, i])

        @pl.when(has_down if upward else has_up)
        def _():
            line_copy(x_in.at[at, i], at, i, upward).wait_recv()
            x_in[at, i] = add(own, arrived[at, i]).astype(bf16)

        @pl.when(jnp.logical_not(has_down if upward else has_up))
        def _():
            x_in[at, i] = own.astype(bf16)

        line_copy(x_in.at[at, i], at, i, upward).start()

    def line_last(at, k, upward):
        arrived = up_in if upward else down_in
        own = grads.at[(2 * at + k) * slots + most]

        @pl.when(has_down if upward else has_up)
        def _():
            line_copy(own, at, most + k, upward).wait_recv()
            arrived[at, most + k] = add(own[...], arrived[at, most + k]).astype(bf16)
            line_copy(arrived.at[at, most + k], at, most + k, upward).start()

        @pl.when(jnp.logical_not(has_down if upward else has_up))
        def _():
            line_copy(own, at, most + k, upward).start()

    def each_way(step, work):
        @pl.when(lines - 1 - step > line)
        def _():
            work(lines - 1 - step, True)

        @pl.when(step < line)
        def _():
            work(step, False)

    small_start()
    for turn in range(AHEAD):
        x_needed(turn)
    for step in range(lines - 1):
        for k in range(2):
            each_way(step, lambda at, upward, k=k: line_last(at, k, upward))
        event()
        for i in range(most):
            x_needed(step * most + i + AHEAD)
            each_way(step, lambda at, upward, i=i: line_most(at, i, upward))
            event()

    def gathered_last(k):
        return grads[(2 * line + k) * slots + most].astype(f32)

    owned_ref[most] = gathered_last(side)
    to_send = gathered_last(1 - side)
    last_out[...] = to_send

    @pl.when(has_down)
    def _():
        for k in range(2):
            line_copy(last_in, line, most + k, True).wait_recv()
        owned_ref[most] = owned_ref[most] + up_in[line, most + side].astype(f32)
        last_out[...] = last_out[...] + up_in[line, most + 1 - side].astype(f32)

    @pl.when(has_up)
    def _():
        for k in range(2):
            line_copy(last_in, line, most + k, False).wait_recv()
        owned_ref[most] = owned_ref[most] + down_in[line, most + side].astype(f32)
        last_out[...] = last_out[...] + down_in[line, most + 1 - side].astype(f32)

    x_in[line, most] = last_out[...].astype(bf16)
    last_copy = remote(x_in.at[line, most], last_in, last_sems.at[0], last_sems.at[1], across)
    last_copy.start()
    for turn in range((lines - 1) * most + AHEAD, lines * most):
        x_needed(turn)
    while small:
        small.pop(0)[1]()

    def finish(i, carry):
        x_copy(line, i).wait_recv()
        owned_ref[i] = add(grads[(2 * line + side) * slots + i], x_in[line, i])

        @pl.when(has_down)
        def _():
            line_copy(last_in, line, i, True).wait_recv()
            owned_ref[i] = owned_ref[i] + up_in[line, i].astype(f32)

        @pl.when(has_up)
        def _():
            line_copy(last_in, line, i, False).wait_recv()
            owned_ref[i] = owned_ref[i] + down_in[line, i].astype(f32)

        return carry

    lax.fori_loop(0, most, finish, 0)
    last_copy.wait()
    owned_ref[most] = owned_ref[most] + last_in[...].astype(f32)
    small_end()

    def x_sent(at):
        def one(i, carry):
            x_copy(at, i).wait_send()
            return carry

        lax.fori_loop(0, most, one, 0)

    def line_sent(at, upward):
        def one(i, carry):
            line_copy(last_in, at, i, upward).wait_send()
            return carry

        lax.fori_loop(0, slots + 1, one, 0)

    x_sent(line)
    for step in range(lines - 1):
        each_way(step, lambda at, upward: x_sent(at))
        each_way(step, line_sent)


def reduce_call(grads, near, far, extra, dp_size):
    slots_all, side, width = grads.shape
    slots = slots_all // dp_size
    lines = dp_size // 2
    small_rows = HEADDIM + extra.shape[0]
    group = small_rows // lines
    spec = pl.BlockSpec(memory_space=pltpu.VMEM)
    sems = pltpu.SemaphoreType.DMA
    return pl.pallas_call(
        functools.partial(reduce_kernel, lines),
        in_specs=[spec] * 4,
        out_specs=[spec] * 2,
        out_shape=[
            jax.ShapeDtypeStruct((slots, side, width), f32),
            jax.ShapeDtypeStruct((4, 2, small_rows, width // 2), f32),
        ],
        scratch_shapes=[
            pltpu.VMEM((lines, slots, side, width), bf16),
            pltpu.VMEM((lines, slots + 1, side, width), bf16),
            pltpu.VMEM((lines, slots + 1, side, width), bf16),
            pltpu.VMEM((side, width), f32),
            pltpu.VMEM((side, width), bf16),
            pltpu.VMEM((2, small_rows, width // 2), f32),
            pltpu.VMEM((small_rows, width // 2), f32),
            pltpu.VMEM((lines - 1, group, width // 2), f32),
            pltpu.VMEM((group, width // 2), f32),
            pltpu.VMEM((lines - 1, group, width // 2), f32),
            sems((lines, slots)), sems((lines, slots)),
            sems((lines, slots + 1)), sems((lines, slots + 1)),
            sems((lines, slots + 1)), sems((lines, slots + 1)),
            sems((2,)), sems((2, 5)), sems((2, lines - 1)), sems((2, lines - 1)),
        ],
        compiler_params=pltpu.CompilerParams(
            collective_id=1, has_side_effects=True, vmem_limit_bytes=56 * 2**20
        ),
        cost_estimate=pl.CostEstimate(flops=10**11, bytes_accessed=40 * 2**20, transcendentals=0),
        name="reduce_grads",
    )(grads, near, far, extra)


def small_rule(rate, weight, moment, gradient):
    moment_new = small_decay * moment + (1.0 - small_decay) * gradient
    return moment_new, weight - rate * moment_new


def muon_kernel(
    rate, small_rate_now,
    grad_ref, totals_ref, moment_ref, master_ref,
    state_moment, state_proj, step_moment, step_proj, gain_moment, gain, head_moment, head, conv_moment, conv,
    shared_moment, shared,
    moment_out, master_out,
    state_moment_out, state_out, step_moment_out, step_out, gain_moment_out, gain_out, head_moment_out,
    head_out, conv_moment_out, conv_out, shared_moment_out, shared_out,
):
    tensor = lax.axis_index("tensor")
    rule = functools.partial(small_rule, small_rate_now)

    def row(at, row_at):
        return jnp.concatenate(
            [totals_ref[at, k, row_at : row_at + 1, :] for k in range(2)], axis=1
        )

    def over_tensor(row_at):
        return row(0, row_at) + row(1, row_at) + row(2, row_at) + row(3, row_at)

    for k in range(2):
        parts = [
            jnp.concatenate([totals_ref[2 * k + j, c, 0:HEADDIM, :] for c in range(2)], axis=1)
            for j in range(2)
        ]
        lanes = lanes_of(k)
        state_moment_out[:, lanes], state_out[:, lanes] = rule(
            state_proj[:, lanes], state_moment[:, lanes], jnp.concatenate(parts, axis=0).T
        )
    heads = step_proj.shape[0]
    extra = HEADDIM
    own = [totals_ref[tensor, k, extra : extra + 32, :] for k in range(2)]
    step_moment_out[...], step_out[...] = rule(
        step_proj[...], step_moment[...], jnp.concatenate(own, axis=1)[0:heads]
    )
    gain_moment_out[...], gain_out[...] = rule(gain[...], gain_moment[...], over_tensor(extra + GAIN_ROW))
    head_moment_out[...], head_out[...] = rule(
        head[...], head_moment[...], own[0][HEAD_ROW : HEAD_ROW + 3, 0:heads]
    )
    inner = conv.shape[1]
    per_line = 2 * own[0].shape[1] // inner
    conv_total = jnp.concatenate(own, axis=1)
    for k in range(6):
        at = (k % per_line) * inner
        line = 16 + k // per_line
        one = slice(k, k + 1)
        conv_moment_out[one, :], conv_out[one, :] = rule(
            conv[one, :], conv_moment[one, :], conv_total[line : line + 1, at : at + inner]
        )
    shared_total = over_tensor(extra + SHARED_ROW)
    for k in range(5):
        one = slice(k, k + 1)
        shared_moment_out[one, :], shared_out[one, :] = rule(
            shared[one, :], shared_moment[one, :], shared_total[:, 2 * LANES * k : 2 * LANES * (k + 1)]
        )

    first_coef, second_coef, third_coef = schulz_coefs
    side = HEADDIM
    same = iota((side, side), 0) == iota((side, side), 1)
    eye = jnp.where(same, 1.0, 0.0).astype(f32)
    slots = grad_ref.shape[0]
    grams, totals, scales = [], [], []
    for s in range(slots):
        moment = muon_decay * moment_ref[s] + grad_ref[s].astype(f32)
        moment_out[s] = moment
        square = jnp.sum(jnp.sum(moment * moment, axis=1, keepdims=True), axis=0, keepdims=True)
        scale = 1.0 / (jnp.sqrt(square) + 1e-07)
        scaled = moment * scale
        grams.append(dot_nt(scaled, scaled, exact_mode))
        totals.append(eye)
        scales.append(scale)
    for _ in range(NS_STEPS):
        for s in range(slots):
            gram = grams[s]
            factor = (
                first_coef * eye + second_coef * gram + third_coef * dot_nn(gram, gram, exact_mode)
            )
            totals[s] = dot_nn(factor, totals[s], exact_mode)
            grams[s] = dot_nn(dot_nn(factor, gram, exact_mode), factor, exact_mode)
    for s in range(slots):
        ortho = dot_nn(totals[s], moment_out[s] * scales[s], exact_mode)
        master_out[s] = master_ref[s] - rate * ortho


def muon_call(grad, totals, moment, master, small, tokens_all):
    slots, side, width = moment.shape
    spec = pl.BlockSpec(memory_space=pltpu.VMEM)
    return pl.pallas_call(
        functools.partial(
            muon_kernel, muon_rate * math.sqrt(max(width, side)), small_rate / math.sqrt(tokens_all)
        ),
        in_specs=[spec] * (4 + len(small)),
        out_specs=[spec] * (2 + len(small)),
        out_shape=[jax.ShapeDtypeStruct(moment.shape, f32)] * 2
        + [jax.ShapeDtypeStruct(array.shape, f32) for array in small],
        compiler_params=pltpu.CompilerParams(vmem_limit_bytes=56 * 2**20),
        name="muon",
    )(grad, totals, moment, master, *small)


def pad_to(array, rows, columns):
    return jnp.pad(array, ((0, rows - array.shape[0]), (0, columns - array.shape[1])))


def swap(values, bit):
    return lax.ppermute(values, "tensor", [(t, t ^ bit) for t in range(4)])


def place_half(full, half):
    core = lax.axis_index("tensor") % 2
    return lax.dynamic_update_slice(full, swap(half, 1), ((1 - core) * half.shape[0], 0))


def per_device(
    hidden_in,
    out_grad,
    seq_lengths,
    owner_map,
    muon_master,
    muon_moment,
    state_proj,
    state_moment,
    step_proj,
    step_moment,
    norm_gain,
    gain_moment,
    head_params,
    head_moment,
    conv_params,
    conv_moment,
    state_conv,
    state_conv_moment,
):
    tok_rows, width = hidden_in.shape
    heads = step_proj.shape[1]
    inner = conv_params.shape[1]
    dp_size = lax.axis_size("dp")
    inner_all = inner * lax.axis_size("tensor")
    slots = muon_master.shape[0] * dp_size
    core = lax.axis_index("tensor") % 2
    chip = lax.axis_index("tensor") // 2
    ends = jnp.concatenate([jnp.cumsum(seq_lengths[0], dtype=jnp.int32), core[None].astype(jnp.int32)])
    seq_count = seq_lengths.shape[1]
    master = muon_master.transpose(0, 2, 1)
    moment = muon_moment.transpose(0, 2, 1)
    stack = gather_call(master.astype(bf16), dp_size)
    narrow = pad_to(jnp.concatenate([state_proj, step_proj], axis=1), width, NARROW).astype(bf16)
    gain = norm_gain[None, :]
    head_rows = pad_to(head_params, 8, LANES)
    conv_rows = pad_to(conv_params, 8, inner)
    shared_rows = pad_to(state_conv, 8, state_conv.shape[1])
    free = jnp.all(owner_map[None, :] != jnp.arange(slots, dtype=jnp.int32)[:, None], axis=1)
    free = free.astype(jnp.int32)
    group_rows = 8 * (dp_size // 2)
    extra_rows = -(-(HEADDIM + 32) // group_rows) * group_rows - HEADDIM

    normed, *saved, sums, mine, other = forward_call(
        owner_map, ends, hidden_in, out_grad, stack, gain, narrow, head_rows, conv_rows, shared_rows, heads
    )
    sums, near = exchange_call(sums, mine, other)
    far = swap(near, 2)
    dboth, scaled, mine, other, mine_narrow, other_narrow, extra = backward_call(
        owner_map, ends, hidden_in, saved, sums, stack, narrow, gain, head_rows, conv_rows, shared_rows, heads,
        inner_all, extra_rows,
    )

    got = swap(other, 1)
    got_narrow = swap(other_narrow, 1)
    far, scaled = lax.optimization_barrier((far, scaled))
    rows_spec = pl.BlockSpec((8, SUB), lambda i, ends: (0, ends[seq_count] * (tok_rows // SUB // 2) + i))
    block_full, block_half = half_call(
        functools.partial(branch_kernel, inner_all, seq_count), "block_out", ends, [near, far], [hidden_in],
        ([sums], [rows_spec]),
    )
    block_out = place_half(block_full, block_half)
    scaled, block_half = lax.optimization_barrier((scaled, block_half))
    slotted = grads_call(owner_map, ends, free, scaled, out_grad, 2 * heads, True, None)
    slotted, got, got_narrow = lax.optimization_barrier((slotted, got, got_narrow))
    pair = mine_narrow + got_narrow
    near_narrow = lax.dynamic_index_in_dim(pair, chip, 0, keepdims=False)
    send_narrow = lax.dynamic_index_in_dim(pair, 1 - chip, 0, keepdims=False)
    far_narrow = swap(send_narrow, 2)
    send_narrow, got = lax.optimization_barrier((send_narrow, got))
    near_grad = (mine.astype(f32) + got.astype(f32)).astype(bf16)
    far_grad = swap(near_grad, 2)
    near_grad, near_narrow, dboth = lax.optimization_barrier((near_grad, near_narrow, dboth))
    slotted = grads_call(owner_map, ends, free, dboth, normed, 0, False, slotted)
    owned, totals = reduce_call(slotted, near_narrow, far_narrow, extra, dp_size)
    owned, totals, far_grad = lax.optimization_barrier((owned, totals, far_grad))
    gain_spec = pl.BlockSpec(gain.shape, lambda i, ends: (0, 0))
    input_full, input_half = half_call(
        functools.partial(input_kernel, seq_count), "input_grad", ends, [near_grad, far_grad],
        [hidden_in, out_grad], ([gain], [gain_spec]),
    )
    input_grad = place_half(input_full, input_half)
    owned, input_half = lax.optimization_barrier((owned, input_half))
    small = [
        state_moment, state_proj, step_moment.T, step_proj.T, gain_moment[None, :], gain, head_moment,
        head_params, conv_moment, conv_params, state_conv_moment, state_conv,
    ]
    moment_new, master_new, *small_new = muon_call(owned, totals, moment, master, small, tok_rows * dp_size)
    state_moment_new, state_proj_new, step_moment_new, step_proj_new = small_new[:4]
    gain_moment_new, norm_gain_new, head_moment_new, head_params_new = small_new[4:8]
    conv_moment_new, conv_params_new, state_conv_moment_new, state_conv_new = small_new[8:]
    step_moment_new, step_proj_new = step_moment_new.T, step_proj_new.T
    gain_moment_new, norm_gain_new = gain_moment_new[0], norm_gain_new[0]
    return (
        block_out,
        input_grad,
        moment_new.transpose(0, 2, 1),
        master_new.transpose(0, 2, 1),
        state_moment_new,
        state_proj_new,
        step_moment_new,
        step_proj_new,
        gain_moment_new,
        norm_gain_new,
        head_moment_new,
        head_params_new,
        conv_moment_new,
        conv_params_new,
        state_conv_moment_new,
        state_conv_new,
    )


def solution(mesh):
    in_specs = (
        P("dp", None),
        P("dp", None),
        P("dp", None),
        P(),
        P("dp", None, "tensor"),
        P("dp", None, "tensor"),
        P(),
        P(),
        P(None, "tensor"),
        P(None, "tensor"),
        P(),
        P(),
        P(None, "tensor"),
        P(None, "tensor"),
        P(None, "tensor"),
        P(None, "tensor"),
        P(),
        P(),
    )
    out_specs = (
        P("dp", None),
        P("dp", None),
        P("dp", None, "tensor"),
        P("dp", None, "tensor"),
        P(),
        P(),
        P(None, "tensor"),
        P(None, "tensor"),
        P(),
        P(),
        P(None, "tensor"),
        P(None, "tensor"),
        P(None, "tensor"),
        P(None, "tensor"),
        P(),
        P(),
    )
    return jax.shard_map(
        per_device, mesh=mesh, in_specs=in_specs, out_specs=out_specs, check_vma=False
    )
```

```python
import functools
import math

import jax
import jax.numpy as jnp
from jax import lax
from jax.experimental import pallas as pl
from jax.experimental.pallas import tpu as pltpu
from jax.sharding import PartitionSpec as P

HEADDIM = 64
NS_STEPS = 5
ROWS = 256
SUB = 128
LANES = 128
NARROW = 384
CHUNK = 768
GAIN_ROW, SHARED_ROW, HEAD_ROW = 19, 20, 21
AHEAD = 5
HALF_ROWS = 256

exact_mode = lax.Precision.HIGHEST
norm_eps = 1e-05
schulz_coefs = (3.4445, -4.775, 2.0315)
muon_decay = 0.95
muon_rate = 0.02
small_decay = 0.9
small_rate = 2.0
log2_e = 1.4426950408889634
f32 = jnp.float32
bf16 = jnp.bfloat16
far_below = -1e30


def dot_nn(left, right, precision=None):
    return lax.dot_general(
        left, right, (((1,), (0,)), ((), ())), precision=precision, preferred_element_type=f32
    )


def dot_nt(left, right, precision=None):
    return lax.dot_general(
        left, right, (((1,), (1,)), ((), ())), precision=precision, preferred_element_type=f32
    )


def dot_tn(left, right, precision=None):
    return lax.dot_general(
        left, right, (((0,), (0,)), ((), ())), precision=precision, preferred_element_type=f32
    )


def dot_pieces(ones, values):
    total = None
    for _ in range(3):
        piece = values.astype(bf16)
        values = values - piece.astype(f32)
        part = dot_nn(ones, piece)
        total = part if total is None else total + part
    return total


def sigmoid(values):
    return 0.5 * jnp.tanh(0.5 * values) + 0.5


def iota(shape, dim):
    return lax.broadcasted_iota(jnp.int32, shape, dim)


def segment_at(place, ends_ref, count):
    total = (place >= ends_ref[0]).astype(jnp.int32)
    for k in range(1, count):
        total = total + (place >= ends_ref[k]).astype(jnp.int32)
    return total


def step_terms(step_part, head_ref):
    shifted = step_part + head_ref[0:1, :]
    small = jnp.exp(-jnp.abs(shifted))
    tail = jnp.where(
        small < 0.01, small * (1.0 - small * (0.5 - small * (1.0 / 3.0))), jnp.log(1.0 + small)
    )
    step = jnp.maximum(shifted, 0.0) + tail
    decay = -jnp.exp(head_ref[1:2, :])
    log_rate = step * (decay * log2_e)
    lower = (iota((SUB, SUB), 0) >= iota((SUB, SUB), 1)).astype(bf16)
    cum = dot_pieces(lower, log_rate)
    source = cum - jnp.log(step) * log2_e
    return shifted, step, decay, cum, source


def expand(values, pair):
    shape = (values.shape[0], LANES)
    low = jnp.broadcast_to(values[:, 2 * pair : 2 * pair + 1], shape)
    high = jnp.broadcast_to(values[:, 2 * pair + 1 : 2 * pair + 2], shape)
    return jnp.where(iota(shape, 1) < HEADDIM, low, high)


def split_pair(values):
    low = iota(values.shape, 1) < HEADDIM
    zero = jnp.zeros_like(values)
    return jnp.where(low, values, zero), jnp.where(low, zero, values)


def lanes_of(pair):
    return slice(pair * LANES, (pair + 1) * LANES)


def shift_mask(place, shift, ends_ref, count, rows_all):
    other = place + shift
    inside = (other >= 0) & (other < rows_all)
    same = segment_at(place, ends_ref, count) == segment_at(other, ends_ref, count)
    return jnp.where(inside & same, 1.0, 0.0).astype(f32)


def conv_tile(buf_ref, first, lanes, taps, masks):
    total = taps[4:5, :] + taps[3:4, :] * buf_ref[first + 8 : first + 8 + SUB, lanes]
    for back in (1, 2, 3):
        rows = buf_ref[first + 8 - back : first + 8 - back + SUB, lanes]
        total = total + taps[3 - back : 4 - back, :] * (rows * masks[back - 1])
    return total


def block_terms(base, ends_ref, count):
    row_at = base + iota((SUB, SUB), 0)
    col_at = base + iota((SUB, SUB), 1)
    seg_row = segment_at(row_at, ends_ref, count)
    seg_col = segment_at(col_at, ends_ref, count)
    seg_last = segment_at(base + SUB - 1, ends_ref, count)
    seg_before = jnp.where(base == 0, -1, segment_at(base - 1, ends_ref, count))
    carried = jnp.where(seg_row == seg_before, 1.0, 0.0).astype(f32)
    tail_same = jnp.where(seg_row == seg_last, 1.0, 0.0).astype(f32)
    through = jnp.where(seg_last == seg_before, 1.0, 0.0).astype(f32)
    same = seg_row == seg_col
    return row_at, col_at, same, carried, tail_same, through


def store_half(values, block, blocks, core, mine_ref, other_ref):
    is_mine = block // (blocks // 2) == core

    @pl.when(is_mine)
    def _():
        mine_ref[...] = values

    @pl.when(jnp.logical_not(is_mine))
    def _():
        other_ref[...] = values


def half_specs(width, blocks, seq_count, block_of):
    def index(half, block):
        return jnp.where(half == 0, jnp.minimum(block, blocks // 2 - 1), jnp.maximum(block - blocks // 2, 0))

    def mine(i, place, ends):
        return (index(ends[seq_count], block_of(i)), 0)

    def other(i, place, ends):
        return (index(1 - ends[seq_count], block_of(i)), 0)

    return [pl.BlockSpec((ROWS, width), mine), pl.BlockSpec((ROWS, width), other)]


def load_weights(stack_ref, place_ref, held_ref, sems, first, count):
    copies = []
    for m in range(count):
        copies.append(
            pltpu.make_async_copy(
                stack_ref.at[place_ref[first + m]],
                held_ref.at[pl.ds(m * HEADDIM, HEADDIM)],
                sems.at[m],
            )
        )
    for copy in copies:
        copy.start()
    return copies


def fold_rows(values):
    return jnp.sum(values.reshape(values.shape[0] // 8, 8, values.shape[1]), axis=0)


def saved_views(low_ref, high_ref, inner):
    wide = [low_ref.at[:, k * inner : (k + 1) * inner] for k in range(5)]
    shared = [
        low_ref.at[:, 5 * inner + 2 * LANES * k : 5 * inner + 2 * LANES * (k + 1)] for k in range(3)
    ]
    return (*wide, *shared, high_ref.at[:, 0:inner], high_ref.at[:, inner : inner + LANES])


def project_units(normed_ref, cot_ref, narrow_ref, weights, targets, row_at, last_end, inner):
    next_gate, next_in, next_scaled, next_narrow = targets
    units = []

    def one(target, at, weight_row, left_ref, masked):
        def unit():
            part = dot_nt(left_ref[...], weights[weight_row + at : weight_row + at + 2 * LANES, :])
            if masked:
                part = jnp.where(row_at < last_end, part, 0.0)
            target[:, at : at + 2 * LANES] = part.astype(bf16)

        return unit

    for at in range(0, inner, 2 * LANES):
        units.append(one(next_in, at, inner, normed_ref, False))
    units.append(lambda: next_narrow.__setitem__(Ellipsis, dot_nn(normed_ref[...], narrow_ref[...])))
    for at in range(0, inner, 2 * LANES):
        units.append(one(next_gate, at, 0, normed_ref, False))
        units.append(one(next_scaled, at, 2 * inner, cot_ref, True))
    return units


def forward_kernel(
    heads, seq_count, rows_all,
    place_ref, ends_ref,
    hidden_ref, cot_ref, stack_ref, gain_ref, narrow_ref, head_ref, conv_ref, shared_ref,
    normed_ref, low_ref, high_ref, state_ref, sums_ref, mine_ref, other_ref,
    weights, sems, in_buf, shared_buf, next_gate, next_in, next_scaled,
    next_narrow, state, low_buf, tail_buf, across,
):
    gate_ref, input_ref, x_ref, slope_ref, dscaled_ref, shared_in_ref, bc_ref, bc_slope_ref, mixed_ref, step_ref = (
        saved_views(low_ref, high_ref, heads * HEADDIM)
    )
    turn = pl.program_id(0)
    blocks = pl.num_programs(0) - 1
    block = turn - 1
    inner = heads * HEADDIM
    pairs = heads // 2

    def normalize():
        hidden = hidden_ref[...].astype(f32)
        inv_rms = lax.rsqrt(jnp.mean(hidden * hidden, axis=1, keepdims=True) + norm_eps)
        normed_ref[...] = (hidden * inv_rms * gain_ref[0:1, :]).astype(bf16)

    row_here = jnp.minimum(turn, blocks - 1) * ROWS + iota((ROWS, 2 * LANES), 0)
    targets = (next_gate, next_in, next_scaled, next_narrow)
    units = project_units(
        normed_ref, cot_ref, narrow_ref, weights, targets, row_here, ends_ref[seq_count - 1], inner
    )

    def take_next():
        in_buf[0:8, :] = in_buf[ROWS : ROWS + 8, :]
        shared_buf[0:8, :] = shared_buf[ROWS : ROWS + 8, :]
        in_buf[8:, :] = next_in[...].astype(f32)
        input_ref[...] = next_in[...]
        gate_ref[...] = next_gate[...]
        dscaled_ref[...] = next_scaled[...]
        shared_buf[8:, :] = next_narrow[:, 0 : 2 * LANES]
        shared_in_ref[...] = next_narrow[:, 0 : 2 * LANES].astype(bf16)
        step_ref[...] = next_narrow[:, 2 * LANES : 3 * LANES]

    @pl.when(turn == 0)
    def _():
        copies = load_weights(stack_ref, place_ref, weights, sems, 0, 3 * heads)
        in_buf[ROWS : ROWS + 8, :] = jnp.zeros((8, inner), f32)
        shared_buf[ROWS : ROWS + 8, :] = jnp.zeros((8, 2 * LANES), f32)
        state[...] = jnp.zeros_like(state)
        normalize()
        for copy in copies:
            copy.wait()
        for unit in units:
            unit()

    @pl.when(turn > 0)
    def _():
        take_next()
        normalize()
        pending = list(units)
        first_row = block * ROWS
        for sub in range(ROWS // SUB):
            first = sub * SUB
            here = slice(first, first + SUB)
            base = first_row + first
            row_at, col_at, same, carried, tail_same, through = block_terms(base, ends_ref, seq_count)
            causal = jnp.where(same & (row_at >= col_at), 0.0, far_below).astype(f32)
            masks = [shift_mask(row_at, -back, ends_ref, seq_count, rows_all) for back in (1, 2, 3)]
            bc = []
            for part in range(2):
                lanes = lanes_of(part)
                u = conv_tile(shared_buf, first, lanes, shared_ref[:, lanes], masks)
                sig = sigmoid(u)
                bc.append((u * sig).astype(bf16))
                bc_ref[here, lanes] = bc[part]
                bc_slope_ref[here, lanes] = (sig * (1.0 + u * (1.0 - sig))).astype(bf16)
            b_low, c_low = bc
            _, _, _, cum, source = step_terms(step_ref[here, :], head_ref)
            source_row = source.T
            scores = dot_nt(c_low, b_low)
            cum_last = cum[SUB - 1 : SUB, :]
            entry = jnp.exp2(cum) * carried
            leave = jnp.exp2(cum_last - source) * tail_same
            pass_on = jnp.exp2(cum_last) * through
            state_low = state[...].astype(bf16)
            state_ref[sub] = state_low
            across[...] = dot_nn(c_low, state_low)
            square = jnp.zeros((SUB, LANES), f32)
            inner_dot = jnp.zeros((SUB, LANES), f32)
            for pair in range(pairs):
                if pending:
                    pending.pop(0)()
                lanes = lanes_of(pair)
                u = conv_tile(in_buf, first, lanes, conv_ref[:, lanes], masks)
                sig = sigmoid(u)
                x_low = (u * sig).astype(bf16)
                x_ref[here, lanes] = x_low
                slope_ref[here, lanes] = (sig * (1.0 + u * (1.0 - sig))).astype(bf16)
                x = x_low.astype(f32)
                mats = []
                for h in (2 * pair, 2 * pair + 1):
                    gap = cum[:, h : h + 1] - source_row[h : h + 1, :]
                    mats.append((jnp.exp2(gap + causal) * scores).astype(bf16))
                x_a, x_b = split_pair(x_low)
                mixed = dot_nn(jnp.concatenate(mats, axis=1), jnp.concatenate([x_a, x_b], axis=0))
                mixed = mixed + across[:, lanes] * expand(entry, pair)
                mixed = mixed + expand(head_ref[2:3, :], pair) * x
                mixed_ref[here, lanes] = mixed
                gate = gate_ref[here, lanes].astype(f32)
                gated = mixed * (gate * sigmoid(gate))
                gated_gain = gated * conv_ref[5:6, lanes]
                low_buf[here, lanes] = gated_gain.astype(bf16)
                square = square + gated * gated
                inner_dot = inner_dot + dscaled_ref[here, lanes].astype(f32) * gated_gain
                tail_buf[:, lanes] = (x * expand(leave, pair)).astype(bf16)
            fresh = dot_tn(b_low, tail_buf[...])
            for pair in range(pairs):
                lanes = lanes_of(pair)
                state[:, lanes] = state[:, lanes] * expand(pass_on, pair) + fresh[:, lanes]
            sums_ref[0:1, here] = jnp.sum(square.T, axis=0, keepdims=True)
            sums_ref[1:2, here] = jnp.sum(inner_dot.T, axis=0, keepdims=True)
        while pending:
            pending.pop(0)()
        sums_ref[2:8, :] = jnp.zeros((6, ROWS), f32)
        part = dot_nn(low_buf[...], weights[2 * inner : 3 * inner, :]).astype(bf16)
        store_half(part, block, blocks, ends_ref[seq_count], mine_ref, other_ref)


def forward_call(place, ends, hidden, cot, stack, gain, narrow, head_rows, conv_rows, shared_rows, heads):
    rows_all, width = hidden.shape
    inner = heads * HEADDIM
    blocks = rows_all // ROWS

    def ahead(columns):
        return pl.BlockSpec((ROWS, columns), lambda i, *_: (jnp.minimum(i, blocks - 1), 0))

    def rows(columns):
        return pl.BlockSpec((ROWS, columns), lambda i, *_: (jnp.maximum(i - 1, 0), 0))

    whole = pl.BlockSpec(memory_space=pltpu.VMEM)
    columns = [(5 * inner + 6 * LANES, bf16), (inner + LANES, f32)]
    out_shape = [
        jax.ShapeDtypeStruct((rows_all, width), bf16),
        *[jax.ShapeDtypeStruct((rows_all, count), kind) for count, kind in columns],
        jax.ShapeDtypeStruct((rows_all // SUB, LANES, inner), bf16),
        jax.ShapeDtypeStruct((8, rows_all), f32),
        jax.ShapeDtypeStruct((rows_all // 2, width), bf16),
        jax.ShapeDtypeStruct((rows_all // 2, width), bf16),
    ]
    out_specs = [
        ahead(width),
        *[rows(count) for count, _ in columns],
        pl.BlockSpec((ROWS // SUB, LANES, inner), lambda i, *_: (jnp.maximum(i - 1, 0), 0, 0)),
        pl.BlockSpec((8, ROWS), lambda i, *_: (0, jnp.maximum(i - 1, 0))),
        *half_specs(width, blocks, ends.shape[0] - 1, lambda i: jnp.maximum(i - 1, 0)),
    ]
    return pl.pallas_call(
        functools.partial(forward_kernel, heads, ends.shape[0] - 1, rows_all),
        grid_spec=pltpu.PrefetchScalarGridSpec(
            num_scalar_prefetch=2,
            grid=(blocks + 1,),
            in_specs=[
                ahead(width), ahead(width), pl.BlockSpec(memory_space=pl.ANY), whole, whole, whole, whole, whole,
            ],
            out_specs=out_specs,
            scratch_shapes=[
                pltpu.VMEM((3 * inner, width), bf16),
                pltpu.SemaphoreType.DMA((3 * heads,)),
                pltpu.VMEM((ROWS + 8, inner), f32),
                pltpu.VMEM((ROWS + 8, 2 * LANES), f32),
                pltpu.VMEM((ROWS, inner), bf16),
                pltpu.VMEM((ROWS, inner), bf16),
                pltpu.VMEM((ROWS, inner), bf16),
                pltpu.VMEM((ROWS, NARROW), f32),
                pltpu.VMEM((LANES, inner), f32),
                pltpu.VMEM((ROWS, inner), bf16),
                pltpu.VMEM((SUB, inner), bf16),
                pltpu.VMEM((SUB, inner), f32),
            ],
        ),
        out_shape=out_shape,
        compiler_params=pltpu.CompilerParams(
            dimension_semantics=("arbitrary",), vmem_limit_bytes=56 * 2**20
        ),
        cost_estimate=pl.CostEstimate(
            flops=2 * rows_all * width * (4 * inner + NARROW), bytes_accessed=60 * 2**20, transcendentals=0
        ),
        name="mixer_forward",
    )(place, ends, hidden, cot, stack, gain, narrow, head_rows, conv_rows, shared_rows)


def backward_kernel(
    heads, seq_count, rows_all, inner_all,
    place_ref, ends_ref,
    hidden_ref, low_ref, high_ref, state_ref, sums_ref,
    stack_ref, narrow_ref, gain_ref, head_ref, conv_ref, shared_ref,
    dboth_ref, scaled_ref, mine_ref, other_ref, mine_narrow_ref, other_narrow_ref, extra_ref,
    weights, sems, du_buf, dshared_buf, dstate, state_after, from_state, terms, source_terms, tail_buf,
    entry_buf, dnarrow_buf, last_both, last_narrow, dn_buf, conv_grad, shared_grad, head_grad, skip_grad,
    gain_grad, narrow_grad_ref,
):
    gate_ref, input_ref, x_ref, slope_ref, dscaled_ref, shared_in_ref, bc_ref, bc_slope_ref, mixed_ref, step_ref = (
        saved_views(low_ref, high_ref, heads * HEADDIM)
    )
    turn = pl.program_id(0)
    blocks = pl.num_programs(0) - 1
    block = blocks - 1 - turn
    inner = heads * HEADDIM
    pairs = heads // 2
    width = hidden_ref.shape[1]
    wide = 2 * LANES

    @pl.when(turn == 0)
    def _():
        copies = load_weights(stack_ref, place_ref, weights, sems, 0, 2 * heads)
        du_buf[ROWS:, :] = jnp.zeros((8, inner), f32)
        dshared_buf[ROWS:, :] = jnp.zeros((8, 2 * LANES), f32)
        for ref in (
            dstate, state_after, last_both, last_narrow, conv_grad, shared_grad, head_grad, skip_grad,
            gain_grad, narrow_grad_ref,
        ):
            ref[...] = jnp.zeros_like(ref)
        for copy in copies:
            copy.wait()

    def row_units():
        hidden = hidden_ref[...].astype(f32)
        inv_rms = lax.rsqrt(jnp.mean(hidden * hidden, axis=1, keepdims=True) + norm_eps)

        narrow_turned = last_narrow[...].T

        def one(at):
            columns = slice(at, at + wide)

            def unit():
                part = dot_nn(last_both[...], weights[:, columns])
                part = part + dot_nt(last_narrow[...], narrow_ref[columns, :])
                dn_buf[:, columns] = part.astype(bf16)
                unit_rows = hidden_ref[:, columns].astype(f32) * inv_rms
                gain_grad[:, columns] += fold_rows(part * unit_rows)
                normed = (unit_rows * gain_ref[0:1, columns]).astype(bf16)
                narrow_grad_ref[:, columns] += dot_nn(narrow_turned, normed)

            return unit

        return [one(at) for at in range(0, width, wide)]

    def finish_rows():
        store_half(dn_buf[...], block + 1, blocks, ends_ref[seq_count], mine_ref, other_ref)

    @pl.when(turn < blocks)
    def _():
        pending = row_units()
        reduce_heads = (iota((inner, LANES), 0) // HEADDIM == iota((inner, LANES), 1)).astype(bf16)
        first_row = block * ROWS
        kept = []
        for sub in reversed(range(ROWS // SUB)):
            first = sub * SUB
            here = slice(first, first + SUB)
            base = first_row + first
            row_at, col_at, same, carried, tail_same, through = block_terms(base, ends_ref, seq_count)
            causal = jnp.where(same & (row_at <= col_at), 0.0, far_below).astype(f32)
            b_low, c_low = bc_ref[here, 0:LANES], bc_ref[here, LANES : 2 * LANES]
            shifted, step, decay, cum, source = step_terms(step_ref[here, :], head_ref)
            kept.append((here, shifted, step, decay))
            cum_row = cum.T
            scores = dot_nt(b_low, c_low)
            cum_last = cum[SUB - 1 : SUB, :]
            entry = jnp.exp2(cum) * carried
            leave = jnp.exp2(cum_last - source) * tail_same
            pass_on = jnp.exp2(cum_last) * through
            inv_row = lax.rsqrt(sums_ref[0:1, here] * (1.0 / inner_all) + norm_eps)
            fix_row = inv_row * inv_row * inv_row * sums_ref[1:2, here] * (1.0 / inner_all)
            inv = jnp.broadcast_to(inv_row, (SUB, SUB)).T
            fix = jnp.broadcast_to(fix_row, (SUB, SUB)).T
            dstate_low = dstate[...].astype(bf16)
            from_state[...] = dot_nn(b_low, dstate_low)
            dscores = jnp.zeros((SUB, SUB), f32)
            for pair in range(pairs):
                if pending and pair % 2 == 1:
                    pending.pop(0)()
                lanes = lanes_of(pair)
                x_low = x_ref[here, lanes]
                x = x_low.astype(f32)
                slope = slope_ref[here, lanes].astype(f32)
                gate = gate_ref[here, lanes].astype(f32)
                gate_sig = sigmoid(gate)
                gate_silu = gate * gate_sig
                mixed = mixed_ref[here, lanes]
                gated = mixed * gate_silu
                gain = conv_ref[5:6, lanes]
                dscaled = dscaled_ref[here, lanes].astype(f32)
                normal = gated * inv
                scaled_ref[here, lanes] = (normal * gain).astype(bf16)
                conv_grad[5, :, lanes] += fold_rows(dscaled * normal)
                dgated = inv * (dscaled * gain) - gated * fix
                dgate = dgated * mixed * (gate_sig * (1.0 + gate * (1.0 - gate_sig)))
                dboth_ref[here, lanes] = dgate.astype(bf16)
                dmixed = dgated * gate_silu
                dy_low = dmixed.astype(bf16)
                dy = dy_low.astype(f32)
                skip = expand(head_ref[2:3, :], pair)
                skip_grad[:, lanes] += fold_rows(dmixed * x)
                x_parts = split_pair(x_low)
                dy_parts = split_pair(dy_low)
                mats = []
                for k in range(2):
                    h = 2 * pair + k
                    gap = cum_row[h : h + 1, :] - source[:, h : h + 1]
                    decays = jnp.exp2(gap + causal)
                    mats.append((decays * scores).astype(bf16))
                    dscores = dscores + dot_nt(x_parts[k], dy_low) * decays
                dx = dot_nn(jnp.concatenate(mats, axis=1), jnp.concatenate(dy_parts, axis=0))
                leave_here = expand(leave, pair)
                dx = dx + leave_here * from_state[:, lanes]
                source_term = x * dx
                source_terms[here, lanes] = source_term
                terms[here, lanes] = dy * (mixed - skip * x) - source_term
                tail_buf[:, lanes] = (x * leave_here).astype(bf16)
                entry_buf[:, lanes] = (dy * expand(entry, pair)).astype(bf16)
                du_buf[here, lanes] = (dx + skip * dmixed) * slope
            state_low = state_ref[sub]
            dscores_low = dscores.astype(bf16)
            db = dot_nn(dscores_low, c_low) + dot_nt(tail_buf[...], dstate_low)
            dc = dot_tn(dscores_low, b_low) + dot_nt(entry_buf[...], state_low)
            dshared_buf[here, 0:LANES] = db * bc_slope_ref[here, 0:LANES].astype(f32)
            dshared_buf[here, LANES:wide] = dc * bc_slope_ref[here, LANES:wide].astype(f32)
            at_end = jnp.sum(dstate[...] * state_after[...].astype(f32), axis=0, keepdims=True)
            terms[first + SUB - 1 : first + SUB, :] += at_end
            state_after[...] = state_low
            fresh = dot_tn(c_low, entry_buf[...])
            for pair in range(pairs):
                lanes = lanes_of(pair)
                dstate[:, lanes] = dstate[:, lanes] * expand(pass_on, pair) + fresh[:, lanes]
        while pending:
            pending.pop(0)()

        both = jnp.concatenate([terms[...], source_terms[...]], axis=0)
        high = both.astype(bf16)
        low = (both - high.astype(f32)).astype(bf16)
        reduced = dot_nn(high, reduce_heads) + dot_nn(low, reduce_heads)
        upper = (iota((SUB, SUB), 0) <= iota((SUB, SUB), 1)).astype(bf16)

        for sub in range(ROWS // SUB):
            first = sub * SUB
            here = slice(first, first + SUB)
            row_at = first_row + first + iota((SUB, LANES), 0)
            ahead = [shift_mask(row_at, k, ends_ref, seq_count, rows_all) for k in (1, 2, 3)]
            groups = [(pair, True) for pair in range(pairs)] + [(0, False), (1, False)]
            for group, is_wide in groups:
                lanes = lanes_of(group)
                grads, held = (du_buf, input_ref) if is_wide else (dshared_buf, shared_in_ref)
                taps = conv_ref[:, lanes] if is_wide else shared_ref[:, lanes]
                sums = conv_grad if is_wide else shared_grad
                du = grads[here, lanes]
                v = held[here, lanes].astype(f32)
                dv = taps[3:4, :] * du
                sums[3, :, lanes] += fold_rows(du * v)
                sums[4, :, lanes] += fold_rows(du)
                for k in (1, 2, 3):
                    moved = grads[first + k : first + k + SUB, lanes] * ahead[k - 1]
                    dv = dv + taps[3 - k : 4 - k, :] * moved
                    sums[3 - k, :, lanes] += fold_rows(moved * v)
                if is_wide:
                    dboth_ref[here, inner + group * LANES : inner + (group + 1) * LANES] = dv.astype(bf16)
                else:
                    dnarrow_buf[here, lanes] = dv.astype(bf16)
        for here, shifted, step, decay in kept:
            dcum = reduced[here]
            from_source = reduced[ROWS + here.start : ROWS + here.stop]
            dlog = dot_pieces(upper, dcum)
            sig = sigmoid(shifted)
            ratio = jnp.where(shifted < -15.0, 1.0, sig / step)
            dlog_decay = dlog * decay
            dstep = from_source * ratio + dlog_decay * sig
            dnarrow_buf[here, wide:NARROW] = dstep.astype(bf16)
            head_grad[0] += fold_rows(dstep)
            head_grad[1] += fold_rows(dlog_decay * step)
        du_buf[ROWS:, :] = du_buf[0:8, :]
        dshared_buf[ROWS:, :] = dshared_buf[0:8, :]

        @pl.when(turn > 0)
        def _():
            finish_rows()

        last_both[...] = dboth_ref[...]
        last_narrow[...] = dnarrow_buf[...]

    @pl.when(turn == blocks)
    def _():
        for unit in row_units():
            unit()
        finish_rows()
        extra_ref[...] = jnp.zeros_like(extra_ref)
        extra_ref[0:16, :] = narrow_grad_ref[wide : wide + 16, :]
        core = ends_ref[seq_count]
        for k in range(2):
            near = pl.multiple_of((2 * k + core) * HEADDIM, HEADDIM)
            far = pl.multiple_of((2 * k + 1 - core) * HEADDIM, HEADDIM)
            mine_narrow_ref[k] = narrow_grad_ref[pl.ds(near, HEADDIM), :]
            other_narrow_ref[k] = narrow_grad_ref[pl.ds(far, HEADDIM), :]
        per_line = width // inner

        def total(values):
            return jnp.sum(values, axis=0, keepdims=True)

        for k in range(6):
            at = (k % per_line) * inner
            row = 16 + k // per_line
            extra_ref[row : row + 1, at : at + inner] = total(conv_grad[k])
        extra_ref[GAIN_ROW : GAIN_ROW + 1, :] = total(gain_grad[...])
        for k in range(5):
            extra_ref[SHARED_ROW : SHARED_ROW + 1, wide * k : wide * (k + 1)] = total(shared_grad[k])
        for k in range(2):
            extra_ref[HEAD_ROW + k : HEAD_ROW + k + 1, 0:LANES] = total(head_grad[k])
        reduce_all = (iota((inner, LANES), 0) // HEADDIM == iota((inner, LANES), 1)).astype(f32)
        skip_sum = dot_nn(skip_grad[...], reduce_all, exact_mode)
        extra_ref[HEAD_ROW + 2 : HEAD_ROW + 3, 0:LANES] = total(skip_sum)


def backward_call(
    place, ends, hidden, saved, sums, stack, narrow, gain, head_rows, conv_rows, shared_rows, heads,
    inner_all, extra_rows,
):
    rows_all, width = hidden.shape
    inner = heads * HEADDIM
    blocks = rows_all // ROWS

    def rows(columns):
        return pl.BlockSpec((ROWS, columns), lambda i, *_: (jnp.maximum(blocks - 1 - i, 0), 0))

    def behind(i):
        return jnp.minimum(blocks - i, blocks - 1)

    whole = pl.BlockSpec(memory_space=pltpu.VMEM)
    out_shape = [
        jax.ShapeDtypeStruct((rows_all, 2 * inner), bf16),
        jax.ShapeDtypeStruct((rows_all, inner), bf16),
        jax.ShapeDtypeStruct((rows_all // 2, width), bf16),
        jax.ShapeDtypeStruct((rows_all // 2, width), bf16),
        jax.ShapeDtypeStruct((2, HEADDIM, width), f32),
        jax.ShapeDtypeStruct((2, HEADDIM, width), f32),
        jax.ShapeDtypeStruct((extra_rows, width), f32),
    ]
    out_specs = [
        rows(2 * inner), rows(inner),
        *half_specs(width, blocks, ends.shape[0] - 1, behind),
        whole, whole, whole,
    ]
    return pl.pallas_call(
        functools.partial(backward_kernel, heads, ends.shape[0] - 1, rows_all, inner_all),
        grid_spec=pltpu.PrefetchScalarGridSpec(
            num_scalar_prefetch=2,
            grid=(blocks + 1,),
            in_specs=[
                pl.BlockSpec((ROWS, width), lambda i, *_: (behind(i), 0)),
                *[rows(array.shape[1]) for array in saved[:-1]],
                pl.BlockSpec(
                    (ROWS // SUB, LANES, inner), lambda i, *_: (jnp.maximum(blocks - 1 - i, 0), 0, 0)
                ),
                pl.BlockSpec((8, ROWS), lambda i, *_: (0, jnp.maximum(blocks - 1 - i, 0))),
                pl.BlockSpec(memory_space=pl.ANY), whole, whole, whole, whole, whole,
            ],
            out_specs=out_specs,
            scratch_shapes=[
                pltpu.VMEM((2 * inner, width), bf16),
                pltpu.SemaphoreType.DMA((2 * heads,)),
                pltpu.VMEM((ROWS + 8, inner), f32),
                pltpu.VMEM((ROWS + 8, 2 * LANES), f32),
                pltpu.VMEM((LANES, inner), f32),
                pltpu.VMEM((LANES, inner), bf16),
                pltpu.VMEM((SUB, inner), f32),
                pltpu.VMEM((ROWS, inner), f32),
                pltpu.VMEM((ROWS, inner), f32),
                pltpu.VMEM((SUB, inner), bf16),
                pltpu.VMEM((SUB, inner), bf16),
                pltpu.VMEM((ROWS, NARROW), bf16),
                pltpu.VMEM((ROWS, 2 * inner), bf16),
                pltpu.VMEM((ROWS, NARROW), bf16),
                pltpu.VMEM((ROWS, width), bf16),
                pltpu.VMEM((6, 8, inner), f32),
                pltpu.VMEM((5, 8, 2 * LANES), f32),
                pltpu.VMEM((2, 8, LANES), f32),
                pltpu.VMEM((8, inner), f32),
                pltpu.VMEM((8, width), f32),
                pltpu.VMEM((NARROW, width), f32),
            ],
        ),
        out_shape=out_shape,
        compiler_params=pltpu.CompilerParams(
            dimension_semantics=("arbitrary",), vmem_limit_bytes=56 * 2**20
        ),
        cost_estimate=pl.CostEstimate(
            flops=4 * rows_all * width * (2 * inner + NARROW), bytes_accessed=60 * 2**20, transcendentals=0
        ),
        name="mixer_backward",
    )(place, ends, hidden, *saved, sums, stack, narrow, gain, head_rows, conv_rows, shared_rows)


def grads_kernel(
    first_matrix, count, seq_count, clear, mask_right, place_ref, ends_ref, free_ref, left_ref, right_ref,
    *rest,
):
    out_ref, held, sems, free_sems = rest[-4:]
    chunk = pl.program_id(0)
    width = right_ref.shape[1]
    right = right_ref[...]
    if mask_right:
        valid = iota(right.shape, 0) < ends_ref[seq_count - 1]
        right = jnp.where(valid, right.astype(f32), 0.0).astype(bf16)
    held[0 : count * HEADDIM, :] = dot_tn(left_ref[...], right).astype(bf16)
    columns = pl.ds(pl.multiple_of(chunk * width, width), width)
    copies = [
        pltpu.make_async_copy(
            held.at[pl.ds(m * HEADDIM, HEADDIM), :],
            out_ref.at[place_ref[first_matrix + m], :, columns],
            sems.at[m],
        )
        for m in range(count)
    ]
    for copy in copies:
        copy.start()
    if clear:
        held[count * HEADDIM :, :] = jnp.zeros((HEADDIM, width), bf16)

        def clear_copy(s):
            return pltpu.make_async_copy(
                held.at[pl.ds(count * HEADDIM, HEADDIM), :], out_ref.at[s, :, columns], free_sems.at[s]
            )

        for s in range(out_ref.shape[0]):

            @pl.when(free_ref[s] > 0)
            def _(s=s):
                clear_copy(s).start()

        for s in range(out_ref.shape[0]):

            @pl.when(free_ref[s] > 0)
            def _(s=s):
                clear_copy(s).wait()

    for copy in copies:
        copy.wait()


def grads_call(place, ends, free, left, right, first_matrix, mask_right, into):
    rows_all, width = right.shape
    slots = free.shape[0]
    count = left.shape[1] // HEADDIM
    clear = into is None
    held = pl.BlockSpec(memory_space=pl.ANY)
    return pl.pallas_call(
        functools.partial(grads_kernel, first_matrix, count, ends.shape[0] - 1, clear, mask_right),
        grid_spec=pltpu.PrefetchScalarGridSpec(
            num_scalar_prefetch=3,
            grid=(width // CHUNK,),
            in_specs=[
                pl.BlockSpec(left.shape, lambda i, *_: (0, 0), pipeline_mode=pl.Buffered(1)),
                pl.BlockSpec((rows_all, CHUNK), lambda i, *_: (0, i)),
            ]
            + ([] if clear else [held]),
            out_specs=held,
            scratch_shapes=[
                pltpu.VMEM(((count + 1) * HEADDIM, CHUNK), bf16),
                pltpu.SemaphoreType.DMA((count,)),
                pltpu.SemaphoreType.DMA((slots,)),
            ],
        ),
        out_shape=jax.ShapeDtypeStruct((slots, HEADDIM, width), bf16),
        input_output_aliases={} if clear else {5: 0},
        compiler_params=pltpu.CompilerParams(
            dimension_semantics=("arbitrary",), vmem_limit_bytes=56 * 2**20
        ),
        cost_estimate=pl.CostEstimate(
            flops=2 * rows_all * width * left.shape[1], bytes_accessed=30 * 2**20, transcendentals=0
        ),
        name="weight_grads",
    )(place, ends, free, left, right, *([] if clear else [into]))


def exchange_kernel(
    sums_ref, mine_ref, other_ref, total_ref, near_ref, sums_in, part_in, mine_in, sum_sems, part_sems, mine_sems
):
    here = lax.axis_index("dp")
    tensor = lax.axis_index("tensor")
    peers = [(here, (tensor + k) % 4) for k in range(1, 4)]
    other_core = (here, tensor + 1 - 2 * (tensor % 2))
    rows = mine_ref.shape[0]
    greet([(peer, None) for peer in peers])
    parts = [pl.ds(k * ROWS, ROWS) for k in range(rows // ROWS)]

    def part_copy(k):
        return remote(
            other_ref.at[parts[k]], part_in.at[parts[k]], part_sems.at[0, k], part_sems.at[1, k], other_core
        )

    def sum_copy(k):
        return remote(
            sums_ref.at[0:2], sums_in.at[tensor], sum_sems.at[0, k], sum_sems.at[1, k], peers[k]
        )

    def mine_copy(k):
        return pltpu.make_async_copy(mine_ref.at[parts[k]], mine_in.at[parts[k]], mine_sems.at[k])

    for k in range(3):
        sum_copy(k).start()
    for k in range(len(parts)):
        part_copy(k).start()
    for k in range(len(parts)):
        mine_copy(k).start()
    for k in range(3):
        sum_copy(k).wait()
    total = jnp.zeros((2, sums_ref.shape[1]), f32)
    for t in range(4):
        total = total + jnp.where(tensor == t, sums_ref[0:2, :], sums_in[t])
    total_ref[0:2, :] = total
    total_ref[2:8, :] = jnp.zeros((6, sums_ref.shape[1]), f32)
    for k in range(len(parts)):
        mine_copy(k).wait()
        part_copy(k).wait()
        here_rows = parts[k]
        near_ref[here_rows, :] = (
            mine_in[here_rows, :].astype(f32) + part_in[here_rows, :].astype(f32)
        ).astype(bf16)


def exchange_call(sums, mine, other):
    rows, width = mine.shape
    spec = pl.BlockSpec(memory_space=pltpu.VMEM)
    sems = pltpu.SemaphoreType.DMA
    return pl.pallas_call(
        exchange_kernel,
        in_specs=[spec] + [pl.BlockSpec(memory_space=pltpu.HBM)] * 2,
        out_specs=[spec] * 2,
        out_shape=[jax.ShapeDtypeStruct(sums.shape, f32), jax.ShapeDtypeStruct(mine.shape, bf16)],
        scratch_shapes=[
            pltpu.VMEM((4, 2, sums.shape[1]), f32), pltpu.VMEM((rows, width), bf16),
            pltpu.VMEM((rows, width), bf16),
            sems((2, 3)), sems((2, rows // ROWS)), sems((rows // ROWS,)),
        ],
        compiler_params=pltpu.CompilerParams(
            collective_id=2, has_side_effects=True, vmem_limit_bytes=40 * 2**20
        ),
        name="exchange_sums",
    )(sums, mine, other)


def branch_kernel(inner_all, seq_count, ends_ref, near_ref, far_ref, hidden_ref, sums_ref, full_ref, half_ref):
    width = hidden_ref.shape[1]
    blocks = pl.num_programs(0)
    first_row = (ends_ref[seq_count] * blocks + pl.program_id(0)) * HALF_ROWS
    inv_row = lax.rsqrt(sums_ref[0:1, :] * (1.0 / inner_all) + norm_eps)
    inv = jnp.broadcast_to(inv_row, (LANES, HALF_ROWS)).T
    row_at = first_row + iota((HALF_ROWS, LANES), 0)
    valid = jnp.where(row_at < ends_ref[seq_count - 1], 1.0, 0.0).astype(f32)
    for group in range(width // LANES):
        lanes = lanes_of(group)
        branch = (near_ref[:, lanes].astype(f32) + far_ref[:, lanes].astype(f32)) * inv
        result = ((hidden_ref[:, lanes].astype(f32) + branch) * valid).astype(bf16)
        full_ref[:, lanes] = result
        half_ref[:, lanes] = result


def input_kernel(seq_count, ends_ref, near_ref, far_ref, hidden_ref, cot_ref, gain_ref, full_ref, half_ref):
    width = hidden_ref.shape[1]
    blocks = pl.num_programs(0)
    first_row = (ends_ref[seq_count] * blocks + pl.program_id(0)) * HALF_ROWS
    hidden = hidden_ref[...].astype(f32)
    inv_rms = lax.rsqrt(jnp.mean(hidden * hidden, axis=1, keepdims=True) + norm_eps)
    gain_part = (near_ref[...].astype(f32) + far_ref[...].astype(f32)) * gain_ref[0:1, :]
    fix = inv_rms * inv_rms * inv_rms * (jnp.sum(gain_part * hidden, axis=1, keepdims=True) / width)
    row_at = first_row + iota(hidden.shape, 0)
    cot = jnp.where(row_at < ends_ref[seq_count - 1], cot_ref[...].astype(f32), 0.0)
    result = (inv_rms * gain_part - hidden * fix + cot).astype(bf16)
    full_ref[...] = result
    half_ref[...] = result


def half_call(kernel, name, ends, halves, fulls, wholes):
    rows, width = halves[0].shape
    seq_count = ends.shape[0] - 1
    blocks = rows // HALF_ROWS

    def in_full(i, ends):
        return (ends[seq_count] * blocks + i, 0)

    own = pl.BlockSpec((HALF_ROWS, width), lambda i, ends: (i, 0))
    full = pl.BlockSpec((HALF_ROWS, width), in_full)
    return pl.pallas_call(
        kernel,
        grid_spec=pltpu.PrefetchScalarGridSpec(
            num_scalar_prefetch=1,
            grid=(blocks,),
            in_specs=[own] * len(halves) + [full] * len(fulls) + wholes[1],
            out_specs=[full, own],
        ),
        out_shape=[
            jax.ShapeDtypeStruct((2 * rows, width), bf16),
            jax.ShapeDtypeStruct((rows, width), bf16),
        ],
        compiler_params=pltpu.CompilerParams(
            dimension_semantics=("arbitrary",), vmem_limit_bytes=40 * 2**20
        ),
        cost_estimate=pl.CostEstimate(flops=0, bytes_accessed=16 * 2**20, transcendentals=0),
        name=name,
    )(ends, *halves, *fulls, *wholes[0])


def remote(src, dst, send_sem, recv_sem, target):
    return pltpu.make_async_remote_copy(
        src_ref=src,
        dst_ref=dst,
        send_sem=send_sem,
        recv_sem=recv_sem,
        device_id=target,
        device_id_type=pl.DeviceIdType.MESH,
    )


def greet(targets):
    barrier = pltpu.get_barrier_semaphore()
    for target, condition in targets:
        if condition is None:
            pl.semaphore_signal(barrier, inc=1, device_id=target, device_id_type=pl.DeviceIdType.MESH)
        else:

            @pl.when(condition)
            def _(target=target):
                pl.semaphore_signal(
                    barrier, inc=1, device_id=target, device_id_type=pl.DeviceIdType.MESH
                )

    peers = sum(1 if condition is None else condition.astype(jnp.int32) for _, condition in targets)
    pl.semaphore_wait(barrier, peers)


def gather_kernel(
    lines, own_ref, out_ref, local_sem, x_send, x_recv, up_send, up_recv, down_send, down_recv
):
    here = lax.axis_index("dp")
    tensor = lax.axis_index("tensor")
    line, side = here // 2, here % 2
    partner = here + 1 - 2 * side
    slots = own_ref.shape[0]
    most = slots - 1
    has_up, has_down = line < lines - 1, line > 0
    across, above, below = (partner, tensor), (here + 2, tensor), (here - 2, tensor)

    greet([(across, None), (above, has_up), (below, has_down)])
    local = pltpu.make_async_copy(own_ref, out_ref.at[pl.ds(here * slots, slots)], local_sem)
    local.start()
    order = [most] + list(range(min(2, most))) + [slots] + list(range(min(2, most), most))

    def place(at, part):
        device = 2 * at + 1 - side if part == slots else 2 * at + side
        return device * slots + min(part, most)

    def line_copy(step, at, part, upward):
        own = step == 0 and part < slots
        to = out_ref.at[place(at, part)]
        src = own_ref.at[part] if own else to
        if upward:
            return remote(src, to, up_send.at[step, part], up_recv.at[step, part], above)
        return remote(src, to, down_send.at[step, part], down_recv.at[step, part], below)

    def x_copy(device, index, part, own=False):
        to = out_ref.at[device * slots + part]
        return remote(
            own_ref.at[part] if own else to, to, x_send.at[index, part], x_recv.at[index, part], across
        )

    x_copy(here, 0, most, True).start()
    for part in order:
        if part == slots:
            x_copy(partner, 0, most).wait_recv()

        @pl.when(has_up)
        def _(part=part):
            line_copy(0, line, part, True).start()

        @pl.when(has_down)
        def _(part=part):
            line_copy(0, line, part, False).start()

        if part < most:
            x_copy(here, 0, part, True).start()

    for k in range(1, lines):
        for part in order:

            @pl.when(line >= k)
            def _(k=k, part=part):
                line_copy(k - 1, line - k, part, True).wait_recv()
                if k < lines - 1:

                    @pl.when(has_up)
                    def _():
                        line_copy(k, line - k, part, True).start()

                if part < most:
                    x_copy(2 * (line - k) + side, k, part).start()

            @pl.when(line + k < lines)
            def _(k=k, part=part):
                line_copy(k - 1, line + k, part, False).wait_recv()
                if k < lines - 1:

                    @pl.when(has_down)
                    def _():
                        line_copy(k, line + k, part, False).start()

                if part < most:
                    x_copy(2 * (line + k) + side, lines - 1 + k, part).start()

    local.wait()
    x_copy(partner, 0, most).wait_send()
    for part in range(most):
        x_copy(partner, 0, part).wait()
    for k in range(1, lines):
        for part in range(most):

            @pl.when(line >= k)
            def _(k=k, part=part):
                x_copy(2 * (line - k) + 1 - side, k, part).wait()

            @pl.when(line + k < lines)
            def _(k=k, part=part):
                x_copy(2 * (line + k) + 1 - side, lines - 1 + k, part).wait()

    for k in range(lines - 1):
        for part in order:

            @pl.when(has_up & (line >= k))
            def _(k=k, part=part):
                line_copy(k, line - k, part, True).wait_send()

            @pl.when(has_down & (line + k < lines))
            def _(k=k, part=part):
                line_copy(k, line + k, part, False).wait_send()


def gather_call(own, dp_size):
    slots, side, width = own.shape
    lines = dp_size // 2
    step_sems = pltpu.SemaphoreType.DMA((lines - 1, slots + 1))
    x_sems = pltpu.SemaphoreType.DMA((2 * lines - 1, slots))
    return pl.pallas_call(
        functools.partial(gather_kernel, lines),
        in_specs=[pl.BlockSpec(memory_space=pl.ANY)],
        out_specs=pl.BlockSpec(memory_space=pl.ANY),
        out_shape=jax.ShapeDtypeStruct((slots * dp_size, side, width), own.dtype),
        scratch_shapes=[
            pltpu.SemaphoreType.DMA, x_sems, x_sems, step_sems, step_sems, step_sems, step_sems,
        ],
        compiler_params=pltpu.CompilerParams(collective_id=0, has_side_effects=True),
        name="gather_weights",
    )(own)


def reduce_kernel(
    lines,
    grads_ref, near_ref, far_ref, extra_ref, owned_ref, totals_ref,
    grads, load_sems, x_in, up_in, down_in, last_out, last_in, halves, half_in, group_in, group_out, group_back,
    x_send, x_recv, up_send, up_recv, down_send, down_recv, last_sems, small_sems, group_sems, back_sems,
):
    here = lax.axis_index("dp")
    tensor = lax.axis_index("tensor")
    line, side = here // 2, here % 2
    core = tensor % 2
    slots = owned_ref.shape[0]
    most = slots - 1
    width = near_ref.shape[1]
    half = width // 2
    group = halves.shape[1] // lines
    has_up, has_down = line < lines - 1, line > 0
    across = (here + 1 - 2 * side, tensor)
    above, below = (here + 2, tensor), (here - 2, tensor)
    other_core = (here, tensor + 1 - 2 * core)
    other_chip = (here, (tensor + 2) % 4)
    on_line = [(2 * ((line + k) % lines) + side, tensor) for k in range(1, lines)]

    greet([(target, None) for target in [across, other_core, other_chip] + on_line])

    def add(*parts):
        total = parts[0].astype(f32)
        for part in parts[1:]:
            total = total + part.astype(f32)
        return total

    half_copy = remote(halves.at[1 - side], half_in, small_sems.at[0, 0], small_sems.at[1, 0], across)

    def group_copy(k):
        to = (line + k) % lines
        rows = pl.ds(pl.multiple_of(to * group, group), group)
        return remote(
            halves.at[side, rows], group_in.at[k - 1], group_sems.at[0, k - 1], group_sems.at[1, k - 1],
            on_line[k - 1],
        )

    def back_copy(k):
        return remote(
            group_out, group_back.at[k - 1], back_sems.at[0, k - 1], back_sems.at[1, k - 1], on_line[k - 1]
        )

    total_half = remote(
        totals_ref.at[tensor, side], totals_ref.at[tensor, side], small_sems.at[0, 1], small_sems.at[1, 1],
        across,
    )
    total_chip = remote(
        totals_ref.at[tensor], totals_ref.at[tensor], small_sems.at[0, 2], small_sems.at[1, 2], other_chip
    )

    def total_core(k):
        at = core + 2 * k
        return remote(
            totals_ref.at[at], totals_ref.at[at], small_sems.at[0, 3 + k], small_sems.at[1, 3 + k], other_core
        )

    def small_start():
        mine = near_ref[...] + far_ref[...]
        rest = extra_ref[...]
        for k in range(2):
            columns = slice(k * half, (k + 1) * half)
            halves[k, 0:HEADDIM, :] = mine[:, columns]
            halves[k, HEADDIM:, :] = rest[:, columns]
        half_copy.start()

    def small_group():
        half_copy.wait()
        halves[side] = halves[side] + half_in[...]
        for k in range(1, lines):
            group_copy(k).start()

    def small_back():
        for k in range(1, lines):
            group_copy(k).wait()
        rows = pl.ds(pl.multiple_of(line * group, group), group)
        total = halves[side, rows, :]
        for k in range(1, lines):
            total = total + group_in[k - 1]
        group_out[...] = total
        for k in range(1, lines):
            back_copy(k).start()

    def small_half():
        for k in range(1, lines):
            back_copy(k).wait()
        rows = pl.ds(pl.multiple_of(line * group, group), group)
        totals_ref[tensor, side, rows, :] = group_out[...]
        for k in range(1, lines):
            source = (line + lines - k) % lines
            rows = pl.ds(pl.multiple_of(source * group, group), group)
            totals_ref[tensor, side, rows, :] = group_back[k - 1]
        total_half.start()

    def small_chip():
        total_half.wait()
        total_chip.start()

    def small_core():
        total_chip.wait()
        for k in range(2):
            total_core(k).start()

    def small_end():
        for k in range(2):
            total_core(k).wait()

    small = [(1, small_group), (3, small_back), (5, small_half), (8, small_chip), (13, small_core)]
    events = []

    def event():
        events.append(None)
        while small and small[0][0] <= len(events):
            small.pop(0)[1]()

    def last_slot(k):
        return jnp.where(k == side, most, slots)

    loads = []
    for at in range(lines):
        loads.append(
            pltpu.make_async_copy(
                grads_ref.at[pl.ds((2 * at + side) * slots, slots)], grads.at[at, pl.ds(0, slots)],
                load_sems.at[at, 0],
            )
        )
        loads.append(
            pltpu.make_async_copy(
                grads_ref.at[pl.ds((2 * at + 1 - side) * slots + most, 1)], grads.at[at, pl.ds(slots, 1)],
                load_sems.at[at, 1],
            )
        )

    def x_copy(at, i):
        return remote(
            grads_ref.at[(2 * at + 1 - side) * slots + i], x_in.at[at, i], x_send.at[at, i], x_recv.at[at, i], across
        )

    def x_needed(turn):
        step, i = turn // most, turn % most
        if step < lines - 1:
            each_way(step, lambda at, upward: x_copy(at, i).start())
        elif step == lines - 1:
            x_copy(line, i).start()

    def line_copy(src, at, i, upward):
        if upward:
            return remote(src, up_in.at[at, i], up_send.at[at, i], up_recv.at[at, i], above)
        return remote(src, down_in.at[at, i], down_send.at[at, i], down_recv.at[at, i], below)

    def line_most(at, i, upward):
        arrived = up_in if upward else down_in
        x_copy(at, i).wait_recv()
        own = add(grads[at, i], x_in[at, i])

        @pl.when(has_down if upward else has_up)
        def _():
            line_copy(x_in.at[at, i], at, i, upward).wait_recv()
            x_in[at, i] = add(own, arrived[at, i]).astype(bf16)

        @pl.when(jnp.logical_not(has_down if upward else has_up))
        def _():
            x_in[at, i] = own.astype(bf16)

        line_copy(x_in.at[at, i], at, i, upward).start()

    def line_last(at, k, upward):
        arrived = up_in if upward else down_in
        own = grads.at[at, last_slot(k)]

        @pl.when(has_down if upward else has_up)
        def _():
            line_copy(own, at, most + k, upward).wait_recv()
            arrived[at, most + k] = add(own[...], arrived[at, most + k]).astype(bf16)
            line_copy(arrived.at[at, most + k], at, most + k, upward).start()

        @pl.when(jnp.logical_not(has_down if upward else has_up))
        def _():
            line_copy(own, at, most + k, upward).start()

    def each_way(step, work):
        @pl.when(lines - 1 - step > line)
        def _():
            work(lines - 1 - step, True)

        @pl.when(step < line)
        def _():
            work(step, False)

    small_start()
    for turn in range(AHEAD):
        x_needed(turn)
    for load in loads:
        load.start()
    for load in loads:
        load.wait()
    for step in range(lines - 1):
        for k in range(2):
            each_way(step, lambda at, upward, k=k: line_last(at, k, upward))
        event()
        for i in range(most):
            x_needed(step * most + i + AHEAD)
            each_way(step, lambda at, upward, i=i: line_most(at, i, upward))
            event()

    def gathered_last(k):
        return grads[line, last_slot(k)].astype(f32)

    owned_ref[most] = gathered_last(side)
    to_send = gathered_last(1 - side)
    last_out[...] = to_send

    @pl.when(has_down)
    def _():
        for k in range(2):
            line_copy(last_in, line, most + k, True).wait_recv()
        owned_ref[most] = owned_ref[most] + up_in[line, most + side].astype(f32)
        last_out[...] = last_out[...] + up_in[line, most + 1 - side].astype(f32)

    @pl.when(has_up)
    def _():
        for k in range(2):
            line_copy(last_in, line, most + k, False).wait_recv()
        owned_ref[most] = owned_ref[most] + down_in[line, most + side].astype(f32)
        last_out[...] = last_out[...] + down_in[line, most + 1 - side].astype(f32)

    x_in[line, most] = last_out[...].astype(bf16)
    last_copy = remote(x_in.at[line, most], last_in, last_sems.at[0], last_sems.at[1], across)
    last_copy.start()
    for turn in range((lines - 1) * most + AHEAD, lines * most):
        x_needed(turn)
    while small:
        small.pop(0)[1]()

    def finish(i, carry):
        x_copy(line, i).wait_recv()
        owned_ref[i] = add(grads[line, i], x_in[line, i])

        @pl.when(has_down)
        def _():
            line_copy(last_in, line, i, True).wait_recv()
            owned_ref[i] = owned_ref[i] + up_in[line, i].astype(f32)

        @pl.when(has_up)
        def _():
            line_copy(last_in, line, i, False).wait_recv()
            owned_ref[i] = owned_ref[i] + down_in[line, i].astype(f32)

        return carry

    lax.fori_loop(0, most, finish, 0)
    last_copy.wait()
    owned_ref[most] = owned_ref[most] + last_in[...].astype(f32)
    small_end()

    def x_sent(at):
        def one(i, carry):
            x_copy(at, i).wait_send()
            return carry

        lax.fori_loop(0, most, one, 0)

    def line_sent(at, upward):
        def one(i, carry):
            line_copy(last_in, at, i, upward).wait_send()
            return carry

        lax.fori_loop(0, slots + 1, one, 0)

    x_sent(line)
    for step in range(lines - 1):
        each_way(step, lambda at, upward: x_sent(at))
        each_way(step, line_sent)


def reduce_call(grads, near, far, extra, dp_size):
    slots_all, side, width = grads.shape
    slots = slots_all // dp_size
    lines = dp_size // 2
    small_rows = HEADDIM + extra.shape[0]
    group = small_rows // lines
    spec = pl.BlockSpec(memory_space=pltpu.VMEM)
    sems = pltpu.SemaphoreType.DMA
    return pl.pallas_call(
        functools.partial(reduce_kernel, lines),
        in_specs=[pl.BlockSpec(memory_space=pltpu.HBM)] + [spec] * 3,
        out_specs=[spec] * 2,
        out_shape=[
            jax.ShapeDtypeStruct((slots, side, width), f32),
            jax.ShapeDtypeStruct((4, 2, small_rows, width // 2), f32),
        ],
        scratch_shapes=[
            pltpu.VMEM((lines, slots + 1, side, width), bf16),
            sems((lines, 2)),
            pltpu.VMEM((lines, slots, side, width), bf16),
            pltpu.VMEM((lines, slots + 1, side, width), bf16),
            pltpu.VMEM((lines, slots + 1, side, width), bf16),
            pltpu.VMEM((side, width), f32),
            pltpu.VMEM((side, width), bf16),
            pltpu.VMEM((2, small_rows, width // 2), f32),
            pltpu.VMEM((small_rows, width // 2), f32),
            pltpu.VMEM((lines - 1, group, width // 2), f32),
            pltpu.VMEM((group, width // 2), f32),
            pltpu.VMEM((lines - 1, group, width // 2), f32),
            sems((lines, slots)), sems((lines, slots)),
            sems((lines, slots + 1)), sems((lines, slots + 1)),
            sems((lines, slots + 1)), sems((lines, slots + 1)),
            sems((2,)), sems((2, 5)), sems((2, lines - 1)), sems((2, lines - 1)),
        ],
        compiler_params=pltpu.CompilerParams(
            collective_id=1, has_side_effects=True, vmem_limit_bytes=56 * 2**20
        ),
        cost_estimate=pl.CostEstimate(flops=10**11, bytes_accessed=40 * 2**20, transcendentals=0),
        name="reduce_grads",
    )(grads, near, far, extra)


def small_rule(rate, weight, moment, gradient):
    moment_new = small_decay * moment + (1.0 - small_decay) * gradient
    return moment_new, weight - rate * moment_new


def muon_kernel(
    rate, small_rate_now,
    grad_ref, totals_ref, moment_ref, master_ref,
    state_moment, state_proj, step_moment, step_proj, gain_moment, gain, head_moment, head, conv_moment, conv,
    shared_moment, shared,
    moment_out, master_out,
    state_moment_out, state_out, step_moment_out, step_out, gain_moment_out, gain_out, head_moment_out,
    head_out, conv_moment_out, conv_out, shared_moment_out, shared_out,
):
    tensor = lax.axis_index("tensor")
    rule = functools.partial(small_rule, small_rate_now)

    def row(at, row_at):
        return jnp.concatenate(
            [totals_ref[at, k, row_at : row_at + 1, :] for k in range(2)], axis=1
        )

    def over_tensor(row_at):
        return row(0, row_at) + row(1, row_at) + row(2, row_at) + row(3, row_at)

    for k in range(2):
        parts = [
            jnp.concatenate([totals_ref[2 * k + j, c, 0:HEADDIM, :] for c in range(2)], axis=1)
            for j in range(2)
        ]
        lanes = lanes_of(k)
        state_moment_out[:, lanes], state_out[:, lanes] = rule(
            state_proj[:, lanes], state_moment[:, lanes], jnp.concatenate(parts, axis=0).T
        )
    heads = step_proj.shape[0]
    extra = HEADDIM
    own = [totals_ref[tensor, k, extra : extra + 32, :] for k in range(2)]
    step_moment_out[...], step_out[...] = rule(
        step_proj[...], step_moment[...], jnp.concatenate(own, axis=1)[0:heads]
    )
    gain_moment_out[...], gain_out[...] = rule(gain[...], gain_moment[...], over_tensor(extra + GAIN_ROW))
    head_moment_out[...], head_out[...] = rule(
        head[...], head_moment[...], own[0][HEAD_ROW : HEAD_ROW + 3, 0:heads]
    )
    inner = conv.shape[1]
    per_line = 2 * own[0].shape[1] // inner
    conv_total = jnp.concatenate(own, axis=1)
    for k in range(6):
        at = (k % per_line) * inner
        line = 16 + k // per_line
        one = slice(k, k + 1)
        conv_moment_out[one, :], conv_out[one, :] = rule(
            conv[one, :], conv_moment[one, :], conv_total[line : line + 1, at : at + inner]
        )
    shared_total = over_tensor(extra + SHARED_ROW)
    for k in range(5):
        one = slice(k, k + 1)
        shared_moment_out[one, :], shared_out[one, :] = rule(
            shared[one, :], shared_moment[one, :], shared_total[:, 2 * LANES * k : 2 * LANES * (k + 1)]
        )

    first_coef, second_coef, third_coef = schulz_coefs
    side = HEADDIM
    same = iota((side, side), 0) == iota((side, side), 1)
    eye = jnp.where(same, 1.0, 0.0).astype(f32)
    slots = grad_ref.shape[0]
    grams, totals, scales = [], [], []
    for s in range(slots):
        moment = muon_decay * moment_ref[s] + grad_ref[s].astype(f32)
        moment_out[s] = moment
        square = jnp.sum(jnp.sum(moment * moment, axis=1, keepdims=True), axis=0, keepdims=True)
        scale = 1.0 / (jnp.sqrt(square) + 1e-07)
        scaled = moment * scale
        grams.append(dot_nt(scaled, scaled, exact_mode))
        totals.append(eye)
        scales.append(scale)
    for _ in range(NS_STEPS):
        for s in range(slots):
            gram = grams[s]
            factor = (
                first_coef * eye + second_coef * gram + third_coef * dot_nn(gram, gram, exact_mode)
            )
            totals[s] = dot_nn(factor, totals[s], exact_mode)
            grams[s] = dot_nn(dot_nn(factor, gram, exact_mode), factor, exact_mode)
    for s in range(slots):
        ortho = dot_nn(totals[s], moment_out[s] * scales[s], exact_mode)
        master_out[s] = master_ref[s] - rate * ortho


def muon_call(grad, totals, moment, master, small, tokens_all):
    slots, side, width = moment.shape
    spec = pl.BlockSpec(memory_space=pltpu.VMEM)
    return pl.pallas_call(
        functools.partial(
            muon_kernel, muon_rate * math.sqrt(max(width, side)), small_rate / math.sqrt(tokens_all)
        ),
        in_specs=[spec] * (4 + len(small)),
        out_specs=[spec] * (2 + len(small)),
        out_shape=[jax.ShapeDtypeStruct(moment.shape, f32)] * 2
        + [jax.ShapeDtypeStruct(array.shape, f32) for array in small],
        compiler_params=pltpu.CompilerParams(vmem_limit_bytes=56 * 2**20),
        name="muon",
    )(grad, totals, moment, master, *small)


def pad_to(array, rows, columns):
    return jnp.pad(array, ((0, rows - array.shape[0]), (0, columns - array.shape[1])))


def swap(values, bit):
    return lax.ppermute(values, "tensor", [(t, t ^ bit) for t in range(4)])


def place_half(full, half):
    core = lax.axis_index("tensor") % 2
    return lax.dynamic_update_slice(full, swap(half, 1), ((1 - core) * half.shape[0], 0))


def per_device(
    hidden_in,
    out_grad,
    seq_lengths,
    owner_map,
    muon_master,
    muon_moment,
    state_proj,
    state_moment,
    step_proj,
    step_moment,
    norm_gain,
    gain_moment,
    head_params,
    head_moment,
    conv_params,
    conv_moment,
    state_conv,
    state_conv_moment,
):
    tok_rows, width = hidden_in.shape
    heads = step_proj.shape[1]
    inner = conv_params.shape[1]
    dp_size = lax.axis_size("dp")
    inner_all = inner * lax.axis_size("tensor")
    slots = muon_master.shape[0] * dp_size
    core = lax.axis_index("tensor") % 2
    chip = lax.axis_index("tensor") // 2
    ends = jnp.concatenate([jnp.cumsum(seq_lengths[0], dtype=jnp.int32), core[None].astype(jnp.int32)])
    seq_count = seq_lengths.shape[1]
    master = muon_master.transpose(0, 2, 1)
    moment = muon_moment.transpose(0, 2, 1)
    stack = gather_call(master.astype(bf16), dp_size)
    narrow = pad_to(jnp.concatenate([state_proj, step_proj], axis=1), width, NARROW).astype(bf16)
    gain = norm_gain[None, :]
    head_rows = pad_to(head_params, 8, LANES)
    conv_rows = pad_to(conv_params, 8, inner)
    shared_rows = pad_to(state_conv, 8, state_conv.shape[1])
    free = jnp.all(owner_map[None, :] != jnp.arange(slots, dtype=jnp.int32)[:, None], axis=1)
    free = free.astype(jnp.int32)
    group_rows = 8 * (dp_size // 2)
    extra_rows = -(-(HEADDIM + 32) // group_rows) * group_rows - HEADDIM

    normed, *saved, sums, mine, other = forward_call(
        owner_map, ends, hidden_in, out_grad, stack, gain, narrow, head_rows, conv_rows, shared_rows, heads
    )
    sums, near = exchange_call(sums, mine, other)
    far = swap(near, 2)
    dboth, scaled, mine, other, mine_narrow, other_narrow, extra = backward_call(
        owner_map, ends, hidden_in, saved, sums, stack, narrow, gain, head_rows, conv_rows, shared_rows, heads,
        inner_all, extra_rows,
    )

    got = swap(other, 1)
    got_narrow = swap(other_narrow, 1)
    far, scaled = lax.optimization_barrier((far, scaled))
    rows_spec = pl.BlockSpec((8, HALF_ROWS), lambda i, ends: (0, ends[seq_count] * (tok_rows // HALF_ROWS // 2) + i))
    block_full, block_half = half_call(
        functools.partial(branch_kernel, inner_all, seq_count), "block_out", ends, [near, far], [hidden_in],
        ([sums], [rows_spec]),
    )
    block_out = place_half(block_full, block_half)
    scaled, block_half = lax.optimization_barrier((scaled, block_half))
    slotted = grads_call(owner_map, ends, free, scaled, out_grad, 2 * heads, True, None)
    slotted, got, got_narrow = lax.optimization_barrier((slotted, got, got_narrow))
    pair = mine_narrow + got_narrow
    near_narrow = lax.dynamic_index_in_dim(pair, chip, 0, keepdims=False)
    send_narrow = lax.dynamic_index_in_dim(pair, 1 - chip, 0, keepdims=False)
    far_narrow = swap(send_narrow, 2)
    send_narrow, got = lax.optimization_barrier((send_narrow, got))
    near_grad = (mine.astype(f32) + got.astype(f32)).astype(bf16)
    far_grad = swap(near_grad, 2)
    near_grad, near_narrow, dboth = lax.optimization_barrier((near_grad, near_narrow, dboth))
    slotted = grads_call(owner_map, ends, free, dboth, normed, 0, False, slotted)
    owned, totals = reduce_call(slotted, near_narrow, far_narrow, extra, dp_size)
    owned, totals, far_grad = lax.optimization_barrier((owned, totals, far_grad))
    gain_spec = pl.BlockSpec(gain.shape, lambda i, ends: (0, 0))
    input_full, input_half = half_call(
        functools.partial(input_kernel, seq_count), "input_grad", ends, [near_grad, far_grad],
        [hidden_in, out_grad], ([gain], [gain_spec]),
    )
    input_grad = place_half(input_full, input_half)
    owned, input_half = lax.optimization_barrier((owned, input_half))
    small = [
        state_moment, state_proj, step_moment.T, step_proj.T, gain_moment[None, :], gain, head_moment,
        head_params, conv_moment, conv_params, state_conv_moment, state_conv,
    ]
    moment_new, master_new, *small_new = muon_call(owned, totals, moment, master, small, tok_rows * dp_size)
    state_moment_new, state_proj_new, step_moment_new, step_proj_new = small_new[:4]
    gain_moment_new, norm_gain_new, head_moment_new, head_params_new = small_new[4:8]
    conv_moment_new, conv_params_new, state_conv_moment_new, state_conv_new = small_new[8:]
    step_moment_new, step_proj_new = step_moment_new.T, step_proj_new.T
    gain_moment_new, norm_gain_new = gain_moment_new[0], norm_gain_new[0]
    return (
        block_out,
        input_grad,
        moment_new.transpose(0, 2, 1),
        master_new.transpose(0, 2, 1),
        state_moment_new,
        state_proj_new,
        step_moment_new,
        step_proj_new,
        gain_moment_new,
        norm_gain_new,
        head_moment_new,
        head_params_new,
        conv_moment_new,
        conv_params_new,
        state_conv_moment_new,
        state_conv_new,
    )


def solution(mesh):
    in_specs = (
        P("dp", None),
        P("dp", None),
        P("dp", None),
        P(),
        P("dp", None, "tensor"),
        P("dp", None, "tensor"),
        P(),
        P(),
        P(None, "tensor"),
        P(None, "tensor"),
        P(),
        P(),
        P(None, "tensor"),
        P(None, "tensor"),
        P(None, "tensor"),
        P(None, "tensor"),
        P(),
        P(),
    )
    out_specs = (
        P("dp", None),
        P("dp", None),
        P("dp", None, "tensor"),
        P("dp", None, "tensor"),
        P(),
        P(),
        P(None, "tensor"),
        P(None, "tensor"),
        P(),
        P(),
        P(None, "tensor"),
        P(None, "tensor"),
        P(None, "tensor"),
        P(None, "tensor"),
        P(),
        P(),
    )
    return jax.shard_map(
        per_device, mesh=mesh, in_specs=in_specs, out_specs=out_specs, check_vma=False
    )
```

```python
import functools
import math

import jax
import jax.numpy as jnp
from jax import lax
from jax.experimental import pallas as pl
from jax.experimental.pallas import tpu as pltpu
from jax.sharding import PartitionSpec as P

HEADDIM = 64
NS_STEPS = 5
ROWS = 256
SUB = 128
LANES = 128
NARROW = 384
CHUNK = 768
GAIN_ROW, SHARED_ROW, HEAD_ROW = 19, 20, 21
AHEAD = 5
HALF_ROWS = 512

exact_mode = lax.Precision.HIGHEST
norm_eps = 1e-05
schulz_coefs = (3.4445, -4.775, 2.0315)
muon_decay = 0.95
muon_rate = 0.02
small_decay = 0.9
small_rate = 2.0
log2_e = 1.4426950408889634
f32 = jnp.float32
bf16 = jnp.bfloat16
far_below = -1e30


def dot_nn(left, right, precision=None):
    return lax.dot_general(
        left, right, (((1,), (0,)), ((), ())), precision=precision, preferred_element_type=f32
    )


def dot_nt(left, right, precision=None):
    return lax.dot_general(
        left, right, (((1,), (1,)), ((), ())), precision=precision, preferred_element_type=f32
    )


def dot_tn(left, right, precision=None):
    return lax.dot_general(
        left, right, (((0,), (0,)), ((), ())), precision=precision, preferred_element_type=f32
    )


def dot_pieces(ones, values):
    total = None
    for _ in range(3):
        piece = values.astype(bf16)
        values = values - piece.astype(f32)
        part = dot_nn(ones, piece)
        total = part if total is None else total + part
    return total


def sigmoid(values):
    return 0.5 * jnp.tanh(0.5 * values) + 0.5


def iota(shape, dim):
    return lax.broadcasted_iota(jnp.int32, shape, dim)


def segment_at(place, ends_ref, count):
    total = (place >= ends_ref[0]).astype(jnp.int32)
    for k in range(1, count):
        total = total + (place >= ends_ref[k]).astype(jnp.int32)
    return total


def step_terms(step_part, head_ref):
    shifted = step_part + head_ref[0:1, :]
    small = jnp.exp(-jnp.abs(shifted))
    tail = jnp.where(
        small < 0.01, small * (1.0 - small * (0.5 - small * (1.0 / 3.0))), jnp.log(1.0 + small)
    )
    step = jnp.maximum(shifted, 0.0) + tail
    decay = -jnp.exp(head_ref[1:2, :])
    log_rate = step * (decay * log2_e)
    lower = (iota((SUB, SUB), 0) >= iota((SUB, SUB), 1)).astype(bf16)
    cum = dot_pieces(lower, log_rate)
    source = cum - jnp.log(step) * log2_e
    return shifted, step, decay, cum, source


def expand(values, pair):
    shape = (values.shape[0], LANES)
    low = jnp.broadcast_to(values[:, 2 * pair : 2 * pair + 1], shape)
    high = jnp.broadcast_to(values[:, 2 * pair + 1 : 2 * pair + 2], shape)
    return jnp.where(iota(shape, 1) < HEADDIM, low, high)


def split_pair(values):
    low = iota(values.shape, 1) < HEADDIM
    zero = jnp.zeros_like(values)
    return jnp.where(low, values, zero), jnp.where(low, zero, values)


def lanes_of(pair):
    return slice(pair * LANES, (pair + 1) * LANES)


def shift_mask(place, shift, ends_ref, count, rows_all):
    other = place + shift
    inside = (other >= 0) & (other < rows_all)
    same = segment_at(place, ends_ref, count) == segment_at(other, ends_ref, count)
    return jnp.where(inside & same, 1.0, 0.0).astype(f32)


def conv_tile(buf_ref, first, lanes, taps, masks):
    total = taps[4:5, :] + taps[3:4, :] * buf_ref[first + 8 : first + 8 + SUB, lanes]
    for back in (1, 2, 3):
        rows = buf_ref[first + 8 - back : first + 8 - back + SUB, lanes]
        total = total + taps[3 - back : 4 - back, :] * (rows * masks[back - 1])
    return total


def block_terms(base, ends_ref, count):
    row_at = base + iota((SUB, SUB), 0)
    col_at = base + iota((SUB, SUB), 1)
    seg_row = segment_at(row_at, ends_ref, count)
    seg_col = segment_at(col_at, ends_ref, count)
    seg_last = segment_at(base + SUB - 1, ends_ref, count)
    seg_before = jnp.where(base == 0, -1, segment_at(base - 1, ends_ref, count))
    carried = jnp.where(seg_row == seg_before, 1.0, 0.0).astype(f32)
    tail_same = jnp.where(seg_row == seg_last, 1.0, 0.0).astype(f32)
    through = jnp.where(seg_last == seg_before, 1.0, 0.0).astype(f32)
    same = seg_row == seg_col
    return row_at, col_at, same, carried, tail_same, through


def store_half(values, block, blocks, core, mine_ref, other_ref):
    is_mine = block // (blocks // 2) == core

    @pl.when(is_mine)
    def _():
        mine_ref[...] = values

    @pl.when(jnp.logical_not(is_mine))
    def _():
        other_ref[...] = values


def half_specs(width, blocks, seq_count, block_of):
    def index(half, block):
        return jnp.where(half == 0, jnp.minimum(block, blocks // 2 - 1), jnp.maximum(block - blocks // 2, 0))

    def mine(i, place, ends):
        return (index(ends[seq_count], block_of(i)), 0)

    def other(i, place, ends):
        return (index(1 - ends[seq_count], block_of(i)), 0)

    return [pl.BlockSpec((ROWS, width), mine), pl.BlockSpec((ROWS, width), other)]


def load_weights(stack_ref, place_ref, held_ref, sems, first, count):
    copies = []
    for m in range(count):
        copies.append(
            pltpu.make_async_copy(
                stack_ref.at[place_ref[first + m]],
                held_ref.at[pl.ds(m * HEADDIM, HEADDIM)],
                sems.at[m],
            )
        )
    for copy in copies:
        copy.start()
    return copies


def fold_rows(values):
    return jnp.sum(values.reshape(values.shape[0] // 8, 8, values.shape[1]), axis=0)


def saved_views(low_ref, high_ref, inner):
    wide = [low_ref.at[:, k * inner : (k + 1) * inner] for k in range(5)]
    shared = [
        low_ref.at[:, 5 * inner + 2 * LANES * k : 5 * inner + 2 * LANES * (k + 1)] for k in range(3)
    ]
    return (*wide, *shared, high_ref.at[:, 0:inner], high_ref.at[:, inner : inner + LANES])


def project_units(normed_ref, cot_ref, narrow_ref, weights, targets, row_at, last_end, inner):
    next_gate, next_in, next_scaled, next_narrow = targets
    units = []

    def one(target, at, weight_row, left_ref, masked):
        def unit():
            part = dot_nt(left_ref[...], weights[weight_row + at : weight_row + at + 2 * LANES, :])
            if masked:
                part = jnp.where(row_at < last_end, part, 0.0)
            target[:, at : at + 2 * LANES] = part.astype(bf16)

        return unit

    for at in range(0, inner, 2 * LANES):
        units.append(one(next_in, at, inner, normed_ref, False))
    units.append(lambda: next_narrow.__setitem__(Ellipsis, dot_nn(normed_ref[...], narrow_ref[...])))
    for at in range(0, inner, 2 * LANES):
        units.append(one(next_gate, at, 0, normed_ref, False))
        units.append(one(next_scaled, at, 2 * inner, cot_ref, True))
    return units


def forward_kernel(
    heads, seq_count, rows_all,
    place_ref, ends_ref,
    hidden_ref, cot_ref, stack_ref, gain_ref, narrow_ref, head_ref, conv_ref, shared_ref,
    normed_ref, low_ref, high_ref, state_ref, sums_ref, mine_ref, other_ref,
    weights, sems, in_buf, shared_buf, next_gate, next_in, next_scaled,
    next_narrow, state, low_buf, tail_buf, across,
):
    gate_ref, input_ref, x_ref, slope_ref, dscaled_ref, shared_in_ref, bc_ref, bc_slope_ref, mixed_ref, step_ref = (
        saved_views(low_ref, high_ref, heads * HEADDIM)
    )
    turn = pl.program_id(0)
    blocks = pl.num_programs(0) - 1
    block = turn - 1
    inner = heads * HEADDIM
    pairs = heads // 2

    def normalize():
        hidden = hidden_ref[...].astype(f32)
        inv_rms = lax.rsqrt(jnp.mean(hidden * hidden, axis=1, keepdims=True) + norm_eps)
        normed_ref[...] = (hidden * inv_rms * gain_ref[0:1, :]).astype(bf16)

    row_here = jnp.minimum(turn, blocks - 1) * ROWS + iota((ROWS, 2 * LANES), 0)
    targets = (next_gate, next_in, next_scaled, next_narrow)
    units = project_units(
        normed_ref, cot_ref, narrow_ref, weights, targets, row_here, ends_ref[seq_count - 1], inner
    )

    def take_next():
        in_buf[0:8, :] = in_buf[ROWS : ROWS + 8, :]
        shared_buf[0:8, :] = shared_buf[ROWS : ROWS + 8, :]
        in_buf[8:, :] = next_in[...].astype(f32)
        input_ref[...] = next_in[...]
        gate_ref[...] = next_gate[...]
        dscaled_ref[...] = next_scaled[...]
        shared_buf[8:, :] = next_narrow[:, 0 : 2 * LANES]
        shared_in_ref[...] = next_narrow[:, 0 : 2 * LANES].astype(bf16)
        step_ref[...] = next_narrow[:, 2 * LANES : 3 * LANES]

    @pl.when(turn == 0)
    def _():
        copies = load_weights(stack_ref, place_ref, weights, sems, 0, 3 * heads)
        in_buf[ROWS : ROWS + 8, :] = jnp.zeros((8, inner), f32)
        shared_buf[ROWS : ROWS + 8, :] = jnp.zeros((8, 2 * LANES), f32)
        state[...] = jnp.zeros_like(state)
        normalize()
        for copy in copies:
            copy.wait()
        for unit in units:
            unit()

    @pl.when(turn > 0)
    def _():
        take_next()
        normalize()
        pending = list(units)
        first_row = block * ROWS
        for sub in range(ROWS // SUB):
            first = sub * SUB
            here = slice(first, first + SUB)
            base = first_row + first
            row_at, col_at, same, carried, tail_same, through = block_terms(base, ends_ref, seq_count)
            causal = jnp.where(same & (row_at >= col_at), 0.0, far_below).astype(f32)
            masks = [shift_mask(row_at, -back, ends_ref, seq_count, rows_all) for back in (1, 2, 3)]
            bc = []
            for part in range(2):
                lanes = lanes_of(part)
                u = conv_tile(shared_buf, first, lanes, shared_ref[:, lanes], masks)
                sig = sigmoid(u)
                bc.append((u * sig).astype(bf16))
                bc_ref[here, lanes] = bc[part]
                bc_slope_ref[here, lanes] = (sig * (1.0 + u * (1.0 - sig))).astype(bf16)
            b_low, c_low = bc
            _, _, _, cum, source = step_terms(step_ref[here, :], head_ref)
            source_row = source.T
            scores = dot_nt(c_low, b_low)
            cum_last = cum[SUB - 1 : SUB, :]
            entry = jnp.exp2(cum) * carried
            leave = jnp.exp2(cum_last - source) * tail_same
            pass_on = jnp.exp2(cum_last) * through
            state_low = state[...].astype(bf16)
            state_ref[sub] = state_low
            across[...] = dot_nn(c_low, state_low)
            square = jnp.zeros((SUB, LANES), f32)
            inner_dot = jnp.zeros((SUB, LANES), f32)
            for pair in range(pairs):
                if pending:
                    pending.pop(0)()
                lanes = lanes_of(pair)
                u = conv_tile(in_buf, first, lanes, conv_ref[:, lanes], masks)
                sig = sigmoid(u)
                x_low = (u * sig).astype(bf16)
                x_ref[here, lanes] = x_low
                slope_ref[here, lanes] = (sig * (1.0 + u * (1.0 - sig))).astype(bf16)
                x = x_low.astype(f32)
                mats = []
                for h in (2 * pair, 2 * pair + 1):
                    gap = cum[:, h : h + 1] - source_row[h : h + 1, :]
                    mats.append((jnp.exp2(gap + causal) * scores).astype(bf16))
                x_a, x_b = split_pair(x_low)
                mixed = dot_nn(jnp.concatenate(mats, axis=1), jnp.concatenate([x_a, x_b], axis=0))
                mixed = mixed + across[:, lanes] * expand(entry, pair)
                mixed = mixed + expand(head_ref[2:3, :], pair) * x
                mixed_ref[here, lanes] = mixed
                gate = gate_ref[here, lanes].astype(f32)
                gated = mixed * (gate * sigmoid(gate))
                gated_gain = gated * conv_ref[5:6, lanes]
                low_buf[here, lanes] = gated_gain.astype(bf16)
                square = square + gated * gated
                inner_dot = inner_dot + dscaled_ref[here, lanes].astype(f32) * gated_gain
                tail_buf[:, lanes] = (x * expand(leave, pair)).astype(bf16)
            fresh = dot_tn(b_low, tail_buf[...])
            for pair in range(pairs):
                lanes = lanes_of(pair)
                state[:, lanes] = state[:, lanes] * expand(pass_on, pair) + fresh[:, lanes]
            sums_ref[0:1, here] = jnp.sum(square.T, axis=0, keepdims=True)
            sums_ref[1:2, here] = jnp.sum(inner_dot.T, axis=0, keepdims=True)
        while pending:
            pending.pop(0)()
        sums_ref[2:8, :] = jnp.zeros((6, ROWS), f32)
        part = dot_nn(low_buf[...], weights[2 * inner : 3 * inner, :]).astype(bf16)
        store_half(part, block, blocks, ends_ref[seq_count], mine_ref, other_ref)


def forward_call(place, ends, hidden, cot, stack, gain, narrow, head_rows, conv_rows, shared_rows, heads):
    rows_all, width = hidden.shape
    inner = heads * HEADDIM
    blocks = rows_all // ROWS

    def ahead(columns):
        return pl.BlockSpec((ROWS, columns), lambda i, *_: (jnp.minimum(i, blocks - 1), 0))

    def rows(columns):
        return pl.BlockSpec((ROWS, columns), lambda i, *_: (jnp.maximum(i - 1, 0), 0))

    whole = pl.BlockSpec(memory_space=pltpu.VMEM)
    columns = [(5 * inner + 6 * LANES, bf16), (inner + LANES, f32)]
    out_shape = [
        jax.ShapeDtypeStruct((rows_all, width), bf16),
        *[jax.ShapeDtypeStruct((rows_all, count), kind) for count, kind in columns],
        jax.ShapeDtypeStruct((rows_all // SUB, LANES, inner), bf16),
        jax.ShapeDtypeStruct((8, rows_all), f32),
        jax.ShapeDtypeStruct((rows_all // 2, width), bf16),
        jax.ShapeDtypeStruct((rows_all // 2, width), bf16),
    ]
    out_specs = [
        ahead(width),
        *[rows(count) for count, _ in columns],
        pl.BlockSpec((ROWS // SUB, LANES, inner), lambda i, *_: (jnp.maximum(i - 1, 0), 0, 0)),
        pl.BlockSpec((8, ROWS), lambda i, *_: (0, jnp.maximum(i - 1, 0))),
        *half_specs(width, blocks, ends.shape[0] - 1, lambda i: jnp.maximum(i - 1, 0)),
    ]
    return pl.pallas_call(
        functools.partial(forward_kernel, heads, ends.shape[0] - 1, rows_all),
        grid_spec=pltpu.PrefetchScalarGridSpec(
            num_scalar_prefetch=2,
            grid=(blocks + 1,),
            in_specs=[
                ahead(width), ahead(width), pl.BlockSpec(memory_space=pl.ANY), whole, whole, whole, whole, whole,
            ],
            out_specs=out_specs,
            scratch_shapes=[
                pltpu.VMEM((3 * inner, width), bf16),
                pltpu.SemaphoreType.DMA((3 * heads,)),
                pltpu.VMEM((ROWS + 8, inner), f32),
                pltpu.VMEM((ROWS + 8, 2 * LANES), f32),
                pltpu.VMEM((ROWS, inner), bf16),
                pltpu.VMEM((ROWS, inner), bf16),
                pltpu.VMEM((ROWS, inner), bf16),
                pltpu.VMEM((ROWS, NARROW), f32),
                pltpu.VMEM((LANES, inner), f32),
                pltpu.VMEM((ROWS, inner), bf16),
                pltpu.VMEM((SUB, inner), bf16),
                pltpu.VMEM((SUB, inner), f32),
            ],
        ),
        out_shape=out_shape,
        compiler_params=pltpu.CompilerParams(
            dimension_semantics=("arbitrary",), vmem_limit_bytes=56 * 2**20
        ),
        cost_estimate=pl.CostEstimate(
            flops=2 * rows_all * width * (4 * inner + NARROW), bytes_accessed=60 * 2**20, transcendentals=0
        ),
        name="mixer_forward",
    )(place, ends, hidden, cot, stack, gain, narrow, head_rows, conv_rows, shared_rows)


def backward_kernel(
    heads, seq_count, rows_all, inner_all,
    place_ref, ends_ref,
    hidden_ref, low_ref, high_ref, state_ref, sums_ref,
    stack_ref, narrow_ref, gain_ref, head_ref, conv_ref, shared_ref,
    dboth_ref, scaled_ref, mine_ref, other_ref, mine_narrow_ref, other_narrow_ref, extra_ref,
    weights, sems, du_buf, dshared_buf, dstate, state_after, from_state, terms, source_terms, tail_buf,
    entry_buf, dnarrow_buf, last_both, last_narrow, dn_buf, conv_grad, shared_grad, head_grad, skip_grad,
    gain_grad, narrow_grad_ref,
):
    gate_ref, input_ref, x_ref, slope_ref, dscaled_ref, shared_in_ref, bc_ref, bc_slope_ref, mixed_ref, step_ref = (
        saved_views(low_ref, high_ref, heads * HEADDIM)
    )
    turn = pl.program_id(0)
    blocks = pl.num_programs(0) - 1
    block = blocks - 1 - turn
    inner = heads * HEADDIM
    pairs = heads // 2
    width = hidden_ref.shape[1]
    wide = 2 * LANES

    @pl.when(turn == 0)
    def _():
        copies = load_weights(stack_ref, place_ref, weights, sems, 0, 2 * heads)
        du_buf[ROWS:, :] = jnp.zeros((8, inner), f32)
        dshared_buf[ROWS:, :] = jnp.zeros((8, 2 * LANES), f32)
        for ref in (
            dstate, state_after, last_both, last_narrow, conv_grad, shared_grad, head_grad, skip_grad,
            gain_grad, narrow_grad_ref,
        ):
            ref[...] = jnp.zeros_like(ref)
        for copy in copies:
            copy.wait()

    def row_units():
        hidden = hidden_ref[...].astype(f32)
        inv_rms = lax.rsqrt(jnp.mean(hidden * hidden, axis=1, keepdims=True) + norm_eps)

        narrow_turned = last_narrow[...].T

        def one(at):
            columns = slice(at, at + wide)

            def unit():
                part = dot_nn(last_both[...], weights[:, columns])
                part = part + dot_nt(last_narrow[...], narrow_ref[columns, :])
                dn_buf[:, columns] = part.astype(bf16)
                unit_rows = hidden_ref[:, columns].astype(f32) * inv_rms
                gain_grad[:, columns] += fold_rows(part * unit_rows)
                normed = (unit_rows * gain_ref[0:1, columns]).astype(bf16)
                narrow_grad_ref[:, columns] += dot_nn(narrow_turned, normed)

            return unit

        return [one(at) for at in range(0, width, wide)]

    def finish_rows():
        store_half(dn_buf[...], block + 1, blocks, ends_ref[seq_count], mine_ref, other_ref)

    @pl.when(turn < blocks)
    def _():
        pending = row_units()
        reduce_heads = (iota((inner, LANES), 0) // HEADDIM == iota((inner, LANES), 1)).astype(bf16)
        first_row = block * ROWS
        kept = []
        for sub in reversed(range(ROWS // SUB)):
            first = sub * SUB
            here = slice(first, first + SUB)
            base = first_row + first
            row_at, col_at, same, carried, tail_same, through = block_terms(base, ends_ref, seq_count)
            causal = jnp.where(same & (row_at <= col_at), 0.0, far_below).astype(f32)
            b_low, c_low = bc_ref[here, 0:LANES], bc_ref[here, LANES : 2 * LANES]
            shifted, step, decay, cum, source = step_terms(step_ref[here, :], head_ref)
            kept.append((here, shifted, step, decay))
            cum_row = cum.T
            scores = dot_nt(b_low, c_low)
            cum_last = cum[SUB - 1 : SUB, :]
            entry = jnp.exp2(cum) * carried
            leave = jnp.exp2(cum_last - source) * tail_same
            pass_on = jnp.exp2(cum_last) * through
            inv_row = lax.rsqrt(sums_ref[0:1, here] * (1.0 / inner_all) + norm_eps)
            fix_row = inv_row * inv_row * inv_row * sums_ref[1:2, here] * (1.0 / inner_all)
            inv = jnp.broadcast_to(inv_row, (SUB, SUB)).T
            fix = jnp.broadcast_to(fix_row, (SUB, SUB)).T
            dstate_low = dstate[...].astype(bf16)
            from_state[...] = dot_nn(b_low, dstate_low)
            dscores = jnp.zeros((SUB, SUB), f32)
            for pair in range(pairs):
                if pending and pair % 2 == 1:
                    pending.pop(0)()
                lanes = lanes_of(pair)
                x_low = x_ref[here, lanes]
                x = x_low.astype(f32)
                slope = slope_ref[here, lanes].astype(f32)
                gate = gate_ref[here, lanes].astype(f32)
                gate_sig = sigmoid(gate)
                gate_silu = gate * gate_sig
                mixed = mixed_ref[here, lanes]
                gated = mixed * gate_silu
                gain = conv_ref[5:6, lanes]
                dscaled = dscaled_ref[here, lanes].astype(f32)
                normal = gated * inv
                scaled_ref[here, lanes] = (normal * gain).astype(bf16)
                conv_grad[5, :, lanes] += fold_rows(dscaled * normal)
                dgated = inv * (dscaled * gain) - gated * fix
                dgate = dgated * mixed * (gate_sig * (1.0 + gate * (1.0 - gate_sig)))
                dboth_ref[here, lanes] = dgate.astype(bf16)
                dmixed = dgated * gate_silu
                dy_low = dmixed.astype(bf16)
                dy = dy_low.astype(f32)
                skip = expand(head_ref[2:3, :], pair)
                skip_grad[:, lanes] += fold_rows(dmixed * x)
                x_parts = split_pair(x_low)
                dy_parts = split_pair(dy_low)
                mats = []
                for k in range(2):
                    h = 2 * pair + k
                    gap = cum_row[h : h + 1, :] - source[:, h : h + 1]
                    decays = jnp.exp2(gap + causal)
                    mats.append((decays * scores).astype(bf16))
                    dscores = dscores + dot_nt(x_parts[k], dy_low) * decays
                dx = dot_nn(jnp.concatenate(mats, axis=1), jnp.concatenate(dy_parts, axis=0))
                leave_here = expand(leave, pair)
                dx = dx + leave_here * from_state[:, lanes]
                source_term = x * dx
                source_terms[here, lanes] = source_term
                terms[here, lanes] = dy * (mixed - skip * x) - source_term
                tail_buf[:, lanes] = (x * leave_here).astype(bf16)
                entry_buf[:, lanes] = (dy * expand(entry, pair)).astype(bf16)
                du_buf[here, lanes] = (dx + skip * dmixed) * slope
            state_low = state_ref[sub]
            dscores_low = dscores.astype(bf16)
            db = dot_nn(dscores_low, c_low) + dot_nt(tail_buf[...], dstate_low)
            dc = dot_tn(dscores_low, b_low) + dot_nt(entry_buf[...], state_low)
            dshared_buf[here, 0:LANES] = db * bc_slope_ref[here, 0:LANES].astype(f32)
            dshared_buf[here, LANES:wide] = dc * bc_slope_ref[here, LANES:wide].astype(f32)
            at_end = jnp.sum(dstate[...] * state_after[...].astype(f32), axis=0, keepdims=True)
            terms[first + SUB - 1 : first + SUB, :] += at_end
            state_after[...] = state_low
            fresh = dot_tn(c_low, entry_buf[...])
            for pair in range(pairs):
                lanes = lanes_of(pair)
                dstate[:, lanes] = dstate[:, lanes] * expand(pass_on, pair) + fresh[:, lanes]
        while pending:
            pending.pop(0)()

        both = jnp.concatenate([terms[...], source_terms[...]], axis=0)
        high = both.astype(bf16)
        low = (both - high.astype(f32)).astype(bf16)
        reduced = dot_nn(high, reduce_heads) + dot_nn(low, reduce_heads)
        upper = (iota((SUB, SUB), 0) <= iota((SUB, SUB), 1)).astype(bf16)

        for sub in range(ROWS // SUB):
            first = sub * SUB
            here = slice(first, first + SUB)
            row_at = first_row + first + iota((SUB, LANES), 0)
            ahead = [shift_mask(row_at, k, ends_ref, seq_count, rows_all) for k in (1, 2, 3)]
            groups = [(pair, True) for pair in range(pairs)] + [(0, False), (1, False)]
            for group, is_wide in groups:
                lanes = lanes_of(group)
                grads, held = (du_buf, input_ref) if is_wide else (dshared_buf, shared_in_ref)
                taps = conv_ref[:, lanes] if is_wide else shared_ref[:, lanes]
                sums = conv_grad if is_wide else shared_grad
                du = grads[here, lanes]
                v = held[here, lanes].astype(f32)
                dv = taps[3:4, :] * du
                sums[3, :, lanes] += fold_rows(du * v)
                sums[4, :, lanes] += fold_rows(du)
                for k in (1, 2, 3):
                    moved = grads[first + k : first + k + SUB, lanes] * ahead[k - 1]
                    dv = dv + taps[3 - k : 4 - k, :] * moved
                    sums[3 - k, :, lanes] += fold_rows(moved * v)
                if is_wide:
                    dboth_ref[here, inner + group * LANES : inner + (group + 1) * LANES] = dv.astype(bf16)
                else:
                    dnarrow_buf[here, lanes] = dv.astype(bf16)
        for here, shifted, step, decay in kept:
            dcum = reduced[here]
            from_source = reduced[ROWS + here.start : ROWS + here.stop]
            dlog = dot_pieces(upper, dcum)
            sig = sigmoid(shifted)
            ratio = jnp.where(shifted < -15.0, 1.0, sig / step)
            dlog_decay = dlog * decay
            dstep = from_source * ratio + dlog_decay * sig
            dnarrow_buf[here, wide:NARROW] = dstep.astype(bf16)
            head_grad[0] += fold_rows(dstep)
            head_grad[1] += fold_rows(dlog_decay * step)
        du_buf[ROWS:, :] = du_buf[0:8, :]
        dshared_buf[ROWS:, :] = dshared_buf[0:8, :]

        @pl.when(turn > 0)
        def _():
            finish_rows()

        last_both[...] = dboth_ref[...]
        last_narrow[...] = dnarrow_buf[...]

    @pl.when(turn == blocks)
    def _():
        for unit in row_units():
            unit()
        finish_rows()
        extra_ref[...] = jnp.zeros_like(extra_ref)
        extra_ref[0:16, :] = narrow_grad_ref[wide : wide + 16, :]
        core = ends_ref[seq_count]
        for k in range(2):
            near = pl.multiple_of((2 * k + core) * HEADDIM, HEADDIM)
            far = pl.multiple_of((2 * k + 1 - core) * HEADDIM, HEADDIM)
            mine_narrow_ref[k] = narrow_grad_ref[pl.ds(near, HEADDIM), :]
            other_narrow_ref[k] = narrow_grad_ref[pl.ds(far, HEADDIM), :]
        per_line = width // inner

        def total(values):
            return jnp.sum(values, axis=0, keepdims=True)

        for k in range(6):
            at = (k % per_line) * inner
            row = 16 + k // per_line
            extra_ref[row : row + 1, at : at + inner] = total(conv_grad[k])
        extra_ref[GAIN_ROW : GAIN_ROW + 1, :] = total(gain_grad[...])
        for k in range(5):
            extra_ref[SHARED_ROW : SHARED_ROW + 1, wide * k : wide * (k + 1)] = total(shared_grad[k])
        for k in range(2):
            extra_ref[HEAD_ROW + k : HEAD_ROW + k + 1, 0:LANES] = total(head_grad[k])
        reduce_all = (iota((inner, LANES), 0) // HEADDIM == iota((inner, LANES), 1)).astype(f32)
        skip_sum = dot_nn(skip_grad[...], reduce_all, exact_mode)
        extra_ref[HEAD_ROW + 2 : HEAD_ROW + 3, 0:LANES] = total(skip_sum)


def backward_call(
    place, ends, hidden, saved, sums, stack, narrow, gain, head_rows, conv_rows, shared_rows, heads,
    inner_all, extra_rows,
):
    rows_all, width = hidden.shape
    inner = heads * HEADDIM
    blocks = rows_all // ROWS

    def rows(columns):
        return pl.BlockSpec((ROWS, columns), lambda i, *_: (jnp.maximum(blocks - 1 - i, 0), 0))

    def behind(i):
        return jnp.minimum(blocks - i, blocks - 1)

    whole = pl.BlockSpec(memory_space=pltpu.VMEM)
    out_shape = [
        jax.ShapeDtypeStruct((rows_all, 2 * inner), bf16),
        jax.ShapeDtypeStruct((rows_all, inner), bf16),
        jax.ShapeDtypeStruct((rows_all // 2, width), bf16),
        jax.ShapeDtypeStruct((rows_all // 2, width), bf16),
        jax.ShapeDtypeStruct((2, HEADDIM, width), f32),
        jax.ShapeDtypeStruct((2, HEADDIM, width), f32),
        jax.ShapeDtypeStruct((extra_rows, width), f32),
    ]
    out_specs = [
        rows(2 * inner), rows(inner),
        *half_specs(width, blocks, ends.shape[0] - 1, behind),
        whole, whole, whole,
    ]
    return pl.pallas_call(
        functools.partial(backward_kernel, heads, ends.shape[0] - 1, rows_all, inner_all),
        grid_spec=pltpu.PrefetchScalarGridSpec(
            num_scalar_prefetch=2,
            grid=(blocks + 1,),
            in_specs=[
                pl.BlockSpec((ROWS, width), lambda i, *_: (behind(i), 0)),
                *[rows(array.shape[1]) for array in saved[:-1]],
                pl.BlockSpec(
                    (ROWS // SUB, LANES, inner), lambda i, *_: (jnp.maximum(blocks - 1 - i, 0), 0, 0)
                ),
                pl.BlockSpec((8, ROWS), lambda i, *_: (0, jnp.maximum(blocks - 1 - i, 0))),
                pl.BlockSpec(memory_space=pl.ANY), whole, whole, whole, whole, whole,
            ],
            out_specs=out_specs,
            scratch_shapes=[
                pltpu.VMEM((2 * inner, width), bf16),
                pltpu.SemaphoreType.DMA((2 * heads,)),
                pltpu.VMEM((ROWS + 8, inner), f32),
                pltpu.VMEM((ROWS + 8, 2 * LANES), f32),
                pltpu.VMEM((LANES, inner), f32),
                pltpu.VMEM((LANES, inner), bf16),
                pltpu.VMEM((SUB, inner), f32),
                pltpu.VMEM((ROWS, inner), f32),
                pltpu.VMEM((ROWS, inner), f32),
                pltpu.VMEM((SUB, inner), bf16),
                pltpu.VMEM((SUB, inner), bf16),
                pltpu.VMEM((ROWS, NARROW), bf16),
                pltpu.VMEM((ROWS, 2 * inner), bf16),
                pltpu.VMEM((ROWS, NARROW), bf16),
                pltpu.VMEM((ROWS, width), bf16),
                pltpu.VMEM((6, 8, inner), f32),
                pltpu.VMEM((5, 8, 2 * LANES), f32),
                pltpu.VMEM((2, 8, LANES), f32),
                pltpu.VMEM((8, inner), f32),
                pltpu.VMEM((8, width), f32),
                pltpu.VMEM((NARROW, width), f32),
            ],
        ),
        out_shape=out_shape,
        compiler_params=pltpu.CompilerParams(
            dimension_semantics=("arbitrary",), vmem_limit_bytes=56 * 2**20
        ),
        cost_estimate=pl.CostEstimate(
            flops=4 * rows_all * width * (2 * inner + NARROW), bytes_accessed=60 * 2**20, transcendentals=0
        ),
        name="mixer_backward",
    )(place, ends, hidden, *saved, sums, stack, narrow, gain, head_rows, conv_rows, shared_rows)


def grads_kernel(
    first_matrix, count, seq_count, clear, mask_right, place_ref, ends_ref, free_ref, left_ref, right_ref,
    *rest,
):
    out_ref, held, sems, free_sems = rest[-4:]
    chunk = pl.program_id(0)
    width = right_ref.shape[1]
    right = right_ref[...]
    if mask_right:
        valid = iota(right.shape, 0) < ends_ref[seq_count - 1]
        right = jnp.where(valid, right.astype(f32), 0.0).astype(bf16)
    held[0 : count * HEADDIM, :] = dot_tn(left_ref[...], right).astype(bf16)
    columns = pl.ds(pl.multiple_of(chunk * width, width), width)
    copies = [
        pltpu.make_async_copy(
            held.at[pl.ds(m * HEADDIM, HEADDIM), :],
            out_ref.at[place_ref[first_matrix + m], :, columns],
            sems.at[m],
        )
        for m in range(count)
    ]
    for copy in copies:
        copy.start()
    if clear:
        held[count * HEADDIM :, :] = jnp.zeros((HEADDIM, width), bf16)

        def clear_copy(s):
            return pltpu.make_async_copy(
                held.at[pl.ds(count * HEADDIM, HEADDIM), :], out_ref.at[s, :, columns], free_sems.at[s]
            )

        for s in range(out_ref.shape[0]):

            @pl.when(free_ref[s] > 0)
            def _(s=s):
                clear_copy(s).start()

        for s in range(out_ref.shape[0]):

            @pl.when(free_ref[s] > 0)
            def _(s=s):
                clear_copy(s).wait()

    for copy in copies:
        copy.wait()


def grads_call(place, ends, free, left, right, first_matrix, mask_right, into):
    rows_all, width = right.shape
    slots = free.shape[0]
    count = left.shape[1] // HEADDIM
    clear = into is None
    held = pl.BlockSpec(memory_space=pl.ANY)
    return pl.pallas_call(
        functools.partial(grads_kernel, first_matrix, count, ends.shape[0] - 1, clear, mask_right),
        grid_spec=pltpu.PrefetchScalarGridSpec(
            num_scalar_prefetch=3,
            grid=(width // CHUNK,),
            in_specs=[
                pl.BlockSpec(left.shape, lambda i, *_: (0, 0), pipeline_mode=pl.Buffered(1)),
                pl.BlockSpec((rows_all, CHUNK), lambda i, *_: (0, i)),
            ]
            + ([] if clear else [held]),
            out_specs=held,
            scratch_shapes=[
                pltpu.VMEM(((count + 1) * HEADDIM, CHUNK), bf16),
                pltpu.SemaphoreType.DMA((count,)),
                pltpu.SemaphoreType.DMA((slots,)),
            ],
        ),
        out_shape=jax.ShapeDtypeStruct((slots, HEADDIM, width), bf16),
        input_output_aliases={} if clear else {5: 0},
        compiler_params=pltpu.CompilerParams(
            dimension_semantics=("arbitrary",), vmem_limit_bytes=56 * 2**20
        ),
        cost_estimate=pl.CostEstimate(
            flops=2 * rows_all * width * left.shape[1], bytes_accessed=30 * 2**20, transcendentals=0
        ),
        name="weight_grads",
    )(place, ends, free, left, right, *([] if clear else [into]))


def exchange_kernel(
    sums_ref, mine_ref, other_ref, total_ref, near_ref, sums_in, part_in, mine_in, sum_sems, part_sems, mine_sems
):
    here = lax.axis_index("dp")
    tensor = lax.axis_index("tensor")
    peers = [(here, (tensor + k) % 4) for k in range(1, 4)]
    other_core = (here, tensor + 1 - 2 * (tensor % 2))
    rows = mine_ref.shape[0]
    greet([(peer, None) for peer in peers])
    parts = [pl.ds(k * ROWS, ROWS) for k in range(rows // ROWS)]

    def part_copy(k):
        return remote(
            other_ref.at[parts[k]], part_in.at[parts[k]], part_sems.at[0, k], part_sems.at[1, k], other_core
        )

    def sum_copy(k):
        return remote(
            sums_ref.at[0:2], sums_in.at[tensor], sum_sems.at[0, k], sum_sems.at[1, k], peers[k]
        )

    def mine_copy(k):
        return pltpu.make_async_copy(mine_ref.at[parts[k]], mine_in.at[parts[k]], mine_sems.at[k])

    for k in range(3):
        sum_copy(k).start()
    for k in range(len(parts)):
        part_copy(k).start()
    for k in range(len(parts)):
        mine_copy(k).start()
    for k in range(3):
        sum_copy(k).wait()
    total = jnp.zeros((2, sums_ref.shape[1]), f32)
    for t in range(4):
        total = total + jnp.where(tensor == t, sums_ref[0:2, :], sums_in[t])
    total_ref[0:2, :] = total
    total_ref[2:8, :] = jnp.zeros((6, sums_ref.shape[1]), f32)
    for k in range(len(parts)):
        mine_copy(k).wait()
        part_copy(k).wait()
        here_rows = parts[k]
        near_ref[here_rows, :] = (
            mine_in[here_rows, :].astype(f32) + part_in[here_rows, :].astype(f32)
        ).astype(bf16)


def exchange_call(sums, mine, other):
    rows, width = mine.shape
    spec = pl.BlockSpec(memory_space=pltpu.VMEM)
    sems = pltpu.SemaphoreType.DMA
    return pl.pallas_call(
        exchange_kernel,
        in_specs=[spec] + [pl.BlockSpec(memory_space=pltpu.HBM)] * 2,
        out_specs=[spec] * 2,
        out_shape=[jax.ShapeDtypeStruct(sums.shape, f32), jax.ShapeDtypeStruct(mine.shape, bf16)],
        scratch_shapes=[
            pltpu.VMEM((4, 2, sums.shape[1]), f32), pltpu.VMEM((rows, width), bf16),
            pltpu.VMEM((rows, width), bf16),
            sems((2, 3)), sems((2, rows // ROWS)), sems((rows // ROWS,)),
        ],
        compiler_params=pltpu.CompilerParams(
            collective_id=2, has_side_effects=True, vmem_limit_bytes=40 * 2**20
        ),
        name="exchange_sums",
    )(sums, mine, other)


def branch_kernel(inner_all, seq_count, ends_ref, near_ref, far_ref, hidden_ref, sums_ref, full_ref, half_ref):
    width = hidden_ref.shape[1]
    blocks = pl.num_programs(0)
    first_row = (ends_ref[seq_count] * blocks + pl.program_id(0)) * HALF_ROWS
    inv_row = lax.rsqrt(sums_ref[0:1, :] * (1.0 / inner_all) + norm_eps)
    inv = jnp.broadcast_to(inv_row, (LANES, HALF_ROWS)).T
    row_at = first_row + iota((HALF_ROWS, LANES), 0)
    valid = jnp.where(row_at < ends_ref[seq_count - 1], 1.0, 0.0).astype(f32)
    for group in range(width // LANES):
        lanes = lanes_of(group)
        branch = (near_ref[:, lanes].astype(f32) + far_ref[:, lanes].astype(f32)) * inv
        result = ((hidden_ref[:, lanes].astype(f32) + branch) * valid).astype(bf16)
        full_ref[:, lanes] = result
        half_ref[:, lanes] = result


def input_kernel(seq_count, ends_ref, near_ref, far_ref, hidden_ref, cot_ref, gain_ref, full_ref, half_ref):
    width = hidden_ref.shape[1]
    blocks = pl.num_programs(0)
    first_row = (ends_ref[seq_count] * blocks + pl.program_id(0)) * HALF_ROWS
    hidden = hidden_ref[...].astype(f32)
    inv_rms = lax.rsqrt(jnp.mean(hidden * hidden, axis=1, keepdims=True) + norm_eps)
    gain_part = (near_ref[...].astype(f32) + far_ref[...].astype(f32)) * gain_ref[0:1, :]
    fix = inv_rms * inv_rms * inv_rms * (jnp.sum(gain_part * hidden, axis=1, keepdims=True) / width)
    row_at = first_row + iota(hidden.shape, 0)
    cot = jnp.where(row_at < ends_ref[seq_count - 1], cot_ref[...].astype(f32), 0.0)
    result = (inv_rms * gain_part - hidden * fix + cot).astype(bf16)
    full_ref[...] = result
    half_ref[...] = result


def half_call(kernel, name, ends, halves, fulls, wholes):
    rows, width = halves[0].shape
    seq_count = ends.shape[0] - 1
    blocks = rows // HALF_ROWS

    def in_full(i, ends):
        return (ends[seq_count] * blocks + i, 0)

    own = pl.BlockSpec((HALF_ROWS, width), lambda i, ends: (i, 0))
    full = pl.BlockSpec((HALF_ROWS, width), in_full)
    return pl.pallas_call(
        kernel,
        grid_spec=pltpu.PrefetchScalarGridSpec(
            num_scalar_prefetch=1,
            grid=(blocks,),
            in_specs=[own] * len(halves) + [full] * len(fulls) + wholes[1],
            out_specs=[full, own],
        ),
        out_shape=[
            jax.ShapeDtypeStruct((2 * rows, width), bf16),
            jax.ShapeDtypeStruct((rows, width), bf16),
        ],
        compiler_params=pltpu.CompilerParams(
            dimension_semantics=("arbitrary",), vmem_limit_bytes=40 * 2**20
        ),
        cost_estimate=pl.CostEstimate(flops=0, bytes_accessed=16 * 2**20, transcendentals=0),
        name=name,
    )(ends, *halves, *fulls, *wholes[0])


def remote(src, dst, send_sem, recv_sem, target):
    return pltpu.make_async_remote_copy(
        src_ref=src,
        dst_ref=dst,
        send_sem=send_sem,
        recv_sem=recv_sem,
        device_id=target,
        device_id_type=pl.DeviceIdType.MESH,
    )


def greet(targets):
    barrier = pltpu.get_barrier_semaphore()
    for target, condition in targets:
        if condition is None:
            pl.semaphore_signal(barrier, inc=1, device_id=target, device_id_type=pl.DeviceIdType.MESH)
        else:

            @pl.when(condition)
            def _(target=target):
                pl.semaphore_signal(
                    barrier, inc=1, device_id=target, device_id_type=pl.DeviceIdType.MESH
                )

    peers = sum(1 if condition is None else condition.astype(jnp.int32) for _, condition in targets)
    pl.semaphore_wait(barrier, peers)


def gather_kernel(
    lines, own_ref, out_ref, local_sem, x_send, x_recv, up_send, up_recv, down_send, down_recv
):
    here = lax.axis_index("dp")
    tensor = lax.axis_index("tensor")
    line, side = here // 2, here % 2
    partner = here + 1 - 2 * side
    slots = own_ref.shape[0]
    most = slots - 1
    has_up, has_down = line < lines - 1, line > 0
    across, above, below = (partner, tensor), (here + 2, tensor), (here - 2, tensor)

    greet([(across, None), (above, has_up), (below, has_down)])
    local = pltpu.make_async_copy(own_ref, out_ref.at[pl.ds(here * slots, slots)], local_sem)
    local.start()
    order = [most] + list(range(min(2, most))) + [slots] + list(range(min(2, most), most))

    def place(at, part):
        device = 2 * at + 1 - side if part == slots else 2 * at + side
        return device * slots + min(part, most)

    def line_copy(step, at, part, upward):
        own = step == 0 and part < slots
        to = out_ref.at[place(at, part)]
        src = own_ref.at[part] if own else to
        if upward:
            return remote(src, to, up_send.at[step, part], up_recv.at[step, part], above)
        return remote(src, to, down_send.at[step, part], down_recv.at[step, part], below)

    def x_copy(device, index, part, own=False):
        to = out_ref.at[device * slots + part]
        return remote(
            own_ref.at[part] if own else to, to, x_send.at[index, part], x_recv.at[index, part], across
        )

    x_copy(here, 0, most, True).start()
    for part in order:
        if part == slots:
            x_copy(partner, 0, most).wait_recv()

        @pl.when(has_up)
        def _(part=part):
            line_copy(0, line, part, True).start()

        @pl.when(has_down)
        def _(part=part):
            line_copy(0, line, part, False).start()

        if part < most:
            x_copy(here, 0, part, True).start()

    for k in range(1, lines):
        for part in order:

            @pl.when(line >= k)
            def _(k=k, part=part):
                line_copy(k - 1, line - k, part, True).wait_recv()
                if k < lines - 1:

                    @pl.when(has_up)
                    def _():
                        line_copy(k, line - k, part, True).start()

                if part < most:
                    x_copy(2 * (line - k) + side, k, part).start()

            @pl.when(line + k < lines)
            def _(k=k, part=part):
                line_copy(k - 1, line + k, part, False).wait_recv()
                if k < lines - 1:

                    @pl.when(has_down)
                    def _():
                        line_copy(k, line + k, part, False).start()

                if part < most:
                    x_copy(2 * (line + k) + side, lines - 1 + k, part).start()

    local.wait()
    x_copy(partner, 0, most).wait_send()
    for part in range(most):
        x_copy(partner, 0, part).wait()
    for k in range(1, lines):
        for part in range(most):

            @pl.when(line >= k)
            def _(k=k, part=part):
                x_copy(2 * (line - k) + 1 - side, k, part).wait()

            @pl.when(line + k < lines)
            def _(k=k, part=part):
                x_copy(2 * (line + k) + 1 - side, lines - 1 + k, part).wait()

    for k in range(lines - 1):
        for part in order:

            @pl.when(has_up & (line >= k))
            def _(k=k, part=part):
                line_copy(k, line - k, part, True).wait_send()

            @pl.when(has_down & (line + k < lines))
            def _(k=k, part=part):
                line_copy(k, line + k, part, False).wait_send()


def gather_call(own, dp_size):
    slots, side, width = own.shape
    lines = dp_size // 2
    step_sems = pltpu.SemaphoreType.DMA((lines - 1, slots + 1))
    x_sems = pltpu.SemaphoreType.DMA((2 * lines - 1, slots))
    return pl.pallas_call(
        functools.partial(gather_kernel, lines),
        in_specs=[pl.BlockSpec(memory_space=pl.ANY)],
        out_specs=pl.BlockSpec(memory_space=pl.ANY),
        out_shape=jax.ShapeDtypeStruct((slots * dp_size, side, width), own.dtype),
        scratch_shapes=[
            pltpu.SemaphoreType.DMA, x_sems, x_sems, step_sems, step_sems, step_sems, step_sems,
        ],
        compiler_params=pltpu.CompilerParams(collective_id=0, has_side_effects=True),
        name="gather_weights",
    )(own)


def reduce_kernel(
    lines,
    grads_ref, near_ref, far_ref, extra_ref, owned_ref, totals_ref,
    grads, load_sems, x_in, up_in, down_in, last_out, last_in, halves, half_in, group_in, group_out, group_back,
    x_send, x_recv, up_send, up_recv, down_send, down_recv, last_sems, small_sems, group_sems, back_sems,
):
    here = lax.axis_index("dp")
    tensor = lax.axis_index("tensor")
    line, side = here // 2, here % 2
    core = tensor % 2
    slots = owned_ref.shape[0]
    most = slots - 1
    width = near_ref.shape[1]
    half = width // 2
    group = halves.shape[1] // lines
    has_up, has_down = line < lines - 1, line > 0
    across = (here + 1 - 2 * side, tensor)
    above, below = (here + 2, tensor), (here - 2, tensor)
    other_core = (here, tensor + 1 - 2 * core)
    other_chip = (here, (tensor + 2) % 4)
    on_line = [(2 * ((line + k) % lines) + side, tensor) for k in range(1, lines)]

    greet([(target, None) for target in [across, other_core, other_chip] + on_line])

    def add(*parts):
        total = parts[0].astype(f32)
        for part in parts[1:]:
            total = total + part.astype(f32)
        return total

    half_copy = remote(halves.at[1 - side], half_in, small_sems.at[0, 0], small_sems.at[1, 0], across)

    def group_copy(k):
        to = (line + k) % lines
        rows = pl.ds(pl.multiple_of(to * group, group), group)
        return remote(
            halves.at[side, rows], group_in.at[k - 1], group_sems.at[0, k - 1], group_sems.at[1, k - 1],
            on_line[k - 1],
        )

    def back_copy(k):
        return remote(
            group_out, group_back.at[k - 1], back_sems.at[0, k - 1], back_sems.at[1, k - 1], on_line[k - 1]
        )

    total_half = remote(
        totals_ref.at[tensor, side], totals_ref.at[tensor, side], small_sems.at[0, 1], small_sems.at[1, 1],
        across,
    )
    total_chip = remote(
        totals_ref.at[tensor], totals_ref.at[tensor], small_sems.at[0, 2], small_sems.at[1, 2], other_chip
    )

    def total_core(k):
        at = core + 2 * k
        return remote(
            totals_ref.at[at], totals_ref.at[at], small_sems.at[0, 3 + k], small_sems.at[1, 3 + k], other_core
        )

    def small_start():
        mine = near_ref[...] + far_ref[...]
        rest = extra_ref[...]
        for k in range(2):
            columns = slice(k * half, (k + 1) * half)
            halves[k, 0:HEADDIM, :] = mine[:, columns]
            halves[k, HEADDIM:, :] = rest[:, columns]
        half_copy.start()

    def small_group():
        half_copy.wait()
        halves[side] = halves[side] + half_in[...]
        for k in range(1, lines):
            group_copy(k).start()

    def small_back():
        for k in range(1, lines):
            group_copy(k).wait()
        rows = pl.ds(pl.multiple_of(line * group, group), group)
        total = halves[side, rows, :]
        for k in range(1, lines):
            total = total + group_in[k - 1]
        group_out[...] = total
        for k in range(1, lines):
            back_copy(k).start()

    def small_half():
        for k in range(1, lines):
            back_copy(k).wait()
        rows = pl.ds(pl.multiple_of(line * group, group), group)
        totals_ref[tensor, side, rows, :] = group_out[...]
        for k in range(1, lines):
            source = (line + lines - k) % lines
            rows = pl.ds(pl.multiple_of(source * group, group), group)
            totals_ref[tensor, side, rows, :] = group_back[k - 1]
        total_half.start()

    def small_chip():
        total_half.wait()
        total_chip.start()

    def small_core():
        total_chip.wait()
        for k in range(2):
            total_core(k).start()

    def small_end():
        for k in range(2):
            total_core(k).wait()

    small = [(1, small_group), (3, small_back), (5, small_half), (8, small_chip), (13, small_core)]
    events = []

    def event():
        events.append(None)
        while small and small[0][0] <= len(events):
            small.pop(0)[1]()

    def last_slot(k):
        return jnp.where(k == side, most, slots)

    loads = []
    for at in range(lines):
        loads.append(
            pltpu.make_async_copy(
                grads_ref.at[pl.ds((2 * at + side) * slots, slots)], grads.at[at, pl.ds(0, slots)],
                load_sems.at[at, 0],
            )
        )
        loads.append(
            pltpu.make_async_copy(
                grads_ref.at[pl.ds((2 * at + 1 - side) * slots + most, 1)], grads.at[at, pl.ds(slots, 1)],
                load_sems.at[at, 1],
            )
        )

    def x_copy(at, i):
        return remote(
            grads_ref.at[(2 * at + 1 - side) * slots + i], x_in.at[at, i], x_send.at[at, i], x_recv.at[at, i], across
        )

    def x_needed(turn):
        step, i = turn // most, turn % most
        if step < lines - 1:
            each_way(step, lambda at, upward: x_copy(at, i).start())
        elif step == lines - 1:
            x_copy(line, i).start()

    def line_copy(src, at, i, upward):
        if upward:
            return remote(src, up_in.at[at, i], up_send.at[at, i], up_recv.at[at, i], above)
        return remote(src, down_in.at[at, i], down_send.at[at, i], down_recv.at[at, i], below)

    def line_most(at, i, upward):
        arrived = up_in if upward else down_in
        x_copy(at, i).wait_recv()
        own = add(grads[at, i], x_in[at, i])

        @pl.when(has_down if upward else has_up)
        def _():
            line_copy(x_in.at[at, i], at, i, upward).wait_recv()
            x_in[at, i] = add(own, arrived[at, i]).astype(bf16)

        @pl.when(jnp.logical_not(has_down if upward else has_up))
        def _():
            x_in[at, i] = own.astype(bf16)

        line_copy(x_in.at[at, i], at, i, upward).start()

    def line_last(at, k, upward):
        arrived = up_in if upward else down_in
        own = grads.at[at, last_slot(k)]

        @pl.when(has_down if upward else has_up)
        def _():
            line_copy(own, at, most + k, upward).wait_recv()
            arrived[at, most + k] = add(own[...], arrived[at, most + k]).astype(bf16)
            line_copy(arrived.at[at, most + k], at, most + k, upward).start()

        @pl.when(jnp.logical_not(has_down if upward else has_up))
        def _():
            line_copy(own, at, most + k, upward).start()

    def each_way(step, work):
        @pl.when(lines - 1 - step > line)
        def _():
            work(lines - 1 - step, True)

        @pl.when(step < line)
        def _():
            work(step, False)

    small_start()
    for turn in range(AHEAD):
        x_needed(turn)
    for load in loads:
        load.start()
    for load in loads:
        load.wait()
    for step in range(lines - 1):
        for k in range(2):
            each_way(step, lambda at, upward, k=k: line_last(at, k, upward))
        event()
        for i in range(most):
            x_needed(step * most + i + AHEAD)
            each_way(step, lambda at, upward, i=i: line_most(at, i, upward))
            event()

    def gathered_last(k):
        return grads[line, last_slot(k)].astype(f32)

    owned_ref[most] = gathered_last(side)
    to_send = gathered_last(1 - side)
    last_out[...] = to_send

    @pl.when(has_down)
    def _():
        for k in range(2):
            line_copy(last_in, line, most + k, True).wait_recv()
        owned_ref[most] = owned_ref[most] + up_in[line, most + side].astype(f32)
        last_out[...] = last_out[...] + up_in[line, most + 1 - side].astype(f32)

    @pl.when(has_up)
    def _():
        for k in range(2):
            line_copy(last_in, line, most + k, False).wait_recv()
        owned_ref[most] = owned_ref[most] + down_in[line, most + side].astype(f32)
        last_out[...] = last_out[...] + down_in[line, most + 1 - side].astype(f32)

    x_in[line, most] = last_out[...].astype(bf16)
    last_copy = remote(x_in.at[line, most], last_in, last_sems.at[0], last_sems.at[1], across)
    last_copy.start()
    for turn in range((lines - 1) * most + AHEAD, lines * most):
        x_needed(turn)
    while small:
        small.pop(0)[1]()

    def finish(i, carry):
        x_copy(line, i).wait_recv()
        owned_ref[i] = add(grads[line, i], x_in[line, i])

        @pl.when(has_down)
        def _():
            line_copy(last_in, line, i, True).wait_recv()
            owned_ref[i] = owned_ref[i] + up_in[line, i].astype(f32)

        @pl.when(has_up)
        def _():
            line_copy(last_in, line, i, False).wait_recv()
            owned_ref[i] = owned_ref[i] + down_in[line, i].astype(f32)

        return carry

    lax.fori_loop(0, most, finish, 0)
    last_copy.wait()
    owned_ref[most] = owned_ref[most] + last_in[...].astype(f32)
    small_end()

    def x_sent(at):
        def one(i, carry):
            x_copy(at, i).wait_send()
            return carry

        lax.fori_loop(0, most, one, 0)

    def line_sent(at, upward):
        def one(i, carry):
            line_copy(last_in, at, i, upward).wait_send()
            return carry

        lax.fori_loop(0, slots + 1, one, 0)

    x_sent(line)
    for step in range(lines - 1):
        each_way(step, lambda at, upward: x_sent(at))
        each_way(step, line_sent)


def reduce_call(grads, near, far, extra, dp_size):
    slots_all, side, width = grads.shape
    slots = slots_all // dp_size
    lines = dp_size // 2
    small_rows = HEADDIM + extra.shape[0]
    group = small_rows // lines
    pieces = 2 * side * width * lines * (4 * slots + 3)
    spec = pl.BlockSpec(memory_space=pltpu.VMEM)
    sems = pltpu.SemaphoreType.DMA
    return pl.pallas_call(
        functools.partial(reduce_kernel, lines),
        in_specs=[pl.BlockSpec(memory_space=pltpu.HBM)] + [spec] * 3,
        out_specs=[spec] * 2,
        out_shape=[
            jax.ShapeDtypeStruct((slots, side, width), f32),
            jax.ShapeDtypeStruct((4, 2, small_rows, width // 2), f32),
        ],
        scratch_shapes=[
            pltpu.VMEM((lines, slots + 1, side, width), bf16),
            sems((lines, 2)),
            pltpu.VMEM((lines, slots, side, width), bf16),
            pltpu.VMEM((lines, slots + 1, side, width), bf16),
            pltpu.VMEM((lines, slots + 1, side, width), bf16),
            pltpu.VMEM((side, width), f32),
            pltpu.VMEM((side, width), bf16),
            pltpu.VMEM((2, small_rows, width // 2), f32),
            pltpu.VMEM((small_rows, width // 2), f32),
            pltpu.VMEM((lines - 1, group, width // 2), f32),
            pltpu.VMEM((group, width // 2), f32),
            pltpu.VMEM((lines - 1, group, width // 2), f32),
            sems((lines, slots)), sems((lines, slots)),
            sems((lines, slots + 1)), sems((lines, slots + 1)),
            sems((lines, slots + 1)), sems((lines, slots + 1)),
            sems((2,)), sems((2, 5)), sems((2, lines - 1)), sems((2, lines - 1)),
        ],
        compiler_params=pltpu.CompilerParams(
            collective_id=1, has_side_effects=True, vmem_limit_bytes=pieces + 16 * 2**20
        ),
        cost_estimate=pl.CostEstimate(flops=10**11, bytes_accessed=40 * 2**20, transcendentals=0),
        name="reduce_grads",
    )(grads, near, far, extra)


def small_rule(rate, weight, moment, gradient):
    moment_new = small_decay * moment + (1.0 - small_decay) * gradient
    return moment_new, weight - rate * moment_new


def muon_kernel(
    rate, small_rate_now,
    grad_ref, totals_ref, moment_ref, master_ref,
    state_moment, state_proj, step_moment, step_proj, gain_moment, gain, head_moment, head, conv_moment, conv,
    shared_moment, shared,
    moment_out, master_out,
    state_moment_out, state_out, step_moment_out, step_out, gain_moment_out, gain_out, head_moment_out,
    head_out, conv_moment_out, conv_out, shared_moment_out, shared_out,
):
    tensor = lax.axis_index("tensor")
    rule = functools.partial(small_rule, small_rate_now)

    def row(at, row_at):
        return jnp.concatenate(
            [totals_ref[at, k, row_at : row_at + 1, :] for k in range(2)], axis=1
        )

    def over_tensor(row_at):
        return row(0, row_at) + row(1, row_at) + row(2, row_at) + row(3, row_at)

    for k in range(2):
        parts = [
            jnp.concatenate([totals_ref[2 * k + j, c, 0:HEADDIM, :] for c in range(2)], axis=1)
            for j in range(2)
        ]
        lanes = lanes_of(k)
        state_moment_out[:, lanes], state_out[:, lanes] = rule(
            state_proj[:, lanes], state_moment[:, lanes], jnp.concatenate(parts, axis=0).T
        )
    heads = step_proj.shape[0]
    extra = HEADDIM
    own = [totals_ref[tensor, k, extra : extra + 32, :] for k in range(2)]
    step_moment_out[...], step_out[...] = rule(
        step_proj[...], step_moment[...], jnp.concatenate(own, axis=1)[0:heads]
    )
    gain_moment_out[...], gain_out[...] = rule(gain[...], gain_moment[...], over_tensor(extra + GAIN_ROW))
    head_moment_out[...], head_out[...] = rule(
        head[...], head_moment[...], own[0][HEAD_ROW : HEAD_ROW + 3, 0:heads]
    )
    inner = conv.shape[1]
    per_line = 2 * own[0].shape[1] // inner
    conv_total = jnp.concatenate(own, axis=1)
    for k in range(6):
        at = (k % per_line) * inner
        line = 16 + k // per_line
        one = slice(k, k + 1)
        conv_moment_out[one, :], conv_out[one, :] = rule(
            conv[one, :], conv_moment[one, :], conv_total[line : line + 1, at : at + inner]
        )
    shared_total = over_tensor(extra + SHARED_ROW)
    for k in range(5):
        one = slice(k, k + 1)
        shared_moment_out[one, :], shared_out[one, :] = rule(
            shared[one, :], shared_moment[one, :], shared_total[:, 2 * LANES * k : 2 * LANES * (k + 1)]
        )

    first_coef, second_coef, third_coef = schulz_coefs
    side = HEADDIM
    same = iota((side, side), 0) == iota((side, side), 1)
    eye = jnp.where(same, 1.0, 0.0).astype(f32)
    slots = grad_ref.shape[0]
    grams, totals, scales = [], [], []
    for s in range(slots):
        moment = muon_decay * moment_ref[s] + grad_ref[s].astype(f32)
        moment_out[s] = moment
        square = jnp.sum(jnp.sum(moment * moment, axis=1, keepdims=True), axis=0, keepdims=True)
        scale = 1.0 / (jnp.sqrt(square) + 1e-07)
        scaled = moment * scale
        grams.append(dot_nt(scaled, scaled, exact_mode))
        totals.append(eye)
        scales.append(scale)
    for _ in range(NS_STEPS):
        for s in range(slots):
            gram = grams[s]
            factor = (
                first_coef * eye + second_coef * gram + third_coef * dot_nn(gram, gram, exact_mode)
            )
            totals[s] = dot_nn(factor, totals[s], exact_mode)
            grams[s] = dot_nn(dot_nn(factor, gram, exact_mode), factor, exact_mode)
    for s in range(slots):
        ortho = dot_nn(totals[s], moment_out[s] * scales[s], exact_mode)
        master_out[s] = master_ref[s] - rate * ortho


def muon_call(grad, totals, moment, master, small, tokens_all):
    slots, side, width = moment.shape
    spec = pl.BlockSpec(memory_space=pltpu.VMEM)
    return pl.pallas_call(
        functools.partial(
            muon_kernel, muon_rate * math.sqrt(max(width, side)), small_rate / math.sqrt(tokens_all)
        ),
        in_specs=[spec] * (4 + len(small)),
        out_specs=[spec] * (2 + len(small)),
        out_shape=[jax.ShapeDtypeStruct(moment.shape, f32)] * 2
        + [jax.ShapeDtypeStruct(array.shape, f32) for array in small],
        compiler_params=pltpu.CompilerParams(vmem_limit_bytes=36 * 2**20),
        name="muon",
    )(grad, totals, moment, master, *small)


def pad_to(array, rows, columns):
    return jnp.pad(array, ((0, rows - array.shape[0]), (0, columns - array.shape[1])))


def swap(values, bit):
    return lax.ppermute(values, "tensor", [(t, t ^ bit) for t in range(4)])


def place_half(full, half):
    core = lax.axis_index("tensor") % 2
    return lax.dynamic_update_slice(full, swap(half, 1), ((1 - core) * half.shape[0], 0))


def per_device(
    hidden_in,
    out_grad,
    seq_lengths,
    owner_map,
    muon_master,
    muon_moment,
    state_proj,
    state_moment,
    step_proj,
    step_moment,
    norm_gain,
    gain_moment,
    head_params,
    head_moment,
    conv_params,
    conv_moment,
    state_conv,
    state_conv_moment,
):
    tok_rows, width = hidden_in.shape
    heads = step_proj.shape[1]
    inner = conv_params.shape[1]
    dp_size = lax.axis_size("dp")
    inner_all = inner * lax.axis_size("tensor")
    slots = muon_master.shape[0] * dp_size
    core = lax.axis_index("tensor") % 2
    chip = lax.axis_index("tensor") // 2
    ends = jnp.concatenate([jnp.cumsum(seq_lengths[0], dtype=jnp.int32), core[None].astype(jnp.int32)])
    seq_count = seq_lengths.shape[1]
    master = muon_master.transpose(0, 2, 1)
    moment = muon_moment.transpose(0, 2, 1)
    stack = gather_call(master.astype(bf16), dp_size)
    narrow = pad_to(jnp.concatenate([state_proj, step_proj], axis=1), width, NARROW).astype(bf16)
    gain = norm_gain[None, :]
    head_rows = pad_to(head_params, 8, LANES)
    conv_rows = pad_to(conv_params, 8, inner)
    shared_rows = pad_to(state_conv, 8, state_conv.shape[1])
    free = jnp.all(owner_map[None, :] != jnp.arange(slots, dtype=jnp.int32)[:, None], axis=1)
    free = free.astype(jnp.int32)
    group_rows = 8 * (dp_size // 2)
    extra_rows = -(-(HEADDIM + 32) // group_rows) * group_rows - HEADDIM

    normed, *saved, sums, mine, other = forward_call(
        owner_map, ends, hidden_in, out_grad, stack, gain, narrow, head_rows, conv_rows, shared_rows, heads
    )
    sums, near = exchange_call(sums, mine, other)
    far = swap(near, 2)
    dboth, scaled, mine, other, mine_narrow, other_narrow, extra = backward_call(
        owner_map, ends, hidden_in, saved, sums, stack, narrow, gain, head_rows, conv_rows, shared_rows, heads,
        inner_all, extra_rows,
    )

    got = swap(other, 1)
    got_narrow = swap(other_narrow, 1)
    far, scaled = lax.optimization_barrier((far, scaled))
    rows_spec = pl.BlockSpec((8, HALF_ROWS), lambda i, ends: (0, ends[seq_count] * (tok_rows // HALF_ROWS // 2) + i))
    block_full, block_half = half_call(
        functools.partial(branch_kernel, inner_all, seq_count), "block_out", ends, [near, far], [hidden_in],
        ([sums], [rows_spec]),
    )
    block_out = place_half(block_full, block_half)
    scaled, block_half = lax.optimization_barrier((scaled, block_half))
    slotted = grads_call(owner_map, ends, free, scaled, out_grad, 2 * heads, True, None)
    slotted, got, got_narrow = lax.optimization_barrier((slotted, got, got_narrow))
    pair = mine_narrow + got_narrow
    near_narrow = lax.dynamic_index_in_dim(pair, chip, 0, keepdims=False)
    send_narrow = lax.dynamic_index_in_dim(pair, 1 - chip, 0, keepdims=False)
    far_narrow = swap(send_narrow, 2)
    send_narrow, got = lax.optimization_barrier((send_narrow, got))
    near_grad = (mine.astype(f32) + got.astype(f32)).astype(bf16)
    far_grad = swap(near_grad, 2)
    near_grad, near_narrow, dboth = lax.optimization_barrier((near_grad, near_narrow, dboth))
    slotted = grads_call(owner_map, ends, free, dboth, normed, 0, False, slotted)
    owned, totals = reduce_call(slotted, near_narrow, far_narrow, extra, dp_size)
    owned, totals, far_grad = lax.optimization_barrier((owned, totals, far_grad))
    gain_spec = pl.BlockSpec(gain.shape, lambda i, ends: (0, 0))
    input_full, input_half = half_call(
        functools.partial(input_kernel, seq_count), "input_grad", ends, [near_grad, far_grad],
        [hidden_in, out_grad], ([gain], [gain_spec]),
    )
    input_grad = place_half(input_full, input_half)
    owned, input_half = lax.optimization_barrier((owned, input_half))
    small = [
        state_moment, state_proj, step_moment.T, step_proj.T, gain_moment[None, :], gain, head_moment,
        head_params, conv_moment, conv_params, state_conv_moment, state_conv,
    ]
    moment_new, master_new, *small_new = muon_call(owned, totals, moment, master, small, tok_rows * dp_size)
    state_moment_new, state_proj_new, step_moment_new, step_proj_new = small_new[:4]
    gain_moment_new, norm_gain_new, head_moment_new, head_params_new = small_new[4:8]
    conv_moment_new, conv_params_new, state_conv_moment_new, state_conv_new = small_new[8:]
    step_moment_new, step_proj_new = step_moment_new.T, step_proj_new.T
    gain_moment_new, norm_gain_new = gain_moment_new[0], norm_gain_new[0]
    return (
        block_out,
        input_grad,
        moment_new.transpose(0, 2, 1),
        master_new.transpose(0, 2, 1),
        state_moment_new,
        state_proj_new,
        step_moment_new,
        step_proj_new,
        gain_moment_new,
        norm_gain_new,
        head_moment_new,
        head_params_new,
        conv_moment_new,
        conv_params_new,
        state_conv_moment_new,
        state_conv_new,
    )


def solution(mesh):
    in_specs = (
        P("dp", None),
        P("dp", None),
        P("dp", None),
        P(),
        P("dp", None, "tensor"),
        P("dp", None, "tensor"),
        P(),
        P(),
        P(None, "tensor"),
        P(None, "tensor"),
        P(),
        P(),
        P(None, "tensor"),
        P(None, "tensor"),
        P(None, "tensor"),
        P(None, "tensor"),
        P(),
        P(),
    )
    out_specs = (
        P("dp", None),
        P("dp", None),
        P("dp", None, "tensor"),
        P("dp", None, "tensor"),
        P(),
        P(),
        P(None, "tensor"),
        P(None, "tensor"),
        P(),
        P(),
        P(None, "tensor"),
        P(None, "tensor"),
        P(None, "tensor"),
        P(None, "tensor"),
        P(),
        P(),
    )
    return jax.shard_map(
        per_device, mesh=mesh, in_specs=in_specs, out_specs=out_specs, check_vma=False
    )
```
